32 devices in a mesh: ctx: 8 (over y, x, core), fsdp: 4 (over z).
Axes of the slice: x: 2, y: 2, z: 4, core: 2. Of those that a mesh axis runs over, the one named last changes fastest.
Arguments:
- tokens: float32 [8, 2048, 1024], P('fsdp', 'ctx'), may hold values from -6 to 6
- segments: int32 [8, 2048], P('fsdp', 'ctx'), may hold values from 0 to 2047, as said below
- query_weight: float32 [1024, 1024], P('fsdp'), may hold values from -0.1875 to 0.1875
- query_bias: float32 [1024], P('fsdp'), may hold values from -1.75 to 1.75
- key_weight: float32 [1024, 1024], P('fsdp'), may hold values from -0.1875 to 0.1875
- value_weight: float32 [1024, 1024], P('fsdp'), may hold values from -0.1875 to 0.1875
- value_bias: float32 [1024], P('fsdp'), may hold values from -0.3125 to 0.3125
- output_weight: float32 [1024, 1024], P('fsdp'), may hold values from -2 to 2
- output_bias: float32 [1024], P('fsdp'), may hold values from -1.75 to 1.75
- first_gain: float32 [1024], P('fsdp'), may hold values from 0.5 to 1.5
- first_shift: float32 [1024], P('fsdp'), may hold values from -1.75 to 1.75
- expand_weight: float32 [1024, 4096], P('fsdp'), may hold values from -0.1875 to 0.1875
- expand_bias: float32 [4096], P('fsdp'), may hold values from -1.75 to 1.75
- reduce_weight: float32 [4096, 1024], P('fsdp'), may hold values from -0.09375 to 0.09375
- reduce_bias: float32 [1024], P('fsdp'), may hold values from -1.75 to 1.75
- second_gain: float32 [1024], P('fsdp'), may hold values from 0.5 to 1.5
- second_shift: float32 [1024], P('fsdp'), may hold values from -1.75 to 1.75
- cotangent: float32 [8, 2048, 1024], P('fsdp', 'ctx'), may hold values from -6 to 6
Outputs:
- layer_output: float32 [8, 2048, 1024], P('fsdp', 'ctx')
- grad_tokens: float32 [8, 2048, 1024], P('fsdp', 'ctx')
- grad_query_weight: float32 [1024, 1024], P('fsdp')
- grad_query_bias: float32 [1024], P('fsdp')
- grad_key_weight: float32 [1024, 1024], P('fsdp')
- grad_value_weight: float32 [1024, 1024], P('fsdp')
- grad_value_bias: float32 [1024], P('fsdp')
- grad_output_weight: float32 [1024, 1024], P('fsdp')
- grad_output_bias: float32 [1024], P('fsdp')
- grad_first_gain: float32 [1024], P('fsdp')
- grad_first_shift: float32 [1024], P('fsdp')
- grad_expand_weight: float32 [1024, 4096], P('fsdp')
- grad_expand_bias: float32 [4096], P('fsdp')
- grad_reduce_weight: float32 [4096, 1024], P('fsdp')
- grad_reduce_bias: float32 [1024], P('fsdp')
- grad_second_gain: float32 [1024], P('fsdp')
- grad_second_shift: float32 [1024], P('fsdp')
The draws below stay inside these ranges and needn't reach their ends.
Inputs may be any that keep to these rules, and one draw needn't show every extreme that they name: `segments`: A token's segment number is the position, within its sequence, of the last token of its document; it never falls along a sequence. Of the 2 sequences at each index of fsdp, one (which one varies) starts with a document of one token at position 0, followed by a document that ends within the last half of 256 positions, with at most one short document after it; in the others every document but the last holds 200 to 2000 tokens.
All inputs are finite; a program needn't handle non-finite values.
Results may differ from the reference program's by a relative error of at most 0.024.
Values may be sent and summed in bfloat16 or wider, within the bound.
No kernel may reach another device: no remote copies, remote signals or barrier semaphores. Data moves between devices by JAX's collectives and lax.ppermute only.
A program may use at most 192 MiB of HBM per device.

```python
import jax
import jax.numpy as jnp
from jax import lax

D = 1024
HEADS = 16
HEAD = 64
FF = 4096
SHARD = 256
SEQ_DEV = 2
DOC_MIN = 200
DOC_MAX = 2000
SEQS = 8
LEN = 2048


def draw_segments(key, part):
    key = jax.random.fold_in(key, 7)
    pick_key, edge_key, length_key = jax.random.split(key, 3)
    chosen = jax.random.randint(pick_key, (SEQS // SEQ_DEV,), 0, SEQ_DEV)
    spans = jnp.arange(SEQS) % SEQ_DEV == jnp.repeat(chosen, SEQ_DEV)
    half = max(SHARD // 2, 2)
    edges = jax.random.randint(edge_key, (SEQS, 2), 1, half)
    place = jnp.arange(LEN)[None, :]
    first_end = jnp.zeros((SEQS, 1), jnp.int32)
    long_end = LEN - edges[:, 1:2] - 1
    spanning = jnp.where(place <= first_end, first_end, jnp.where(place <= long_end, long_end, LEN - 1))
    count = LEN // DOC_MIN + 1
    lengths = jax.random.randint(length_key, (SEQS, count), DOC_MIN, DOC_MAX + 1)
    ends = jnp.minimum(jnp.cumsum(lengths, axis=1) - 1, LEN - 1)
    ragged = jnp.min(jnp.where(ends[:, None, :] >= place[:, :, None], ends[:, None, :], LEN - 1), axis=2)
    return jnp.where(spans[:, None], spanning, ragged).astype(jnp.int32)


def block_levels(stream_key, dims, shards, smallest, high):
    def one(position, blocks):
        draws = jax.random.uniform(jax.random.fold_in(jax.random.fold_in(stream_key, 6), position), (blocks,), jnp.float32, smallest / len(shards), high / len(shards))
        return jnp.repeat(jnp.exp(draws), dims[position] // blocks).reshape((-1,) + (1,) * (len(dims) - position - 1))

    factor_of = one(*shards[0])
    for cut in shards[1:]:
        factor_of = factor_of * one(*cut)
    return factor_of


def scatter_about(key, shape, width, reach, shards=(), dtype=jnp.bfloat16):
    loudness = block_levels(key, shape, shards, -0.22, 0.18) if shards else 1.0
    values = jax.random.normal(key, shape, jnp.float32) * width * loudness
    return jnp.minimum(jnp.maximum(values, -reach), reach).astype(dtype)


def setup_inputs(seed: int = 0) -> dict:
    arg_keys = jax.random.split(jax.random.key(seed), 19)
    return {
        "tokens": scatter_about(arg_keys[0], (SEQS, LEN, D), 1.0, 6.0, ((0, 4), (1, 8)), jnp.float32),
        "segments": draw_segments(jax.random.fold_in(arg_keys[18], 71), 0),
        "query_weight": scatter_about(arg_keys[2], (D, D), D ** -0.5, 0.1875, ((0, 4),), jnp.float32),
        "query_bias": scatter_about(arg_keys[3], (D,), 0.3, 1.75, ((0, 4),), jnp.float32),
        "key_weight": scatter_about(arg_keys[4], (D, D), D ** -0.5, 0.1875, ((0, 4),), jnp.float32),
        "value_weight": scatter_about(arg_keys[5], (D, D), D ** -0.5, 0.1875, ((0, 4),), jnp.float32),
        "value_bias": scatter_about(arg_keys[6], (D,), 0.05, 0.3125, ((0, 4),), jnp.float32),
        "output_weight": scatter_about(arg_keys[7], (D, D), 8 ** -0.5, 2.0, ((0, 4),), jnp.float32),
        "output_bias": scatter_about(arg_keys[8], (D,), 0.3, 1.75, ((0, 4),), jnp.float32),
        "first_gain": jnp.clip(1.0 + 0.1 * jax.random.normal(arg_keys[9], (D,), jnp.float32), 0.5, 1.5),
        "first_shift": scatter_about(arg_keys[10], (D,), 0.3, 1.75, ((0, 4),), jnp.float32),
        "expand_weight": scatter_about(arg_keys[11], (D, FF), D ** -0.5, 0.1875, ((0, 4),), jnp.float32),
        "expand_bias": scatter_about(arg_keys[12], (FF,), 0.3, 1.75, ((0, 4),), jnp.float32),
        "reduce_weight": scatter_about(arg_keys[13], (FF, D), FF ** -0.5, 0.09375, ((0, 4),), jnp.float32),
        "reduce_bias": scatter_about(arg_keys[14], (D,), 0.3, 1.75, ((0, 4),), jnp.float32),
        "second_gain": jnp.clip(1.0 + 0.1 * jax.random.normal(arg_keys[15], (D,), jnp.float32), 0.5, 1.5),
        "second_shift": scatter_about(arg_keys[16], (D,), 0.3, 1.75, ((0, 4),), jnp.float32),
        "cotangent": scatter_about(arg_keys[17], (SEQS, LEN, D), 1.0, 6.0, ((0, 4), (1, 8)), jnp.float32),
    }


@jax.custom_vjp
def low(v):
    return lax.optimization_barrier(v.astype(jnp.bfloat16)).astype(jnp.float32)

@jax.custom_vjp
def low_back(v):
    return v

def low_keep(v):
    return (low(v), None)

def low_pass(kept, grad):
    return (grad,)

def back_keep(v):
    return (v, None)

def back_low(kept, grad):
    return (low(grad),)
low.defvjp(low_keep, low_pass)
low_back.defvjp(back_keep, back_low)
EPS = 1e-05
NEG = -1e+30
SQRT_HALF = 0.7071067811865476

def matmul(left, right):
    return jnp.matmul(left, right, precision=lax.Precision.HIGHEST)

def layer_norm(values, gain, shift):
    mean = lax.optimization_barrier(jnp.mean(values, axis=-1, keepdims=True))
    centred = values - mean
    var = lax.optimization_barrier(jnp.mean(centred * centred, axis=-1, keepdims=True))
    return centred * lax.rsqrt(var + EPS) * gain + shift

def block_attention(query_block, seg_block, keys, values, seg_keys):
    scores = jnp.einsum('qhd,khd->hqk', query_block, keys, precision=lax.Precision.HIGHEST)
    scores = low_back(scores)
    mask = (seg_block[:, None] == seg_keys[None, :])[None]
    masked = jnp.where(mask, scores, NEG)
    top = lax.optimization_barrier(jnp.max(masked, axis=-1, keepdims=True))
    expo = jnp.exp(masked - top)
    probs = expo / lax.optimization_barrier(jnp.sum(expo, axis=-1, keepdims=True))
    return jnp.einsum('hqk,khd->qhd', low(probs), values, precision=lax.Precision.HIGHEST)

def sequence_attention(inputs):
    query, keys, values, seg = inputs
    block = min(512, LEN)
    query_blocks = query.reshape(LEN // block, block, HEADS, HEAD)
    seg_blocks = seg.reshape(LEN // block, block)

    def one_block(pair):
        return block_attention(pair[0], pair[1], keys, values, seg)
    out = lax.map(jax.checkpoint(one_block), (query_blocks, seg_blocks))
    return out.reshape(LEN, HEADS * HEAD)

def reference(tokens, segments, query_weight, query_bias, key_weight, value_weight, value_bias, output_weight, output_bias, first_gain, first_shift, expand_weight, expand_bias, reduce_weight, reduce_bias, second_gain, second_shift, cotangent):
    scale = HEAD ** (-0.5)

    def forward(inputs, w_query, b_query, w_key, w_value, b_value, w_output, b_output, gain_a, shift_a, w_expand, b_expand, w_reduce, b_reduce, gain_b, shift_b):
        low_in = low(inputs)
        query = low(low_back((matmul(low_in, low(w_query)) + b_query) * scale))
        keys = low(low_back(matmul(low_in, low(w_key))))
        values = low(low_back(matmul(low_in, low(w_value)) + b_value))
        shape = (SEQS, LEN, HEADS, HEAD)
        context = lax.map(sequence_attention, (query.reshape(shape), keys.reshape(shape), values.reshape(shape), segments))
        context = low(low_back(context))
        branch = low_back(matmul(context, low(w_output)) + b_output)
        hidden = layer_norm(inputs + branch, gain_a, shift_a)
        expand = low_back(matmul(low(hidden), low(w_expand)) + b_expand)
        active = low(expand * 0.5 * (1.0 + lax.erf(expand * SQRT_HALF)))
        reduced = low_back(matmul(active, low(w_reduce)) + b_reduce)
        return layer_norm(hidden + reduced, gain_b, shift_b)
    result, pullback = jax.vjp(forward, tokens, query_weight, query_bias, key_weight, value_weight, value_bias, output_weight, output_bias, first_gain, first_shift, expand_weight, expand_bias, reduce_weight, reduce_bias, second_gain, second_shift)
    grads = pullback(cotangent)
    return (result, grads[0], grads[1], grads[2], grads[3], grads[4], grads[5], grads[6], grads[7], grads[8], grads[9], grads[10], grads[11], grads[12], grads[13], grads[14], grads[15])
```

```python
import functools

import jax
import jax.numpy as jnp
from jax import lax
from jax.experimental import pallas as pl
from jax.experimental.pallas import tpu as pltpu
from jax.sharding import PartitionSpec as P

HEAD = 64
LANES = 128
EPS = 1e-05
BIG = 1e30
LOG2E = 1.4426950408889634
SQRT_HALF = 0.7071067811865476
DENSITY = 0.3989422804014327
BF = jnp.bfloat16
F32 = jnp.float32


def dot_nn(left, right):
    return jnp.dot(left, right, preferred_element_type=F32)


def dot_tn(left, right):
    return lax.dot_general(left, right, (((0,), (0,)), ((), ())), preferred_element_type=F32)


def dot_nt(left, right):
    return lax.dot_general(left, right, (((1,), (1,)), ((), ())), preferred_element_type=F32)


def exchange(value, axis, k):
    count = lax.axis_size(axis)
    return lax.ppermute(value, axis, [(i, i ^ k) for i in range(count)])


def peer(value, k):
    return exchange(value, "ctx", k)


def after(value, *needed):
    return lax.optimization_barrier((value, needed))[0]


def plane_list(count):
    return list(range(0, count, 2)) + list(range(1, count, 2))


def plane_order():
    return plane_list(lax.axis_size("ctx"))


def gather_even(value, low_first):
    count = lax.axis_size("ctx")
    got = {0: value}
    for k in range(2, count, 2):
        bits = [1 << b for b in range(1, count.bit_length()) if k >> b & 1]
        step = bits[-1] if low_first else bits[0]
        got[k] = peer(got[k ^ step], step)
    return [got[k] for k in range(0, count, 2)]


def by_owner(parts, axis, order=None, mesh_axis="ctx"):
    order = order or plane_order()
    stacked = jnp.stack([parts[order.index(k)] for k in range(len(order))])
    me = lax.axis_index(mesh_axis)
    return jnp.concatenate(
        [lax.dynamic_index_in_dim(stacked, me ^ g, 0, keepdims=False) for g in range(len(order))], axis=axis
    )


def rows_to_heads(value, width):
    count = lax.axis_size("ctx")
    me = lax.axis_index("ctx")
    mine, other = [], []
    for k in range(0, count, 2):
        to = me ^ k
        first = lax.dynamic_slice_in_dim(value, to * width, width, 1)
        second = lax.dynamic_slice_in_dim(value, (to ^ 1) * width, width, 1)
        got = jnp.concatenate([first, second], axis=1)
        if k:
            got = peer(got, k)
        mine.append(got[:, :width])
        other.append(got[:, width:])
    return jnp.concatenate(mine + [peer(jnp.concatenate(other, axis=0), 1)], axis=0)


def heads_to_rows(value):
    count = lax.axis_size("ctx")
    rows, width = value.shape[0] // count, value.shape[1]
    half = value.shape[0] // 2
    both = jnp.concatenate([value[:half], peer(value[half:], 1)], axis=1)
    even, odd = [], []
    for i, k in enumerate(range(0, count, 2)):
        got = both[i * rows : (i + 1) * rows]
        if k:
            got = peer(got, k)
        even.append(got[:, :width])
        odd.append(got[:, width:])
    return even + odd


def reduce_even(blocks, low_first):
    count = lax.axis_size("ctx")
    bits = [1 << b for b in range(1, count.bit_length() - 1)]
    if not low_first:
        bits = bits[::-1]
    held = dict(zip(range(0, count, 2), blocks))
    for bit in bits:
        sent = [k for k in held if k & bit]
        got = peer(jnp.stack([held[k] for k in sent]), bit)
        got = {k ^ bit: got[i] for i, k in enumerate(sent)}
        held = {k: (held[k].astype(F32) + got[k].astype(F32)).astype(BF) for k in held if not k & bit}
    return held[0]


def gather_shards(value):
    depth = lax.axis_size("fsdp")
    parts = [value[None]] + [exchange(value, "fsdp", j)[None] for j in range(1, depth)]
    return by_owner(parts, 0, list(range(depth)), "fsdp")


def reduce_shards(value):
    depth = lax.axis_size("fsdp")
    me = lax.axis_index("fsdp")
    total = lax.dynamic_index_in_dim(value, me, 0, keepdims=False).astype(F32)
    for j in range(1, depth):
        sent = lax.dynamic_index_in_dim(value, me ^ j, 0, keepdims=False)
        total = total + exchange(sent, "fsdp", j).astype(F32)
    return total


def in_terms(vector, count):
    terms = []
    for _ in range(count):
        terms.append(vector.astype(BF))
        vector = vector - terms[-1].astype(F32)
    return terms


def whole(shape):
    return pl.BlockSpec(shape, lambda *i: (0,) * len(shape))


def params(limit=48):
    return pltpu.CompilerParams(vmem_limit_bytes=limit << 20)


def cost(flops, size):
    return pl.CostEstimate(flops=flops, bytes_accessed=size, transcendentals=0)


def mask_columns(seg, bits):
    lane = jnp.arange(LANES) % HEAD
    bit = (seg[:, None] >> jnp.minimum(lane // 2, 30)) & 1
    flip = bit ^ (lane & 1)
    used = lane < 2 * bits
    for_query = jnp.where(used & (flip == 1), -BIG, 0.0).astype(BF)
    for_key = jnp.where(used, 1 - flip, ((lane >= 60) & (lane < 63)).astype(jnp.int32)).astype(BF)
    return for_query, for_key


def lane_index():
    return lax.broadcasted_iota(jnp.int32, (1, LANES), 1)


def merge(main, extra, h):
    lane = lane_index()
    return jnp.where((lane < HEAD) if h == 0 else (lane >= HEAD), main, extra)


def with_terms(extra, number):
    lane = lane_index() % HEAD
    first = number.astype(BF).astype(F32)
    rest = number - first
    second = rest.astype(BF).astype(F32)
    third = rest - second
    terms = jnp.where(lane == 60, first, jnp.where(lane == 61, second, third)).astype(BF)
    return jnp.where((lane >= 60) & (lane < 63), terms, extra)


def forward_kernel(q, k, v, mask_q, mask_k, out, lse, key_side, value_side, *, heads):
    lane = lane_index()

    @pl.when(pl.program_id(0) == 0)
    def _():
        for h in range(heads):
            key_side[h] = merge(k[...], mask_k[...], h)
            value_side[h] = merge(v[...], jnp.ones((1, LANES), BF), h)

    whole, whole_lse = None, None
    for h in range(heads):
        scores = dot_nt(merge(q[...], mask_q[...], h), key_side[h])
        top = jnp.max(scores, axis=1, keepdims=True)
        weights = jnp.exp2(scores - top).astype(BF)
        both = dot_nn(weights, value_side[h])
        total = pltpu.roll(both, HEAD, 1)
        context, log_total = both / total, top + jnp.log2(total)
        if whole is None:
            whole, whole_lse = context, log_total
        else:
            whole = jnp.where(lane < HEAD, whole, context)
            whole_lse = jnp.where(lane < HEAD, whole_lse, log_total)
    out[...] = whole.astype(BF)
    lse[...] = whole_lse


def attend(qkv, mask_q, mask_k, heads, block):
    count = qkv.shape[0]
    part = lambda j: pl.BlockSpec((block, LANES), lambda i: (i, j))
    full = lambda j: pl.BlockSpec((count, LANES), lambda i: (0, j))
    products = 2 * 2 * count * count * LANES * heads
    return pl.pallas_call(
        functools.partial(forward_kernel, heads=heads),
        grid=(count // block,),
        in_specs=[part(0), full(1), full(2), part(0), full(0)],
        out_specs=[part(0), part(0)],
        out_shape=[jax.ShapeDtypeStruct((count, LANES), BF), jax.ShapeDtypeStruct((count, LANES), F32)],
        scratch_shapes=[pltpu.VMEM((heads, count, LANES), BF), pltpu.VMEM((heads, count, LANES), BF)],
        compiler_params=pltpu.CompilerParams(vmem_limit_bytes=48 << 20),
        cost_estimate=pl.CostEstimate(
            flops=products * 2, bytes_accessed=12 * count * LANES, transcendentals=count * count * heads
        ),
        name="attend",
    )(qkv, qkv, qkv, mask_q, mask_k)


def backward_kernel(*refs, heads, steps, block, pieces):
    q, k, v, mask_q, mask_k, out, lse = refs[:7]
    parts = refs[7 : 7 + pieces]
    grads, key_side, value_side, dk_t, dv_t, dc_all = refs[7 + pieces :]
    lane = lane_index()
    step = pl.program_id(0)

    @pl.when(step == 0)
    def _():
        ones = ((lane % HEAD >= 60) & (lane % HEAD < 63)).astype(F32).astype(BF)
        for h in range(heads):
            key_side[h] = merge(k[...], mask_k[...], h)
            value_side[h] = merge(v[...], ones, h)
        dk_t[...] = jnp.zeros_like(dk_t)
        dv_t[...] = jnp.zeros_like(dv_t)
        if pieces == 1:
            dc_all[...] = parts[0][...]
        else:
            for i in range(pieces):
                dc_all[i * block : (i + 1) * block, :] = parts[i][:, :LANES]
                dc_all[(pieces + i) * block : (pieces + i + 1) * block, :] = parts[i][:, LANES:]

    dc = dc_all.at[pl.ds(pl.multiple_of(step * block, block), block), :]
    product = dc[...].astype(F32) * out[...].astype(F32)
    low = jnp.sum(jnp.where(lane < HEAD, product, 0.0), axis=1, keepdims=True)
    high = jnp.sum(jnp.where(lane < HEAD, 0.0, product), axis=1, keepdims=True)
    query_extra = with_terms(mask_q[...], -pltpu.roll(lse[...], HEAD, 1))
    grad_extra = with_terms(jnp.zeros((1, LANES), BF), jnp.where(lane < HEAD, -high, -low))
    q_t, dc_t = q[...].T, dc[...].T
    dq = None
    for h in range(heads):
        probs = jnp.exp2(dot_nt(merge(q[...], query_extra, h), key_side[h]))
        centred = dot_nt(merge(dc[...], grad_extra, h), value_side[h])
        ds = (probs * centred).astype(BF)
        part = dot_nn(ds, key_side[h])
        dq = part if dq is None else jnp.where(lane < HEAD, dq, part)
        own = slice(HEAD * h, HEAD * h + HEAD)
        dk_t[own, :] += dot_nn(q_t[own, :], ds)
        dv_t[own, :] += dot_nn(dc_t[own, :], probs.astype(BF))
    grads[pl.ds(pl.multiple_of(step * block, block), block), :LANES] = (
        dq.astype(BF).astype(F32) * HEAD**-0.5
    ).astype(BF)

    @pl.when(step == steps - 1)
    def _():
        grads[:, LANES : 2 * LANES] = (dk_t[...] * (1.0 / LOG2E)).T.astype(BF)
        grads[:, 2 * LANES :] = dv_t[...].T.astype(BF)


def attend_back(qkv, mask_q, mask_k, dc, out, lse, heads, block):
    dc = dc if isinstance(dc, list) else [dc]
    count = qkv.shape[0]
    part = lambda j: pl.BlockSpec((block, LANES), lambda i: (i, j))
    full = lambda j: pl.BlockSpec((count, LANES), lambda i: (0, j))
    products = 5 * 2 * count * count * LANES * heads
    return pl.pallas_call(
        functools.partial(backward_kernel, heads=heads, steps=count // block, block=block, pieces=len(dc)),
        grid=(count // block,),
        in_specs=[part(0), full(1), full(2), part(0), full(0), part(0), part(0)] + [whole(v.shape) for v in dc],
        out_specs=pl.BlockSpec((count, 3 * LANES), lambda i: (0, 0)),
        out_shape=jax.ShapeDtypeStruct((count, 3 * LANES), BF),
        scratch_shapes=[
            pltpu.VMEM((heads, count, LANES), BF),
            pltpu.VMEM((heads, count, LANES), BF),
            pltpu.VMEM((LANES, count), F32),
            pltpu.VMEM((LANES, count), F32),
            pltpu.VMEM((count, LANES), BF),
        ],
        compiler_params=pltpu.CompilerParams(vmem_limit_bytes=56 << 20),
        cost_estimate=pl.CostEstimate(
            flops=products, bytes_accessed=16 * count * LANES, transcendentals=count * count * heads
        ),
        name="attend_back",
    )(qkv, qkv, qkv, mask_q, mask_k, out, lse, *dc)


def project_kernel(*refs, blocks):
    weight, bias, factor, out = refs[blocks:]
    row = 0
    for ref in refs[:blocks]:
        got = (dot_nn(ref[...], weight[...]) + bias[...]) * factor[...]
        out[row : row + ref.shape[0], :] = got.astype(BF)
        row += ref.shape[0]


def project(blocks, weight, bias, factor):
    width, line = weight.shape
    args = (*blocks, weight, bias[None], factor[None])
    shape = (sum(v.shape[0] for v in blocks), line)
    return pl.pallas_call(
        functools.partial(project_kernel, blocks=len(blocks)),
        in_specs=[whole(v.shape) for v in args],
        out_specs=whole(shape),
        out_shape=jax.ShapeDtypeStruct(shape, BF),
        grid=(1,),
        compiler_params=params(),
        cost_estimate=cost(2 * shape[0] * width * line, 2 * shape[0] * (width + line)),
        name="project",
    )(*args)


def flatten_blocks(blocks):
    flat, parts = [], []
    for n, block in enumerate(blocks):
        first = 0
        for part in block:
            flat.append(part)
            parts.append((n, first))
            first += part.shape[0]
    return flat, tuple(parts)


def assemble_kernel(me, *refs, parts, thin, folds):
    out = refs[-1]
    shard = len({n for n, _ in parts}) * thin
    block = refs[0].shape[2]
    order = plane_list(len({n for n, _ in parts}))
    for ref, (n, first) in zip(refs, parts):
        for z in range(ref.shape[0]):
            row = pl.multiple_of((first + z) * shard + (me[0] ^ order[n]) * thin, thin)
            for f in range(folds):
                out[pl.ds(row, thin), f * block : (f + 1) * block] = ref[z, f * thin : (f + 1) * thin, :]


def assemble_output(blocks, shard, thin, me):
    flat, parts = flatten_blocks(blocks)
    _, tall, block = flat[0].shape
    strip = tall - shard
    folds = strip // thin
    width = folds * block
    specs = [pl.BlockSpec((v.shape[0], strip, block), lambda i: (0, shard // strip, 0)) for v in flat]
    return pl.pallas_call(
        functools.partial(assemble_kernel, parts=parts, thin=thin, folds=folds),
        grid=(1,),
        in_specs=[pl.BlockSpec(memory_space=pltpu.SMEM)] + specs,
        out_specs=whole((width, width)),
        out_shape=jax.ShapeDtypeStruct((width, width), BF),
        compiler_params=params(),
        cost_estimate=cost(0, 4 * width * width),
        name="assemble_output",
    )(me, *flat)


def branch_kernel(me, *refs, pieces, aliased):
    weight, tokens, bias, gain, shift = refs[pieces : pieces + 5]
    context, hidden, low, normed, inverse = refs[pieces + 5 + aliased :]
    second = (me[0] & 1) == 1
    pair = refs[0].shape[1]
    for i in range(pieces):
        at = pl.multiple_of(((me[0] ^ (2 * i)) // 2) * pair, pair)
        got = refs[i][...]
        swapped = jnp.concatenate([got[:, pair // 2 :], got[:, : pair // 2]], axis=1)
        context[:, pl.ds(at, pair)] = jnp.where(second, swapped, got)
    total = tokens[...] + dot_nn(context[...], weight[...]) + bias[...]
    mean = jnp.mean(total, axis=1, keepdims=True)
    centred = total - mean
    scale = lax.rsqrt(jnp.mean(centred * centred, axis=1, keepdims=True) + EPS)
    unit = centred * scale
    out = unit * gain[...] + shift[...]
    hidden[...] = out
    low[...] = out.astype(BF)
    normed[...] = unit
    inverse[...] = jnp.broadcast_to(scale, inverse.shape)


def branch(s, me, pieces, weight, tokens, bias, gain, shift, earlier):
    batch, rows, width = tokens.shape
    at = pl.BlockSpec((None, rows, width), lambda i: (s, 0, 0))
    thin = pl.BlockSpec((None, rows, LANES), lambda i: (s, 0, 0))
    vec = whole((1, width))
    earlier = earlier or ()
    first = 1 + len(pieces) + 5
    full = lambda t: jax.ShapeDtypeStruct((batch, rows, width), t)
    return pl.pallas_call(
        functools.partial(branch_kernel, pieces=len(pieces), aliased=len(earlier)),
        grid=(1,),
        in_specs=[pl.BlockSpec(memory_space=pltpu.SMEM)]
        + [whole(v.shape) for v in pieces]
        + [whole(weight.shape), at, vec, vec, vec]
        + [pl.BlockSpec(memory_space=pl.ANY)] * len(earlier),
        out_specs=[at, at, at, at, thin],
        out_shape=[full(BF), full(F32), full(BF), full(F32), jax.ShapeDtypeStruct((batch, rows, LANES), F32)],
        input_output_aliases={first + i: i for i in range(len(earlier))},
        compiler_params=params(),
        cost_estimate=cost(2 * rows * width * width, 2 * width * width + 18 * rows * width),
        name="branch",
    )(me, *pieces, weight, tokens, bias[None], gain[None], shift[None], *earlier)


def fetch_blocks(refs, parts, slots, sems, step, middle, shard):
    def copies(i):
        made = []
        for j, (ref, (n, first)) in enumerate(zip(refs, parts)):
            if n % middle == i:
                target = slots.at[i % 2, n // middle, pl.ds(first, ref.shape[0])]
                made.append(pltpu.make_async_copy(ref.at[:, :shard, :], target, sems.at[j]))
        return made

    for i in range(middle):

        @pl.when(step == i)
        def _():
            if i == 0:
                for copy in copies(0):
                    copy.start()
            if i + 1 < middle:
                for copy in copies(i + 1):
                    copy.start()
            for copy in copies(i):
                copy.wait()


def expand_kernel(*refs, middle, depth, parts):
    low, bias_even, bias_odd = refs[:3]
    blocks = refs[3 : 3 + len(parts)]
    outs = refs[3 + len(parts) : 7 + len(parts)]
    slots, sems = refs[7 + len(parts) :]
    step = pl.program_id(0)
    shard = slots.shape[3]
    fetch_blocks(blocks, parts, slots, sems, step, middle, shard)
    slot = step % 2
    rows = low.shape[0] // 2
    for parity, bias in enumerate((bias_even, bias_odd)):
        for part in range(2):
            at = slice(part * rows, part * rows + rows)
            total = bias[...]
            for z in range(depth):
                total = total + dot_nn(low[at, z * shard : (z + 1) * shard], slots[slot, parity, z])
            cdf = 0.5 * (1.0 + lax.erf(total * SQRT_HALF))
            outs[parity][at, :] = (total * cdf).astype(BF)
            outs[2 + parity][at, :] = (cdf + total * DENSITY * jnp.exp(-0.5 * total * total)).astype(BF)


def expand_forward(low, bias_halves, blocks, shard):
    rows, width = low.shape
    middle = len(blocks) // 2
    depth = width // shard
    block = blocks[0][0].shape[2]
    flat, parts = flatten_blocks(blocks)
    bias = pl.BlockSpec((None, 1, block), lambda i: (i, 0, 0))
    out = pl.BlockSpec((rows, block), lambda i: (0, i))
    return pl.pallas_call(
        functools.partial(expand_kernel, middle=middle, depth=depth, parts=parts),
        grid=(middle,),
        in_specs=[whole(low.shape), bias, bias] + [pl.BlockSpec(memory_space=pl.ANY)] * len(flat),
        out_specs=[out] * 4,
        out_shape=[jax.ShapeDtypeStruct((rows, middle * block), BF)] * 4,
        scratch_shapes=[pltpu.VMEM((2, 2, depth, shard, block), BF), pltpu.SemaphoreType.DMA((len(flat),))],
        compiler_params=params(),
        cost_estimate=cost(4 * rows * width * middle * block, 4 * width * middle * block + 8 * rows * middle * block),
        name="expand",
    )(low, *bias_halves, *flat)


def norm_back(grad, normed, inverse, gain):
    scaled = grad * gain
    first = jnp.mean(scaled, axis=1, keepdims=True)
    second = jnp.mean(scaled * normed, axis=1, keepdims=True)
    return inverse * (scaled - first - normed * second)


def reduce_kernel(
    act_even, act_odd, w_even, w_odd, hidden, grad_out, bias, gain, shift, result, du, low, sums, total, *, steps
):
    step = pl.program_id(0)
    block = act_even.shape[1]
    width = total.shape[1]
    part = dot_nn(act_even[...], w_even[...].reshape(block, width))
    part = part + dot_nn(act_odd[...], w_odd[...].reshape(block, width))

    @pl.when(step == 0)
    def _():
        total[...] = part + bias[...]
        sums[...] = jnp.zeros_like(sums)

    @pl.when(step > 0)
    def _():
        total[...] += part

    @pl.when(step == steps - 1)
    def _():
        rows = 64

        @pl.loop(0, total.shape[0] // rows)
        def _(i):
            at = pl.ds(pl.multiple_of(i * rows, rows), rows)
            value = total[at, :] + hidden[at, :]
            mean = jnp.mean(value, axis=1, keepdims=True)
            centred = value - mean
            inverse = lax.rsqrt(jnp.mean(centred * centred, axis=1, keepdims=True) + EPS)
            normed = centred * inverse
            result[at, :] = normed * gain[...] + shift[...]
            grad = grad_out[at, :]
            back = norm_back(grad, normed, inverse, gain[...])
            du[at, :] = back
            rounded = back.astype(BF)
            low[at, :] = rounded
            sums[0:1, :] += jnp.sum(grad * normed, axis=0, keepdims=True)
            sums[1:2, :] += jnp.sum(grad, axis=0, keepdims=True)
            sums[2:3, :] += jnp.sum(rounded.astype(F32), axis=0, keepdims=True)


def reduce_forward(acts, weights, hidden, grad_out, bias, gain, shift):
    rows, width = hidden.shape
    depth, middle, piece, _ = weights[0].shape
    block = depth * piece
    act = pl.BlockSpec((rows, block), lambda i: (0, i))
    weight = pl.BlockSpec((depth, None, piece, width), lambda i: (0, i, 0, 0))
    full, vec = whole((rows, width)), whole((1, width))
    return pl.pallas_call(
        functools.partial(reduce_kernel, steps=middle),
        grid=(middle,),
        in_specs=[act, act, weight, weight, full, full, vec, vec, vec],
        out_specs=[full, full, full, whole((8, width))],
        out_shape=[
            jax.ShapeDtypeStruct((rows, width), F32),
            jax.ShapeDtypeStruct((rows, width), F32),
            jax.ShapeDtypeStruct((rows, width), BF),
            jax.ShapeDtypeStruct((8, width), F32),
        ],
        scratch_shapes=[pltpu.VMEM((rows, width), F32)],
        compiler_params=params(),
        cost_estimate=cost(4 * rows * width * middle * block, 4 * width * middle * block + 16 * rows * width),
        name="reduce",
    )(*acts, *weights, hidden, grad_out, bias[None], gain[None], shift[None])


def feed_back_kernel(*refs, middle, depth, steps, parts):
    low, w_even, w_odd, slope_even, slope_odd, du_second, normed, inverse, gain = refs[:9]
    refs = refs[9:]
    blocks = refs[: len(parts)]
    de_even, de_odd, bias_even, bias_odd, du, da, sums = refs[len(parts) : 7 + len(parts)]
    slots, sems, total = refs[7 + len(parts) :]
    step = pl.program_id(0)
    shard, block = slots.shape[3], slots.shape[4]
    width = total.shape[1]
    fetch_blocks(blocks, parts, slots, sems, step, middle, shard)
    slot = step % 2

    @pl.when(step == 0)
    def _():
        total[...] = du_second[...]
        sums[...] = jnp.zeros_like(sums)

    for parity, (weight, slope, de, bias) in enumerate(
        ((w_even, slope_even, de_even, bias_even), (w_odd, slope_odd, de_odd, bias_odd))
    ):
        grad = dot_nt(low[...], weight[...].reshape(block, width)) * slope[...].astype(F32)
        rounded = grad.astype(BF)
        de[...] = rounded
        bias[...] = jnp.sum(rounded.astype(F32), axis=0, keepdims=True)
        for z in range(depth):
            total[:, z * shard : (z + 1) * shard] += dot_nt(rounded, slots[slot, parity, z])

    @pl.when(step == steps - 1)
    def _():
        rows = 64

        @pl.loop(0, total.shape[0] // rows)
        def _(i):
            at = pl.ds(pl.multiple_of(i * rows, rows), rows)
            grad, unit = total[at, :], normed[at, :]
            back = norm_back(grad, unit, inverse[at, 0:1], gain[...])
            du[at, :] = back
            rounded = back.astype(BF)
            da[at, :] = rounded
            sums[0:1, :] += jnp.sum(grad * unit, axis=0, keepdims=True)
            sums[1:2, :] += jnp.sum(grad, axis=0, keepdims=True)
            sums[2:3, :] += jnp.sum(rounded.astype(F32), axis=0, keepdims=True)


def feed_back(low, weights, slopes, du_second, normed, inverse, gain, blocks, shard):
    rows, width = low.shape
    depth, middle, piece, _ = weights[0].shape
    block = depth * piece
    flat, parts = flatten_blocks(blocks)
    act = pl.BlockSpec((rows, block), lambda i: (0, i))
    bias = pl.BlockSpec((None, 1, block), lambda i: (i, 0, 0))
    weight = pl.BlockSpec((depth, None, piece, width), lambda i: (0, i, 0, 0))
    full, vec = whole((rows, width)), whole((1, width))
    return pl.pallas_call(
        functools.partial(feed_back_kernel, middle=middle, depth=depth, steps=middle, parts=parts),
        grid=(middle,),
        in_specs=[full, weight, weight, act, act, full, full, whole((rows, LANES)), vec]
        + [pl.BlockSpec(memory_space=pl.ANY)] * len(flat),
        out_specs=[act, act, bias, bias, full, full, whole((8, width))],
        out_shape=[
            jax.ShapeDtypeStruct((rows, middle * block), BF),
            jax.ShapeDtypeStruct((rows, middle * block), BF),
            jax.ShapeDtypeStruct((middle, 1, block), F32),
            jax.ShapeDtypeStruct((middle, 1, block), F32),
            jax.ShapeDtypeStruct((rows, width), F32),
            jax.ShapeDtypeStruct((rows, width), BF),
            jax.ShapeDtypeStruct((8, width), F32),
        ],
        scratch_shapes=[
            pltpu.VMEM((2, 2, depth, shard, block), BF),
            pltpu.SemaphoreType.DMA((len(flat),)),
            pltpu.VMEM((rows, width), F32),
        ],
        compiler_params=params(56),
        cost_estimate=cost(8 * rows * width * middle * block, 8 * width * middle * block + 16 * rows * width),
        name="feed_back",
    )(low, *weights, *slopes, du_second, normed, inverse, gain[None], *flat)


def context_back_kernel(me, da, weight, mine, other, whole_grad, *, middle):
    whole_grad[...] = dot_nt(da[...], weight[...]).astype(BF)
    rows = da.shape[0]
    width = mine.shape[1]
    second = (me[0] & 1) == 1
    for i in range(middle):
        at = pl.multiple_of(((me[0] ^ (2 * i)) // 2) * 2 * width, 2 * width)
        pair = whole_grad[:, pl.ds(at, 2 * width)]
        low, high = pair[:, :width], pair[:, width:]
        mine[i * rows : (i + 1) * rows, :] = jnp.where(second, high, low)
        other[i * rows : (i + 1) * rows, :] = jnp.where(second, low, high)


def context_back(s, me, da, weight, own_width, middle):
    _, rows, width = da.shape
    shape = (middle * rows, own_width)
    return pl.pallas_call(
        functools.partial(context_back_kernel, middle=middle),
        grid=(1,),
        in_specs=[
            pl.BlockSpec(memory_space=pltpu.SMEM),
            pl.BlockSpec((None, rows, width), lambda i: (s, 0, 0)),
            whole(weight.shape),
        ],
        out_specs=[whole(shape)] * 2,
        out_shape=[jax.ShapeDtypeStruct(shape, BF)] * 2,
        scratch_shapes=[pltpu.VMEM((rows, width), BF)],
        compiler_params=params(),
        cost_estimate=cost(2 * rows * width * width, 2 * width * width + 4 * rows * width),
        name="context_back",
    )(me, da, weight)


def gradient_kernel(act, other_act, grad, other_grad, out):
    depth, piece, width = out.shape
    total = dot_tn(act[...], grad[...]) + dot_tn(other_act[...], other_grad[...])
    out[...] = total.astype(BF).reshape(depth, piece, width)


def reduce_gradient(act, other_act, grad, other_grad, depth, piece):
    rows, width = grad.shape
    block = depth * piece
    middle = act.shape[1] // block
    column = pl.BlockSpec((rows, block), lambda i: (0, i))
    full = whole((rows, width))
    return pl.pallas_call(
        gradient_kernel,
        grid=(middle,),
        in_specs=[column, column, full, full],
        out_specs=pl.BlockSpec((depth, None, piece, width), lambda i: (0, i, 0, 0)),
        out_shape=jax.ShapeDtypeStruct((depth, middle, piece, width), BF),
        compiler_params=params(),
        cost_estimate=cost(4 * rows * width * middle * block, 2 * width * middle * block + 4 * rows * middle * block),
        name="reduce_gradient",
    )(act, other_act, grad, other_grad)


def expand_gradient_kernel(
    me, low, other_low, context, other_context, de, other_de, da, other_da, kept_a, sent_a, kept_b, sent_b, *, middle
):
    block = de.shape[1] // middle
    rows = kept_a.shape[1]
    own = kept_a.shape[2] - block
    first, second = low[...].T, other_low[...].T
    third, fourth = context[...].T, other_context[...].T
    for i in range(middle):
        at = slice(i * block, (i + 1) * block)
        wide = (dot_nn(first, de[:, at]) + dot_nn(second, other_de[:, at])).astype(BF)
        where = pl.ds(pl.multiple_of((me[0] ^ (2 * i)) * own, own), own)
        thin = (dot_nn(third, da[:, where]) + dot_nn(fourth, other_da[:, where])).astype(BF)
        for target, n, part in (
            (sent_a if i >= 2 else kept_a, i % 2, slice(0, rows)),
            (sent_b if i % 2 else kept_b, i // 2, slice(rows, 2 * rows)),
        ):
            target[n, :, :block] = wide[part]
            target[n, :, block:] = thin[part]


def expand_gradient(me, low, other_low, context, other_context, de, other_de, da, other_da, own):
    rows, width = low.shape
    middle = 4
    block = de.shape[1] // middle
    args = (low, other_low, context, other_context, de, other_de, da, other_da)
    shape = (2, width // 2, block + own)
    return pl.pallas_call(
        functools.partial(expand_gradient_kernel, middle=middle),
        grid=(1,),
        in_specs=[pl.BlockSpec(memory_space=pltpu.SMEM)] + [whole(v.shape) for v in args],
        out_specs=[whole(shape)] * 4,
        out_shape=[jax.ShapeDtypeStruct(shape, BF)] * 4,
        compiler_params=params(56),
        cost_estimate=cost(4 * rows * width * middle * (block + own), 4 * width * middle * block),
        name="expand_gradient",
    )(me, *args)


def unpack_expand_kernel(me, *refs, depth):
    wide, thin = refs[-2:]
    count = len(refs) - 2
    block = wide.shape[1] // count
    piece, own = block // depth, thin.shape[1] // count
    for n, k in enumerate(plane_list(count)):
        g = me[0] ^ k
        for z in range(depth):
            at = pl.multiple_of(z * count * piece + g * piece, piece)
            wide[:, pl.ds(at, piece)] = refs[n][:, z * piece : (z + 1) * piece].astype(F32)
        thin[:, pl.ds(pl.multiple_of(g * own, own), own)] = refs[n][:, block:].astype(F32)


def unpack_expand(me, blocks, depth, hidden, width):
    shard = blocks[0].shape[0]
    shapes = [(shard, hidden), (shard, width)]
    return pl.pallas_call(
        functools.partial(unpack_expand_kernel, depth=depth),
        grid=(1,),
        in_specs=[pl.BlockSpec(memory_space=pltpu.SMEM)] + [whole(v.shape) for v in blocks],
        out_specs=[whole(v) for v in shapes],
        out_shape=[jax.ShapeDtypeStruct(v, F32) for v in shapes],
        compiler_params=params(),
        cost_estimate=cost(0, 6 * shard * (hidden + width)),
        name="unpack_expand",
    )(me, *blocks)


def unpack_heads_kernel(me, *refs):
    outs, bias = refs[-4:-1], refs[-1]
    count = len(refs) - 4
    shard, width = outs[0].shape
    own = width // count
    bias[...] = jnp.zeros_like(bias)
    for n, k in enumerate(plane_list(count)):
        where = pl.ds(pl.multiple_of((me[0] ^ k) * own, own), own)
        tail = refs[n][shard : shard + 16, :].astype(F32)
        for t in range(3):
            at = slice(t * own, (t + 1) * own)
            outs[t][:, where] = refs[n][:shard, at].astype(F32)
            bias[t : t + 1, where] = tail[0:1, at] + tail[1:2, at]


def unpack_heads(me, blocks, shard, width):
    shapes = [(shard, width)] * 3 + [(8, width)]
    return pl.pallas_call(
        unpack_heads_kernel,
        grid=(1,),
        in_specs=[pl.BlockSpec(memory_space=pltpu.SMEM)] + [whole(v.shape) for v in blocks],
        out_specs=[whole(v) for v in shapes],
        out_shape=[jax.ShapeDtypeStruct(v, F32) for v in shapes],
        compiler_params=params(),
        cost_estimate=cost(0, 18 * shard * width),
        name="unpack_heads",
    )(me, *blocks)


def heads_gradient_kernel(*refs, blocks, last):
    if last:
        grads, before = refs[blocks : blocks + 2]
        out, sums, total = refs[blocks + 2 :]
        total[...] = before[...]
    else:
        grads = refs[blocks]
        total, sums = refs[blocks + 1 :]
        total[...] = jnp.zeros_like(total)
    row = 0
    for ref in refs[:blocks]:
        total[...] += dot_tn(grads[row : row + ref.shape[0], :], ref[...])
        row += ref.shape[0]
    sums[...] = jnp.broadcast_to(jnp.sum(grads[...].astype(F32), axis=0, keepdims=True), sums.shape)
    if last:
        out[...] = total[...].T.astype(BF)


def heads_gradient(blocks, grads, before=None):
    line = grads.shape[1]
    width = blocks[0].shape[1]
    last = before is not None
    args = (*blocks, grads) + ((before,) if last else ())
    shapes = [jax.ShapeDtypeStruct((width, line), BF) if last else jax.ShapeDtypeStruct((line, width), F32)]
    shapes.append(jax.ShapeDtypeStruct((8, line), F32))
    return pl.pallas_call(
        functools.partial(heads_gradient_kernel, blocks=len(blocks), last=last),
        grid=(1,),
        in_specs=[whole(v.shape) for v in args],
        out_specs=[whole(v.shape) for v in shapes],
        out_shape=shapes,
        scratch_shapes=[pltpu.VMEM((line, width), F32)] if last else [],
        compiler_params=params(),
        cost_estimate=cost(2 * grads.shape[0] * width * line, 2 * grads.shape[0] * width + 6 * width * line),
        name="heads_gradient",
    )(*args)


def normalize(values, gain, shift):
    mean = jnp.mean(values, axis=-1, keepdims=True)
    centred = values - mean
    inverse = lax.rsqrt(jnp.mean(centred * centred, axis=-1, keepdims=True) + EPS)
    normed = centred * inverse
    return normed * gain + shift, normed, inverse


def normalize_back(grad, normed, inverse, gain):
    scaled = grad * gain
    inner = (
        scaled
        - jnp.mean(scaled, axis=-1, keepdims=True)
        - normed * jnp.mean(scaled * normed, axis=-1, keepdims=True)
    )
    return inner * inverse, jnp.sum(grad * normed, axis=0), jnp.sum(grad, axis=0)


def column_sums(values):
    return jnp.sum(values.astype(F32), axis=0)


def plain_body(
    tokens,
    segments,
    query_weight,
    query_bias,
    key_weight,
    value_weight,
    value_bias,
    output_weight,
    output_bias,
    first_gain,
    first_shift,
    expand_weight,
    expand_bias,
    reduce_weight,
    reduce_bias,
    second_gain,
    second_shift,
    cotangent,
):
    batch, rows, width = tokens.shape
    count, depth = lax.axis_size("ctx"), lax.axis_size("fsdp")
    me, my_shard = lax.axis_index("ctx"), lax.axis_index("fsdp")
    shard = query_weight.shape[0]
    hidden = expand_weight.shape[1]
    own_width = width // count
    heads = own_width // HEAD
    piece = hidden // depth // count
    block = depth * piece
    half = hidden // 2
    order = plane_order()
    evens = order[: count // 2]
    scale = HEAD**-0.5
    bits = (count * rows - 1).bit_length()

    columns = lambda w: lax.dynamic_slice_in_dim(w, me * own_width, own_width, 1).astype(BF)
    names = (query_bias, value_bias, output_bias, first_gain, first_shift, reduce_bias, second_gain, second_shift)
    packed = jnp.concatenate(names + (expand_bias,))
    terms = jnp.concatenate(in_terms(packed, 3))
    line = 3 * own_width
    lines = -(-terms.shape[0] // (16 * line)) * 16
    terms = jnp.pad(terms, (0, lines * line - terms.shape[0])).reshape(lines, line)
    own_heads = jnp.concatenate([columns(query_weight), columns(key_weight), columns(value_weight)], axis=1)
    own_heads = gather_shards(jnp.concatenate([own_heads, terms], axis=0))
    packed = own_heads[:, shard:].reshape(depth, lines * line)[:, : 3 * packed.shape[0]]
    packed = jnp.sum(packed.reshape(depth, 3, -1).astype(F32), axis=1)
    own_heads = own_heads[:, :shard].reshape(width, line)
    (bias_query, bias_value, bias_output, gain_first, shift_first, bias_reduce, gain_second, shift_second) = (
        packed[:, i * shard : (i + 1) * shard].reshape(width) for i in range(len(names))
    )
    wide_bias = packed[:, len(names) * shard :].reshape(depth, count, piece)
    bias_halves = [
        jnp.stack([lax.dynamic_index_in_dim(wide_bias, me ^ k, 1, keepdims=False) for k in ks], axis=1).reshape(half)
        for ks in (evens, order[count // 2 :])
    ]
    own_part = lambda v: lax.dynamic_slice_in_dim(v, me * own_width, own_width, 0)
    head_bias = jnp.concatenate([own_part(bias_query), jnp.zeros((own_width,), F32), own_part(bias_value)])
    head_scale = jnp.concatenate([jnp.full((own_width,), scale * LOG2E, F32), jnp.ones((2 * own_width,), F32)])

    thin = shard // count
    folds = width // block
    strip = lax.dynamic_slice_in_dim(output_weight, me * thin, thin, 0).astype(BF)
    strip = jnp.concatenate([strip[:, i * block : (i + 1) * block] for i in range(folds)], axis=0)
    block_expand = lax.dynamic_slice_in_dim(expand_weight.reshape(shard, depth, count * piece), me * piece, piece, 2)
    block_expand = jnp.concatenate([block_expand.reshape(shard, block).astype(BF), strip], axis=0)
    block_expand = lax.all_gather(block_expand, "fsdp", axis=0)
    block_reduce = lax.dynamic_slice_in_dim(reduce_weight, me * piece, piece, 0).astype(BF)
    block_reduce = lax.all_gather(block_reduce, "fsdp", axis=0)

    groups = jnp.stack([w.reshape(shard, count, own_width) for w in (query_weight, key_weight, value_weight)], axis=2)
    half_heads = jnp.concatenate(
        [lax.dynamic_index_in_dim(groups, me ^ k, 1, keepdims=False).reshape(shard, line).astype(BF) for k in evens],
        axis=1,
    )
    half_heads = lax.all_gather(half_heads, "fsdp", axis=0, tiled=True)
    other_heads = peer(half_heads, 1)

    seg = segments
    for b in range(count.bit_length() - 1):
        seg = jnp.concatenate([seg, peer(seg, 1 << b)], axis=1)
    seg = seg.reshape(batch, count, rows)
    seg = jnp.concatenate([seg[:, k] for k in order], axis=1)

    lanes = lambda v: v if own_width == LANES else jnp.pad(v, ((0, 0), (0, LANES - own_width)))
    kept, context_parts = [], []
    for s in range(batch):
        even = jnp.concatenate(gather_even(tokens[s].astype(BF), s % 2 == 0), axis=0)
        odd = peer(even, 1)
        qkv = jnp.concatenate([dot_nn(even, own_heads), dot_nn(odd, own_heads)], axis=0)
        qkv = ((qkv + head_bias) * head_scale).astype(BF)
        if own_width != LANES:
            qkv = jnp.concatenate([lanes(qkv[:, i * own_width : (i + 1) * own_width]) for i in range(3)], axis=1)
        mask_q, mask_k = mask_columns(seg[s], bits)
        out, lse = attend(qkv, mask_q, mask_k, heads, rows)
        kept.append((even, odd, qkv, mask_q, mask_k, out, lse))
        context_parts.append(by_owner(heads_to_rows(out[:, :own_width]), 1))

    got_expand = gather_even(block_expand, True)
    got_expand += [peer(v, 1) for v in got_expand]
    got_reduce = gather_even(block_reduce, False)
    got_reduce += [peer(v, 1) for v in got_reduce]
    full_output = by_owner(
        [
            jnp.concatenate([v[:, shard + i * thin : shard + (i + 1) * thin] for i in range(folds)], axis=2)
            for v in got_expand
        ],
        1,
    ).reshape(width, width)
    middle = count // 2
    expand_halves = [
        jnp.concatenate([v[:, :shard].reshape(width, depth, piece) for v in vs], axis=2).reshape(width, half)
        for vs in (got_expand[:middle], got_expand[middle:])
    ]
    reduce_halves = [
        jnp.concatenate(vs, axis=1).reshape(half, width) for vs in (got_reduce[:middle], got_reduce[middle:])
    ]

    firsts = []
    for s in range(batch):
        branch = dot_nn(context_parts[s], full_output) + bias_output
        firsts.append(normalize(tokens[s] + branch, gain_first, shift_first))
    hidden_in, normed_first, inverse_first = (jnp.concatenate(v, axis=0) for v in zip(*firsts))
    context_low = jnp.concatenate(context_parts, axis=0)
    hidden_low = hidden_in.astype(BF)
    halves = []
    reduced = bias_reduce
    for weight, back, bias in zip(expand_halves, reduce_halves, bias_halves):
        expand = dot_nn(hidden_low, weight) + bias
        cdf = 0.5 * (1.0 + lax.erf(expand * SQRT_HALF))
        active = (expand * cdf).astype(BF)
        slope = cdf + expand * DENSITY * jnp.exp(-0.5 * expand * expand)
        reduced = reduced + dot_nn(active, back)
        halves.append((weight, back, active, slope.astype(BF)))
    result, normed_second, inverse_second = normalize(hidden_in + reduced, gain_second, shift_second)

    grad_out = cotangent.reshape(batch * rows, width)
    grad_sum_second, grad_gain_second, grad_shift_second = normalize_back(
        grad_out, normed_second, inverse_second, gain_second
    )
    grad_reduced = grad_sum_second.astype(BF)
    grad_bias_reduce = column_sums(grad_reduced)

    def chip_sum(make):
        got = peer(make(1).astype(BF), 1)
        return (make(0) + got.astype(F32)).astype(BF)

    sum_reduce = chip_sum(lambda i: dot_tn(halves[i][2], grad_reduced))
    sum_reduce = lax.psum_scatter(sum_reduce, "fsdp", scatter_dimension=0, tiled=True)
    sum_reduce = reduce_even(jnp.split(sum_reduce, middle, axis=0), False)

    grad_hidden = grad_sum_second
    grad_expands = []
    for weight, back, active, slope in halves:
        grad_expand = (dot_nt(grad_reduced, back) * slope.astype(F32)).astype(BF)
        grad_hidden = grad_hidden + dot_nt(grad_expand, weight)
        grad_expands.append(grad_expand)
    grad_bias_expand = [column_sums(g).reshape(depth, middle, piece) for g in grad_expands]
    grad_pre, grad_gain_first, grad_shift_first = normalize_back(
        grad_hidden, normed_first, inverse_first, gain_first
    )
    grad_branch = grad_pre.astype(BF)
    grad_bias_output = column_sums(grad_branch)
    grad_context = dot_nt(grad_branch, full_output).astype(BF)

    sum_expand = chip_sum(lambda i: dot_tn(hidden_low, grad_expands[i])).reshape(width, depth, middle, piece)
    sum_expand = reduce_even([sum_expand[:, :, i].reshape(width, block) for i in range(middle)], True)
    branch_blocks = jnp.concatenate(
        [lax.dynamic_slice_in_dim(grad_branch, (me ^ k) * own_width, own_width, 1) for k in order], axis=1
    )
    sum_output = chip_sum(
        lambda i: dot_tn(context_low, branch_blocks[:, i * width // 2 : (i + 1) * width // 2])
    )
    sum_output = reduce_even(jnp.split(sum_output, middle, axis=1), False)
    sum_expand = jnp.concatenate([sum_expand, sum_output], axis=1)
    sum_expand = lax.psum_scatter(sum_expand, "fsdp", scatter_dimension=0, tiled=True)

    grads = []
    for s in range(batch):
        even, odd, qkv, mask_q, mask_k, out, lse = kept[s]
        dc = lanes(rows_to_heads(grad_context[s * rows : (s + 1) * rows], own_width))
        got = attend_back(qkv, mask_q, mask_k, dc, out, lse, heads, rows)
        if own_width != LANES:
            got = jnp.concatenate([got[:, i * LANES : i * LANES + own_width] for i in range(3)], axis=1)
        grads.append(got)
    middle_row = count * rows // 2
    grad_heads = sum(
        dot_tn(kept[s][0], grads[s][:middle_row]) + dot_tn(kept[s][1], grads[s][middle_row:]) for s in range(batch)
    ).astype(BF)
    grad_head_bias = jnp.pad(
        jnp.stack(in_terms(sum(column_sums(g) for g in grads), 2)), ((0, 14), (0, 0))
    )
    home_heads = jnp.concatenate(
        [grad_heads.reshape(depth, shard, line), jnp.broadcast_to(grad_head_bias, (depth, 16, line))], axis=1
    )
    home_heads = reduce_shards(home_heads)
    home_heads = jnp.concatenate(
        [home_heads[:shard].astype(BF)]
        + [v[None] for v in in_terms(home_heads[shard] + home_heads[shard + 1], 2)]
        + [jnp.zeros((14, line), BF)],
        axis=0,
    )
    back_rows = [heads_to_rows(g) for g in grads]
    back_even = jnp.concatenate([jnp.concatenate(r[:middle], axis=1) for r in back_rows], axis=0)
    back_odd = jnp.concatenate([jnp.concatenate(r[middle:], axis=1) for r in back_rows], axis=0)
    grad_in = grad_pre + dot_nt(back_even, half_heads) + dot_nt(back_odd, other_heads)

    def spread(value, low_first):
        got = gather_even(value, low_first)
        odd = peer(jnp.stack(got), 1)
        return by_owner([v[None] for v in got] + [odd[i : i + 1] for i in range(middle)], 0)

    wide = lax.all_gather(sum_expand, "ctx", axis=0)
    grad_expand_weight = jnp.transpose(wide[:, :, :block].reshape(count, shard, depth, piece), (1, 2, 0, 3))
    grad_expand_weight = grad_expand_weight.reshape(shard, hidden).astype(F32)
    grad_output_weight = jnp.transpose(wide[:, :, block:], (1, 0, 2)).reshape(shard, width).astype(F32)
    grad_reduce_weight = lax.all_gather(sum_reduce, "ctx", axis=0, tiled=True).astype(F32)
    wide_heads = spread(home_heads, True)
    wide_shards = jnp.transpose(wide_heads[:, :shard].reshape(count, shard, 3, own_width), (2, 1, 0, 3))
    grad_query_weight, grad_key_weight, grad_value_weight = (
        wide_shards[i].reshape(shard, width).astype(F32) for i in range(3)
    )
    wide_biases = jnp.sum(wide_heads[:, shard : shard + 2].astype(F32), axis=1).reshape(count, 3, own_width)
    own_shard = lambda v: lax.dynamic_slice_in_dim(v.reshape(width), my_shard * shard, shard, 0)

    vectors = (
        grad_bias_output,
        grad_gain_first,
        grad_shift_first,
        grad_bias_reduce,
        grad_gain_second,
        grad_shift_second,
    )
    wide_bias = by_owner([g[:, i] for g in grad_bias_expand for i in range(middle)], 1)
    small = jnp.concatenate([v.reshape(depth, shard) for v in vectors] + [wide_bias], axis=1)
    for b in range(count.bit_length() - 1):
        small = small + peer(small, 1 << b)
    small = reduce_shards(small)
    vec = [small[i * shard : (i + 1) * shard] for i in range(len(vectors))]
    vec_expand = small[len(vectors) * shard :]
    return (
        result.reshape(batch, rows, width),
        grad_in.reshape(batch, rows, width),
        grad_query_weight,
        own_shard(wide_biases[:, 0]),
        grad_key_weight,
        grad_value_weight,
        own_shard(wide_biases[:, 2]),
        grad_output_weight,
        vec[0],
        vec[1],
        vec[2],
        grad_expand_weight,
        vec_expand,
        grad_reduce_weight,
        vec[3],
        vec[4],
        vec[5],
    )


def even_pieces(own, other):
    rows = own.shape[0]
    both = jnp.concatenate([own, other], axis=1)
    middle = lax.axis_size("ctx") // 2
    rows = rows // middle
    pieces = [both[i * rows : (i + 1) * rows] for i in range(middle)]
    return [pieces[0]] + [peer(pieces[i], 2 * i) for i in range(1, middle)]


def body(
    tokens,
    segments,
    query_weight,
    query_bias,
    key_weight,
    value_weight,
    value_bias,
    output_weight,
    output_bias,
    first_gain,
    first_shift,
    expand_weight,
    expand_bias,
    reduce_weight,
    reduce_bias,
    second_gain,
    second_shift,
    cotangent,
):
    batch, rows, width = tokens.shape
    count, depth = lax.axis_size("ctx"), lax.axis_size("fsdp")
    me, my_shard = lax.axis_index("ctx"), lax.axis_index("fsdp")
    me_array = me.astype(jnp.int32).reshape(1)
    shard = query_weight.shape[0]
    hidden = expand_weight.shape[1]
    own_width = width // count
    heads = own_width // HEAD
    piece = hidden // depth // count
    block = depth * piece
    middle = count // 2
    order = plane_order()
    evens, odds = order[:middle], order[middle:]
    scale = HEAD**-0.5
    bits = (count * rows - 1).bit_length()
    all_rows = batch * rows

    columns = lambda w: lax.dynamic_slice_in_dim(w, me * own_width, own_width, 1).astype(BF)
    names = (query_bias, value_bias, output_bias, first_gain, first_shift, reduce_bias, second_gain, second_shift)
    packed = jnp.concatenate(names + (expand_bias,))
    size = packed.shape[0]
    terms = jnp.concatenate(in_terms(packed, 3))
    line = 3 * own_width
    lines = -(-terms.shape[0] // (16 * line)) * 16
    terms = jnp.pad(terms, (0, lines * line - terms.shape[0])).reshape(lines, line)
    own_heads = jnp.concatenate([columns(query_weight), columns(key_weight), columns(value_weight)], axis=1)
    own_heads = gather_shards(jnp.concatenate([own_heads, terms], axis=0))
    packed = own_heads[:, shard:].reshape(depth, lines * line)[:, : 3 * size]
    packed = jnp.sum(packed.reshape(depth, 3, -1).astype(F32), axis=1)
    own_heads = own_heads[:, :shard].reshape(width, line)
    (bias_query, bias_value, bias_output, gain_first, shift_first, bias_reduce, gain_second, shift_second) = (
        packed[:, i * shard : (i + 1) * shard].reshape(width) for i in range(len(names))
    )
    wide_bias = packed[:, len(names) * shard :].reshape(depth, count, piece)
    bias_halves = [
        jnp.stack([lax.dynamic_index_in_dim(wide_bias, me ^ k, 1, keepdims=False).reshape(1, block) for k in ks])
        for ks in (evens, odds)
    ]
    own_part = lambda v: lax.dynamic_slice_in_dim(v, me * own_width, own_width, 0)
    head_bias = jnp.concatenate([own_part(bias_query), jnp.zeros((own_width,), F32), own_part(bias_value)])
    head_scale = jnp.concatenate([jnp.full((own_width,), scale * LOG2E, F32), jnp.ones((2 * own_width,), F32)])

    thin = shard // count
    folds = width // block
    strip = lax.dynamic_slice_in_dim(output_weight, me * thin, thin, 0).astype(BF)
    strip = jnp.concatenate([strip[:, i * block : (i + 1) * block] for i in range(folds)], axis=0)
    block_expand = [
        lax.dynamic_slice_in_dim(expand_weight, (z * count + me) * piece, piece, 1).astype(BF) for z in range(depth)
    ]
    block_expand = jnp.concatenate([jnp.concatenate(block_expand, axis=1), strip], axis=0)
    block_expand = lax.all_gather(block_expand, "fsdp", axis=0)

    reduce_blocks = [lax.dynamic_slice_in_dim(reduce_weight, (me ^ k) * piece, piece, 0).astype(BF) for k in evens]
    reduce_own = lax.all_gather(jnp.stack(reduce_blocks), "fsdp", axis=0)

    def plane(value):
        first, second = peer(value, 2), peer(value, 4)
        part = value.shape[0] // 2
        return first, second, (peer(first[:part], 4), peer(second[part:], 2))

    def chip(blocks):
        return blocks + [jax.tree.map(lambda v: peer(v, 1), b) for b in blocks]

    low_in = [tokens[s].astype(BF) for s in range(batch)]
    first = plane(low_in[0])
    seg = after(segments, first[0])
    for b in range(count.bit_length() - 1):
        seg = jnp.concatenate([seg, peer(seg, 1 << b)], axis=1)
    seg = seg.reshape(batch, count, rows)
    seg = jnp.concatenate([seg[:, k] for k in order], axis=1)
    masks = [mask_columns(seg[s], bits) for s in range(batch)]
    second = plane(after(low_in[1], first[0], first[1]))
    kept = []
    for s, got in enumerate((first, second)):
        blocks = chip([(low_in[s],), (got[0],), (got[1],), got[2]])
        blocks = [v for b in blocks for v in b]
        qkv = project(blocks, own_heads, head_bias, head_scale)
        if s == 0:
            qkv = after(qkv, second[0], second[1])
        out, lse = attend(qkv, *masks[s], heads, rows)
        kept.append((blocks, qkv, *masks[s], out, lse))
    sent = [kept[s][4] for s in range(batch)]

    expand_plane = plane(after(block_expand, sent[0]))
    got_expand = chip([(block_expand,), (expand_plane[0],), (expand_plane[1],), expand_plane[2]])
    full_output = assemble_output(got_expand, shard, thin, me_array)

    earlier = None
    for s in range(batch):
        half = sent[s].shape[0] // 2
        pieces = even_pieces(sent[s][:half], peer(sent[s][half:], 1))
        earlier = branch(s, me_array, pieces, full_output, tokens, bias_output, gain_first, shift_first, earlier)
    context_low, hidden_in, hidden_low, normed_first, inverse_first = (
        v.reshape(all_rows, v.shape[2]) for v in earlier
    )

    act_even, act_odd, slope_even, slope_odd = expand_forward(hidden_low, bias_halves, got_expand, shard)
    reduce_own = after(reduce_own, hidden_low)
    reduce_halves = [reduce_own, peer(reduce_own, 1)]
    result, du_second, dr, sums_second = reduce_forward(
        (act_even, act_odd),
        reduce_halves,
        hidden_in,
        cotangent.reshape(all_rows, width),
        bias_reduce,
        gain_second,
        shift_second,
    )

    de_even, de_odd, sums_even, sums_odd, grad_pre, da, sums_first = feed_back(
        dr, reduce_halves, (slope_even, slope_odd), du_second, normed_first, inverse_first, gain_first, got_expand, shard
    )
    da_parts = da.reshape(batch, rows, width)
    own_grads, other_grads = zip(
        *(context_back(s, me_array, da_parts, full_output, own_width, middle) for s in range(batch))
    )
    dc = [even_pieces(own_grads[0], peer(other_grads[0], 1))]

    other_low, other_context = peer(hidden_low, 1), peer(context_low, 1)
    other_de, other_da = peer(de_odd, 1), peer(da, 1)
    kept_a, sent_a, kept_b, sent_b = expand_gradient(
        me_array, hidden_low, other_low, context_low, other_context, de_even, other_de, da, other_da, own_width
    )
    got_a, got_b = peer(sent_a, 4), peer(sent_b, 2)

    other_act, other_dr = peer(act_odd, 1), peer(dr, 1)
    sum_reduce = reduce_gradient(act_even, other_act, dr, other_dr, depth, piece)

    dc[0][0] = after(dc[0][0], kept_a, sum_reduce)
    dc.append(even_pieces(own_grads[1], peer(other_grads[1], 1)))
    sum_reduce = lax.psum_scatter(sum_reduce, "fsdp", scatter_dimension=0, tiled=False)

    add = lambda a, b: (a.astype(F32) + b.astype(F32)).astype(BF)
    half = count * rows // 2
    before, head_sums = None, 0.0
    grad_in, grads = [], []
    for s in range(batch):
        blocks, qkv, mask_q, mask_k, out, lse = kept[s]
        grads.append(attend_back(qkv, mask_q, mask_k, dc[s], out, lse, heads, rows))
        if s == 0:
            got_a, got_b = after((got_a, got_b), grads[0])
            next_a, next_b = add(kept_a, got_a), add(kept_b, got_b)
            got_a, got_b = peer(next_a[1], 2), peer(next_b[1], 4)
        before, sums = heads_gradient(blocks, grads[s], before)
        head_sums = head_sums + sums[0]
        away = peer(dot_nt(grads[s][half:], own_heads).astype(BF), 1)
        home = (dot_nt(grads[s][:half], own_heads) + away.astype(F32)).astype(BF)
        if s == 0:
            dc[1][0] = after(dc[1][0], home)
        got = [home[:rows]] + [peer(home[i * rows : (i + 1) * rows], 2 * i) for i in range(1, middle)]
        grad_in.append((s, got))
    got_a, got_b = after((got_a, got_b), grads[1])
    sum_expand = jnp.concatenate([add(next_a[0], got_a), add(next_b[0], got_b)], axis=0)
    sum_expand = lax.psum_scatter(sum_expand, "fsdp", scatter_dimension=0, tiled=True)
    sum_reduce = reduce_even([after(sum_reduce, grads[1])[i] for i in range(middle)], False)
    grad_in = [
        grad_pre[s * rows : (s + 1) * rows] + sum(v.astype(F32) for v in got) for s, got in grad_in
    ]
    grad_heads = before
    grad_head_bias = jnp.pad(jnp.stack(in_terms(head_sums, 2)), ((0, 14), (0, 0)))
    home_heads = jnp.concatenate(
        [grad_heads.reshape(depth, shard, line), jnp.broadcast_to(grad_head_bias, (depth, 16, line))], axis=1
    )
    home_heads = reduce_shards(home_heads)
    home_heads = jnp.concatenate(
        [home_heads[:shard].astype(BF)]
        + [v[None] for v in in_terms(home_heads[shard] + home_heads[shard + 1], 2)]
        + [jnp.zeros((14, line), BF)],
        axis=0,
    )

    def spread(value):
        got = plane(value)
        got = (value, got[0], got[1], jnp.concatenate(got[2], axis=0))
        return [*got] + [peer(v, 1) for v in got]

    grad_query_weight, grad_key_weight, grad_value_weight, wide_biases = unpack_heads(
        me_array, spread(home_heads), shard, width
    )
    grad_expand_weight, grad_output_weight = unpack_expand(me_array, spread(sum_expand), depth, hidden, width)
    grad_reduce_weight = lax.all_gather(sum_reduce, "ctx", axis=0, tiled=True).astype(F32)
    own_shard = lambda v: lax.dynamic_slice_in_dim(v, my_shard * shard, shard, 0)

    vectors = (sums_first[2], sums_first[0], sums_first[1], sums_second[2], sums_second[0], sums_second[1])
    wide_bias = by_owner(
        [sums[i, 0].reshape(depth, 1, piece) for sums in (sums_even, sums_odd) for i in range(middle)], 1
    ).reshape(depth, hidden // depth)
    small = jnp.concatenate([v.reshape(depth, shard) for v in vectors] + [wide_bias], axis=1)
    for b in range(count.bit_length() - 1):
        small = small + peer(small, 1 << b)
    small = reduce_shards(small)
    vec = [small[i * shard : (i + 1) * shard] for i in range(len(vectors))]
    vec_expand = small[len(vectors) * shard :]
    return (
        result.reshape(batch, rows, width),
        jnp.stack(grad_in),
        grad_query_weight,
        own_shard(wide_biases[0]),
        grad_key_weight,
        grad_value_weight,
        own_shard(wide_biases[2]),
        grad_output_weight,
        vec[0],
        vec[1],
        vec[2],
        grad_expand_weight,
        vec_expand,
        grad_reduce_weight,
        vec[3],
        vec[4],
        vec[5],
    )


def solution(mesh):
    seq = P("fsdp", "ctx", None)
    mat = P("fsdp", None)
    vec = P("fsdp")
    in_specs = (
        seq,
        P("fsdp", "ctx"),
        mat,
        vec,
        mat,
        mat,
        vec,
        mat,
        vec,
        vec,
        vec,
        mat,
        vec,
        mat,
        vec,
        vec,
        vec,
        seq,
    )
    out_specs = (seq, seq, mat, vec, mat, mat, vec, mat, vec, vec, vec, mat, vec, mat, vec, vec, vec)
    count, depth = mesh.shape["ctx"], mesh.shape["fsdp"]

    def layer(*args):
        width, hidden = args[0].shape[2], args[11].shape[1]
        piece, own_width = hidden // depth // count, width // count
        tiled = count == 8 and args[0].shape[0] == 2 and piece % LANES == 0 and own_width == LANES
        tiled = tiled and width // depth // count % 16 == 0
        return (body if tiled else plain_body)(*args)

    return jax.shard_map(layer, mesh=mesh, in_specs=in_specs, out_specs=out_specs, check_vma=False)
```

```python
import functools

import jax
import jax.numpy as jnp
from jax import lax
from jax.experimental import pallas as pl
from jax.experimental.pallas import tpu as pltpu
from jax.sharding import PartitionSpec as P

HEAD = 64
LANES = 128
VMEM_LIMIT = 62 << 20
COST_SHARE = 64
EPS = 1e-05
BIG = 1e30
LOG2E = 1.4426950408889634
SQRT_HALF = 0.7071067811865476
DENSITY = 0.3989422804014327
BF = jnp.bfloat16
F32 = jnp.float32


def dot_nn(left, right):
    return jnp.dot(left, right, preferred_element_type=F32)


def dot_tn(left, right):
    return lax.dot_general(left, right, (((0,), (0,)), ((), ())), preferred_element_type=F32)


def dot_nt(left, right):
    return lax.dot_general(left, right, (((1,), (1,)), ((), ())), preferred_element_type=F32)


def exchange(value, axis, k):
    count = lax.axis_size(axis)
    return lax.ppermute(value, axis, [(i, i ^ k) for i in range(count)])


def peer(value, k):
    return exchange(value, "ctx", k)


def after(value, *needed):
    return lax.optimization_barrier((value, needed))[0]


def join(*values):
    return lax.optimization_barrier(values)


def plane_list(count):
    return list(range(0, count, 2)) + list(range(1, count, 2))


def plane_order():
    return plane_list(lax.axis_size("ctx"))


def gather_even(value, low_first):
    count = lax.axis_size("ctx")
    got = {0: value}
    for k in range(2, count, 2):
        bits = [1 << b for b in range(1, count.bit_length()) if k >> b & 1]
        step = bits[-1] if low_first else bits[0]
        got[k] = peer(got[k ^ step], step)
    return [got[k] for k in range(0, count, 2)]


def by_owner(parts, axis, order=None, mesh_axis="ctx"):
    order = order or plane_order()
    stacked = jnp.stack([parts[order.index(k)] for k in range(len(order))])
    me = lax.axis_index(mesh_axis)
    return jnp.concatenate(
        [lax.dynamic_index_in_dim(stacked, me ^ g, 0, keepdims=False) for g in range(len(order))], axis=axis
    )


def rows_to_heads(value, width):
    count = lax.axis_size("ctx")
    me = lax.axis_index("ctx")
    mine, other = [], []
    for k in range(0, count, 2):
        to = me ^ k
        first = lax.dynamic_slice_in_dim(value, to * width, width, 1)
        second = lax.dynamic_slice_in_dim(value, (to ^ 1) * width, width, 1)
        got = jnp.concatenate([first, second], axis=1)
        if k:
            got = peer(got, k)
        mine.append(got[:, :width])
        other.append(got[:, width:])
    return jnp.concatenate(mine + [peer(jnp.concatenate(other, axis=0), 1)], axis=0)


def heads_to_rows(value):
    count = lax.axis_size("ctx")
    rows, width = value.shape[0] // count, value.shape[1]
    half = value.shape[0] // 2
    both = jnp.concatenate([value[:half], peer(value[half:], 1)], axis=1)
    even, odd = [], []
    for i, k in enumerate(range(0, count, 2)):
        got = both[i * rows : (i + 1) * rows]
        if k:
            got = peer(got, k)
        even.append(got[:, :width])
        odd.append(got[:, width:])
    return even + odd


def reduce_even(blocks, low_first):
    count = lax.axis_size("ctx")
    bits = [1 << b for b in range(1, count.bit_length() - 1)]
    if not low_first:
        bits = bits[::-1]
    held = dict(zip(range(0, count, 2), blocks))
    for bit in bits:
        sent = [k for k in held if k & bit]
        got = peer(jnp.stack([held[k] for k in sent]), bit)
        got = {k ^ bit: got[i] for i, k in enumerate(sent)}
        held = {k: (held[k].astype(F32) + got[k].astype(F32)).astype(BF) for k in held if not k & bit}
    return held[0]


def gather_shards(value):
    depth = lax.axis_size("fsdp")
    parts = [value[None]] + [exchange(value, "fsdp", j)[None] for j in range(1, depth)]
    return by_owner(parts, 0, list(range(depth)), "fsdp")


def reduce_shards(value):
    depth = lax.axis_size("fsdp")
    me = lax.axis_index("fsdp")
    total = lax.dynamic_index_in_dim(value, me, 0, keepdims=False).astype(F32)
    for j in range(1, depth):
        sent = lax.dynamic_index_in_dim(value, me ^ j, 0, keepdims=False)
        total = total + exchange(sent, "fsdp", j).astype(F32)
    return total


def gather_doubling(value):
    got = value[None]
    step = 1
    while step < lax.axis_size("fsdp"):
        got = jnp.concatenate([got, exchange(got, "fsdp", step)], axis=0)
        step *= 2
    return got


def in_terms(vector, count):
    terms = []
    for _ in range(count):
        terms.append(vector.astype(BF))
        vector = vector - terms[-1].astype(F32)
    return terms


def whole(shape):
    return pl.BlockSpec(shape, lambda *i: (0,) * len(shape))


def params(limit=VMEM_LIMIT):
    return pltpu.CompilerParams(vmem_limit_bytes=limit)


def cost(flops, size, exps=0):
    return pl.CostEstimate(
        flops=flops // COST_SHARE, bytes_accessed=size // COST_SHARE, transcendentals=exps // COST_SHARE
    )


def mask_columns(seg, bits):
    lane = jnp.arange(LANES) % HEAD
    bit = (seg[:, None] >> jnp.minimum(lane // 2, 30)) & 1
    flip = bit ^ (lane & 1)
    used = lane < 2 * bits
    for_query = jnp.where(used & (flip == 1), -BIG, 0.0).astype(BF)
    for_key = jnp.where(used, 1 - flip, ((lane >= 60) & (lane < 63)).astype(jnp.int32)).astype(BF)
    return for_query, for_key


def lane_index():
    return lax.broadcasted_iota(jnp.int32, (1, LANES), 1)


def merge(main, extra, h):
    lane = lane_index()
    return jnp.where((lane < HEAD) if h == 0 else (lane >= HEAD), main, extra)


def with_terms(extra, number):
    lane = lane_index() % HEAD
    first = number.astype(BF).astype(F32)
    rest = number - first
    second = rest.astype(BF).astype(F32)
    third = rest - second
    terms = jnp.where(lane == 60, first, jnp.where(lane == 61, second, third)).astype(BF)
    return jnp.where((lane >= 60) & (lane < 63), terms, extra)


def forward_kernel(q, k, v, mask_q, mask_k, out, lse, key_side, value_side, *, heads):
    lane = lane_index()

    @pl.when(pl.program_id(0) == 0)
    def _():
        for h in range(heads):
            key_side[h] = merge(k[...], mask_k[...], h)
            value_side[h] = merge(v[...], jnp.ones((1, LANES), BF), h)

    whole, whole_lse = None, None
    for h in range(heads):
        scores = dot_nt(merge(q[...], mask_q[...], h), key_side[h])
        top = jnp.max(scores, axis=1, keepdims=True)
        weights = jnp.exp2(scores - top).astype(BF)
        both = dot_nn(weights, value_side[h])
        total = pltpu.roll(both, HEAD, 1)
        context, log_total = both / total, top + jnp.log2(total)
        if whole is None:
            whole, whole_lse = context, log_total
        else:
            whole = jnp.where(lane < HEAD, whole, context)
            whole_lse = jnp.where(lane < HEAD, whole_lse, log_total)
    out[...] = whole.astype(BF)
    lse[...] = whole_lse


def attend(qkv, mask_q, mask_k, heads, block):
    count = qkv.shape[0]
    part = lambda j: pl.BlockSpec((block, LANES), lambda i: (i, j))
    full = lambda j: pl.BlockSpec((count, LANES), lambda i: (0, j))
    products = 2 * 2 * count * count * LANES * heads
    return pl.pallas_call(
        functools.partial(forward_kernel, heads=heads),
        grid=(count // block,),
        in_specs=[part(0), full(1), full(2), part(0), full(0)],
        out_specs=[part(0), part(0)],
        out_shape=[jax.ShapeDtypeStruct((count, LANES), BF), jax.ShapeDtypeStruct((count, LANES), F32)],
        scratch_shapes=[pltpu.VMEM((heads, count, LANES), BF), pltpu.VMEM((heads, count, LANES), BF)],
        compiler_params=params(48 << 20),
        cost_estimate=cost(products * 2, 12 * count * LANES, count * count * heads),
        name="attend",
    )(qkv, qkv, qkv, mask_q, mask_k)


def backward_kernel(*refs, heads, first, steps, total, block, pieces):
    q, k, v, mask_q, mask_k, out, lse = refs[:7]
    parts = refs[7 : 7 + pieces]
    refs = refs[7 + pieces :]
    if first:
        grads_before, dk_before, dv_before = refs[:3]
        refs = refs[3:]
    grads = refs[0]
    if steps < total:
        dk_t, dv_t = refs[1:3]
        key_side, value_side, dc_all = refs[3:]
    else:
        key_side, value_side, dc_all, dk_t, dv_t = refs[1:]
    lane = lane_index()
    step = pl.program_id(0)

    @pl.when(step == 0)
    def _():
        ones = ((lane % HEAD >= 60) & (lane % HEAD < 63)).astype(F32).astype(BF)
        for h in range(heads):
            key_side[h] = merge(k[...], mask_k[...], h)
            value_side[h] = merge(v[...], ones, h)
        if first:
            dk_t[...] = dk_before[...]
            dv_t[...] = dv_before[...]
            grads[: first * block, :LANES] = grads_before[...]
        else:
            dk_t[...] = jnp.zeros_like(dk_t)
            dv_t[...] = jnp.zeros_like(dv_t)
        if pieces == 1:
            dc_all[...] = parts[0][...]
        else:
            for i in range(pieces):
                dc_all[i * block : (i + 1) * block, :] = parts[i][:, :LANES]
                dc_all[(pieces + i) * block : (pieces + i + 1) * block, :] = parts[i][:, LANES:]

    dc = dc_all.at[pl.ds(pl.multiple_of((first + step) * block, block), block), :]
    product = dc[...].astype(F32) * out[...].astype(F32)
    low = jnp.sum(jnp.where(lane < HEAD, product, 0.0), axis=1, keepdims=True)
    high = jnp.sum(jnp.where(lane < HEAD, 0.0, product), axis=1, keepdims=True)
    query_extra = with_terms(mask_q[...], -pltpu.roll(lse[...], HEAD, 1))
    grad_extra = with_terms(jnp.zeros((1, LANES), BF), jnp.where(lane < HEAD, -high, -low))
    q_t, dc_t = q[...].T, dc[...].T
    dq = None
    for h in range(heads):
        probs = jnp.exp2(dot_nt(merge(q[...], query_extra, h), key_side[h]))
        centred = dot_nt(merge(dc[...], grad_extra, h), value_side[h])
        ds = (probs * centred).astype(BF)
        part = dot_nn(ds, key_side[h])
        dq = part if dq is None else jnp.where(lane < HEAD, dq, part)
        own = slice(HEAD * h, HEAD * h + HEAD)
        dk_t[own, :] += dot_nn(q_t[own, :], ds)
        dv_t[own, :] += dot_nn(dc_t[own, :], probs.astype(BF))
    at = step * block if steps < total else (first + step) * block
    grads[pl.ds(pl.multiple_of(at, block), block), :LANES] = (dq.astype(BF).astype(F32) * HEAD**-0.5).astype(BF)
    if steps == total:

        @pl.when(step == steps - first - 1)
        def _():
            grads[:, LANES : 2 * LANES] = (dk_t[...] * (1.0 / LOG2E)).T.astype(BF)
            grads[:, 2 * LANES :] = dv_t[...].T.astype(BF)


def attend_back(qkv, mask_q, mask_k, dc, out, lse, heads, block, part=None, before=None, place=0):
    dc = dc if isinstance(dc, list) else [dc]
    count = qkv.shape[0]
    total = count // block
    first = total // 2 if part == 1 else 0
    steps = total // 2 if part == 0 else total
    piece = lambda j: pl.BlockSpec((block, LANES), lambda i: (first + i, j))
    full = lambda j: pl.BlockSpec((count, LANES), lambda i: (0, j))
    products = 5 * 2 * count * count * LANES * heads
    side = (LANES, count)
    shapes = [jax.ShapeDtypeStruct((count, 3 * LANES), BF)]
    scratch = [
        pltpu.VMEM((heads, count, LANES), BF),
        pltpu.VMEM((heads, count, LANES), BF),
        pltpu.VMEM((count, LANES), BF),
    ]
    if part == 0:
        shapes = [jax.ShapeDtypeStruct((count // 2, LANES), BF)] + [jax.ShapeDtypeStruct(side, F32)] * 2
    else:
        scratch += [pltpu.VMEM(side, F32)] * 2
    before = before or []
    got = pl.pallas_call(
        functools.partial(
            backward_kernel, heads=heads, first=first, steps=steps, total=total, block=block, pieces=len(dc)
        ),
        grid=(steps - first,),
        in_specs=[piece(0), full(1), full(2), piece(0), full(0), piece(0), piece(0)]
        + [pl.BlockSpec((block if len(dc) > 1 else count, v.shape[1]), lambda i: (place, 0)) for v in dc]
        + [whole(v.shape) for v in before],
        out_specs=[whole(v.shape) for v in shapes],
        out_shape=shapes,
        scratch_shapes=scratch,
        compiler_params=params(),
        cost_estimate=cost(products, 16 * count * LANES, count * count * heads),
        name="attend_back",
    )(qkv, qkv, qkv, mask_q, mask_k, out, lse, *dc, *before)
    return got if part == 0 else got[0]


def project_kernel(*refs, blocks, rows, bits):
    weight, bias, factor, out, mask_q, mask_k = refs[blocks:]
    lane = lane_index() % HEAD
    used = lane < 2 * bits
    fixed = ((lane >= 60) & (lane < 63)).astype(F32).astype(BF)
    for i, ref in enumerate(refs[:blocks]):
        at = slice(i * rows, (i + 1) * rows)
        got = (dot_nn(ref[:rows, :], weight[...]) + bias[...]) * factor[...]
        out[at, :] = got.astype(BF)
        parts = ref[rows : rows + 16, : 2 * rows].astype(F32)
        number = (parts[:8, :rows] * 64 + parts[:8, rows:]).T[:, :1].astype(jnp.int32)
        flip = ((number >> (lane // 2)) & 1) ^ (lane & 1)
        mask_q[at, :] = jnp.where(used & (flip == 1), -BIG, 0.0).astype(BF)
        mask_k[at, :] = jnp.where(used, (1 - flip).astype(F32).astype(BF), fixed)


def project(blocks, rows, weight, bias, factor, bits):
    width, line = weight.shape
    args = (*blocks, weight, bias[None], factor[None])
    count = rows * len(blocks)
    shapes = [(count, line), (count, LANES), (count, LANES)]
    return pl.pallas_call(
        functools.partial(project_kernel, blocks=len(blocks), rows=rows, bits=bits),
        in_specs=[whole(v.shape) for v in args],
        out_specs=[whole(v) for v in shapes],
        out_shape=[jax.ShapeDtypeStruct(v, BF) for v in shapes],
        grid=(1,),
        compiler_params=params(),
        cost_estimate=cost(2 * count * width * line, 2 * count * (width + line)),
        name="project",
    )(*args)


def flatten_blocks(blocks):
    flat, parts = [], []
    for n, block in enumerate(blocks):
        first = 0
        for part in block:
            flat.append(part)
            parts.append((n, first))
            first += part.shape[0]
    return flat, tuple(parts)


def assemble_kernel(me, *refs, parts, thin, folds):
    out = refs[-1]
    shard = len({n for n, _ in parts}) * thin
    block = refs[0].shape[2]
    order = plane_list(len({n for n, _ in parts}))
    for ref, (n, first) in zip(refs, parts):
        for z in range(ref.shape[0]):
            row = pl.multiple_of((first + z) * shard + (me[0] ^ order[n]) * thin, thin)
            for f in range(folds):
                out[pl.ds(row, thin), f * block : (f + 1) * block] = ref[z, f * thin : (f + 1) * thin, :]


def assemble_output(blocks, shard, thin, me):
    flat, parts = flatten_blocks(blocks)
    _, tall, block = flat[0].shape
    strip = tall - shard
    folds = strip // thin
    width = folds * block
    specs = [pl.BlockSpec((v.shape[0], strip, block), lambda i: (0, shard // strip, 0)) for v in flat]
    return pl.pallas_call(
        functools.partial(assemble_kernel, parts=parts, thin=thin, folds=folds),
        grid=(1,),
        in_specs=[pl.BlockSpec(memory_space=pltpu.SMEM)] + specs,
        out_specs=whole((width, width)),
        out_shape=jax.ShapeDtypeStruct((width, width), BF),
        compiler_params=params(),
        cost_estimate=cost(0, 4 * width * width),
        name="assemble_output",
    )(me, *flat)


def branch_kernel(me, *refs, pieces, aliased):
    weight, tokens, bias, gain, shift = refs[pieces : pieces + 5]
    context, hidden, low, normed, inverse = refs[pieces + 5 + aliased :]
    second = (me[0] & 1) == 1
    pair = refs[0].shape[1]
    for i in range(pieces):
        at = pl.multiple_of(((me[0] ^ (2 * i)) // 2) * pair, pair)
        got = refs[i][...]
        swapped = jnp.concatenate([got[:, pair // 2 :], got[:, : pair // 2]], axis=1)
        context[:, pl.ds(at, pair)] = jnp.where(second, swapped, got)
    total = tokens[...] + dot_nn(context[...], weight[...]) + bias[...]
    mean = jnp.mean(total, axis=1, keepdims=True)
    centred = total - mean
    scale = lax.rsqrt(jnp.mean(centred * centred, axis=1, keepdims=True) + EPS)
    unit = centred * scale
    out = unit * gain[...] + shift[...]
    hidden[...] = out
    low[...] = out.astype(BF)
    normed[...] = unit
    inverse[...] = jnp.broadcast_to(scale, inverse.shape)


def branch(s, me, pieces, weight, tokens, bias, gain, shift, earlier):
    batch, rows, width = tokens.shape
    at = pl.BlockSpec((None, rows, width), lambda i: (s, 0, 0))
    thin = pl.BlockSpec((None, rows, LANES), lambda i: (s, 0, 0))
    vec = whole((1, width))
    earlier = earlier or ()
    first = 1 + len(pieces) + 5
    full = lambda t: jax.ShapeDtypeStruct((batch, rows, width), t)
    return pl.pallas_call(
        functools.partial(branch_kernel, pieces=len(pieces), aliased=len(earlier)),
        grid=(1,),
        in_specs=[pl.BlockSpec(memory_space=pltpu.SMEM)]
        + [whole(v.shape) for v in pieces]
        + [whole(weight.shape), at, vec, vec, vec]
        + [pl.BlockSpec(memory_space=pl.ANY)] * len(earlier),
        out_specs=[at, at, at, at, thin],
        out_shape=[full(BF), full(F32), full(BF), full(F32), jax.ShapeDtypeStruct((batch, rows, LANES), F32)],
        input_output_aliases={first + i: i for i in range(len(earlier))},
        compiler_params=params(),
        cost_estimate=cost(2 * rows * width * width, 2 * width * width + 18 * rows * width),
        name="branch",
    )(me, *pieces, weight, tokens, bias[None], gain[None], shift[None], *earlier)


def fetch_blocks(refs, parts, slots, sems, step, middle, shard):
    def copies(i):
        made = []
        for j, (ref, (n, first)) in enumerate(zip(refs, parts)):
            if n % middle == i:
                target = slots.at[i % 2, n // middle, pl.ds(first, ref.shape[0])]
                made.append(pltpu.make_async_copy(ref.at[:, :shard, :], target, sems.at[j]))
        return made

    for i in range(middle):

        @pl.when(step == i)
        def _():
            if i == 0:
                for copy in copies(0):
                    copy.start()
            if i + 1 < middle:
                for copy in copies(i + 1):
                    copy.start()
            for copy in copies(i):
                copy.wait()


def expand_kernel(*refs, middle, depth, parts):
    low, bias_even, bias_odd = refs[:3]
    blocks = refs[3 : 3 + len(parts)]
    outs = refs[3 + len(parts) : 7 + len(parts)]
    slots, sems = refs[7 + len(parts) :]
    step = pl.program_id(0)
    shard = slots.shape[3]
    fetch_blocks(blocks, parts, slots, sems, step, middle, shard)
    slot = step % 2
    rows = low.shape[0] // 2
    for parity, bias in enumerate((bias_even, bias_odd)):
        for part in range(2):
            at = slice(part * rows, part * rows + rows)
            total = bias[...]
            for z in range(depth):
                total = total + dot_nn(low[at, z * shard : (z + 1) * shard], slots[slot, parity, z])
            cdf = 0.5 * (1.0 + lax.erf(total * SQRT_HALF))
            outs[parity][at, :] = (total * cdf).astype(BF)
            outs[2 + parity][at, :] = (cdf + total * DENSITY * jnp.exp(-0.5 * total * total)).astype(BF)


def expand_forward(low, bias_halves, blocks, shard):
    rows, width = low.shape
    middle = len(blocks) // 2
    depth = width // shard
    block = blocks[0][0].shape[2]
    flat, parts = flatten_blocks(blocks)
    bias = pl.BlockSpec((None, 1, block), lambda i: (i, 0, 0))
    out = pl.BlockSpec((rows, block), lambda i: (0, i))
    return pl.pallas_call(
        functools.partial(expand_kernel, middle=middle, depth=depth, parts=parts),
        grid=(middle,),
        in_specs=[whole(low.shape), bias, bias] + [pl.BlockSpec(memory_space=pl.ANY)] * len(flat),
        out_specs=[out] * 4,
        out_shape=[jax.ShapeDtypeStruct((rows, middle * block), BF)] * 4,
        scratch_shapes=[pltpu.VMEM((2, 2, depth, shard, block), BF), pltpu.SemaphoreType.DMA((len(flat),))],
        compiler_params=params(),
        cost_estimate=cost(4 * rows * width * middle * block, 4 * width * middle * block + 8 * rows * middle * block),
        name="expand",
    )(low, *bias_halves, *flat)


def norm_back(grad, normed, inverse, gain):
    scaled = grad * gain
    first = jnp.mean(scaled, axis=1, keepdims=True)
    second = jnp.mean(scaled * normed, axis=1, keepdims=True)
    return inverse * (scaled - first - normed * second)


def reduce_kernel(
    act_even, act_odd, w_even, w_odd, hidden, grad_out, bias, gain, shift, result, du, low, sums, total, *, steps
):
    step = pl.program_id(0)
    block = act_even.shape[1]
    width = total.shape[1]
    part = dot_nn(act_even[...], w_even[...].reshape(block, width))
    part = part + dot_nn(act_odd[...], w_odd[...].reshape(block, width))

    @pl.when(step == 0)
    def _():
        total[...] = part + bias[...]
        sums[...] = jnp.zeros_like(sums)

    @pl.when(step > 0)
    def _():
        total[...] += part

    @pl.when(step == steps - 1)
    def _():
        rows = 64

        @pl.loop(0, total.shape[0] // rows)
        def _(i):
            at = pl.ds(pl.multiple_of(i * rows, rows), rows)
            value = total[at, :] + hidden[at, :]
            mean = jnp.mean(value, axis=1, keepdims=True)
            centred = value - mean
            inverse = lax.rsqrt(jnp.mean(centred * centred, axis=1, keepdims=True) + EPS)
            normed = centred * inverse
            result[at, :] = normed * gain[...] + shift[...]
            grad = grad_out[at, :]
            back = norm_back(grad, normed, inverse, gain[...])
            du[at, :] = back
            rounded = back.astype(BF)
            low[at, :] = rounded
            sums[0:1, :] += jnp.sum(grad * normed, axis=0, keepdims=True)
            sums[1:2, :] += jnp.sum(grad, axis=0, keepdims=True)
            sums[2:3, :] += jnp.sum(rounded.astype(F32), axis=0, keepdims=True)


def reduce_forward(acts, weights, hidden, grad_out, bias, gain, shift):
    rows, width = hidden.shape
    depth, middle, piece, _ = weights[0].shape
    block = depth * piece
    act = pl.BlockSpec((rows, block), lambda i: (0, i))
    weight = pl.BlockSpec((depth, None, piece, width), lambda i: (0, i, 0, 0))
    full, vec = whole((rows, width)), whole((1, width))
    return pl.pallas_call(
        functools.partial(reduce_kernel, steps=middle),
        grid=(middle,),
        in_specs=[act, act, weight, weight, full, full, vec, vec, vec],
        out_specs=[full, full, full, whole((8, width))],
        out_shape=[
            jax.ShapeDtypeStruct((rows, width), F32),
            jax.ShapeDtypeStruct((rows, width), F32),
            jax.ShapeDtypeStruct((rows, width), BF),
            jax.ShapeDtypeStruct((8, width), F32),
        ],
        scratch_shapes=[pltpu.VMEM((rows, width), F32)],
        compiler_params=params(),
        cost_estimate=cost(4 * rows * width * middle * block, 4 * width * middle * block + 16 * rows * width),
        name="reduce",
    )(*acts, *weights, hidden, grad_out, bias[None], gain[None], shift[None])


def feed_back_kernel(*refs, middle, depth, steps, parts):
    low, w_even, w_odd, slope_even, slope_odd, du_second, normed, inverse, gain = refs[:9]
    refs = refs[9:]
    blocks = refs[: len(parts)]
    de_even, de_odd, bias_even, bias_odd, du, da, sums = refs[len(parts) : 7 + len(parts)]
    slots, sems, total = refs[7 + len(parts) :]
    step = pl.program_id(0)
    shard, block = slots.shape[3], slots.shape[4]
    width = total.shape[1]
    fetch_blocks(blocks, parts, slots, sems, step, middle, shard)
    slot = step % 2

    @pl.when(step == 0)
    def _():
        total[...] = du_second[...]
        sums[...] = jnp.zeros_like(sums)

    for parity, (weight, slope, de, bias) in enumerate(
        ((w_even, slope_even, de_even, bias_even), (w_odd, slope_odd, de_odd, bias_odd))
    ):
        grad = dot_nt(low[...], weight[...].reshape(block, width)) * slope[...].astype(F32)
        rounded = grad.astype(BF)
        de[...] = rounded
        bias[...] = jnp.sum(rounded.astype(F32), axis=0, keepdims=True)
        for z in range(depth):
            total[:, z * shard : (z + 1) * shard] += dot_nt(rounded, slots[slot, parity, z])

    @pl.when(step == steps - 1)
    def _():
        rows = 64

        @pl.loop(0, total.shape[0] // rows)
        def _(i):
            at = pl.ds(pl.multiple_of(i * rows, rows), rows)
            grad, unit = total[at, :], normed[at, :]
            back = norm_back(grad, unit, inverse[at, 0:1], gain[...])
            du[at, :] = back
            rounded = back.astype(BF)
            da[at, :] = rounded
            sums[0:1, :] += jnp.sum(grad * unit, axis=0, keepdims=True)
            sums[1:2, :] += jnp.sum(grad, axis=0, keepdims=True)
            sums[2:3, :] += jnp.sum(rounded.astype(F32), axis=0, keepdims=True)


def feed_back(low, weights, slopes, du_second, normed, inverse, gain, blocks, shard):
    rows, width = low.shape
    depth, middle, piece, _ = weights[0].shape
    block = depth * piece
    flat, parts = flatten_blocks(blocks)
    act = pl.BlockSpec((rows, block), lambda i: (0, i))
    bias = pl.BlockSpec((None, 1, block), lambda i: (i, 0, 0))
    weight = pl.BlockSpec((depth, None, piece, width), lambda i: (0, i, 0, 0))
    full, vec = whole((rows, width)), whole((1, width))
    return pl.pallas_call(
        functools.partial(feed_back_kernel, middle=middle, depth=depth, steps=middle, parts=parts),
        grid=(middle,),
        in_specs=[full, weight, weight, act, act, full, full, whole((rows, LANES)), vec]
        + [pl.BlockSpec(memory_space=pl.ANY)] * len(flat),
        out_specs=[act, act, bias, bias, full, full, whole((8, width))],
        out_shape=[
            jax.ShapeDtypeStruct((rows, middle * block), BF),
            jax.ShapeDtypeStruct((rows, middle * block), BF),
            jax.ShapeDtypeStruct((middle, 1, block), F32),
            jax.ShapeDtypeStruct((middle, 1, block), F32),
            jax.ShapeDtypeStruct((rows, width), F32),
            jax.ShapeDtypeStruct((rows, width), BF),
            jax.ShapeDtypeStruct((8, width), F32),
        ],
        scratch_shapes=[
            pltpu.VMEM((2, 2, depth, shard, block), BF),
            pltpu.SemaphoreType.DMA((len(flat),)),
            pltpu.VMEM((rows, width), F32),
        ],
        compiler_params=params(),
        cost_estimate=cost(8 * rows * width * middle * block, 8 * width * middle * block + 16 * rows * width),
        name="feed_back",
    )(low, *weights, *slopes, du_second, normed, inverse, gain[None], *flat)


def context_back_kernel(me, da, weight, *refs, middle):
    outs, whole_grad = refs[:-1], refs[-1]
    whole_grad[...] = dot_nt(da[...], weight[...]).astype(BF)
    rows = da.shape[0]
    mine, other = outs
    width = mine.shape[1]
    second = (me[0] & 1) == 1
    for i in range(middle):
        at = pl.multiple_of(((me[0] ^ (2 * i)) // 2) * 2 * width, 2 * width)
        pair = whole_grad[:, pl.ds(at, 2 * width)]
        low, high = pair[:, :width], pair[:, width:]
        mine[i * rows : (i + 1) * rows, :] = jnp.where(second, high, low)
        other[i * rows : (i + 1) * rows, :] = jnp.where(second, low, high)


def context_back(me, da, weight, own_width, middle):
    rows, width = da.shape
    shape = (middle * rows, own_width)
    return pl.pallas_call(
        functools.partial(context_back_kernel, middle=middle),
        grid=(1,),
        in_specs=[pl.BlockSpec(memory_space=pltpu.SMEM), whole(da.shape), whole(weight.shape)],
        out_specs=[whole(shape)] * 2,
        out_shape=[jax.ShapeDtypeStruct(shape, BF)] * 2,
        scratch_shapes=[pltpu.VMEM((rows, width), BF)],
        compiler_params=params(),
        cost_estimate=cost(2 * rows * width * width, 2 * width * width + 4 * rows * width),
        name="context_back",
    )(me, da, weight)


def gradient_kernel(act, other_act, grad, other_grad, out):
    depth, piece, width = out.shape
    total = dot_tn(act[...], grad[...]) + dot_tn(other_act[...], other_grad[...])
    out[...] = total.astype(BF).reshape(depth, piece, width)


def reduce_gradient(act, other_act, grad, other_grad, depth, piece):
    rows, width = grad.shape
    block = depth * piece
    middle = act.shape[1] // block
    column = pl.BlockSpec((rows, block), lambda i: (0, i))
    full = whole((rows, width))
    return pl.pallas_call(
        gradient_kernel,
        grid=(middle,),
        in_specs=[column, column, full, full],
        out_specs=pl.BlockSpec((depth, None, piece, width), lambda i: (0, i, 0, 0)),
        out_shape=jax.ShapeDtypeStruct((depth, middle, piece, width), BF),
        compiler_params=params(),
        cost_estimate=cost(4 * rows * width * middle * block, 2 * width * middle * block + 4 * rows * middle * block),
        name="reduce_gradient",
    )(act, other_act, grad, other_grad)


EXTRA = 16


def expand_gradient_kernel(
    me, low, other_low, context, other_context, de, other_de, da, other_da, small, *outs, middle, own, share
):
    block = de.shape[1] // middle
    depth = small.shape[0]
    shard = low.shape[1] // depth
    tall = shard + EXTRA
    first, second = low[...].T, other_low[...].T
    third, fourth = context[...].T, other_context[...].T
    kept_a, sent_a, kept_b, sent_b = outs
    for i in range(middle):
        at = slice(i * block, (i + 1) * block)
        target = me[0] ^ (2 * i)
        wide = (dot_nn(first, de[:, at]) + dot_nn(second, other_de[:, at])).astype(BF)
        where = pl.ds(pl.multiple_of(target * own, own), own)
        thin = (dot_nn(third, da[:, where]) + dot_nn(fourth, other_da[:, where])).astype(BF)
        for out, n, part in (
            (sent_a if i >= 2 else kept_a, i % 2, range(depth // 2)),
            (sent_b if i % 2 else kept_b, i // 2, range(depth // 2, depth)),
        ):
            for z in part:
                row = (z - part[0]) * tall
                out[n, row : row + shard, :block] = wide[z * shard : (z + 1) * shard]
                out[n, row : row + shard, block:] = thin[z * shard : (z + 1) * shard]
                line = small[z : z + 1, pl.ds(pl.multiple_of(target * share, share), share)].astype(BF)
                line = jnp.concatenate([line, jnp.zeros((1, block + own - share), BF)], axis=1)
                out[n, row + shard : row + tall, :] = jnp.broadcast_to(line, (EXTRA, block + own))


def expand_gradient(me, low, other_low, context, other_context, de, other_de, da, other_da, small, own):
    rows, width = low.shape
    middle = 4
    depth = small.shape[0]
    block = de.shape[1] // middle
    args = (low, other_low, context, other_context, de, other_de, da, other_da, small)
    shape = (2, width // 2 + EXTRA * depth // 2, block + own)
    share = small.shape[1] // (2 * middle)
    return pl.pallas_call(
        functools.partial(expand_gradient_kernel, middle=middle, own=own, share=share),
        grid=(1,),
        in_specs=[pl.BlockSpec(memory_space=pltpu.SMEM)] + [whole(v.shape) for v in args],
        out_specs=[whole(shape)] * 4,
        out_shape=[jax.ShapeDtypeStruct(shape, BF)] * 4,
        compiler_params=params(),
        cost_estimate=cost(4 * rows * width * middle * (block + own), 4 * width * middle * block),
        name="expand_gradient",
    )(me, *args)


def unpack_expand_kernel(blocks, wide, thin, small, *, depth):
    count = blocks.shape[0]
    shard = wide.shape[0]
    block = wide.shape[1] // count
    piece, own = block // depth, thin.shape[1] // count
    for g in range(count):
        for z in range(depth):
            at = (z * count + g) * piece
            wide[:, at : at + piece] = blocks[g, :shard, z * piece : (z + 1) * piece].astype(F32)
        thin[:, g * own : (g + 1) * own] = blocks[g, :shard, block:].astype(F32)
        small[g : g + 1, :] = blocks[g, shard : shard + EXTRA, : small.shape[1]].astype(F32)[0:1]


def unpack_expand(blocks, depth, hidden, width, share):
    shard = blocks.shape[1] - EXTRA
    shapes = [(shard, hidden), (shard, width), (blocks.shape[0], share)]
    return pl.pallas_call(
        functools.partial(unpack_expand_kernel, depth=depth),
        grid=(1,),
        in_specs=[whole(blocks.shape)],
        out_specs=[whole(v) for v in shapes],
        out_shape=[jax.ShapeDtypeStruct(v, F32) for v in shapes],
        compiler_params=params(),
        cost_estimate=cost(0, 6 * shard * (hidden + width)),
        name="unpack_expand",
    )(blocks)


def unpack_reduce_kernel(me, *refs):
    out = refs[-1]
    rows = refs[0].shape[0]
    for n, k in enumerate(plane_list(len(refs) - 1)):
        out[pl.ds(pl.multiple_of((me[0] ^ k) * rows, rows), rows), :] = refs[n][...].astype(F32)


def unpack_reduce(me, blocks):
    rows, width = blocks[0].shape
    shape = (rows * len(blocks), width)
    return pl.pallas_call(
        unpack_reduce_kernel,
        grid=(1,),
        in_specs=[pl.BlockSpec(memory_space=pltpu.SMEM)] + [whole(v.shape) for v in blocks],
        out_specs=whole(shape),
        out_shape=jax.ShapeDtypeStruct(shape, F32),
        compiler_params=params(),
        cost_estimate=cost(0, 6 * shape[0] * width),
        name="unpack_reduce",
    )(me, *blocks)


def input_part_kernel(grads, weight, *refs, with_away):
    got = dot_nn(grads[...], weight[...])
    if with_away:
        got = got + refs[0][...].astype(F32)
        outs = refs[1:]
    else:
        outs = refs
    rows = outs[0].shape[0]
    for i, out in enumerate(outs):
        out[...] = got[i * rows : (i + 1) * rows].astype(BF)


def input_part(grads, weight, half, away=None, pieces=1):
    count, line = grads.shape
    rows, width = count // 2, weight.shape[1]
    more = () if away is None else (away,)
    shape = (rows // pieces, width)
    got = pl.pallas_call(
        functools.partial(input_part_kernel, with_away=away is not None),
        grid=(1,),
        in_specs=[pl.BlockSpec((rows, line), lambda i: (half, 0)), whole(weight.shape)] + [whole(v.shape) for v in more],
        out_specs=[whole(shape)] * pieces,
        out_shape=[jax.ShapeDtypeStruct(shape, BF)] * pieces,
        compiler_params=params(),
        cost_estimate=cost(2 * rows * width * line, 4 * rows * width),
        name="input_part",
    )(grads, weight, *more)
    return got if pieces > 1 else got[0]


def input_kernel(before, *refs):
    out = refs[-1]
    rows = refs[0].shape[0]
    half = len(refs) // 2
    for s in range(2):
        total = before[s * rows : (s + 1) * rows, :]
        for ref in refs[s * half : (s + 1) * half]:
            total = total + ref[...].astype(F32)
        out[s] = total


def input_sum(before, first, second):
    rows, width = first[0].shape
    return pl.pallas_call(
        input_kernel,
        grid=(1,),
        in_specs=[whole(before.shape)] + [whole(v.shape) for v in (*first, *second)],
        out_specs=whole((2, rows, width)),
        out_shape=jax.ShapeDtypeStruct((2, rows, width), F32),
        compiler_params=params(),
        cost_estimate=cost(0, 32 * rows * width),
        name="input_sum",
    )(before, *first, *second)


def unpack_heads_kernel(me, *refs):
    outs, bias = refs[-4:-1], refs[-1]
    count = len(refs) - 4
    shard, width = outs[0].shape
    own = width // count
    bias[...] = jnp.zeros_like(bias)
    for n, k in enumerate(plane_list(count)):
        where = pl.ds(pl.multiple_of((me[0] ^ k) * own, own), own)
        tail = refs[n][shard : shard + 16, :].astype(F32)
        for t in range(3):
            at = slice(t * own, (t + 1) * own)
            outs[t][:, where] = refs[n][:shard, at].astype(F32)
            bias[t : t + 1, where] = tail[0:1, at] + tail[1:2, at]


def unpack_heads(me, blocks, shard, width):
    shapes = [(shard, width)] * 3 + [(8, width)]
    return pl.pallas_call(
        unpack_heads_kernel,
        grid=(1,),
        in_specs=[pl.BlockSpec(memory_space=pltpu.SMEM)] + [whole(v.shape) for v in blocks],
        out_specs=[whole(v) for v in shapes],
        out_shape=[jax.ShapeDtypeStruct(v, F32) for v in shapes],
        compiler_params=params(),
        cost_estimate=cost(0, 18 * shard * width),
        name="unpack_heads",
    )(me, *blocks)


def heads_gradient_kernel(*refs, blocks, last):
    grads = refs[blocks]
    if last:
        before, out, sums, tokens = refs[blocks + 1 :]
    else:
        out, sums, tokens = refs[blocks + 1 :]
    rows = grads.shape[0] // blocks
    for i, ref in enumerate(refs[:blocks]):
        tokens[i * rows : (i + 1) * rows, :] = ref[:rows, :]
    total = dot_tn(grads[...], tokens[...])
    sums[...] = jnp.broadcast_to(jnp.sum(grads[...].astype(F32), axis=0, keepdims=True), sums.shape)
    if last:
        out[...] = (total + before[...]).T.astype(BF)
    else:
        out[...] = total


def heads_gradient(blocks, grads, before=None):
    line = grads.shape[1]
    width = blocks[0].shape[1]
    last = before is not None
    args = (*blocks, grads) + ((before,) if last else ())
    shapes = [jax.ShapeDtypeStruct((width, line), BF) if last else jax.ShapeDtypeStruct((line, width), F32)]
    shapes.append(jax.ShapeDtypeStruct((8, line), F32))
    return pl.pallas_call(
        functools.partial(heads_gradient_kernel, blocks=len(blocks), last=last),
        grid=(1,),
        in_specs=[whole(v.shape) for v in args],
        out_specs=[whole(v.shape) for v in shapes],
        out_shape=shapes,
        scratch_shapes=[pltpu.VMEM((grads.shape[0], width), BF)],
        compiler_params=params(),
        cost_estimate=cost(2 * grads.shape[0] * width * line, 2 * grads.shape[0] * width + 6 * width * line),
        name="heads_gradient",
    )(*args)


def normalize(values, gain, shift):
    mean = jnp.mean(values, axis=-1, keepdims=True)
    centred = values - mean
    inverse = lax.rsqrt(jnp.mean(centred * centred, axis=-1, keepdims=True) + EPS)
    normed = centred * inverse
    return normed * gain + shift, normed, inverse


def normalize_back(grad, normed, inverse, gain):
    scaled = grad * gain
    inner = (
        scaled
        - jnp.mean(scaled, axis=-1, keepdims=True)
        - normed * jnp.mean(scaled * normed, axis=-1, keepdims=True)
    )
    return inner * inverse, jnp.sum(grad * normed, axis=0), jnp.sum(grad, axis=0)


def column_sums(values):
    return jnp.sum(values.astype(F32), axis=0)


def plain_body(
    tokens,
    segments,
    query_weight,
    query_bias,
    key_weight,
    value_weight,
    value_bias,
    output_weight,
    output_bias,
    first_gain,
    first_shift,
    expand_weight,
    expand_bias,
    reduce_weight,
    reduce_bias,
    second_gain,
    second_shift,
    cotangent,
):
    batch, rows, width = tokens.shape
    count, depth = lax.axis_size("ctx"), lax.axis_size("fsdp")
    me, my_shard = lax.axis_index("ctx"), lax.axis_index("fsdp")
    shard = query_weight.shape[0]
    hidden = expand_weight.shape[1]
    own_width = width // count
    heads = own_width // HEAD
    piece = hidden // depth // count
    block = depth * piece
    half = hidden // 2
    order = plane_order()
    evens = order[: count // 2]
    scale = HEAD**-0.5
    bits = (count * rows - 1).bit_length()

    columns = lambda w: lax.dynamic_slice_in_dim(w, me * own_width, own_width, 1).astype(BF)
    names = (query_bias, value_bias, output_bias, first_gain, first_shift, reduce_bias, second_gain, second_shift)
    packed = jnp.concatenate(names + (expand_bias,))
    terms = jnp.concatenate(in_terms(packed, 3))
    line = 3 * own_width
    lines = -(-terms.shape[0] // (16 * line)) * 16
    terms = jnp.pad(terms, (0, lines * line - terms.shape[0])).reshape(lines, line)
    own_heads = jnp.concatenate([columns(query_weight), columns(key_weight), columns(value_weight)], axis=1)
    own_heads = gather_shards(jnp.concatenate([own_heads, terms], axis=0))
    packed = own_heads[:, shard:].reshape(depth, lines * line)[:, : 3 * packed.shape[0]]
    packed = jnp.sum(packed.reshape(depth, 3, -1).astype(F32), axis=1)
    own_heads = own_heads[:, :shard].reshape(width, line)
    (bias_query, bias_value, bias_output, gain_first, shift_first, bias_reduce, gain_second, shift_second) = (
        packed[:, i * shard : (i + 1) * shard].reshape(width) for i in range(len(names))
    )
    wide_bias = packed[:, len(names) * shard :].reshape(depth, count, piece)
    bias_halves = [
        jnp.stack([lax.dynamic_index_in_dim(wide_bias, me ^ k, 1, keepdims=False) for k in ks], axis=1).reshape(half)
        for ks in (evens, order[count // 2 :])
    ]
    own_part = lambda v: lax.dynamic_slice_in_dim(v, me * own_width, own_width, 0)
    head_bias = jnp.concatenate([own_part(bias_query), jnp.zeros((own_width,), F32), own_part(bias_value)])
    head_scale = jnp.concatenate([jnp.full((own_width,), scale * LOG2E, F32), jnp.ones((2 * own_width,), F32)])

    thin = shard // count
    folds = width // block
    strip = lax.dynamic_slice_in_dim(output_weight, me * thin, thin, 0).astype(BF)
    strip = jnp.concatenate([strip[:, i * block : (i + 1) * block] for i in range(folds)], axis=0)
    block_expand = lax.dynamic_slice_in_dim(expand_weight.reshape(shard, depth, count * piece), me * piece, piece, 2)
    block_expand = jnp.concatenate([block_expand.reshape(shard, block).astype(BF), strip], axis=0)
    block_expand = lax.all_gather(block_expand, "fsdp", axis=0)
    block_reduce = lax.dynamic_slice_in_dim(reduce_weight, me * piece, piece, 0).astype(BF)
    block_reduce = lax.all_gather(block_reduce, "fsdp", axis=0)

    groups = jnp.stack([w.reshape(shard, count, own_width) for w in (query_weight, key_weight, value_weight)], axis=2)
    half_heads = jnp.concatenate(
        [lax.dynamic_index_in_dim(groups, me ^ k, 1, keepdims=False).reshape(shard, line).astype(BF) for k in evens],
        axis=1,
    )
    half_heads = lax.all_gather(half_heads, "fsdp", axis=0, tiled=True)
    other_heads = peer(half_heads, 1)

    seg = segments
    for b in range(count.bit_length() - 1):
        seg = jnp.concatenate([seg, peer(seg, 1 << b)], axis=1)
    seg = seg.reshape(batch, count, rows)
    seg = jnp.concatenate([seg[:, k] for k in order], axis=1)

    lanes = lambda v: v if own_width == LANES else jnp.pad(v, ((0, 0), (0, LANES - own_width)))
    kept, context_parts = [], []
    for s in range(batch):
        even = jnp.concatenate(gather_even(tokens[s].astype(BF), s % 2 == 0), axis=0)
        odd = peer(even, 1)
        qkv = jnp.concatenate([dot_nn(even, own_heads), dot_nn(odd, own_heads)], axis=0)
        qkv = ((qkv + head_bias) * head_scale).astype(BF)
        if own_width != LANES:
            qkv = jnp.concatenate([lanes(qkv[:, i * own_width : (i + 1) * own_width]) for i in range(3)], axis=1)
        mask_q, mask_k = mask_columns(seg[s], bits)
        out, lse = attend(qkv, mask_q, mask_k, heads, rows)
        kept.append((even, odd, qkv, mask_q, mask_k, out, lse))
        context_parts.append(by_owner(heads_to_rows(out[:, :own_width]), 1))

    got_expand = gather_even(block_expand, True)
    got_expand += [peer(v, 1) for v in got_expand]
    got_reduce = gather_even(block_reduce, False)
    got_reduce += [peer(v, 1) for v in got_reduce]
    full_output = by_owner(
        [
            jnp.concatenate([v[:, shard + i * thin : shard + (i + 1) * thin] for i in range(folds)], axis=2)
            for v in got_expand
        ],
        1,
    ).reshape(width, width)
    middle = count // 2
    expand_halves = [
        jnp.concatenate([v[:, :shard].reshape(width, depth, piece) for v in vs], axis=2).reshape(width, half)
        for vs in (got_expand[:middle], got_expand[middle:])
    ]
    reduce_halves = [
        jnp.concatenate(vs, axis=1).reshape(half, width) for vs in (got_reduce[:middle], got_reduce[middle:])
    ]

    firsts = []
    for s in range(batch):
        branch = dot_nn(context_parts[s], full_output) + bias_output
        firsts.append(normalize(tokens[s] + branch, gain_first, shift_first))
    hidden_in, normed_first, inverse_first = (jnp.concatenate(v, axis=0) for v in zip(*firsts))
    context_low = jnp.concatenate(context_parts, axis=0)
    hidden_low = hidden_in.astype(BF)
    halves = []
    reduced = bias_reduce
    for weight, back, bias in zip(expand_halves, reduce_halves, bias_halves):
        expand = dot_nn(hidden_low, weight) + bias
        cdf = 0.5 * (1.0 + lax.erf(expand * SQRT_HALF))
        active = (expand * cdf).astype(BF)
        slope = cdf + expand * DENSITY * jnp.exp(-0.5 * expand * expand)
        reduced = reduced + dot_nn(active, back)
        halves.append((weight, back, active, slope.astype(BF)))
    result, normed_second, inverse_second = normalize(hidden_in + reduced, gain_second, shift_second)

    grad_out = cotangent.reshape(batch * rows, width)
    grad_sum_second, grad_gain_second, grad_shift_second = normalize_back(
        grad_out, normed_second, inverse_second, gain_second
    )
    grad_reduced = grad_sum_second.astype(BF)
    grad_bias_reduce = column_sums(grad_reduced)

    def chip_sum(make):
        got = peer(make(1).astype(BF), 1)
        return (make(0) + got.astype(F32)).astype(BF)

    sum_reduce = chip_sum(lambda i: dot_tn(halves[i][2], grad_reduced))
    sum_reduce = lax.psum_scatter(sum_reduce, "fsdp", scatter_dimension=0, tiled=True)
    sum_reduce = reduce_even(jnp.split(sum_reduce, middle, axis=0), False)

    grad_hidden = grad_sum_second
    grad_expands = []
    for weight, back, active, slope in halves:
        grad_expand = (dot_nt(grad_reduced, back) * slope.astype(F32)).astype(BF)
        grad_hidden = grad_hidden + dot_nt(grad_expand, weight)
        grad_expands.append(grad_expand)
    grad_bias_expand = [column_sums(g).reshape(depth, middle, piece) for g in grad_expands]
    grad_pre, grad_gain_first, grad_shift_first = normalize_back(
        grad_hidden, normed_first, inverse_first, gain_first
    )
    grad_branch = grad_pre.astype(BF)
    grad_bias_output = column_sums(grad_branch)
    grad_context = dot_nt(grad_branch, full_output).astype(BF)

    sum_expand = chip_sum(lambda i: dot_tn(hidden_low, grad_expands[i])).reshape(width, depth, middle, piece)
    sum_expand = reduce_even([sum_expand[:, :, i].reshape(width, block) for i in range(middle)], True)
    branch_blocks = jnp.concatenate(
        [lax.dynamic_slice_in_dim(grad_branch, (me ^ k) * own_width, own_width, 1) for k in order], axis=1
    )
    sum_output = chip_sum(
        lambda i: dot_tn(context_low, branch_blocks[:, i * width // 2 : (i + 1) * width // 2])
    )
    sum_output = reduce_even(jnp.split(sum_output, middle, axis=1), False)
    sum_expand = jnp.concatenate([sum_expand, sum_output], axis=1)
    sum_expand = lax.psum_scatter(sum_expand, "fsdp", scatter_dimension=0, tiled=True)

    grads = []
    for s in range(batch):
        even, odd, qkv, mask_q, mask_k, out, lse = kept[s]
        dc = lanes(rows_to_heads(grad_context[s * rows : (s + 1) * rows], own_width))
        got = attend_back(qkv, mask_q, mask_k, dc, out, lse, heads, rows)
        if own_width != LANES:
            got = jnp.concatenate([got[:, i * LANES : i * LANES + own_width] for i in range(3)], axis=1)
        grads.append(got)
    middle_row = count * rows // 2
    grad_heads = sum(
        dot_tn(kept[s][0], grads[s][:middle_row]) + dot_tn(kept[s][1], grads[s][middle_row:]) for s in range(batch)
    ).astype(BF)
    grad_head_bias = jnp.pad(
        jnp.stack(in_terms(sum(column_sums(g) for g in grads), 2)), ((0, 14), (0, 0))
    )
    home_heads = jnp.concatenate(
        [grad_heads.reshape(depth, shard, line), jnp.broadcast_to(grad_head_bias, (depth, 16, line))], axis=1
    )
    home_heads = reduce_shards(home_heads)
    home_heads = jnp.concatenate(
        [home_heads[:shard].astype(BF)]
        + [v[None] for v in in_terms(home_heads[shard] + home_heads[shard + 1], 2)]
        + [jnp.zeros((14, line), BF)],
        axis=0,
    )
    back_rows = [heads_to_rows(g) for g in grads]
    back_even = jnp.concatenate([jnp.concatenate(r[:middle], axis=1) for r in back_rows], axis=0)
    back_odd = jnp.concatenate([jnp.concatenate(r[middle:], axis=1) for r in back_rows], axis=0)
    grad_in = grad_pre + dot_nt(back_even, half_heads) + dot_nt(back_odd, other_heads)

    def spread(value, low_first):
        got = gather_even(value, low_first)
        odd = peer(jnp.stack(got), 1)
        return by_owner([v[None] for v in got] + [odd[i : i + 1] for i in range(middle)], 0)

    wide = lax.all_gather(sum_expand, "ctx", axis=0)
    grad_expand_weight = jnp.transpose(wide[:, :, :block].reshape(count, shard, depth, piece), (1, 2, 0, 3))
    grad_expand_weight = grad_expand_weight.reshape(shard, hidden).astype(F32)
    grad_output_weight = jnp.transpose(wide[:, :, block:], (1, 0, 2)).reshape(shard, width).astype(F32)
    grad_reduce_weight = lax.all_gather(sum_reduce, "ctx", axis=0, tiled=True).astype(F32)
    wide_heads = spread(home_heads, True)
    wide_shards = jnp.transpose(wide_heads[:, :shard].reshape(count, shard, 3, own_width), (2, 1, 0, 3))
    grad_query_weight, grad_key_weight, grad_value_weight = (
        wide_shards[i].reshape(shard, width).astype(F32) for i in range(3)
    )
    wide_biases = jnp.sum(wide_heads[:, shard : shard + 2].astype(F32), axis=1).reshape(count, 3, own_width)
    own_shard = lambda v: lax.dynamic_slice_in_dim(v.reshape(width), my_shard * shard, shard, 0)

    vectors = (
        grad_bias_output,
        grad_gain_first,
        grad_shift_first,
        grad_bias_reduce,
        grad_gain_second,
        grad_shift_second,
    )
    wide_bias = by_owner([g[:, i] for g in grad_bias_expand for i in range(middle)], 1)
    small = jnp.concatenate([v.reshape(depth, shard) for v in vectors] + [wide_bias], axis=1)
    for b in range(count.bit_length() - 1):
        small = small + peer(small, 1 << b)
    small = reduce_shards(small)
    vec = [small[i * shard : (i + 1) * shard] for i in range(len(vectors))]
    vec_expand = small[len(vectors) * shard :]
    return (
        result.reshape(batch, rows, width),
        grad_in.reshape(batch, rows, width),
        grad_query_weight,
        own_shard(wide_biases[:, 0]),
        grad_key_weight,
        grad_value_weight,
        own_shard(wide_biases[:, 2]),
        grad_output_weight,
        vec[0],
        vec[1],
        vec[2],
        grad_expand_weight,
        vec_expand,
        grad_reduce_weight,
        vec[3],
        vec[4],
        vec[5],
    )


def even_pieces(own, other):
    rows = own.shape[0]
    both = jnp.concatenate([own, other], axis=1)
    middle = lax.axis_size("ctx") // 2
    rows = rows // middle
    pieces = [both[i * rows : (i + 1) * rows] for i in range(middle)]
    return [pieces[0]] + [peer(pieces[i], 2 * i) for i in range(1, middle)]


def body(
    tokens,
    segments,
    query_weight,
    query_bias,
    key_weight,
    value_weight,
    value_bias,
    output_weight,
    output_bias,
    first_gain,
    first_shift,
    expand_weight,
    expand_bias,
    reduce_weight,
    reduce_bias,
    second_gain,
    second_shift,
    cotangent,
):
    batch, rows, width = tokens.shape
    count, depth = lax.axis_size("ctx"), lax.axis_size("fsdp")
    me, my_shard = lax.axis_index("ctx"), lax.axis_index("fsdp")
    me_array = me.astype(jnp.int32).reshape(1)
    shard = query_weight.shape[0]
    hidden = expand_weight.shape[1]
    own_width = width // count
    heads = own_width // HEAD
    piece = hidden // depth // count
    block = depth * piece
    middle = count // 2
    order = plane_order()
    evens, odds = order[:middle], order[middle:]
    scale = HEAD**-0.5
    bits = (count * rows - 1).bit_length()
    all_rows = batch * rows

    columns = lambda w: lax.dynamic_slice_in_dim(w, me * own_width, own_width, 1).astype(BF)
    names = (query_bias, value_bias, output_bias, first_gain, first_shift, reduce_bias, second_gain, second_shift)
    packed = jnp.concatenate(names + (expand_bias,))
    size = packed.shape[0]
    terms = jnp.concatenate(in_terms(packed, 3))
    line = 3 * own_width
    lines = -(-terms.shape[0] // (16 * line)) * 16
    terms = jnp.pad(terms, (0, lines * line - terms.shape[0])).reshape(lines, line)
    own_heads = jnp.concatenate([columns(query_weight), columns(key_weight), columns(value_weight)], axis=1)
    shard_parts = gather_doubling(jnp.concatenate([own_heads, terms], axis=0))

    def plane(value, *needed):
        first, second = after((peer(value, 2), peer(value, 4)), *needed)
        part = value.shape[0] // 2
        return first, second, (peer(first[:part], 4), peer(second[part:], 2))

    def chip(blocks):
        return blocks + [jax.tree.map(lambda v: peer(v, 1), b) for b in blocks]

    def direct(value):
        return [value] + [peer(value, k) for k in evens[1:]]

    low_in = []
    for s in range(batch):
        numbers = jnp.concatenate([segments[s] // 64, segments[s] % 64]).astype(BF)
        numbers = jnp.pad(numbers[None], ((0, EXTRA - 1), (0, width - 2 * rows)))
        low_in.append(jnp.concatenate([tokens[s].astype(BF), numbers], axis=0))

    first_got, shard_parts, low_in = join(direct(low_in[0]), shard_parts, low_in)
    first_blocks = chip(first_got)
    own_heads = by_owner([shard_parts[j : j + 1] for j in range(depth)], 0, list(range(depth)), "fsdp")
    packed = own_heads[:, shard:].reshape(depth, lines * line)[:, : 3 * size]
    packed = jnp.sum(packed.reshape(depth, 3, -1).astype(F32), axis=1)
    own_heads = own_heads[:, :shard].reshape(width, line)
    (bias_query, bias_value, bias_output, gain_first, shift_first, bias_reduce, gain_second, shift_second) = (
        packed[:, i * shard : (i + 1) * shard].reshape(width) for i in range(len(names))
    )
    wide_bias = packed[:, len(names) * shard :].reshape(depth, count, piece)
    bias_halves = [
        jnp.stack([lax.dynamic_index_in_dim(wide_bias, me ^ k, 1, keepdims=False).reshape(1, block) for k in ks])
        for ks in (evens, odds)
    ]
    own_part = lambda v: lax.dynamic_slice_in_dim(v, me * own_width, own_width, 0)
    head_bias = jnp.concatenate([own_part(bias_query), jnp.zeros((own_width,), F32), own_part(bias_value)])
    head_scale = jnp.concatenate([jnp.full((own_width,), scale * LOG2E, F32), jnp.ones((2 * own_width,), F32)])

    thin = shard // count
    folds = width // block
    strip = lax.dynamic_slice_in_dim(output_weight, me * thin, thin, 0).astype(BF)
    strip = jnp.concatenate([strip[:, i * block : (i + 1) * block] for i in range(folds)], axis=0)
    block_expand = [
        lax.dynamic_slice_in_dim(expand_weight, (z * count + me) * piece, piece, 1).astype(BF) for z in range(depth)
    ]
    block_expand = jnp.concatenate([jnp.concatenate(block_expand, axis=1), strip], axis=0)
    block_expand = lax.all_gather(after(block_expand, first_got[1]), "fsdp", axis=0)

    reduce_blocks = [lax.dynamic_slice_in_dim(reduce_weight, (me ^ k) * piece, piece, 0).astype(BF) for k in evens]

    halfway = count * rows // 2
    heads_across = own_heads.T
    first_qkv, *first_masks = project(first_blocks, rows, own_heads, head_bias, head_scale, bits)
    first_out, first_lse, second_got = join(
        *attend(first_qkv, *first_masks, heads, rows), direct(low_in[1])
    )
    second_blocks = chip(second_got)
    (second_qkv, *second_masks), other_out = join(
        project(second_blocks, rows, own_heads, head_bias, head_scale, bits), peer(first_out[halfway:], 1)
    )

    reduce_own = lax.all_gather(after(jnp.stack(reduce_blocks), second_got[1]), "fsdp", axis=0)
    second_out, second_lse, first_pieces, near = join(
        *attend(second_qkv, *second_masks, heads, rows),
        even_pieces(first_out[:halfway], other_out),
        (block_expand, peer(block_expand, 2), peer(block_expand, 4)),
    )
    part = depth // 2
    far = peer(near[1][:part], 4), peer(near[2][part:], 2)
    got_expand, second_pieces = join(
        chip([*((v,) for v in near), far]), even_pieces(second_out[:halfway], peer(second_out[halfway:], 1))
    )
    full_output = assemble_output(got_expand, shard, thin, me_array)
    kept = [
        (first_blocks, first_qkv, *first_masks, first_out, first_lse),
        (second_blocks, second_qkv, *second_masks, second_out, second_lse),
    ]

    earlier = None
    for s, pieces in enumerate((first_pieces, second_pieces)):
        earlier = branch(s, me_array, pieces, full_output, tokens, bias_output, gain_first, shift_first, earlier)
    context_low, hidden_in, hidden_low, normed_first, inverse_first = (
        v.reshape(all_rows, v.shape[2]) for v in earlier
    )

    act_even, act_odd, slope_even, slope_odd, other_low, other_context, reduce_own = join(
        *expand_forward(hidden_low, bias_halves, got_expand, shard),
        peer(hidden_low, 1),
        peer(context_low, 1),
        reduce_own,
    )
    reduce_halves = [reduce_own, peer(reduce_own, 1)]
    result, du_second, dr, sums_second, other_act = join(
        *reduce_forward(
            (act_even, act_odd),
            reduce_halves,
            hidden_in,
            cotangent.reshape(all_rows, width),
            bias_reduce,
            gain_second,
            shift_second,
        ),
        peer(act_odd, 1),
    )

    sum_reduce = reduce_gradient(act_even, other_act, dr, peer(dr, 1), depth, piece)
    sum_reduce, dr = join(sum_reduce, dr)
    sum_reduce = lax.psum_scatter(sum_reduce, "fsdp", scatter_dimension=0, tiled=False)

    de_even, de_odd, sums_even, sums_odd, grad_pre, da, sums_first = feed_back(
        dr,
        reduce_halves,
        (slope_even, slope_odd),
        du_second,
        normed_first,
        inverse_first,
        gain_first,
        got_expand,
        shard,
    )

    vectors = (sums_first[2], sums_first[0], sums_first[1], sums_second[2], sums_second[0], sums_second[1])
    wide_bias = by_owner(
        [sums[i, 0].reshape(depth, 1, piece) for sums in (sums_even, sums_odd) for i in range(middle)], 1
    ).reshape(depth, hidden // depth)
    small = jnp.concatenate([v.reshape(depth, shard) for v in vectors] + [wide_bias], axis=1)
    share = -(-small.shape[1] // (count * LANES)) * LANES
    small = jnp.pad(small, ((0, 0), (0, share * count - small.shape[1])))
    de_even, da, own_grads, other_grads, other_de, other_da, small, other_small = join(
        de_even,
        da,
        *context_back(me_array, da, full_output, own_width, middle),
        peer(de_odd, 1),
        peer(da, 1),
        small,
        peer(small, 1),
    )

    sums, dc = join(
        expand_gradient(
            me_array,
            hidden_low,
            other_low,
            context_low,
            other_context,
            de_even,
            other_de,
            da,
            other_da,
            small + other_small,
            own_width,
        ),
        even_pieces(own_grads, peer(other_grads, 1)),
    )
    kept_a, sent_a, kept_b, sent_b = sums

    add = lambda a, b: (a.astype(F32) + b.astype(F32)).astype(BF)
    to_owner = lambda parts: [parts[0]] + [peer(parts[i], 2 * i) for i in range(1, middle)]

    def back(s, dc, part=None, before=None):
        _, qkv, mask_q, mask_k, out, lse = kept[s]
        return attend_back(qkv, mask_q, mask_k, dc, out, lse, heads, rows, part, before, s)

    first_grads, got_a, got_b = join(back(0, dc), peer(sent_a, 4), peer(sent_b, 2))
    odd = input_part(first_grads, heads_across, 1)
    first_grads, odd = join(first_grads, odd)
    away, next_a, next_b, first_grads = join(peer(odd, 1), add(kept_a, got_a), add(kept_b, got_b), first_grads)
    home = input_part(first_grads, heads_across, 0, away, middle)
    home, first_grads, dc, sum_reduce = join(home, first_grads, dc, sum_reduce)
    before, first_sums = heads_gradient(kept[0][0], first_grads, None)
    before, dc = join(before, dc)
    upper, got_a, got_b, got_reduce = join(
        back(1, dc, 0),
        peer(next_a[1], 2),
        peer(next_b[1], 4),
        to_owner(sum_reduce),
    )
    sum_expand = jnp.concatenate([add(next_a[0], got_a), add(next_b[0], got_b)], axis=0)
    sum_reduce = sum(v.astype(F32) for v in got_reduce).astype(BF)
    upper, sum_expand, sum_reduce = join(upper, sum_expand, sum_reduce)
    sum_expand = lax.psum_scatter(sum_expand, "fsdp", scatter_dimension=0, tiled=True)
    second_grads, from_first = join(back(1, dc, 1, upper), to_owner(home))

    odd = input_part(second_grads, heads_across, 1)
    second_grads, odd = join(second_grads, odd)
    (grad_heads, sums), away, got_reduce, second_grads = join(
        heads_gradient(kept[1][0], second_grads, before), peer(odd, 1), direct(sum_reduce), second_grads
    )
    head_sums = first_sums[0] + sums[0]
    grad_head_bias = jnp.pad(jnp.stack(in_terms(head_sums, 2)), ((0, 14), (0, 0)))
    home_heads = jnp.concatenate(
        [grad_heads.reshape(depth, shard, line), jnp.broadcast_to(grad_head_bias, (depth, 16, line))], axis=1
    )
    shard_got = jnp.stack(
        [lax.dynamic_index_in_dim(home_heads, my_shard ^ j, 0, keepdims=False) for j in range(depth)]
    )
    step = depth // 2
    got = exchange(shard_got[step:], "fsdp", step)
    home, sum_expand = join(input_part(second_grads, heads_across, 0, away, middle), sum_expand)
    wide_expand = lax.all_gather(sum_expand, "ctx", axis=0)
    got, from_second, grad_reduce_weight = join(got, to_owner(home), unpack_reduce(me_array, chip(got_reduce)))
    shard_got = add(shard_got[:step], got)
    while step > 1:
        step //= 2
        shard_got = add(shard_got[:step], exchange(shard_got[step:], "fsdp", step))
    total = shard_got[0]
    tail = total[shard].astype(F32) + total[shard + 1].astype(F32)
    home_heads = jnp.concatenate(
        [total[:shard]] + [v[None] for v in in_terms(tail, 2)] + [jnp.zeros((14, line), BF)], axis=0
    )
    heads_got = chip(direct(home_heads))
    grad_in = input_sum(grad_pre, from_first, from_second)
    grad_expand_weight, grad_output_weight, small_sum = unpack_expand(wide_expand, depth, hidden, width, share)
    small_sum = small_sum.reshape(-1)
    grad_query_weight, grad_key_weight, grad_value_weight, wide_biases = unpack_heads(
        me_array, heads_got, shard, width
    )
    own_shard = lambda v: lax.dynamic_slice_in_dim(v, my_shard * shard, shard, 0)

    vec = [small_sum[i * shard : (i + 1) * shard] for i in range(len(vectors))]
    vec_expand = small_sum[len(vectors) * shard : len(vectors) * shard + hidden // depth]
    return (
        result.reshape(batch, rows, width),
        grad_in,
        grad_query_weight,
        own_shard(wide_biases[0]),
        grad_key_weight,
        grad_value_weight,
        own_shard(wide_biases[2]),
        grad_output_weight,
        vec[0],
        vec[1],
        vec[2],
        grad_expand_weight,
        vec_expand,
        grad_reduce_weight,
        vec[3],
        vec[4],
        vec[5],
    )


def solution(mesh):
    seq = P("fsdp", "ctx", None)
    mat = P("fsdp", None)
    vec = P("fsdp")
    in_specs = (
        seq,
        P("fsdp", "ctx"),
        mat,
        vec,
        mat,
        mat,
        vec,
        mat,
        vec,
        vec,
        vec,
        mat,
        vec,
        mat,
        vec,
        vec,
        vec,
        seq,
    )
    out_specs = (seq, seq, mat, vec, mat, mat, vec, mat, vec, vec, vec, mat, vec, mat, vec, vec, vec)
    count, depth = mesh.shape["ctx"], mesh.shape["fsdp"]

    def layer(*args):
        width, hidden = args[0].shape[2], args[11].shape[1]
        piece, own_width = hidden // depth // count, width // count
        tiled = count == 8 and args[0].shape[0] == 2 and piece % LANES == 0 and own_width == LANES
        tiled = tiled and width // depth // count % 16 == 0
        return (body if tiled else plain_body)(*args)

    return jax.shard_map(layer, mesh=mesh, in_specs=in_specs, out_specs=out_specs, check_vma=False)
```

```python
import functools

import jax
import jax.numpy as jnp
from jax import lax
from jax.experimental import pallas as pl
from jax.experimental.pallas import tpu as pltpu
from jax.sharding import PartitionSpec as P

HEAD = 64
LANES = 128
VMEM_LIMIT = 62 << 20
COST_SHARE = 64
EPS = 1e-05
BIG = 1e30
LOG2E = 1.4426950408889634
SQRT_HALF = 0.7071067811865476
DENSITY = 0.3989422804014327
BF = jnp.bfloat16
F32 = jnp.float32


def dot_nn(left, right):
    return jnp.dot(left, right, preferred_element_type=F32)


def dot_tn(left, right):
    return lax.dot_general(left, right, (((0,), (0,)), ((), ())), preferred_element_type=F32)


def dot_nt(left, right):
    return lax.dot_general(left, right, (((1,), (1,)), ((), ())), preferred_element_type=F32)


def exchange(value, axis, k):
    count = lax.axis_size(axis)
    return lax.ppermute(value, axis, [(i, i ^ k) for i in range(count)])


def peer(value, k):
    return exchange(value, "ctx", k)


def after(value, *needed):
    return lax.optimization_barrier((value, needed))[0]


def join(*values):
    return lax.optimization_barrier(values)


def plane_list(count):
    return list(range(0, count, 2)) + list(range(1, count, 2))


def plane_order():
    return plane_list(lax.axis_size("ctx"))


def gather_even(value, low_first):
    count = lax.axis_size("ctx")
    got = {0: value}
    for k in range(2, count, 2):
        bits = [1 << b for b in range(1, count.bit_length()) if k >> b & 1]
        step = bits[-1] if low_first else bits[0]
        got[k] = peer(got[k ^ step], step)
    return [got[k] for k in range(0, count, 2)]


def by_owner(parts, axis, order=None, mesh_axis="ctx"):
    order = order or plane_order()
    stacked = jnp.stack([parts[order.index(k)] for k in range(len(order))])
    me = lax.axis_index(mesh_axis)
    return jnp.concatenate(
        [lax.dynamic_index_in_dim(stacked, me ^ g, 0, keepdims=False) for g in range(len(order))], axis=axis
    )


def rows_to_heads(value, width):
    count = lax.axis_size("ctx")
    me = lax.axis_index("ctx")
    mine, other = [], []
    for k in range(0, count, 2):
        to = me ^ k
        first = lax.dynamic_slice_in_dim(value, to * width, width, 1)
        second = lax.dynamic_slice_in_dim(value, (to ^ 1) * width, width, 1)
        got = jnp.concatenate([first, second], axis=1)
        if k:
            got = peer(got, k)
        mine.append(got[:, :width])
        other.append(got[:, width:])
    return jnp.concatenate(mine + [peer(jnp.concatenate(other, axis=0), 1)], axis=0)


def heads_to_rows(value):
    count = lax.axis_size("ctx")
    rows, width = value.shape[0] // count, value.shape[1]
    half = value.shape[0] // 2
    both = jnp.concatenate([value[:half], peer(value[half:], 1)], axis=1)
    even, odd = [], []
    for i, k in enumerate(range(0, count, 2)):
        got = both[i * rows : (i + 1) * rows]
        if k:
            got = peer(got, k)
        even.append(got[:, :width])
        odd.append(got[:, width:])
    return even + odd


def reduce_even(blocks, low_first):
    count = lax.axis_size("ctx")
    bits = [1 << b for b in range(1, count.bit_length() - 1)]
    if not low_first:
        bits = bits[::-1]
    held = dict(zip(range(0, count, 2), blocks))
    for bit in bits:
        sent = [k for k in held if k & bit]
        got = peer(jnp.stack([held[k] for k in sent]), bit)
        got = {k ^ bit: got[i] for i, k in enumerate(sent)}
        held = {k: (held[k].astype(F32) + got[k].astype(F32)).astype(BF) for k in held if not k & bit}
    return held[0]


def gather_shards(value):
    depth = lax.axis_size("fsdp")
    parts = [value[None]] + [exchange(value, "fsdp", j)[None] for j in range(1, depth)]
    return by_owner(parts, 0, list(range(depth)), "fsdp")


def reduce_shards(value):
    depth = lax.axis_size("fsdp")
    me = lax.axis_index("fsdp")
    total = lax.dynamic_index_in_dim(value, me, 0, keepdims=False).astype(F32)
    for j in range(1, depth):
        sent = lax.dynamic_index_in_dim(value, me ^ j, 0, keepdims=False)
        total = total + exchange(sent, "fsdp", j).astype(F32)
    return total


def gather_doubling(value):
    got = value[None]
    step = 1
    while step < lax.axis_size("fsdp"):
        got = jnp.concatenate([got, exchange(got, "fsdp", step)], axis=0)
        step *= 2
    return got


def in_terms(vector, count):
    terms = []
    for _ in range(count):
        terms.append(vector.astype(BF))
        vector = vector - terms[-1].astype(F32)
    return terms


def whole(shape):
    return pl.BlockSpec(shape, lambda *i: (0,) * len(shape))


def params(limit=VMEM_LIMIT):
    return pltpu.CompilerParams(vmem_limit_bytes=limit)


def cost(flops, size, exps=0):
    return pl.CostEstimate(
        flops=flops // COST_SHARE, bytes_accessed=size // COST_SHARE, transcendentals=exps // COST_SHARE
    )


def mask_columns(seg, bits):
    lane = jnp.arange(LANES) % HEAD
    bit = (seg[:, None] >> jnp.minimum(lane // 2, 30)) & 1
    flip = bit ^ (lane & 1)
    used = lane < 2 * bits
    for_query = jnp.where(used & (flip == 1), -BIG, 0.0).astype(BF)
    for_key = jnp.where(used, 1 - flip, ((lane >= 60) & (lane < 63)).astype(jnp.int32)).astype(BF)
    return for_query, for_key


def lane_index():
    return lax.broadcasted_iota(jnp.int32, (1, LANES), 1)


def merge(main, extra, h):
    lane = lane_index()
    return jnp.where((lane < HEAD) if h == 0 else (lane >= HEAD), main, extra)


def with_terms(extra, number):
    lane = lane_index() % HEAD
    first = number.astype(BF).astype(F32)
    rest = number - first
    second = rest.astype(BF).astype(F32)
    third = rest - second
    terms = jnp.where(lane == 60, first, jnp.where(lane == 61, second, third)).astype(BF)
    return jnp.where((lane >= 60) & (lane < 63), terms, extra)


def forward_kernel(q, k, v, mask_q, mask_k, out, lse, key_side, value_side, *, heads):
    lane = lane_index()

    @pl.when(pl.program_id(0) == 0)
    def _():
        for h in range(heads):
            key_side[h] = merge(k[...], mask_k[...], h)
            value_side[h] = merge(v[...], jnp.ones((1, LANES), BF), h)

    whole, whole_lse = None, None
    for h in range(heads):
        scores = dot_nt(merge(q[...], mask_q[...], h), key_side[h])
        top = jnp.max(scores, axis=1, keepdims=True)
        weights = jnp.exp2(scores - top).astype(BF)
        both = dot_nn(weights, value_side[h])
        total = pltpu.roll(both, HEAD, 1)
        context, log_total = both / total, top + jnp.log2(total)
        if whole is None:
            whole, whole_lse = context, log_total
        else:
            whole = jnp.where(lane < HEAD, whole, context)
            whole_lse = jnp.where(lane < HEAD, whole_lse, log_total)
    out[...] = whole.astype(BF)
    lse[...] = whole_lse


def attend(qkv, mask_q, mask_k, heads, block):
    count = qkv.shape[0]
    part = lambda j: pl.BlockSpec((block, LANES), lambda i: (i, j))
    full = lambda j: pl.BlockSpec((count, LANES), lambda i: (0, j))
    products = 2 * 2 * count * count * LANES * heads
    return pl.pallas_call(
        functools.partial(forward_kernel, heads=heads),
        grid=(count // block,),
        in_specs=[part(0), full(1), full(2), part(0), full(0)],
        out_specs=[part(0), part(0)],
        out_shape=[jax.ShapeDtypeStruct((count, LANES), BF), jax.ShapeDtypeStruct((count, LANES), F32)],
        scratch_shapes=[pltpu.VMEM((heads, count, LANES), BF), pltpu.VMEM((heads, count, LANES), BF)],
        compiler_params=params(),
        cost_estimate=cost(products * 2, 12 * count * LANES, count * count * heads),
        name="attend",
    )(qkv, qkv, qkv, mask_q, mask_k)


def backward_kernel(*refs, heads, first, steps, total, block, pieces):
    q, k, v, mask_q, mask_k, out, lse = refs[:7]
    parts = refs[7 : 7 + pieces]
    refs = refs[7 + pieces :]
    if first:
        grads_before, dk_before, dv_before = refs[:3]
        refs = refs[3:]
    grads = refs[0]
    if steps < total:
        dk_t, dv_t = refs[1:3]
        key_side, value_side, dc_all = refs[3:]
    else:
        key_side, value_side, dc_all, dk_t, dv_t = refs[1:]
    lane = lane_index()
    step = pl.program_id(0)

    @pl.when(step == 0)
    def _():
        ones = ((lane % HEAD >= 60) & (lane % HEAD < 63)).astype(F32).astype(BF)
        for h in range(heads):
            key_side[h] = merge(k[...], mask_k[...], h)
            value_side[h] = merge(v[...], ones, h)
        if first:
            dk_t[...] = dk_before[...]
            dv_t[...] = dv_before[...]
            grads[: first * block, :LANES] = grads_before[...]
        else:
            dk_t[...] = jnp.zeros_like(dk_t)
            dv_t[...] = jnp.zeros_like(dv_t)
        if pieces == 1:
            dc_all[...] = parts[0][...]
        else:
            for i in range(pieces):
                dc_all[i * block : (i + 1) * block, :] = parts[i][:, :LANES]
                dc_all[(pieces + i) * block : (pieces + i + 1) * block, :] = parts[i][:, LANES:]

    dc = dc_all.at[pl.ds(pl.multiple_of((first + step) * block, block), block), :]
    product = dc[...].astype(F32) * out[...].astype(F32)
    low = jnp.sum(jnp.where(lane < HEAD, product, 0.0), axis=1, keepdims=True)
    high = jnp.sum(jnp.where(lane < HEAD, 0.0, product), axis=1, keepdims=True)
    query_extra = with_terms(mask_q[...], -pltpu.roll(lse[...], HEAD, 1))
    grad_extra = with_terms(jnp.zeros((1, LANES), BF), jnp.where(lane < HEAD, -high, -low))
    q_t, dc_t = q[...].T, dc[...].T
    dq = None
    for h in range(heads):
        probs = jnp.exp2(dot_nt(merge(q[...], query_extra, h), key_side[h]))
        centred = dot_nt(merge(dc[...], grad_extra, h), value_side[h])
        ds = (probs * centred).astype(BF)
        part = dot_nn(ds, key_side[h])
        dq = part if dq is None else jnp.where(lane < HEAD, dq, part)
        own = slice(HEAD * h, HEAD * h + HEAD)
        dk_t[own, :] += dot_nn(q_t[own, :], ds)
        dv_t[own, :] += dot_nn(dc_t[own, :], probs.astype(BF))
    at = step * block if steps < total else (first + step) * block
    grads[pl.ds(pl.multiple_of(at, block), block), :LANES] = (dq.astype(BF).astype(F32) * HEAD**-0.5).astype(BF)
    if steps == total:

        @pl.when(step == steps - first - 1)
        def _():
            grads[:, LANES : 2 * LANES] = (dk_t[...] * (1.0 / LOG2E)).T.astype(BF)
            grads[:, 2 * LANES :] = dv_t[...].T.astype(BF)


def attend_back(qkv, mask_q, mask_k, dc, out, lse, heads, block, part=None, before=None, place=0):
    dc = dc if isinstance(dc, list) else [dc]
    count = qkv.shape[0]
    total = count // block
    first = total // 2 if part == 1 else 0
    steps = total // 2 if part == 0 else total
    piece = lambda j: pl.BlockSpec((block, LANES), lambda i: (first + i, j))
    full = lambda j: pl.BlockSpec((count, LANES), lambda i: (0, j))
    products = 5 * 2 * count * count * LANES * heads
    side = (LANES, count)
    shapes = [jax.ShapeDtypeStruct((count, 3 * LANES), BF)]
    scratch = [
        pltpu.VMEM((heads, count, LANES), BF),
        pltpu.VMEM((heads, count, LANES), BF),
        pltpu.VMEM((count, LANES), BF),
    ]
    if part == 0:
        shapes = [jax.ShapeDtypeStruct((count // 2, LANES), BF)] + [jax.ShapeDtypeStruct(side, F32)] * 2
    else:
        scratch += [pltpu.VMEM(side, F32)] * 2
    before = before or []
    got = pl.pallas_call(
        functools.partial(
            backward_kernel, heads=heads, first=first, steps=steps, total=total, block=block, pieces=len(dc)
        ),
        grid=(steps - first,),
        in_specs=[piece(0), full(1), full(2), piece(0), full(0), piece(0), piece(0)]
        + [pl.BlockSpec((block if len(dc) > 1 else count, v.shape[1]), lambda i: (place, 0)) for v in dc]
        + [whole(v.shape) for v in before],
        out_specs=[whole(v.shape) for v in shapes],
        out_shape=shapes,
        scratch_shapes=scratch,
        compiler_params=params(),
        cost_estimate=cost(products, 16 * count * LANES, count * count * heads),
        name="attend_back",
    )(qkv, qkv, qkv, mask_q, mask_k, out, lse, *dc, *before)
    return got if part == 0 else got[0]


def project_kernel(*refs, blocks, rows, bits):
    weight, bias, factor, out, mask_q, mask_k = refs[blocks:]
    lane = lane_index() % HEAD
    used = lane < 2 * bits
    fixed = ((lane >= 60) & (lane < 63)).astype(F32).astype(BF)
    for i, ref in enumerate(refs[:blocks]):
        at = slice(i * rows, (i + 1) * rows)
        got = (dot_nn(ref[:rows, :], weight[...]) + bias[...]) * factor[...]
        out[at, :] = got.astype(BF)
        parts = ref[rows : rows + 16, : 2 * rows].astype(F32)
        number = (parts[:8, :rows] * 64 + parts[:8, rows:]).T[:, :1].astype(jnp.int32)
        flip = ((number >> (lane // 2)) & 1) ^ (lane & 1)
        mask_q[at, :] = jnp.where(used & (flip == 1), -BIG, 0.0).astype(BF)
        mask_k[at, :] = jnp.where(used, (1 - flip).astype(F32).astype(BF), fixed)


def project(blocks, rows, weight, bias, factor, bits):
    width, line = weight.shape
    args = (*blocks, weight, bias[None], factor[None])
    count = rows * len(blocks)
    shapes = [(count, line), (count, LANES), (count, LANES)]
    return pl.pallas_call(
        functools.partial(project_kernel, blocks=len(blocks), rows=rows, bits=bits),
        in_specs=[whole(v.shape) for v in args],
        out_specs=[whole(v) for v in shapes],
        out_shape=[jax.ShapeDtypeStruct(v, BF) for v in shapes],
        grid=(1,),
        compiler_params=params(),
        cost_estimate=cost(2 * count * width * line, 2 * count * (width + line)),
        name="project",
    )(*args)


def flatten_blocks(blocks):
    flat, parts = [], []
    for n, block in enumerate(blocks):
        first = 0
        for part in block:
            flat.append(part)
            parts.append((n, first))
            first += part.shape[0]
    return flat, tuple(parts)


def assemble_kernel(me, *refs, parts, thin, folds):
    out = refs[-1]
    shard = len({n for n, _ in parts}) * thin
    block = refs[0].shape[2]
    order = plane_list(len({n for n, _ in parts}))
    for ref, (n, first) in zip(refs, parts):
        for z in range(ref.shape[0]):
            row = pl.multiple_of((first + z) * shard + (me[0] ^ order[n]) * thin, thin)
            for f in range(folds):
                out[pl.ds(row, thin), f * block : (f + 1) * block] = ref[z, f * thin : (f + 1) * thin, :]


def assemble_output(blocks, shard, thin, me):
    flat, parts = flatten_blocks(blocks)
    _, tall, block = flat[0].shape
    strip = tall - shard
    folds = strip // thin
    width = folds * block
    specs = [pl.BlockSpec((v.shape[0], strip, block), lambda i: (0, shard // strip, 0)) for v in flat]
    return pl.pallas_call(
        functools.partial(assemble_kernel, parts=parts, thin=thin, folds=folds),
        grid=(1,),
        in_specs=[pl.BlockSpec(memory_space=pltpu.SMEM)] + specs,
        out_specs=whole((width, width)),
        out_shape=jax.ShapeDtypeStruct((width, width), BF),
        compiler_params=params(),
        cost_estimate=cost(0, 4 * width * width),
        name="assemble_output",
    )(me, *flat)


def branch_kernel(me, *refs, pieces, aliased):
    weight, tokens, bias, gain, shift = refs[pieces : pieces + 5]
    context, hidden, low, normed, inverse = refs[pieces + 5 + aliased :]
    second = (me[0] & 1) == 1
    pair = refs[0].shape[1]
    for i in range(pieces):
        at = pl.multiple_of(((me[0] ^ (2 * i)) // 2) * pair, pair)
        got = refs[i][...]
        swapped = jnp.concatenate([got[:, pair // 2 :], got[:, : pair // 2]], axis=1)
        context[:, pl.ds(at, pair)] = jnp.where(second, swapped, got)
    total = tokens[...] + dot_nn(context[...], weight[...]) + bias[...]
    mean = jnp.mean(total, axis=1, keepdims=True)
    centred = total - mean
    scale = lax.rsqrt(jnp.mean(centred * centred, axis=1, keepdims=True) + EPS)
    unit = centred * scale
    out = unit * gain[...] + shift[...]
    hidden[...] = out
    low[...] = out.astype(BF)
    normed[...] = unit
    inverse[...] = jnp.broadcast_to(scale, inverse.shape)


def branch(s, me, pieces, weight, tokens, bias, gain, shift, earlier):
    batch, rows, width = tokens.shape
    at = pl.BlockSpec((None, rows, width), lambda i: (s, 0, 0))
    thin = pl.BlockSpec((None, rows, LANES), lambda i: (s, 0, 0))
    vec = whole((1, width))
    earlier = earlier or ()
    first = 1 + len(pieces) + 5
    full = lambda t: jax.ShapeDtypeStruct((batch, rows, width), t)
    return pl.pallas_call(
        functools.partial(branch_kernel, pieces=len(pieces), aliased=len(earlier)),
        grid=(1,),
        in_specs=[pl.BlockSpec(memory_space=pltpu.SMEM)]
        + [whole(v.shape) for v in pieces]
        + [whole(weight.shape), at, vec, vec, vec]
        + [pl.BlockSpec(memory_space=pl.ANY)] * len(earlier),
        out_specs=[at, at, at, at, thin],
        out_shape=[full(BF), full(F32), full(BF), full(F32), jax.ShapeDtypeStruct((batch, rows, LANES), F32)],
        input_output_aliases={first + i: i for i in range(len(earlier))},
        compiler_params=params(),
        cost_estimate=cost(2 * rows * width * width, 2 * width * width + 18 * rows * width),
        name="branch",
    )(me, *pieces, weight, tokens, bias[None], gain[None], shift[None], *earlier)


def norm_back(grad, normed, inverse, gain):
    scaled = grad * gain
    first = jnp.mean(scaled, axis=1, keepdims=True)
    second = jnp.mean(scaled * normed, axis=1, keepdims=True)
    return inverse * (scaled - first - normed * second)


def feed_kernel(*refs, middle, depth, parts):
    low, inverse, bias_even, bias_odd, bias_reduce, gain_second, shift_second, gain_first = refs[:8]
    hidden_at, cot_at, normed_at, second_even, second_odd = refs[8:13]
    blocks = refs[13 : 13 + len(parts)]
    refs = refs[13 + len(parts) :]
    act_even, act_odd, de_even, de_odd, sums_even, sums_odd, result_at, dr_at, du, da, sums_second, sums_first = refs[:12]
    w_first, w_second, slope, hidden, cot, normed, result, dr, total, block_sems, second_sems, sems = refs[12:]
    step = pl.program_id(0)
    rows, width = total.shape
    shard, block = w_first.shape[3], w_first.shape[4]
    chunk = 64

    def first_copies(i):
        made = []
        for j, (ref, (n, first)) in enumerate(zip(blocks, parts)):
            if n % middle == i:
                target = w_first.at[i, n // middle, pl.ds(first, ref.shape[0])]
                made.append(pltpu.make_async_copy(ref.at[:, :shard, :], target, block_sems.at[j]))
        return made

    def second_copies(i):
        return [
            pltpu.make_async_copy(ref.at[:, i], w_second.at[i, parity], second_sems.at[i, parity])
            for parity, ref in enumerate((second_even, second_odd))
        ]

    rest = [
        pltpu.make_async_copy(source, target, sems.at[i])
        for i, (source, target) in enumerate(((hidden_at, hidden), (cot_at, cot), (normed_at, normed)))
    ]
    back = [
        pltpu.make_async_copy(source, target, sems.at[3 + i])
        for i, (source, target) in enumerate(((result, result_at), (dr, dr_at)))
    ]

    @pl.when(step == 0)
    def _():
        for i in range(middle):
            for copy in first_copies(i) + second_copies(i):
                copy.start()
        for copy in rest:
            copy.start()
        sums_second[...] = jnp.zeros_like(sums_second)
        sums_first[...] = jnp.zeros_like(sums_first)

    for i in range(middle):

        @pl.when(step == i)
        def _():
            for copy in first_copies(i) + second_copies(i):
                copy.wait()

    @pl.when(step < middle)
    def _():
        part = None
        for parity, (bias, act) in enumerate(((bias_even, act_even), (bias_odd, act_odd))):
            for at in (slice(0, rows // 2), slice(rows // 2, rows)):
                value = bias[...]
                for z in range(depth):
                    value = value + dot_nn(low[at, z * shard : (z + 1) * shard], w_first[step, parity, z])
                cdf = 0.5 * (1.0 + lax.erf(value * SQRT_HALF))
                act[at, :] = (value * cdf).astype(BF)
                grad = cdf + value * DENSITY * jnp.exp(-0.5 * value * value)
                slope[step, parity, at, :] = grad.astype(BF)
            got = dot_nn(act[...], w_second[step, parity].reshape(block, width))
            part = got if part is None else part + got

        @pl.when(step == 0)
        def _():
            total[...] = part + bias_reduce[...]

        @pl.when(step > 0)
        def _():
            total[...] += part

    @pl.when(step == middle - 1)
    def _():
        rest[0].wait()
        rest[1].wait()

        @pl.loop(0, rows // chunk)
        def _(i):
            at = pl.ds(pl.multiple_of(i * chunk, chunk), chunk)
            value = total[at, :] + hidden[at, :]
            mean = jnp.mean(value, axis=1, keepdims=True)
            centred = value - mean
            scale = lax.rsqrt(jnp.mean(centred * centred, axis=1, keepdims=True) + EPS)
            unit = centred * scale
            result[at, :] = unit * gain_second[...] + shift_second[...]
            grad = cot[at, :]
            grad_sum = norm_back(grad, unit, scale, gain_second[...])
            total[at, :] = grad_sum
            rounded = grad_sum.astype(BF)
            dr[at, :] = rounded
            sums_second[0:1, :] += jnp.sum(grad * unit, axis=0, keepdims=True)
            sums_second[1:2, :] += jnp.sum(grad, axis=0, keepdims=True)
            sums_second[2:3, :] += jnp.sum(rounded.astype(F32), axis=0, keepdims=True)

        for copy in back:
            copy.start()

    @pl.when(step >= middle)
    def _():
        i = step - middle
        for parity, (de, sums) in enumerate(((de_even, sums_even), (de_odd, sums_odd))):
            grad = dot_nt(dr[...], w_second[i, parity].reshape(block, width)) * slope[i, parity].astype(F32)
            rounded = grad.astype(BF)
            de[...] = rounded
            sums[...] = jnp.sum(rounded.astype(F32), axis=0, keepdims=True)
            for z in range(depth):
                total[:, z * shard : (z + 1) * shard] += dot_nt(rounded, w_first[i, parity, z])

    @pl.when(step == 2 * middle - 1)
    def _():
        rest[2].wait()

        @pl.loop(0, rows // chunk)
        def _(i):
            at = pl.ds(pl.multiple_of(i * chunk, chunk), chunk)
            grad, unit = total[at, :], normed[at, :]
            grad_sum = norm_back(grad, unit, inverse[at, 0:1], gain_first[...])
            du[at, :] = grad_sum
            rounded = grad_sum.astype(BF)
            da[at, :] = rounded
            sums_first[0:1, :] += jnp.sum(grad * unit, axis=0, keepdims=True)
            sums_first[1:2, :] += jnp.sum(grad, axis=0, keepdims=True)
            sums_first[2:3, :] += jnp.sum(rounded.astype(F32), axis=0, keepdims=True)

        for copy in back:
            copy.wait()


def feed(low, inverse, bias_halves, bias_reduce, gain_second, shift_second, gain_first, hidden, cot, normed, second, blocks, shard):
    rows, width = low.shape
    depth, middle, piece, _ = second[0].shape
    block = depth * piece
    flat, parts = flatten_blocks(blocks)
    ahead = lambda i: jnp.minimum(i, middle - 1)
    behind = lambda i: jnp.maximum(i - middle, 0)
    bias = pl.BlockSpec((None, 1, block), lambda i: (ahead(i), 0, 0))
    sums = pl.BlockSpec((None, 1, block), lambda i: (behind(i), 0, 0))
    act = pl.BlockSpec((rows, block), lambda i: (0, ahead(i)))
    de = pl.BlockSpec((rows, block), lambda i: (0, behind(i)))
    full, vec, anywhere = whole((rows, width)), whole((1, width)), pl.BlockSpec(memory_space=pl.ANY)
    shape = jax.ShapeDtypeStruct
    return pl.pallas_call(
        functools.partial(feed_kernel, middle=middle, depth=depth, parts=parts),
        grid=(2 * middle,),
        in_specs=[full, whole((rows, LANES)), bias, bias, vec, vec, vec, vec] + [anywhere] * (5 + len(flat)),
        out_specs=[act, act, de, de, sums, sums, anywhere, anywhere, full, full, whole((8, width)), whole((8, width))],
        out_shape=[shape((rows, middle * block), BF)] * 4
        + [shape((middle, 1, block), F32)] * 2
        + [shape((rows, width), F32), shape((rows, width), BF), shape((rows, width), F32), shape((rows, width), BF)]
        + [shape((8, width), F32)] * 2,
        scratch_shapes=[
            pltpu.VMEM((middle, 2, depth, shard, block), BF),
            pltpu.VMEM((middle, 2, depth, piece, width), BF),
            pltpu.VMEM((middle, 2, rows, block), BF),
            pltpu.VMEM((rows, width), F32),
            pltpu.VMEM((rows, width), F32),
            pltpu.VMEM((rows, width), F32),
            pltpu.VMEM((rows, width), F32),
            pltpu.VMEM((rows, width), BF),
            pltpu.VMEM((rows, width), F32),
            pltpu.SemaphoreType.DMA((len(flat),)),
            pltpu.SemaphoreType.DMA((middle, 2)),
            pltpu.SemaphoreType.DMA((5,)),
        ],
        compiler_params=params(),
        cost_estimate=cost(16 * rows * width * middle * block, 8 * width * middle * block + 40 * rows * width),
        name="feed",
    )(
        low,
        inverse,
        *bias_halves,
        bias_reduce[None],
        gain_second[None],
        shift_second[None],
        gain_first[None],
        hidden,
        cot,
        normed,
        *second,
        *flat,
    )


def context_back_kernel(me, da, weight, *refs, middle):
    outs, whole_grad = refs[:-1], refs[-1]
    whole_grad[...] = dot_nt(da[...], weight[...]).astype(BF)
    rows = da.shape[0]
    mine, other = outs
    width = mine.shape[1]
    second = (me[0] & 1) == 1
    for i in range(middle):
        at = pl.multiple_of(((me[0] ^ (2 * i)) // 2) * 2 * width, 2 * width)
        pair = whole_grad[:, pl.ds(at, 2 * width)]
        low, high = pair[:, :width], pair[:, width:]
        mine[i * rows : (i + 1) * rows, :] = jnp.where(second, high, low)
        other[i * rows : (i + 1) * rows, :] = jnp.where(second, low, high)


def context_back(me, da, weight, own_width, middle):
    rows, width = da.shape
    shape = (middle * rows, own_width)
    return pl.pallas_call(
        functools.partial(context_back_kernel, middle=middle),
        grid=(1,),
        in_specs=[pl.BlockSpec(memory_space=pltpu.SMEM), whole(da.shape), whole(weight.shape)],
        out_specs=[whole(shape)] * 2,
        out_shape=[jax.ShapeDtypeStruct(shape, BF)] * 2,
        scratch_shapes=[pltpu.VMEM((rows, width), BF)],
        compiler_params=params(),
        cost_estimate=cost(2 * rows * width * width, 2 * width * width + 4 * rows * width),
        name="context_back",
    )(me, da, weight)


def gradient_kernel(act, other_act, grad, other_grad, out):
    depth, piece, width = out.shape
    total = dot_tn(act[...], grad[...]) + dot_tn(other_act[...], other_grad[...])
    out[...] = total.astype(BF).reshape(depth, piece, width)


def reduce_gradient(act, other_act, grad, other_grad, depth, piece):
    rows, width = grad.shape
    block = depth * piece
    middle = act.shape[1] // block
    column = pl.BlockSpec((rows, block), lambda i: (0, i))
    full = whole((rows, width))
    return pl.pallas_call(
        gradient_kernel,
        grid=(middle,),
        in_specs=[column, column, full, full],
        out_specs=pl.BlockSpec((depth, None, piece, width), lambda i: (0, i, 0, 0)),
        out_shape=jax.ShapeDtypeStruct((depth, middle, piece, width), BF),
        compiler_params=params(),
        cost_estimate=cost(4 * rows * width * middle * block, 2 * width * middle * block + 4 * rows * middle * block),
        name="reduce_gradient",
    )(act, other_act, grad, other_grad)


EXTRA = 16


def expand_gradient_kernel(
    me, low, other_low, context, other_context, de, other_de, da, other_da, small, *outs, middle, own, share
):
    block = de.shape[1] // middle
    depth = small.shape[0]
    shard = low.shape[1] // depth
    tall = shard + EXTRA
    first, second = low[...].T, other_low[...].T
    third, fourth = context[...].T, other_context[...].T
    kept_a, sent_a, kept_b, sent_b = outs
    for i in range(middle):
        at = slice(i * block, (i + 1) * block)
        target = me[0] ^ (2 * i)
        wide = (dot_nn(first, de[:, at]) + dot_nn(second, other_de[:, at])).astype(BF)
        where = pl.ds(pl.multiple_of(target * own, own), own)
        thin = (dot_nn(third, da[:, where]) + dot_nn(fourth, other_da[:, where])).astype(BF)
        for out, n, part in (
            (sent_a if i >= 2 else kept_a, i % 2, range(depth // 2)),
            (sent_b if i % 2 else kept_b, i // 2, range(depth // 2, depth)),
        ):
            for z in part:
                row = (z - part[0]) * tall
                out[n, row : row + shard, :block] = wide[z * shard : (z + 1) * shard]
                out[n, row : row + shard, block:] = thin[z * shard : (z + 1) * shard]
                line = small[z : z + 1, pl.ds(pl.multiple_of(target * share, share), share)].astype(BF)
                line = jnp.concatenate([line, jnp.zeros((1, block + own - share), BF)], axis=1)
                out[n, row + shard : row + tall, :] = jnp.broadcast_to(line, (EXTRA, block + own))


def expand_gradient(me, low, other_low, context, other_context, de, other_de, da, other_da, small, own):
    rows, width = low.shape
    middle = 4
    depth = small.shape[0]
    block = de.shape[1] // middle
    args = (low, other_low, context, other_context, de, other_de, da, other_da, small)
    shape = (2, width // 2 + EXTRA * depth // 2, block + own)
    share = small.shape[1] // (2 * middle)
    return pl.pallas_call(
        functools.partial(expand_gradient_kernel, middle=middle, own=own, share=share),
        grid=(1,),
        in_specs=[pl.BlockSpec(memory_space=pltpu.SMEM)] + [whole(v.shape) for v in args],
        out_specs=[whole(shape)] * 4,
        out_shape=[jax.ShapeDtypeStruct(shape, BF)] * 4,
        compiler_params=params(),
        cost_estimate=cost(4 * rows * width * middle * (block + own), 4 * width * middle * block),
        name="expand_gradient",
    )(me, *args)


def add_kernel(*refs, count):
    for i in range(count):
        mine, got, out = refs[2 * i], refs[2 * i + 1], refs[2 * count + i]
        out[...] = (mine[...].astype(F32) + got[...].astype(F32)).astype(BF)


def add_steps(kept_a, got_a, kept_b, got_b):
    _, rows, width = kept_a.shape
    block = lambda n: pl.BlockSpec((None, rows // 2, width), lambda i: (n, i, 0))
    args = (kept_a, got_a, kept_a, got_a, kept_b, got_b, kept_b, got_b)
    return pl.pallas_call(
        functools.partial(add_kernel, count=4),
        grid=(2,),
        in_specs=[block(n) for n in (0, 0, 1, 1)] * 2,
        out_specs=[pl.BlockSpec((rows // 2, width), lambda i: (i, 0))] * 4,
        out_shape=[jax.ShapeDtypeStruct((rows, width), BF)] * 4,
        compiler_params=params(),
        cost_estimate=cost(0, 12 * rows * width),
        name="add_steps",
    )(*args)


def add_last_kernel(kept_a, got_a, kept_b, got_b, out):
    rows = kept_a.shape[0]
    out[:rows, :] = (kept_a[...].astype(F32) + got_a[...].astype(F32)).astype(BF)
    out[rows:, :] = (kept_b[...].astype(F32) + got_b[...].astype(F32)).astype(BF)


def add_last(kept_a, got_a, kept_b, got_b):
    rows, width = kept_a.shape
    shape = (2 * rows, width)
    return pl.pallas_call(
        add_last_kernel,
        grid=(1,),
        in_specs=[whole((rows, width))] * 4,
        out_specs=whole(shape),
        out_shape=jax.ShapeDtypeStruct(shape, BF),
        compiler_params=params(),
        cost_estimate=cost(0, 12 * rows * width),
        name="add_last",
    )(kept_a, got_a, kept_b, got_b)


def unpack_expand_kernel(blocks, wide, thin, small, *, depth):
    count = blocks.shape[0]
    shard = wide.shape[0]
    block = wide.shape[1] // count
    piece, own = block // depth, thin.shape[1] // count
    for g in range(count):
        for z in range(depth):
            at = (z * count + g) * piece
            wide[:, at : at + piece] = blocks[g, :shard, z * piece : (z + 1) * piece].astype(F32)
        thin[:, g * own : (g + 1) * own] = blocks[g, :shard, block:].astype(F32)
        small[g : g + 1, :] = blocks[g, shard : shard + EXTRA, : small.shape[1]].astype(F32)[0:1]


def unpack_expand(blocks, depth, hidden, width, share):
    shard = blocks.shape[1] - EXTRA
    shapes = [(shard, hidden), (shard, width), (blocks.shape[0], share)]
    return pl.pallas_call(
        functools.partial(unpack_expand_kernel, depth=depth),
        grid=(1,),
        in_specs=[whole(blocks.shape)],
        out_specs=[whole(v) for v in shapes],
        out_shape=[jax.ShapeDtypeStruct(v, F32) for v in shapes],
        compiler_params=params(),
        cost_estimate=cost(0, 6 * shard * (hidden + width)),
        name="unpack_expand",
    )(blocks)


def unpack_reduce_kernel(me, *refs):
    out = refs[-1]
    rows = refs[0].shape[0]
    for n, k in enumerate(plane_list(len(refs) - 1)):
        out[pl.ds(pl.multiple_of((me[0] ^ k) * rows, rows), rows), :] = refs[n][...].astype(F32)


def unpack_reduce(me, blocks):
    rows, width = blocks[0].shape
    shape = (rows * len(blocks), width)
    return pl.pallas_call(
        unpack_reduce_kernel,
        grid=(1,),
        in_specs=[pl.BlockSpec(memory_space=pltpu.SMEM)] + [whole(v.shape) for v in blocks],
        out_specs=whole(shape),
        out_shape=jax.ShapeDtypeStruct(shape, F32),
        compiler_params=params(),
        cost_estimate=cost(0, 6 * shape[0] * width),
        name="unpack_reduce",
    )(me, *blocks)


def input_part_kernel(grads, weight, *refs, with_away):
    got = dot_nn(grads[...], weight[...])
    if with_away:
        got = got + refs[0][...].astype(F32)
        outs = refs[1:]
    else:
        outs = refs
    rows = outs[0].shape[0]
    for i, out in enumerate(outs):
        out[...] = got[i * rows : (i + 1) * rows].astype(BF)


def input_part(grads, weight, half, away=None, pieces=1):
    count, line = grads.shape
    rows, width = count // 2, weight.shape[1]
    more = () if away is None else (away,)
    shape = (rows // pieces, width)
    got = pl.pallas_call(
        functools.partial(input_part_kernel, with_away=away is not None),
        grid=(1,),
        in_specs=[pl.BlockSpec((rows, line), lambda i: (half, 0)), whole(weight.shape)] + [whole(v.shape) for v in more],
        out_specs=[whole(shape)] * pieces,
        out_shape=[jax.ShapeDtypeStruct(shape, BF)] * pieces,
        compiler_params=params(),
        cost_estimate=cost(2 * rows * width * line, 4 * rows * width),
        name="input_part",
    )(grads, weight, *more)
    return got if pieces > 1 else got[0]


def input_kernel(before, *refs):
    out = refs[-1]
    rows = refs[0].shape[0]
    half = len(refs) // 2
    for s in range(2):
        total = before[s * rows : (s + 1) * rows, :]
        for ref in refs[s * half : (s + 1) * half]:
            total = total + ref[...].astype(F32)
        out[s] = total


def input_sum(before, first, second):
    rows, width = first[0].shape
    return pl.pallas_call(
        input_kernel,
        grid=(1,),
        in_specs=[whole(before.shape)] + [whole(v.shape) for v in (*first, *second)],
        out_specs=whole((2, rows, width)),
        out_shape=jax.ShapeDtypeStruct((2, rows, width), F32),
        compiler_params=params(),
        cost_estimate=cost(0, 32 * rows * width),
        name="input_sum",
    )(before, *first, *second)


def unpack_heads_kernel(me, *refs):
    outs, bias = refs[-4:-1], refs[-1]
    count = len(refs) - 4
    shard, width = outs[0].shape
    own = width // count
    bias[...] = jnp.zeros_like(bias)
    for n, k in enumerate(plane_list(count)):
        where = pl.ds(pl.multiple_of((me[0] ^ k) * own, own), own)
        tail = refs[n][shard : shard + 16, :].astype(F32)
        for t in range(3):
            at = slice(t * own, (t + 1) * own)
            outs[t][:, where] = refs[n][:shard, at].astype(F32)
            bias[t : t + 1, where] = tail[0:1, at] + tail[1:2, at]


def unpack_heads(me, blocks, shard, width):
    shapes = [(shard, width)] * 3 + [(8, width)]
    return pl.pallas_call(
        unpack_heads_kernel,
        grid=(1,),
        in_specs=[pl.BlockSpec(memory_space=pltpu.SMEM)] + [whole(v.shape) for v in blocks],
        out_specs=[whole(v) for v in shapes],
        out_shape=[jax.ShapeDtypeStruct(v, F32) for v in shapes],
        compiler_params=params(),
        cost_estimate=cost(0, 18 * shard * width),
        name="unpack_heads",
    )(me, *blocks)


def heads_gradient_kernel(*refs, blocks, last):
    grads = refs[blocks]
    if last:
        before, sums_before, out, tokens, turned = refs[blocks + 1 :]
    else:
        out, sums, tokens = refs[blocks + 1 :]
    rows = grads.shape[0] // blocks
    for i, ref in enumerate(refs[:blocks]):
        tokens[i * rows : (i + 1) * rows, :] = ref[:rows, :]
    total = dot_tn(grads[...], tokens[...])
    column = jnp.sum(grads[...].astype(F32), axis=0, keepdims=True)
    if not last:
        out[...] = total
        sums[...] = jnp.broadcast_to(column, sums.shape)
        return
    turned[...] = (total + before[...]).T.astype(BF)
    column = jnp.broadcast_to(column + sums_before[0:1, :], (EXTRA, column.shape[1]))
    first = column.astype(BF).astype(F32)
    place = lax.broadcasted_iota(jnp.int32, (EXTRA, 1), 0)
    extra = jnp.where(place == 0, first, jnp.where(place == 1, column - first, 0.0)).astype(BF)
    depth = out.shape[0]
    shard = turned.shape[0] // depth
    for j in range(depth):
        out[j, :shard, :] = turned[j * shard : (j + 1) * shard, :]
        out[j, shard:, :] = extra


def heads_gradient(blocks, grads, more=None, depth=1):
    line = grads.shape[1]
    width = blocks[0].shape[1]
    last = more is not None
    args = (*blocks, grads) + (more or ())
    specs = [whole(v.shape) for v in (*blocks, grads)]
    scratch = [pltpu.VMEM((grads.shape[0], width), BF)]
    if last:
        shapes = [jax.ShapeDtypeStruct((depth, width // depth + EXTRA, line), BF)]
        specs += [whole(v.shape) for v in more]
        scratch.append(pltpu.VMEM((width, line), BF))
    else:
        shapes = [jax.ShapeDtypeStruct((line, width), F32), jax.ShapeDtypeStruct((8, line), F32)]
    return pl.pallas_call(
        functools.partial(heads_gradient_kernel, blocks=len(blocks), last=last),
        grid=(1,),
        in_specs=specs,
        out_specs=[whole(v.shape) for v in shapes],
        out_shape=shapes,
        scratch_shapes=scratch,
        compiler_params=params(),
        cost_estimate=cost(2 * grads.shape[0] * width * line, 2 * grads.shape[0] * width + 6 * width * line),
        name="heads_gradient",
    )(*args)


def normalize(values, gain, shift):
    mean = jnp.mean(values, axis=-1, keepdims=True)
    centred = values - mean
    inverse = lax.rsqrt(jnp.mean(centred * centred, axis=-1, keepdims=True) + EPS)
    normed = centred * inverse
    return normed * gain + shift, normed, inverse


def normalize_back(grad, normed, inverse, gain):
    scaled = grad * gain
    inner = (
        scaled
        - jnp.mean(scaled, axis=-1, keepdims=True)
        - normed * jnp.mean(scaled * normed, axis=-1, keepdims=True)
    )
    return inner * inverse, jnp.sum(grad * normed, axis=0), jnp.sum(grad, axis=0)


def column_sums(values):
    return jnp.sum(values.astype(F32), axis=0)


def plain_body(
    tokens,
    segments,
    query_weight,
    query_bias,
    key_weight,
    value_weight,
    value_bias,
    output_weight,
    output_bias,
    first_gain,
    first_shift,
    expand_weight,
    expand_bias,
    reduce_weight,
    reduce_bias,
    second_gain,
    second_shift,
    cotangent,
):
    batch, rows, width = tokens.shape
    count, depth = lax.axis_size("ctx"), lax.axis_size("fsdp")
    me, my_shard = lax.axis_index("ctx"), lax.axis_index("fsdp")
    shard = query_weight.shape[0]
    hidden = expand_weight.shape[1]
    own_width = width // count
    heads = own_width // HEAD
    piece = hidden // depth // count
    block = depth * piece
    half = hidden // 2
    order = plane_order()
    evens = order[: count // 2]
    scale = HEAD**-0.5
    bits = (count * rows - 1).bit_length()

    columns = lambda w: lax.dynamic_slice_in_dim(w, me * own_width, own_width, 1).astype(BF)
    names = (query_bias, value_bias, output_bias, first_gain, first_shift, reduce_bias, second_gain, second_shift)
    packed = jnp.concatenate(names + (expand_bias,))
    terms = jnp.concatenate(in_terms(packed, 3))
    line = 3 * own_width
    lines = -(-terms.shape[0] // (16 * line)) * 16
    terms = jnp.pad(terms, (0, lines * line - terms.shape[0])).reshape(lines, line)
    own_heads = jnp.concatenate([columns(query_weight), columns(key_weight), columns(value_weight)], axis=1)
    own_heads = gather_shards(jnp.concatenate([own_heads, terms], axis=0))
    packed = own_heads[:, shard:].reshape(depth, lines * line)[:, : 3 * packed.shape[0]]
    packed = jnp.sum(packed.reshape(depth, 3, -1).astype(F32), axis=1)
    own_heads = own_heads[:, :shard].reshape(width, line)
    (bias_query, bias_value, bias_output, gain_first, shift_first, bias_reduce, gain_second, shift_second) = (
        packed[:, i * shard : (i + 1) * shard].reshape(width) for i in range(len(names))
    )
    wide_bias = packed[:, len(names) * shard :].reshape(depth, count, piece)
    bias_halves = [
        jnp.stack([lax.dynamic_index_in_dim(wide_bias, me ^ k, 1, keepdims=False) for k in ks], axis=1).reshape(half)
        for ks in (evens, order[count // 2 :])
    ]
    own_part = lambda v: lax.dynamic_slice_in_dim(v, me * own_width, own_width, 0)
    head_bias = jnp.concatenate([own_part(bias_query), jnp.zeros((own_width,), F32), own_part(bias_value)])
    head_scale = jnp.concatenate([jnp.full((own_width,), scale * LOG2E, F32), jnp.ones((2 * own_width,), F32)])

    thin = shard // count
    folds = width // block
    strip = lax.dynamic_slice_in_dim(output_weight, me * thin, thin, 0).astype(BF)
    strip = jnp.concatenate([strip[:, i * block : (i + 1) * block] for i in range(folds)], axis=0)
    block_expand = lax.dynamic_slice_in_dim(expand_weight.reshape(shard, depth, count * piece), me * piece, piece, 2)
    block_expand = jnp.concatenate([block_expand.reshape(shard, block).astype(BF), strip], axis=0)
    block_expand = lax.all_gather(block_expand, "fsdp", axis=0)
    block_reduce = lax.dynamic_slice_in_dim(reduce_weight, me * piece, piece, 0).astype(BF)
    block_reduce = lax.all_gather(block_reduce, "fsdp", axis=0)

    groups = jnp.stack([w.reshape(shard, count, own_width) for w in (query_weight, key_weight, value_weight)], axis=2)
    half_heads = jnp.concatenate(
        [lax.dynamic_index_in_dim(groups, me ^ k, 1, keepdims=False).reshape(shard, line).astype(BF) for k in evens],
        axis=1,
    )
    half_heads = lax.all_gather(half_heads, "fsdp", axis=0, tiled=True)
    other_heads = peer(half_heads, 1)

    seg = segments
    for b in range(count.bit_length() - 1):
        seg = jnp.concatenate([seg, peer(seg, 1 << b)], axis=1)
    seg = seg.reshape(batch, count, rows)
    seg = jnp.concatenate([seg[:, k] for k in order], axis=1)

    lanes = lambda v: v if own_width == LANES else jnp.pad(v, ((0, 0), (0, LANES - own_width)))
    kept, context_parts = [], []
    for s in range(batch):
        even = jnp.concatenate(gather_even(tokens[s].astype(BF), s % 2 == 0), axis=0)
        odd = peer(even, 1)
        qkv = jnp.concatenate([dot_nn(even, own_heads), dot_nn(odd, own_heads)], axis=0)
        qkv = ((qkv + head_bias) * head_scale).astype(BF)
        if own_width != LANES:
            qkv = jnp.concatenate([lanes(qkv[:, i * own_width : (i + 1) * own_width]) for i in range(3)], axis=1)
        mask_q, mask_k = mask_columns(seg[s], bits)
        out, lse = attend(qkv, mask_q, mask_k, heads, rows)
        kept.append((even, odd, qkv, mask_q, mask_k, out, lse))
        context_parts.append(by_owner(heads_to_rows(out[:, :own_width]), 1))

    got_expand = gather_even(block_expand, True)
    got_expand += [peer(v, 1) for v in got_expand]
    got_reduce = gather_even(block_reduce, False)
    got_reduce += [peer(v, 1) for v in got_reduce]
    full_output = by_owner(
        [
            jnp.concatenate([v[:, shard + i * thin : shard + (i + 1) * thin] for i in range(folds)], axis=2)
            for v in got_expand
        ],
        1,
    ).reshape(width, width)
    middle = count // 2
    expand_halves = [
        jnp.concatenate([v[:, :shard].reshape(width, depth, piece) for v in vs], axis=2).reshape(width, half)
        for vs in (got_expand[:middle], got_expand[middle:])
    ]
    reduce_halves = [
        jnp.concatenate(vs, axis=1).reshape(half, width) for vs in (got_reduce[:middle], got_reduce[middle:])
    ]

    firsts = []
    for s in range(batch):
        branch = dot_nn(context_parts[s], full_output) + bias_output
        firsts.append(normalize(tokens[s] + branch, gain_first, shift_first))
    hidden_in, normed_first, inverse_first = (jnp.concatenate(v, axis=0) for v in zip(*firsts))
    context_low = jnp.concatenate(context_parts, axis=0)
    hidden_low = hidden_in.astype(BF)
    halves = []
    reduced = bias_reduce
    for weight, back, bias in zip(expand_halves, reduce_halves, bias_halves):
        expand = dot_nn(hidden_low, weight) + bias
        cdf = 0.5 * (1.0 + lax.erf(expand * SQRT_HALF))
        active = (expand * cdf).astype(BF)
        slope = cdf + expand * DENSITY * jnp.exp(-0.5 * expand * expand)
        reduced = reduced + dot_nn(active, back)
        halves.append((weight, back, active, slope.astype(BF)))
    result, normed_second, inverse_second = normalize(hidden_in + reduced, gain_second, shift_second)

    grad_out = cotangent.reshape(batch * rows, width)
    grad_sum_second, grad_gain_second, grad_shift_second = normalize_back(
        grad_out, normed_second, inverse_second, gain_second
    )
    grad_reduced = grad_sum_second.astype(BF)
    grad_bias_reduce = column_sums(grad_reduced)

    def chip_sum(make):
        got = peer(make(1).astype(BF), 1)
        return (make(0) + got.astype(F32)).astype(BF)

    sum_reduce = chip_sum(lambda i: dot_tn(halves[i][2], grad_reduced))
    sum_reduce = lax.psum_scatter(sum_reduce, "fsdp", scatter_dimension=0, tiled=True)
    sum_reduce = reduce_even(jnp.split(sum_reduce, middle, axis=0), False)

    grad_hidden = grad_sum_second
    grad_expands = []
    for weight, back, active, slope in halves:
        grad_expand = (dot_nt(grad_reduced, back) * slope.astype(F32)).astype(BF)
        grad_hidden = grad_hidden + dot_nt(grad_expand, weight)
        grad_expands.append(grad_expand)
    grad_bias_expand = [column_sums(g).reshape(depth, middle, piece) for g in grad_expands]
    grad_pre, grad_gain_first, grad_shift_first = normalize_back(
        grad_hidden, normed_first, inverse_first, gain_first
    )
    grad_branch = grad_pre.astype(BF)
    grad_bias_output = column_sums(grad_branch)
    grad_context = dot_nt(grad_branch, full_output).astype(BF)

    sum_expand = chip_sum(lambda i: dot_tn(hidden_low, grad_expands[i])).reshape(width, depth, middle, piece)
    sum_expand = reduce_even([sum_expand[:, :, i].reshape(width, block) for i in range(middle)], True)
    branch_blocks = jnp.concatenate(
        [lax.dynamic_slice_in_dim(grad_branch, (me ^ k) * own_width, own_width, 1) for k in order], axis=1
    )
    sum_output = chip_sum(
        lambda i: dot_tn(context_low, branch_blocks[:, i * width // 2 : (i + 1) * width // 2])
    )
    sum_output = reduce_even(jnp.split(sum_output, middle, axis=1), False)
    sum_expand = jnp.concatenate([sum_expand, sum_output], axis=1)
    sum_expand = lax.psum_scatter(sum_expand, "fsdp", scatter_dimension=0, tiled=True)

    grads = []
    for s in range(batch):
        even, odd, qkv, mask_q, mask_k, out, lse = kept[s]
        dc = lanes(rows_to_heads(grad_context[s * rows : (s + 1) * rows], own_width))
        got = attend_back(qkv, mask_q, mask_k, dc, out, lse, heads, rows)
        if own_width != LANES:
            got = jnp.concatenate([got[:, i * LANES : i * LANES + own_width] for i in range(3)], axis=1)
        grads.append(got)
    middle_row = count * rows // 2
    grad_heads = sum(
        dot_tn(kept[s][0], grads[s][:middle_row]) + dot_tn(kept[s][1], grads[s][middle_row:]) for s in range(batch)
    ).astype(BF)
    grad_head_bias = jnp.pad(
        jnp.stack(in_terms(sum(column_sums(g) for g in grads), 2)), ((0, 14), (0, 0))
    )
    home_heads = jnp.concatenate(
        [grad_heads.reshape(depth, shard, line), jnp.broadcast_to(grad_head_bias, (depth, 16, line))], axis=1
    )
    home_heads = reduce_shards(home_heads)
    home_heads = jnp.concatenate(
        [home_heads[:shard].astype(BF)]
        + [v[None] for v in in_terms(home_heads[shard] + home_heads[shard + 1], 2)]
        + [jnp.zeros((14, line), BF)],
        axis=0,
    )
    back_rows = [heads_to_rows(g) for g in grads]
    back_even = jnp.concatenate([jnp.concatenate(r[:middle], axis=1) for r in back_rows], axis=0)
    back_odd = jnp.concatenate([jnp.concatenate(r[middle:], axis=1) for r in back_rows], axis=0)
    grad_in = grad_pre + dot_nt(back_even, half_heads) + dot_nt(back_odd, other_heads)

    def spread(value, low_first):
        got = gather_even(value, low_first)
        odd = peer(jnp.stack(got), 1)
        return by_owner([v[None] for v in got] + [odd[i : i + 1] for i in range(middle)], 0)

    wide = lax.all_gather(sum_expand, "ctx", axis=0)
    grad_expand_weight = jnp.transpose(wide[:, :, :block].reshape(count, shard, depth, piece), (1, 2, 0, 3))
    grad_expand_weight = grad_expand_weight.reshape(shard, hidden).astype(F32)
    grad_output_weight = jnp.transpose(wide[:, :, block:], (1, 0, 2)).reshape(shard, width).astype(F32)
    grad_reduce_weight = lax.all_gather(sum_reduce, "ctx", axis=0, tiled=True).astype(F32)
    wide_heads = spread(home_heads, True)
    wide_shards = jnp.transpose(wide_heads[:, :shard].reshape(count, shard, 3, own_width), (2, 1, 0, 3))
    grad_query_weight, grad_key_weight, grad_value_weight = (
        wide_shards[i].reshape(shard, width).astype(F32) for i in range(3)
    )
    wide_biases = jnp.sum(wide_heads[:, shard : shard + 2].astype(F32), axis=1).reshape(count, 3, own_width)
    own_shard = lambda v: lax.dynamic_slice_in_dim(v.reshape(width), my_shard * shard, shard, 0)

    vectors = (
        grad_bias_output,
        grad_gain_first,
        grad_shift_first,
        grad_bias_reduce,
        grad_gain_second,
        grad_shift_second,
    )
    wide_bias = by_owner([g[:, i] for g in grad_bias_expand for i in range(middle)], 1)
    small = jnp.concatenate([v.reshape(depth, shard) for v in vectors] + [wide_bias], axis=1)
    for b in range(count.bit_length() - 1):
        small = small + peer(small, 1 << b)
    small = reduce_shards(small)
    vec = [small[i * shard : (i + 1) * shard] for i in range(len(vectors))]
    vec_expand = small[len(vectors) * shard :]
    return (
        result.reshape(batch, rows, width),
        grad_in.reshape(batch, rows, width),
        grad_query_weight,
        own_shard(wide_biases[:, 0]),
        grad_key_weight,
        grad_value_weight,
        own_shard(wide_biases[:, 2]),
        grad_output_weight,
        vec[0],
        vec[1],
        vec[2],
        grad_expand_weight,
        vec_expand,
        grad_reduce_weight,
        vec[3],
        vec[4],
        vec[5],
    )


def even_pieces(own, other):
    rows = own.shape[0]
    both = jnp.concatenate([own, other], axis=1)
    middle = lax.axis_size("ctx") // 2
    rows = rows // middle
    pieces = [both[i * rows : (i + 1) * rows] for i in range(middle)]
    return [pieces[0]] + [peer(pieces[i], 2 * i) for i in range(1, middle)]


def body(
    tokens,
    segments,
    query_weight,
    query_bias,
    key_weight,
    value_weight,
    value_bias,
    output_weight,
    output_bias,
    first_gain,
    first_shift,
    expand_weight,
    expand_bias,
    reduce_weight,
    reduce_bias,
    second_gain,
    second_shift,
    cotangent,
):
    batch, rows, width = tokens.shape
    count, depth = lax.axis_size("ctx"), lax.axis_size("fsdp")
    me, my_shard = lax.axis_index("ctx"), lax.axis_index("fsdp")
    me_array = me.astype(jnp.int32).reshape(1)
    shard = query_weight.shape[0]
    hidden = expand_weight.shape[1]
    own_width = width // count
    heads = own_width // HEAD
    piece = hidden // depth // count
    block = depth * piece
    middle = count // 2
    order = plane_order()
    evens, odds = order[:middle], order[middle:]
    scale = HEAD**-0.5
    bits = (count * rows - 1).bit_length()
    all_rows = batch * rows

    columns = lambda w: lax.dynamic_slice_in_dim(w, me * own_width, own_width, 1).astype(BF)
    names = (query_bias, value_bias, output_bias, first_gain, first_shift, reduce_bias, second_gain, second_shift)
    packed = jnp.concatenate(names + (expand_bias,))
    size = packed.shape[0]
    terms = jnp.concatenate(in_terms(packed, 3))
    line = 3 * own_width
    lines = -(-terms.shape[0] // (16 * line)) * 16
    terms = jnp.pad(terms, (0, lines * line - terms.shape[0])).reshape(lines, line)
    own_heads = jnp.concatenate([columns(query_weight), columns(key_weight), columns(value_weight)], axis=1)
    shard_parts = gather_doubling(jnp.concatenate([own_heads, terms], axis=0))

    def plane(value, *needed):
        first, second = after((peer(value, 2), peer(value, 4)), *needed)
        part = value.shape[0] // 2
        return first, second, (peer(first[:part], 4), peer(second[part:], 2))

    def chip(blocks):
        return blocks + [jax.tree.map(lambda v: peer(v, 1), b) for b in blocks]

    def direct(value):
        return [value] + [peer(value, k) for k in evens[1:]]

    low_in = []
    for s in range(batch):
        numbers = jnp.concatenate([segments[s] // 64, segments[s] % 64]).astype(BF)
        numbers = jnp.pad(numbers[None], ((0, EXTRA - 1), (0, width - 2 * rows)))
        low_in.append(jnp.concatenate([tokens[s].astype(BF), numbers], axis=0))

    reduce_blocks = [lax.dynamic_slice_in_dim(reduce_weight, (me ^ k) * piece, piece, 0).astype(BF) for k in evens]
    reduce_blocks = jnp.stack(reduce_blocks)

    first_got, shard_parts, low_in, reduce_blocks = join(direct(low_in[0]), shard_parts, low_in, reduce_blocks)
    first_blocks = chip(first_got)
    own_heads = by_owner([shard_parts[j : j + 1] for j in range(depth)], 0, list(range(depth)), "fsdp")
    packed = own_heads[:, shard:].reshape(depth, lines * line)[:, : 3 * size]
    packed = jnp.sum(packed.reshape(depth, 3, -1).astype(F32), axis=1)
    own_heads = own_heads[:, :shard].reshape(width, line)
    (bias_query, bias_value, bias_output, gain_first, shift_first, bias_reduce, gain_second, shift_second) = (
        packed[:, i * shard : (i + 1) * shard].reshape(width) for i in range(len(names))
    )
    wide_bias = packed[:, len(names) * shard :].reshape(depth, count, piece)
    bias_halves = [
        jnp.stack([lax.dynamic_index_in_dim(wide_bias, me ^ k, 1, keepdims=False).reshape(1, block) for k in ks])
        for ks in (evens, odds)
    ]
    own_part = lambda v: lax.dynamic_slice_in_dim(v, me * own_width, own_width, 0)
    head_bias = jnp.concatenate([own_part(bias_query), jnp.zeros((own_width,), F32), own_part(bias_value)])
    head_scale = jnp.concatenate([jnp.full((own_width,), scale * LOG2E, F32), jnp.ones((2 * own_width,), F32)])

    thin = shard // count
    folds = width // block
    strip = lax.dynamic_slice_in_dim(output_weight, me * thin, thin, 0).astype(BF)
    strip = jnp.concatenate([strip[:, i * block : (i + 1) * block] for i in range(folds)], axis=0)
    block_expand = [
        lax.dynamic_slice_in_dim(expand_weight, (z * count + me) * piece, piece, 1).astype(BF) for z in range(depth)
    ]
    block_expand = jnp.concatenate([jnp.concatenate(block_expand, axis=1), strip], axis=0)
    block_expand = lax.all_gather(after(block_expand, first_got[1]), "fsdp", axis=0)

    halfway = count * rows // 2
    heads_across = own_heads.T
    first_qkv, *first_masks = project(first_blocks, rows, own_heads, head_bias, head_scale, bits)
    first_out, first_lse, second_got = join(
        *attend(first_qkv, *first_masks, heads, rows), direct(low_in[1])
    )
    second_blocks = chip(second_got)
    (second_qkv, *second_masks), other_out = join(
        project(second_blocks, rows, own_heads, head_bias, head_scale, bits), peer(first_out[halfway:], 1)
    )

    reduce_own = lax.all_gather(after(reduce_blocks, second_got[1]), "fsdp", axis=0)
    second_out, second_lse, first_pieces, near = join(
        *attend(second_qkv, *second_masks, heads, rows),
        even_pieces(first_out[:halfway], other_out),
        (block_expand, peer(block_expand, 2), peer(block_expand, 4)),
    )
    part = depth // 2
    far = peer(near[1][:part], 4), peer(near[2][part:], 2)
    far, other_out, near_other = join(far, peer(second_out[halfway:], 1), [peer(v, 1) for v in near])
    got_expand = [*((v,) for v in near), far, *((v,) for v in near_other), tuple(peer(v, 1) for v in far)]
    full_output = assemble_output(got_expand, shard, thin, me_array)
    second_pieces = even_pieces(second_out[:halfway], other_out)
    kept = [
        (first_blocks, first_qkv, *first_masks, first_out, first_lse),
        (second_blocks, second_qkv, *second_masks, second_out, second_lse),
    ]

    earlier = None
    for s, pieces in enumerate((first_pieces, second_pieces)):
        earlier = branch(s, me_array, pieces, full_output, tokens, bias_output, gain_first, shift_first, earlier)
    context_low, hidden_in, hidden_low, normed_first, inverse_first = (
        v.reshape(all_rows, v.shape[2]) for v in earlier
    )

    hidden_low, reduce_own = join(hidden_low, reduce_own)
    (
        (act_even, act_odd, de_even, de_odd, sums_even, sums_odd, result, dr, grad_pre, da, sums_second, sums_first),
        other_low,
        other_context,
    ) = join(
        feed(
            hidden_low,
            inverse_first,
            bias_halves,
            bias_reduce,
            gain_second,
            shift_second,
            gain_first,
            hidden_in,
            cotangent.reshape(all_rows, width),
            normed_first,
            [reduce_own, peer(reduce_own, 1)],
            got_expand,
            shard,
        ),
        peer(hidden_low, 1),
        peer(context_low, 1),
    )

    vectors = (sums_first[2], sums_first[0], sums_first[1], sums_second[2], sums_second[0], sums_second[1])
    wide_bias = by_owner(
        [sums[i, 0].reshape(depth, 1, piece) for sums in (sums_even, sums_odd) for i in range(middle)], 1
    ).reshape(depth, hidden // depth)
    small = jnp.concatenate([v.reshape(depth, shard) for v in vectors] + [wide_bias], axis=1)
    share = -(-small.shape[1] // (count * LANES)) * LANES
    small = jnp.pad(small, ((0, 0), (0, share * count - small.shape[1])))
    da, de_even, de_odd, act_even, dr, small, own_grads, other_grads, other_act, other_dr = join(
        da,
        de_even,
        de_odd,
        act_even,
        dr,
        small,
        *context_back(me_array, da, full_output, own_width, middle),
        peer(act_odd, 1),
        peer(dr, 1),
    )

    sum_reduce, de_even, da, small, other_grads, other_de, other_da, other_small = join(
        reduce_gradient(act_even, other_act, dr, other_dr, depth, piece),
        de_even,
        da,
        small,
        peer(other_grads, 1),
        peer(de_odd, 1),
        peer(da, 1),
        peer(small, 1),
    )
    sum_reduce = lax.psum_scatter(sum_reduce, "fsdp", scatter_dimension=0, tiled=False)

    sums, dc = join(
        expand_gradient(
            me_array,
            hidden_low,
            other_low,
            context_low,
            other_context,
            de_even,
            other_de,
            da,
            other_da,
            small + other_small,
            own_width,
        ),
        even_pieces(own_grads, other_grads),
    )
    kept_a, sent_a, kept_b, sent_b = sums

    add = lambda a, b: (a.astype(F32) + b.astype(F32)).astype(BF)
    to_owner = lambda parts: [parts[0]] + [peer(parts[i], 2 * i) for i in range(1, middle)]

    def back(s, dc, part=None, before=None):
        _, qkv, mask_q, mask_k, out, lse = kept[s]
        return attend_back(qkv, mask_q, mask_k, dc, out, lse, heads, rows, part, before, s)

    first_grads = back(0, dc)
    first_grads, odd, got_a, got_b = join(
        first_grads, input_part(first_grads, heads_across, 1), peer(sent_a, 4), peer(sent_b, 2)
    )
    kept_a, sent_a, kept_b, sent_b = add_steps(kept_a, got_a, kept_b, got_b)
    home, before, got_a, got_b, dc, sum_reduce = join(
        input_part(first_grads, heads_across, 0, peer(odd, 1), middle),
        heads_gradient(kept[0][0], first_grads),
        peer(sent_a, 2),
        peer(sent_b, 4),
        dc,
        sum_reduce,
    )
    sum_expand, dc = join(add_last(kept_a, got_a, kept_b, got_b), dc)
    sum_expand = lax.psum_scatter(sum_expand, "fsdp", scatter_dimension=0, tiled=True)
    upper, got_reduce, first_step, home = join(
        back(1, dc, 0), to_owner(sum_reduce), peer(home[1], 2), [home[0], *home[2:]]
    )
    sum_reduce = sum(v.astype(F32) for v in got_reduce).astype(BF)
    upper, sum_reduce = join(upper, sum_reduce)
    second_grads, from_first, sum_reduce = join(
        back(1, dc, 1, upper),
        [home[0], first_step] + [peer(home[i - 1], 2 * i) for i in range(2, middle)],
        sum_reduce,
    )

    home_heads = heads_gradient(kept[1][0], second_grads, before, depth)[0]
    home_heads, second_grads, sum_expand = join(home_heads, second_grads, sum_expand)
    home_heads = lax.psum_scatter(home_heads, "fsdp", scatter_dimension=0, tiled=False)
    odd, got_reduce, second_grads = join(
        input_part(second_grads, heads_across, 1), direct(sum_reduce), second_grads
    )
    from_second, from_first, home_heads, got_reduce = join(
        to_owner(input_part(second_grads, heads_across, 0, peer(odd, 1), middle)), from_first, home_heads, got_reduce
    )
    wide_expand = lax.all_gather(after(sum_expand, home_heads), "ctx", axis=0)
    tail = home_heads[shard].astype(F32) + home_heads[shard + 1].astype(F32)
    home_heads = jnp.concatenate(
        [home_heads[:shard]] + [v[None] for v in in_terms(tail, 2)] + [jnp.zeros((14, line), BF)], axis=0
    )
    heads_got, grad_in, grad_reduce_weight = join(
        direct(home_heads),
        input_sum(grad_pre, from_first, from_second),
        unpack_reduce(me_array, chip(got_reduce)),
    )
    heads_got = chip(heads_got)
    grad_expand_weight, grad_output_weight, small_sum = unpack_expand(wide_expand, depth, hidden, width, share)
    small_sum = small_sum.reshape(-1)
    grad_query_weight, grad_key_weight, grad_value_weight, wide_biases = unpack_heads(
        me_array, heads_got, shard, width
    )
    own_shard = lambda v: lax.dynamic_slice_in_dim(v, my_shard * shard, shard, 0)

    vec = [small_sum[i * shard : (i + 1) * shard] for i in range(len(vectors))]
    vec_expand = small_sum[len(vectors) * shard : len(vectors) * shard + hidden // depth]
    return (
        result.reshape(batch, rows, width),
        grad_in,
        grad_query_weight,
        own_shard(wide_biases[0]),
        grad_key_weight,
        grad_value_weight,
        own_shard(wide_biases[2]),
        grad_output_weight,
        vec[0],
        vec[1],
        vec[2],
        grad_expand_weight,
        vec_expand,
        grad_reduce_weight,
        vec[3],
        vec[4],
        vec[5],
    )


def solution(mesh):
    seq = P("fsdp", "ctx", None)
    mat = P("fsdp", None)
    vec = P("fsdp")
    in_specs = (
        seq,
        P("fsdp", "ctx"),
        mat,
        vec,
        mat,
        mat,
        vec,
        mat,
        vec,
        vec,
        vec,
        mat,
        vec,
        mat,
        vec,
        vec,
        vec,
        seq,
    )
    out_specs = (seq, seq, mat, vec, mat, mat, vec, mat, vec, vec, vec, mat, vec, mat, vec, vec, vec)
    count, depth = mesh.shape["ctx"], mesh.shape["fsdp"]

    def layer(*args):
        width, hidden = args[0].shape[2], args[11].shape[1]
        piece, own_width = hidden // depth // count, width // count
        tiled = count == 8 and depth == 4 and args[0].shape[0] == 2 and piece % LANES == 0 and own_width == LANES
        tiled = tiled and width // depth // count % 16 == 0
        return (body if tiled else plain_body)(*args)

    return jax.shard_map(layer, mesh=mesh, in_specs=in_specs, out_specs=out_specs, check_vma=False)
```

```python
import functools

import jax
import jax.numpy as jnp
from jax import lax
from jax.experimental import pallas as pl
from jax.experimental.pallas import tpu as pltpu
from jax.sharding import PartitionSpec as P

HEAD = 64
LANES = 128
VMEM_LIMIT = 62 << 20
COST_SHARE = 64
EPS = 1e-05
BIG = 1e30
LOG2E = 1.4426950408889634
SQRT_HALF = 0.7071067811865476
DENSITY = 0.3989422804014327
BF = jnp.bfloat16
F32 = jnp.float32


def dot_nn(left, right):
    return jnp.dot(left, right, preferred_element_type=F32)


def dot_tn(left, right):
    return lax.dot_general(left, right, (((0,), (0,)), ((), ())), preferred_element_type=F32)


def dot_nt(left, right):
    return lax.dot_general(left, right, (((1,), (1,)), ((), ())), preferred_element_type=F32)


def exchange(value, axis, k):
    count = lax.axis_size(axis)
    return lax.ppermute(value, axis, [(i, i ^ k) for i in range(count)])


def peer(value, k):
    return exchange(value, "ctx", k)


def after(value, *needed):
    return lax.optimization_barrier((value, needed))[0]


def join(*values):
    return lax.optimization_barrier(values)


def plane_list(count):
    return list(range(0, count, 2)) + list(range(1, count, 2))


def plane_order():
    return plane_list(lax.axis_size("ctx"))


def gather_even(value, low_first):
    count = lax.axis_size("ctx")
    got = {0: value}
    for k in range(2, count, 2):
        bits = [1 << b for b in range(1, count.bit_length()) if k >> b & 1]
        step = bits[-1] if low_first else bits[0]
        got[k] = peer(got[k ^ step], step)
    return [got[k] for k in range(0, count, 2)]


def by_owner(parts, axis, order=None, mesh_axis="ctx"):
    order = order or plane_order()
    stacked = jnp.stack([parts[order.index(k)] for k in range(len(order))])
    me = lax.axis_index(mesh_axis)
    return jnp.concatenate(
        [lax.dynamic_index_in_dim(stacked, me ^ g, 0, keepdims=False) for g in range(len(order))], axis=axis
    )


def rows_to_heads(value, width):
    count = lax.axis_size("ctx")
    me = lax.axis_index("ctx")
    mine, other = [], []
    for k in range(0, count, 2):
        to = me ^ k
        first = lax.dynamic_slice_in_dim(value, to * width, width, 1)
        second = lax.dynamic_slice_in_dim(value, (to ^ 1) * width, width, 1)
        got = jnp.concatenate([first, second], axis=1)
        if k:
            got = peer(got, k)
        mine.append(got[:, :width])
        other.append(got[:, width:])
    return jnp.concatenate(mine + [peer(jnp.concatenate(other, axis=0), 1)], axis=0)


def heads_to_rows(value):
    count = lax.axis_size("ctx")
    rows, width = value.shape[0] // count, value.shape[1]
    half = value.shape[0] // 2
    both = jnp.concatenate([value[:half], peer(value[half:], 1)], axis=1)
    even, odd = [], []
    for i, k in enumerate(range(0, count, 2)):
        got = both[i * rows : (i + 1) * rows]
        if k:
            got = peer(got, k)
        even.append(got[:, :width])
        odd.append(got[:, width:])
    return even + odd


def reduce_even(blocks, low_first):
    count = lax.axis_size("ctx")
    bits = [1 << b for b in range(1, count.bit_length() - 1)]
    if not low_first:
        bits = bits[::-1]
    held = dict(zip(range(0, count, 2), blocks))
    for bit in bits:
        sent = [k for k in held if k & bit]
        got = peer(jnp.stack([held[k] for k in sent]), bit)
        got = {k ^ bit: got[i] for i, k in enumerate(sent)}
        held = {k: (held[k].astype(F32) + got[k].astype(F32)).astype(BF) for k in held if not k & bit}
    return held[0]


def gather_shards(value):
    depth = lax.axis_size("fsdp")
    parts = [value[None]] + [exchange(value, "fsdp", j)[None] for j in range(1, depth)]
    return by_owner(parts, 0, list(range(depth)), "fsdp")


def reduce_shards(value):
    depth = lax.axis_size("fsdp")
    me = lax.axis_index("fsdp")
    total = lax.dynamic_index_in_dim(value, me, 0, keepdims=False).astype(F32)
    for j in range(1, depth):
        sent = lax.dynamic_index_in_dim(value, me ^ j, 0, keepdims=False)
        total = total + exchange(sent, "fsdp", j).astype(F32)
    return total


def gather_doubling(value):
    got = value[None]
    step = 1
    while step < lax.axis_size("fsdp"):
        got = jnp.concatenate([got, exchange(got, "fsdp", step)], axis=0)
        step *= 2
    return got


def in_terms(vector, count):
    terms = []
    for _ in range(count):
        terms.append(vector.astype(BF))
        vector = vector - terms[-1].astype(F32)
    return terms


def whole(shape):
    return pl.BlockSpec(shape, lambda *i: (0,) * len(shape))


def params(limit=VMEM_LIMIT):
    return pltpu.CompilerParams(vmem_limit_bytes=limit)


def cost(flops, size, exps=0):
    return pl.CostEstimate(
        flops=flops // COST_SHARE, bytes_accessed=size // COST_SHARE, transcendentals=exps // COST_SHARE
    )


def mask_columns(seg, bits):
    lane = jnp.arange(LANES) % HEAD
    bit = (seg[:, None] >> jnp.minimum(lane // 2, 30)) & 1
    flip = bit ^ (lane & 1)
    used = lane < 2 * bits
    for_query = jnp.where(used & (flip == 1), -BIG, 0.0).astype(BF)
    for_key = jnp.where(used, 1 - flip, ((lane >= 60) & (lane < 63)).astype(jnp.int32)).astype(BF)
    return for_query, for_key


def lane_index():
    return lax.broadcasted_iota(jnp.int32, (1, LANES), 1)


def merge(main, extra, h):
    lane = lane_index()
    return jnp.where((lane < HEAD) if h == 0 else (lane >= HEAD), main, extra)


def with_terms(extra, number):
    lane = lane_index() % HEAD
    first = number.astype(BF).astype(F32)
    rest = number - first
    second = rest.astype(BF).astype(F32)
    third = rest - second
    terms = jnp.where(lane == 60, first, jnp.where(lane == 61, second, third)).astype(BF)
    return jnp.where((lane >= 60) & (lane < 63), terms, extra)


def forward_kernel(q, k, v, mask_q, mask_k, out, lse, key_side, value_side, *, heads):
    lane = lane_index()

    @pl.when(pl.program_id(0) == 0)
    def _():
        for h in range(heads):
            key_side[h] = merge(k[...], mask_k[...], h)
            value_side[h] = merge(v[...], jnp.ones((1, LANES), BF), h)

    whole, whole_lse = None, None
    for h in range(heads):
        scores = dot_nt(merge(q[...], mask_q[...], h), key_side[h])
        top = jnp.max(scores, axis=1, keepdims=True)
        weights = jnp.exp2(scores - top).astype(BF)
        both = dot_nn(weights, value_side[h])
        total = pltpu.roll(both, HEAD, 1)
        context, log_total = both / total, top + jnp.log2(total)
        if whole is None:
            whole, whole_lse = context, log_total
        else:
            whole = jnp.where(lane < HEAD, whole, context)
            whole_lse = jnp.where(lane < HEAD, whole_lse, log_total)
    out[...] = whole.astype(BF)
    lse[...] = whole_lse


def attend(qkv, mask_q, mask_k, heads, block):
    count = qkv.shape[0]
    part = lambda j: pl.BlockSpec((block, LANES), lambda i: (i, j))
    full = lambda j: pl.BlockSpec((count, LANES), lambda i: (0, j))
    products = 2 * 2 * count * count * LANES * heads
    return pl.pallas_call(
        functools.partial(forward_kernel, heads=heads),
        grid=(count // block,),
        in_specs=[part(0), full(1), full(2), part(0), full(0)],
        out_specs=[part(0), part(0)],
        out_shape=[jax.ShapeDtypeStruct((count, LANES), BF), jax.ShapeDtypeStruct((count, LANES), F32)],
        scratch_shapes=[pltpu.VMEM((heads, count, LANES), BF), pltpu.VMEM((heads, count, LANES), BF)],
        compiler_params=params(),
        cost_estimate=cost(products * 2, 12 * count * LANES, count * count * heads),
        name="attend",
    )(qkv, qkv, qkv, mask_q, mask_k)


def backward_kernel(*refs, heads, first, steps, total, block, pieces):
    q, k, v, mask_q, mask_k, out, lse = refs[:7]
    parts = refs[7 : 7 + pieces]
    refs = refs[7 + pieces :]
    if first:
        grads_before, dk_before, dv_before = refs[:3]
        refs = refs[3:]
    grads = refs[0]
    if steps < total:
        dk_t, dv_t = refs[1:3]
        key_side, value_side, dc_all = refs[3:]
    else:
        key_side, value_side, dc_all, dk_t, dv_t = refs[1:]
    lane = lane_index()
    step = pl.program_id(0)

    @pl.when(step == 0)
    def _():
        ones = ((lane % HEAD >= 60) & (lane % HEAD < 63)).astype(F32).astype(BF)
        for h in range(heads):
            key_side[h] = merge(k[...], mask_k[...], h)
            value_side[h] = merge(v[...], ones, h)
        if first:
            dk_t[...] = dk_before[...]
            dv_t[...] = dv_before[...]
            grads[: first * block, :LANES] = grads_before[...]
        else:
            dk_t[...] = jnp.zeros_like(dk_t)
            dv_t[...] = jnp.zeros_like(dv_t)
        if pieces == 1:
            dc_all[...] = parts[0][...]
        else:
            for i in range(pieces):
                dc_all[i * block : (i + 1) * block, :] = parts[i][:, :LANES]
                dc_all[(pieces + i) * block : (pieces + i + 1) * block, :] = parts[i][:, LANES:]

    dc = dc_all.at[pl.ds(pl.multiple_of((first + step) * block, block), block), :]
    product = dc[...].astype(F32) * out[...].astype(F32)
    low = jnp.sum(jnp.where(lane < HEAD, product, 0.0), axis=1, keepdims=True)
    high = jnp.sum(jnp.where(lane < HEAD, 0.0, product), axis=1, keepdims=True)
    query_extra = with_terms(mask_q[...], -pltpu.roll(lse[...], HEAD, 1))
    grad_extra = with_terms(jnp.zeros((1, LANES), BF), jnp.where(lane < HEAD, -high, -low))
    q_t, dc_t = q[...].T, dc[...].T
    dq = None
    for h in range(heads):
        probs = jnp.exp2(dot_nt(merge(q[...], query_extra, h), key_side[h]))
        centred = dot_nt(merge(dc[...], grad_extra, h), value_side[h])
        ds = (probs * centred).astype(BF)
        part = dot_nn(ds, key_side[h])
        dq = part if dq is None else jnp.where(lane < HEAD, dq, part)
        own = slice(HEAD * h, HEAD * h + HEAD)
        dk_t[own, :] += dot_nn(q_t[own, :], ds)
        dv_t[own, :] += dot_nn(dc_t[own, :], probs.astype(BF))
    at = step * block if steps < total else (first + step) * block
    grads[pl.ds(pl.multiple_of(at, block), block), :LANES] = (dq.astype(BF).astype(F32) * HEAD**-0.5).astype(BF)
    if steps == total:

        @pl.when(step == steps - first - 1)
        def _():
            grads[:, LANES : 2 * LANES] = (dk_t[...] * (1.0 / LOG2E)).T.astype(BF)
            grads[:, 2 * LANES :] = dv_t[...].T.astype(BF)


def attend_back(qkv, mask_q, mask_k, dc, out, lse, heads, block, part=None, before=None, place=0):
    dc = dc if isinstance(dc, list) else [dc]
    count = qkv.shape[0]
    total = count // block
    first = total // 2 if part == 1 else 0
    steps = total // 2 if part == 0 else total
    piece = lambda j: pl.BlockSpec((block, LANES), lambda i: (first + i, j))
    full = lambda j: pl.BlockSpec((count, LANES), lambda i: (0, j))
    products = 5 * 2 * count * count * LANES * heads
    side = (LANES, count)
    shapes = [jax.ShapeDtypeStruct((count, 3 * LANES), BF)]
    scratch = [
        pltpu.VMEM((heads, count, LANES), BF),
        pltpu.VMEM((heads, count, LANES), BF),
        pltpu.VMEM((count, LANES), BF),
    ]
    if part == 0:
        shapes = [jax.ShapeDtypeStruct((count // 2, LANES), BF)] + [jax.ShapeDtypeStruct(side, F32)] * 2
    else:
        scratch += [pltpu.VMEM(side, F32)] * 2
    before = before or []
    got = pl.pallas_call(
        functools.partial(
            backward_kernel, heads=heads, first=first, steps=steps, total=total, block=block, pieces=len(dc)
        ),
        grid=(steps - first,),
        in_specs=[piece(0), full(1), full(2), piece(0), full(0), piece(0), piece(0)]
        + [pl.BlockSpec((block if len(dc) > 1 else count, v.shape[1]), lambda i: (place, 0)) for v in dc]
        + [whole(v.shape) for v in before],
        out_specs=[whole(v.shape) for v in shapes],
        out_shape=shapes,
        scratch_shapes=scratch,
        compiler_params=params(),
        cost_estimate=cost(products, 16 * count * LANES, count * count * heads),
        name="attend_back",
    )(qkv, qkv, qkv, mask_q, mask_k, out, lse, *dc, *before)
    return got if part == 0 else got[0]


def project_kernel(*refs, blocks, rows, bits):
    weight, bias, factor, out, mask_q, mask_k = refs[blocks:]
    lane = lane_index() % HEAD
    used = lane < 2 * bits
    fixed = ((lane >= 60) & (lane < 63)).astype(F32).astype(BF)
    for i, ref in enumerate(refs[:blocks]):
        at = slice(i * rows, (i + 1) * rows)
        got = (dot_nn(ref[:rows, :], weight[...]) + bias[...]) * factor[...]
        out[at, :] = got.astype(BF)
        parts = ref[rows : rows + 16, : 2 * rows].astype(F32)
        number = (parts[:8, :rows] * 64 + parts[:8, rows:]).T[:, :1].astype(jnp.int32)
        flip = ((number >> (lane // 2)) & 1) ^ (lane & 1)
        mask_q[at, :] = jnp.where(used & (flip == 1), -BIG, 0.0).astype(BF)
        mask_k[at, :] = jnp.where(used, (1 - flip).astype(F32).astype(BF), fixed)


def project(blocks, rows, weight, bias, factor, bits):
    width, line = weight.shape
    args = (*blocks, weight, bias[None], factor[None])
    count = rows * len(blocks)
    shapes = [(count, line), (count, LANES), (count, LANES)]
    return pl.pallas_call(
        functools.partial(project_kernel, blocks=len(blocks), rows=rows, bits=bits),
        in_specs=[whole(v.shape) for v in args],
        out_specs=[whole(v) for v in shapes],
        out_shape=[jax.ShapeDtypeStruct(v, BF) for v in shapes],
        grid=(1,),
        compiler_params=params(),
        cost_estimate=cost(2 * count * width * line, 2 * count * (width + line)),
        name="project",
    )(*args)


def flatten_blocks(blocks):
    flat, parts = [], []
    for n, block in enumerate(blocks):
        first = 0
        for part in block:
            flat.append(part)
            parts.append((n, first))
            first += part.shape[0]
    return flat, tuple(parts)


def assemble_kernel(me, *refs, parts, thin, folds):
    out = refs[-1]
    shard = len({n for n, _ in parts}) * thin
    block = refs[0].shape[2]
    order = plane_list(len({n for n, _ in parts}))
    for ref, (n, first) in zip(refs, parts):
        for z in range(ref.shape[0]):
            row = pl.multiple_of((first + z) * shard + (me[0] ^ order[n]) * thin, thin)
            for f in range(folds):
                out[pl.ds(row, thin), f * block : (f + 1) * block] = ref[z, f * thin : (f + 1) * thin, :]


def assemble_output(blocks, shard, thin, me):
    flat, parts = flatten_blocks(blocks)
    _, tall, block = flat[0].shape
    strip = tall - shard
    folds = strip // thin
    width = folds * block
    specs = [pl.BlockSpec((v.shape[0], strip, block), lambda i: (0, shard // strip, 0)) for v in flat]
    return pl.pallas_call(
        functools.partial(assemble_kernel, parts=parts, thin=thin, folds=folds),
        grid=(1,),
        in_specs=[pl.BlockSpec(memory_space=pltpu.SMEM)] + specs,
        out_specs=whole((width, width)),
        out_shape=jax.ShapeDtypeStruct((width, width), BF),
        compiler_params=params(),
        cost_estimate=cost(0, 4 * width * width),
        name="assemble_output",
    )(me, *flat)


def branch_kernel(me, *refs, pieces, aliased):
    weight, tokens, bias, gain, shift = refs[pieces : pieces + 5]
    context, hidden, low, normed, inverse = refs[pieces + 5 + aliased :]
    second = (me[0] & 1) == 1
    pair = refs[0].shape[1]
    for i in range(pieces):
        at = pl.multiple_of(((me[0] ^ (2 * i)) // 2) * pair, pair)
        got = refs[i][...]
        swapped = jnp.concatenate([got[:, pair // 2 :], got[:, : pair // 2]], axis=1)
        context[:, pl.ds(at, pair)] = jnp.where(second, swapped, got)
    total = tokens[...] + dot_nn(context[...], weight[...]) + bias[...]
    mean = jnp.mean(total, axis=1, keepdims=True)
    centred = total - mean
    scale = lax.rsqrt(jnp.mean(centred * centred, axis=1, keepdims=True) + EPS)
    unit = centred * scale
    out = unit * gain[...] + shift[...]
    hidden[...] = out
    low[...] = out.astype(BF)
    normed[...] = unit
    inverse[...] = jnp.broadcast_to(scale, inverse.shape)


def branch(s, me, pieces, weight, tokens, bias, gain, shift, earlier):
    batch, rows, width = tokens.shape
    at = pl.BlockSpec((None, rows, width), lambda i: (s, 0, 0))
    thin = pl.BlockSpec((None, rows, LANES), lambda i: (s, 0, 0))
    vec = whole((1, width))
    earlier = earlier or ()
    first = 1 + len(pieces) + 5
    full = lambda t: jax.ShapeDtypeStruct((batch, rows, width), t)
    return pl.pallas_call(
        functools.partial(branch_kernel, pieces=len(pieces), aliased=len(earlier)),
        grid=(1,),
        in_specs=[pl.BlockSpec(memory_space=pltpu.SMEM)]
        + [whole(v.shape) for v in pieces]
        + [whole(weight.shape), at, vec, vec, vec]
        + [pl.BlockSpec(memory_space=pl.ANY)] * len(earlier),
        out_specs=[at, at, at, at, thin],
        out_shape=[full(BF), full(F32), full(BF), full(F32), jax.ShapeDtypeStruct((batch, rows, LANES), F32)],
        input_output_aliases={first + i: i for i in range(len(earlier))},
        compiler_params=params(),
        cost_estimate=cost(2 * rows * width * width, 2 * width * width + 18 * rows * width),
        name="branch",
    )(me, *pieces, weight, tokens, bias[None], gain[None], shift[None], *earlier)


def norm_back(grad, normed, inverse, gain):
    scaled = grad * gain
    first = jnp.mean(scaled, axis=1, keepdims=True)
    second = jnp.mean(scaled * normed, axis=1, keepdims=True)
    return inverse * (scaled - first - normed * second)


def feed_kernel(*refs, middle, depth, parts):
    low, inverse, bias_even, bias_odd, bias_reduce, gain_second, shift_second, gain_first = refs[:8]
    hidden_at, cot_at, normed_at, second_even, second_odd = refs[8:13]
    blocks = refs[13 : 13 + len(parts)]
    refs = refs[13 + len(parts) :]
    act_even, act_odd, de_even, de_odd, sums_even, sums_odd, result_at, dr_at, du, da, sums_second, sums_first = refs[:12]
    w_first, w_second, slope, hidden, cot, normed, result, dr, total, block_sems, second_sems, sems = refs[12:]
    step = pl.program_id(0)
    rows, width = total.shape
    shard, block = w_first.shape[3], w_first.shape[4]
    chunk = 64

    def first_copies(i):
        made = []
        for j, (ref, (n, first)) in enumerate(zip(blocks, parts)):
            if n % middle == i:
                target = w_first.at[i, n // middle, pl.ds(first, ref.shape[0])]
                made.append(pltpu.make_async_copy(ref.at[:, :shard, :], target, block_sems.at[j]))
        return made

    def second_copies(i):
        return [
            pltpu.make_async_copy(ref.at[:, i], w_second.at[i, parity], second_sems.at[i, parity])
            for parity, ref in enumerate((second_even, second_odd))
        ]

    rest = [
        pltpu.make_async_copy(source, target, sems.at[i])
        for i, (source, target) in enumerate(((hidden_at, hidden), (cot_at, cot), (normed_at, normed)))
    ]
    back = [
        pltpu.make_async_copy(source, target, sems.at[3 + i])
        for i, (source, target) in enumerate(((result, result_at), (dr, dr_at)))
    ]

    @pl.when(step == 0)
    def _():
        for i in range(middle):
            for copy in first_copies(i) + second_copies(i):
                copy.start()
        for copy in rest:
            copy.start()
        sums_second[...] = jnp.zeros_like(sums_second)
        sums_first[...] = jnp.zeros_like(sums_first)

    for i in range(middle):

        @pl.when(step == i)
        def _():
            for copy in first_copies(i) + second_copies(i):
                copy.wait()

    @pl.when(step < middle)
    def _():
        part = None
        for parity, (bias, act) in enumerate(((bias_even, act_even), (bias_odd, act_odd))):
            for at in (slice(0, rows // 2), slice(rows // 2, rows)):
                value = bias[...]
                for z in range(depth):
                    value = value + dot_nn(low[at, z * shard : (z + 1) * shard], w_first[step, parity, z])
                cdf = 0.5 * (1.0 + lax.erf(value * SQRT_HALF))
                act[at, :] = (value * cdf).astype(BF)
                grad = cdf + value * DENSITY * jnp.exp(-0.5 * value * value)
                slope[step, parity, at, :] = grad.astype(BF)
            got = dot_nn(act[...], w_second[step, parity].reshape(block, width))
            part = got if part is None else part + got

        @pl.when(step == 0)
        def _():
            total[...] = part + bias_reduce[...]

        @pl.when(step > 0)
        def _():
            total[...] += part

    @pl.when(step == middle - 1)
    def _():
        rest[0].wait()
        rest[1].wait()

        @pl.loop(0, rows // chunk)
        def _(i):
            at = pl.ds(pl.multiple_of(i * chunk, chunk), chunk)
            value = total[at, :] + hidden[at, :]
            mean = jnp.mean(value, axis=1, keepdims=True)
            centred = value - mean
            scale = lax.rsqrt(jnp.mean(centred * centred, axis=1, keepdims=True) + EPS)
            unit = centred * scale
            result[at, :] = unit * gain_second[...] + shift_second[...]
            grad = cot[at, :]
            grad_sum = norm_back(grad, unit, scale, gain_second[...])
            total[at, :] = grad_sum
            rounded = grad_sum.astype(BF)
            dr[at, :] = rounded
            sums_second[0:1, :] += jnp.sum(grad * unit, axis=0, keepdims=True)
            sums_second[1:2, :] += jnp.sum(grad, axis=0, keepdims=True)
            sums_second[2:3, :] += jnp.sum(rounded.astype(F32), axis=0, keepdims=True)

        for copy in back:
            copy.start()

    @pl.when(step >= middle)
    def _():
        i = step - middle
        for parity, (de, sums) in enumerate(((de_even, sums_even), (de_odd, sums_odd))):
            grad = dot_nt(dr[...], w_second[i, parity].reshape(block, width)) * slope[i, parity].astype(F32)
            rounded = grad.astype(BF)
            de[...] = rounded
            sums[...] = jnp.sum(rounded.astype(F32), axis=0, keepdims=True)
            for z in range(depth):
                total[:, z * shard : (z + 1) * shard] += dot_nt(rounded, w_first[i, parity, z])

    @pl.when(step == 2 * middle - 1)
    def _():
        rest[2].wait()

        @pl.loop(0, rows // chunk)
        def _(i):
            at = pl.ds(pl.multiple_of(i * chunk, chunk), chunk)
            grad, unit = total[at, :], normed[at, :]
            grad_sum = norm_back(grad, unit, inverse[at, 0:1], gain_first[...])
            du[at, :] = grad_sum
            rounded = grad_sum.astype(BF)
            da[at, :] = rounded
            sums_first[0:1, :] += jnp.sum(grad * unit, axis=0, keepdims=True)
            sums_first[1:2, :] += jnp.sum(grad, axis=0, keepdims=True)
            sums_first[2:3, :] += jnp.sum(rounded.astype(F32), axis=0, keepdims=True)

        for copy in back:
            copy.wait()


def feed(low, inverse, bias_halves, bias_reduce, gain_second, shift_second, gain_first, hidden, cot, normed, second, blocks, shard):
    rows, width = low.shape
    depth, middle, piece, _ = second[0].shape
    block = depth * piece
    flat, parts = flatten_blocks(blocks)
    ahead = lambda i: jnp.minimum(i, middle - 1)
    behind = lambda i: jnp.maximum(i - middle, 0)
    bias = pl.BlockSpec((None, 1, block), lambda i: (ahead(i), 0, 0))
    sums = pl.BlockSpec((None, 1, block), lambda i: (behind(i), 0, 0))
    act = pl.BlockSpec((rows, block), lambda i: (0, ahead(i)))
    de = pl.BlockSpec((rows, block), lambda i: (0, behind(i)))
    full, vec, anywhere = whole((rows, width)), whole((1, width)), pl.BlockSpec(memory_space=pl.ANY)
    shape = jax.ShapeDtypeStruct
    return pl.pallas_call(
        functools.partial(feed_kernel, middle=middle, depth=depth, parts=parts),
        grid=(2 * middle,),
        in_specs=[full, whole((rows, LANES)), bias, bias, vec, vec, vec, vec] + [anywhere] * (5 + len(flat)),
        out_specs=[act, act, de, de, sums, sums, anywhere, anywhere, full, full, whole((8, width)), whole((8, width))],
        out_shape=[shape((rows, middle * block), BF)] * 4
        + [shape((middle, 1, block), F32)] * 2
        + [shape((rows, width), F32), shape((rows, width), BF), shape((rows, width), F32), shape((rows, width), BF)]
        + [shape((8, width), F32)] * 2,
        scratch_shapes=[
            pltpu.VMEM((middle, 2, depth, shard, block), BF),
            pltpu.VMEM((middle, 2, depth, piece, width), BF),
            pltpu.VMEM((middle, 2, rows, block), BF),
            pltpu.VMEM((rows, width), F32),
            pltpu.VMEM((rows, width), F32),
            pltpu.VMEM((rows, width), F32),
            pltpu.VMEM((rows, width), F32),
            pltpu.VMEM((rows, width), BF),
            pltpu.VMEM((rows, width), F32),
            pltpu.SemaphoreType.DMA((len(flat),)),
            pltpu.SemaphoreType.DMA((middle, 2)),
            pltpu.SemaphoreType.DMA((5,)),
        ],
        compiler_params=params(),
        cost_estimate=cost(16 * rows * width * middle * block, 8 * width * middle * block + 40 * rows * width),
        name="feed",
    )(
        low,
        inverse,
        *bias_halves,
        bias_reduce[None],
        gain_second[None],
        shift_second[None],
        gain_first[None],
        hidden,
        cot,
        normed,
        *second,
        *flat,
    )


def context_back_kernel(me, da, weight, *refs, middle):
    outs, whole_grad = refs[:-1], refs[-1]
    whole_grad[...] = dot_nt(da[...], weight[...]).astype(BF)
    rows = da.shape[0]
    mine, other = outs
    width = mine.shape[1]
    second = (me[0] & 1) == 1
    for i in range(middle):
        at = pl.multiple_of(((me[0] ^ (2 * i)) // 2) * 2 * width, 2 * width)
        pair = whole_grad[:, pl.ds(at, 2 * width)]
        low, high = pair[:, :width], pair[:, width:]
        mine[i * rows : (i + 1) * rows, :] = jnp.where(second, high, low)
        other[i * rows : (i + 1) * rows, :] = jnp.where(second, low, high)


def context_back(me, da, weight, own_width, middle):
    rows, width = da.shape
    shape = (middle * rows, own_width)
    return pl.pallas_call(
        functools.partial(context_back_kernel, middle=middle),
        grid=(1,),
        in_specs=[pl.BlockSpec(memory_space=pltpu.SMEM), whole(da.shape), whole(weight.shape)],
        out_specs=[whole(shape)] * 2,
        out_shape=[jax.ShapeDtypeStruct(shape, BF)] * 2,
        scratch_shapes=[pltpu.VMEM((rows, width), BF)],
        compiler_params=params(),
        cost_estimate=cost(2 * rows * width * width, 2 * width * width + 4 * rows * width),
        name="context_back",
    )(me, da, weight)


def gradient_kernel(act, other_act, grad, other_grad, out):
    depth, piece, width = out.shape
    total = dot_tn(act[...], grad[...]) + dot_tn(other_act[...], other_grad[...])
    out[...] = total.astype(BF).reshape(depth, piece, width)


def reduce_gradient(act, other_act, grad, other_grad, depth, piece):
    rows, width = grad.shape
    block = depth * piece
    middle = act.shape[1] // block
    column = pl.BlockSpec((rows, block), lambda i: (0, i))
    full = whole((rows, width))
    return pl.pallas_call(
        gradient_kernel,
        grid=(middle,),
        in_specs=[column, column, full, full],
        out_specs=pl.BlockSpec((depth, None, piece, width), lambda i: (0, i, 0, 0)),
        out_shape=jax.ShapeDtypeStruct((depth, middle, piece, width), BF),
        compiler_params=params(),
        cost_estimate=cost(4 * rows * width * middle * block, 2 * width * middle * block + 4 * rows * middle * block),
        name="reduce_gradient",
    )(act, other_act, grad, other_grad)


EXTRA = 16


def expand_gradient_kernel(
    me, low, other_low, context, other_context, de, other_de, da, other_da, small, *outs, middle, own, share
):
    block = de.shape[1] // middle
    depth = small.shape[0]
    shard = low.shape[1] // depth
    tall = shard + EXTRA
    first, second = low[...].T, other_low[...].T
    third, fourth = context[...].T, other_context[...].T
    kept_a, sent_a, kept_b, sent_b = outs
    for i in range(middle):
        at = slice(i * block, (i + 1) * block)
        target = me[0] ^ (2 * i)
        wide = (dot_nn(first, de[:, at]) + dot_nn(second, other_de[:, at])).astype(BF)
        where = pl.ds(pl.multiple_of(target * own, own), own)
        thin = (dot_nn(third, da[:, where]) + dot_nn(fourth, other_da[:, where])).astype(BF)
        for out, n, part in (
            (sent_a if i >= 2 else kept_a, i % 2, range(depth // 2)),
            (sent_b if i % 2 else kept_b, i // 2, range(depth // 2, depth)),
        ):
            for z in part:
                row = (z - part[0]) * tall
                out[n, row : row + shard, :block] = wide[z * shard : (z + 1) * shard]
                out[n, row : row + shard, block:] = thin[z * shard : (z + 1) * shard]
                line = small[z : z + 1, pl.ds(pl.multiple_of(target * share, share), share)].astype(BF)
                line = jnp.concatenate([line, jnp.zeros((1, block + own - share), BF)], axis=1)
                out[n, row + shard : row + tall, :] = jnp.broadcast_to(line, (EXTRA, block + own))


def expand_gradient(me, low, other_low, context, other_context, de, other_de, da, other_da, small, own):
    rows, width = low.shape
    middle = 4
    depth = small.shape[0]
    block = de.shape[1] // middle
    args = (low, other_low, context, other_context, de, other_de, da, other_da, small)
    shape = (2, width // 2 + EXTRA * depth // 2, block + own)
    share = small.shape[1] // (2 * middle)
    return pl.pallas_call(
        functools.partial(expand_gradient_kernel, middle=middle, own=own, share=share),
        grid=(1,),
        in_specs=[pl.BlockSpec(memory_space=pltpu.SMEM)] + [whole(v.shape) for v in args],
        out_specs=[whole(shape)] * 4,
        out_shape=[jax.ShapeDtypeStruct(shape, BF)] * 4,
        compiler_params=params(),
        cost_estimate=cost(4 * rows * width * middle * (block + own), 4 * width * middle * block),
        name="expand_gradient",
    )(me, *args)


def add_kernel(*refs, count):
    for i in range(count):
        mine, got, out = refs[2 * i], refs[2 * i + 1], refs[2 * count + i]
        out[...] = (mine[...].astype(F32) + got[...].astype(F32)).astype(BF)


def add_steps(kept_a, got_a, kept_b, got_b):
    _, rows, width = kept_a.shape
    block = lambda n: pl.BlockSpec((None, rows // 2, width), lambda i: (n, i, 0))
    args = (kept_a, got_a, kept_a, got_a, kept_b, got_b, kept_b, got_b)
    return pl.pallas_call(
        functools.partial(add_kernel, count=4),
        grid=(2,),
        in_specs=[block(n) for n in (0, 0, 1, 1)] * 2,
        out_specs=[pl.BlockSpec((rows // 2, width), lambda i: (i, 0))] * 4,
        out_shape=[jax.ShapeDtypeStruct((rows, width), BF)] * 4,
        compiler_params=params(),
        cost_estimate=cost(0, 12 * rows * width),
        name="add_steps",
    )(*args)


def add_last_kernel(kept_a, got_a, kept_b, got_b, out):
    rows = kept_a.shape[0]
    out[:rows, :] = (kept_a[...].astype(F32) + got_a[...].astype(F32)).astype(BF)
    out[rows:, :] = (kept_b[...].astype(F32) + got_b[...].astype(F32)).astype(BF)


def add_last(kept_a, got_a, kept_b, got_b):
    rows, width = kept_a.shape
    shape = (2 * rows, width)
    return pl.pallas_call(
        add_last_kernel,
        grid=(1,),
        in_specs=[whole((rows, width))] * 4,
        out_specs=whole(shape),
        out_shape=jax.ShapeDtypeStruct(shape, BF),
        compiler_params=params(),
        cost_estimate=cost(0, 12 * rows * width),
        name="add_last",
    )(kept_a, got_a, kept_b, got_b)


def unpack_expand_kernel(blocks, wide, thin, small, *, depth):
    count = blocks.shape[0]
    shard = wide.shape[0]
    block = wide.shape[1] // count
    piece, own = block // depth, thin.shape[1] // count
    for g in range(count):
        for z in range(depth):
            at = (z * count + g) * piece
            wide[:, at : at + piece] = blocks[g, :shard, z * piece : (z + 1) * piece].astype(F32)
        thin[:, g * own : (g + 1) * own] = blocks[g, :shard, block:].astype(F32)
        small[g : g + 1, :] = blocks[g, shard : shard + EXTRA, : small.shape[1]].astype(F32)[0:1]


def unpack_expand(blocks, depth, hidden, width, share):
    shard = blocks.shape[1] - EXTRA
    shapes = [(shard, hidden), (shard, width), (blocks.shape[0], share)]
    return pl.pallas_call(
        functools.partial(unpack_expand_kernel, depth=depth),
        grid=(1,),
        in_specs=[whole(blocks.shape)],
        out_specs=[whole(v) for v in shapes],
        out_shape=[jax.ShapeDtypeStruct(v, F32) for v in shapes],
        compiler_params=params(),
        cost_estimate=cost(0, 6 * shard * (hidden + width)),
        name="unpack_expand",
    )(blocks)


def unpack_reduce_kernel(me, *refs):
    out = refs[-1]
    rows = refs[0].shape[0]
    for n, k in enumerate(plane_list(len(refs) - 1)):
        out[pl.ds(pl.multiple_of((me[0] ^ k) * rows, rows), rows), :] = refs[n][...].astype(F32)


def unpack_reduce(me, blocks):
    rows, width = blocks[0].shape
    shape = (rows * len(blocks), width)
    return pl.pallas_call(
        unpack_reduce_kernel,
        grid=(1,),
        in_specs=[pl.BlockSpec(memory_space=pltpu.SMEM)] + [whole(v.shape) for v in blocks],
        out_specs=whole(shape),
        out_shape=jax.ShapeDtypeStruct(shape, F32),
        compiler_params=params(),
        cost_estimate=cost(0, 6 * shape[0] * width),
        name="unpack_reduce",
    )(me, *blocks)


def input_part_kernel(grads, weight, *refs, with_away):
    got = dot_nn(grads[...], weight[...])
    if with_away:
        got = got + refs[0][...].astype(F32)
        outs = refs[1:]
    else:
        outs = refs
    rows = outs[0].shape[0]
    for i, out in enumerate(outs):
        out[...] = got[i * rows : (i + 1) * rows].astype(BF)


def input_part(grads, weight, half, away=None, pieces=1):
    count, line = grads.shape
    rows, width = count // 2, weight.shape[1]
    more = () if away is None else (away,)
    shape = (rows // pieces, width)
    got = pl.pallas_call(
        functools.partial(input_part_kernel, with_away=away is not None),
        grid=(1,),
        in_specs=[pl.BlockSpec((rows, line), lambda i: (half, 0)), whole(weight.shape)] + [whole(v.shape) for v in more],
        out_specs=[whole(shape)] * pieces,
        out_shape=[jax.ShapeDtypeStruct(shape, BF)] * pieces,
        compiler_params=params(),
        cost_estimate=cost(2 * rows * width * line, 4 * rows * width),
        name="input_part",
    )(grads, weight, *more)
    return got if pieces > 1 else got[0]


def input_kernel(before, *refs):
    out = refs[-1]
    rows = refs[0].shape[0]
    half = len(refs) // 2
    for s in range(2):
        total = before[s * rows : (s + 1) * rows, :]
        for ref in refs[s * half : (s + 1) * half]:
            total = total + ref[...].astype(F32)
        out[s] = total


def input_sum(before, first, second):
    rows, width = first[0].shape
    return pl.pallas_call(
        input_kernel,
        grid=(1,),
        in_specs=[whole(before.shape)] + [whole(v.shape) for v in (*first, *second)],
        out_specs=whole((2, rows, width)),
        out_shape=jax.ShapeDtypeStruct((2, rows, width), F32),
        compiler_params=params(),
        cost_estimate=cost(0, 32 * rows * width),
        name="input_sum",
    )(before, *first, *second)


def unpack_heads_kernel(me, *refs):
    outs, bias = refs[-4:-1], refs[-1]
    count = len(refs) - 4
    shard, width = outs[0].shape
    own = width // count
    bias[...] = jnp.zeros_like(bias)
    for n, k in enumerate(plane_list(count)):
        where = pl.ds(pl.multiple_of((me[0] ^ k) * own, own), own)
        tail = refs[n][shard : shard + 16, :].astype(F32)
        for t in range(3):
            at = slice(t * own, (t + 1) * own)
            outs[t][:, where] = refs[n][:shard, at].astype(F32)
            bias[t : t + 1, where] = tail[0:1, at] + tail[1:2, at]


def unpack_heads(me, blocks, shard, width):
    shapes = [(shard, width)] * 3 + [(8, width)]
    return pl.pallas_call(
        unpack_heads_kernel,
        grid=(1,),
        in_specs=[pl.BlockSpec(memory_space=pltpu.SMEM)] + [whole(v.shape) for v in blocks],
        out_specs=[whole(v) for v in shapes],
        out_shape=[jax.ShapeDtypeStruct(v, F32) for v in shapes],
        compiler_params=params(),
        cost_estimate=cost(0, 18 * shard * width),
        name="unpack_heads",
    )(me, *blocks)


def heads_gradient_kernel(*refs, blocks, last):
    grads = refs[blocks]
    if last:
        before, sums_before, out, tokens, turned = refs[blocks + 1 :]
    else:
        out, sums, tokens = refs[blocks + 1 :]
    rows = grads.shape[0] // blocks
    for i, ref in enumerate(refs[:blocks]):
        tokens[i * rows : (i + 1) * rows, :] = ref[:rows, :]
    total = dot_tn(grads[...], tokens[...])
    column = jnp.sum(grads[...].astype(F32), axis=0, keepdims=True)
    if not last:
        out[...] = total
        sums[...] = jnp.broadcast_to(column, sums.shape)
        return
    turned[...] = (total + before[...]).T.astype(BF)
    column = jnp.broadcast_to(column + sums_before[0:1, :], (EXTRA, column.shape[1]))
    first = column.astype(BF).astype(F32)
    place = lax.broadcasted_iota(jnp.int32, (EXTRA, 1), 0)
    extra = jnp.where(place == 0, first, jnp.where(place == 1, column - first, 0.0)).astype(BF)
    depth = out.shape[0]
    shard = turned.shape[0] // depth
    for j in range(depth):
        out[j, :shard, :] = turned[j * shard : (j + 1) * shard, :]
        out[j, shard:, :] = extra


def heads_gradient(blocks, grads, more=None, depth=1):
    line = grads.shape[1]
    width = blocks[0].shape[1]
    last = more is not None
    args = (*blocks, grads) + (more or ())
    specs = [whole(v.shape) for v in (*blocks, grads)]
    scratch = [pltpu.VMEM((grads.shape[0], width), BF)]
    if last:
        shapes = [jax.ShapeDtypeStruct((depth, width // depth + EXTRA, line), BF)]
        specs += [whole(v.shape) for v in more]
        scratch.append(pltpu.VMEM((width, line), BF))
    else:
        shapes = [jax.ShapeDtypeStruct((line, width), F32), jax.ShapeDtypeStruct((8, line), F32)]
    return pl.pallas_call(
        functools.partial(heads_gradient_kernel, blocks=len(blocks), last=last),
        grid=(1,),
        in_specs=specs,
        out_specs=[whole(v.shape) for v in shapes],
        out_shape=shapes,
        scratch_shapes=scratch,
        compiler_params=params(),
        cost_estimate=cost(2 * grads.shape[0] * width * line, 2 * grads.shape[0] * width + 6 * width * line),
        name="heads_gradient",
    )(*args)


def normalize(values, gain, shift):
    mean = jnp.mean(values, axis=-1, keepdims=True)
    centred = values - mean
    inverse = lax.rsqrt(jnp.mean(centred * centred, axis=-1, keepdims=True) + EPS)
    normed = centred * inverse
    return normed * gain + shift, normed, inverse


def normalize_back(grad, normed, inverse, gain):
    scaled = grad * gain
    inner = (
        scaled
        - jnp.mean(scaled, axis=-1, keepdims=True)
        - normed * jnp.mean(scaled * normed, axis=-1, keepdims=True)
    )
    return inner * inverse, jnp.sum(grad * normed, axis=0), jnp.sum(grad, axis=0)


def column_sums(values):
    return jnp.sum(values.astype(F32), axis=0)


def plain_body(
    tokens,
    segments,
    query_weight,
    query_bias,
    key_weight,
    value_weight,
    value_bias,
    output_weight,
    output_bias,
    first_gain,
    first_shift,
    expand_weight,
    expand_bias,
    reduce_weight,
    reduce_bias,
    second_gain,
    second_shift,
    cotangent,
):
    batch, rows, width = tokens.shape
    count, depth = lax.axis_size("ctx"), lax.axis_size("fsdp")
    me, my_shard = lax.axis_index("ctx"), lax.axis_index("fsdp")
    shard = query_weight.shape[0]
    hidden = expand_weight.shape[1]
    own_width = width // count
    heads = own_width // HEAD
    piece = hidden // depth // count
    block = depth * piece
    half = hidden // 2
    order = plane_order()
    evens = order[: count // 2]
    scale = HEAD**-0.5
    bits = (count * rows - 1).bit_length()

    columns = lambda w: lax.dynamic_slice_in_dim(w, me * own_width, own_width, 1).astype(BF)
    names = (query_bias, value_bias, output_bias, first_gain, first_shift, reduce_bias, second_gain, second_shift)
    packed = jnp.concatenate(names + (expand_bias,))
    terms = jnp.concatenate(in_terms(packed, 3))
    line = 3 * own_width
    lines = -(-terms.shape[0] // (16 * line)) * 16
    terms = jnp.pad(terms, (0, lines * line - terms.shape[0])).reshape(lines, line)
    own_heads = jnp.concatenate([columns(query_weight), columns(key_weight), columns(value_weight)], axis=1)
    own_heads = gather_shards(jnp.concatenate([own_heads, terms], axis=0))
    packed = own_heads[:, shard:].reshape(depth, lines * line)[:, : 3 * packed.shape[0]]
    packed = jnp.sum(packed.reshape(depth, 3, -1).astype(F32), axis=1)
    own_heads = own_heads[:, :shard].reshape(width, line)
    (bias_query, bias_value, bias_output, gain_first, shift_first, bias_reduce, gain_second, shift_second) = (
        packed[:, i * shard : (i + 1) * shard].reshape(width) for i in range(len(names))
    )
    wide_bias = packed[:, len(names) * shard :].reshape(depth, count, piece)
    bias_halves = [
        jnp.stack([lax.dynamic_index_in_dim(wide_bias, me ^ k, 1, keepdims=False) for k in ks], axis=1).reshape(half)
        for ks in (evens, order[count // 2 :])
    ]
    own_part = lambda v: lax.dynamic_slice_in_dim(v, me * own_width, own_width, 0)
    head_bias = jnp.concatenate([own_part(bias_query), jnp.zeros((own_width,), F32), own_part(bias_value)])
    head_scale = jnp.concatenate([jnp.full((own_width,), scale * LOG2E, F32), jnp.ones((2 * own_width,), F32)])

    thin = shard // count
    folds = width // block
    strip = lax.dynamic_slice_in_dim(output_weight, me * thin, thin, 0).astype(BF)
    strip = jnp.concatenate([strip[:, i * block : (i + 1) * block] for i in range(folds)], axis=0)
    block_expand = lax.dynamic_slice_in_dim(expand_weight.reshape(shard, depth, count * piece), me * piece, piece, 2)
    block_expand = jnp.concatenate([block_expand.reshape(shard, block).astype(BF), strip], axis=0)
    block_expand = lax.all_gather(block_expand, "fsdp", axis=0)
    block_reduce = lax.dynamic_slice_in_dim(reduce_weight, me * piece, piece, 0).astype(BF)
    block_reduce = lax.all_gather(block_reduce, "fsdp", axis=0)

    groups = jnp.stack([w.reshape(shard, count, own_width) for w in (query_weight, key_weight, value_weight)], axis=2)
    half_heads = jnp.concatenate(
        [lax.dynamic_index_in_dim(groups, me ^ k, 1, keepdims=False).reshape(shard, line).astype(BF) for k in evens],
        axis=1,
    )
    half_heads = lax.all_gather(half_heads, "fsdp", axis=0, tiled=True)
    other_heads = peer(half_heads, 1)

    seg = segments
    for b in range(count.bit_length() - 1):
        seg = jnp.concatenate([seg, peer(seg, 1 << b)], axis=1)
    seg = seg.reshape(batch, count, rows)
    seg = jnp.concatenate([seg[:, k] for k in order], axis=1)

    lanes = lambda v: v if own_width == LANES else jnp.pad(v, ((0, 0), (0, LANES - own_width)))
    kept, context_parts = [], []
    for s in range(batch):
        even = jnp.concatenate(gather_even(tokens[s].astype(BF), s % 2 == 0), axis=0)
        odd = peer(even, 1)
        qkv = jnp.concatenate([dot_nn(even, own_heads), dot_nn(odd, own_heads)], axis=0)
        qkv = ((qkv + head_bias) * head_scale).astype(BF)
        if own_width != LANES:
            qkv = jnp.concatenate([lanes(qkv[:, i * own_width : (i + 1) * own_width]) for i in range(3)], axis=1)
        mask_q, mask_k = mask_columns(seg[s], bits)
        out, lse = attend(qkv, mask_q, mask_k, heads, rows)
        kept.append((even, odd, qkv, mask_q, mask_k, out, lse))
        context_parts.append(by_owner(heads_to_rows(out[:, :own_width]), 1))

    got_expand = gather_even(block_expand, True)
    got_expand += [peer(v, 1) for v in got_expand]
    got_reduce = gather_even(block_reduce, False)
    got_reduce += [peer(v, 1) for v in got_reduce]
    full_output = by_owner(
        [
            jnp.concatenate([v[:, shard + i * thin : shard + (i + 1) * thin] for i in range(folds)], axis=2)
            for v in got_expand
        ],
        1,
    ).reshape(width, width)
    middle = count // 2
    expand_halves = [
        jnp.concatenate([v[:, :shard].reshape(width, depth, piece) for v in vs], axis=2).reshape(width, half)
        for vs in (got_expand[:middle], got_expand[middle:])
    ]
    reduce_halves = [
        jnp.concatenate(vs, axis=1).reshape(half, width) for vs in (got_reduce[:middle], got_reduce[middle:])
    ]

    firsts = []
    for s in range(batch):
        branch = dot_nn(context_parts[s], full_output) + bias_output
        firsts.append(normalize(tokens[s] + branch, gain_first, shift_first))
    hidden_in, normed_first, inverse_first = (jnp.concatenate(v, axis=0) for v in zip(*firsts))
    context_low = jnp.concatenate(context_parts, axis=0)
    hidden_low = hidden_in.astype(BF)
    halves = []
    reduced = bias_reduce
    for weight, back, bias in zip(expand_halves, reduce_halves, bias_halves):
        expand = dot_nn(hidden_low, weight) + bias
        cdf = 0.5 * (1.0 + lax.erf(expand * SQRT_HALF))
        active = (expand * cdf).astype(BF)
        slope = cdf + expand * DENSITY * jnp.exp(-0.5 * expand * expand)
        reduced = reduced + dot_nn(active, back)
        halves.append((weight, back, active, slope.astype(BF)))
    result, normed_second, inverse_second = normalize(hidden_in + reduced, gain_second, shift_second)

    grad_out = cotangent.reshape(batch * rows, width)
    grad_sum_second, grad_gain_second, grad_shift_second = normalize_back(
        grad_out, normed_second, inverse_second, gain_second
    )
    grad_reduced = grad_sum_second.astype(BF)
    grad_bias_reduce = column_sums(grad_reduced)

    def chip_sum(make):
        got = peer(make(1).astype(BF), 1)
        return (make(0) + got.astype(F32)).astype(BF)

    sum_reduce = chip_sum(lambda i: dot_tn(halves[i][2], grad_reduced))
    sum_reduce = lax.psum_scatter(sum_reduce, "fsdp", scatter_dimension=0, tiled=True)
    sum_reduce = reduce_even(jnp.split(sum_reduce, middle, axis=0), False)

    grad_hidden = grad_sum_second
    grad_expands = []
    for weight, back, active, slope in halves:
        grad_expand = (dot_nt(grad_reduced, back) * slope.astype(F32)).astype(BF)
        grad_hidden = grad_hidden + dot_nt(grad_expand, weight)
        grad_expands.append(grad_expand)
    grad_bias_expand = [column_sums(g).reshape(depth, middle, piece) for g in grad_expands]
    grad_pre, grad_gain_first, grad_shift_first = normalize_back(
        grad_hidden, normed_first, inverse_first, gain_first
    )
    grad_branch = grad_pre.astype(BF)
    grad_bias_output = column_sums(grad_branch)
    grad_context = dot_nt(grad_branch, full_output).astype(BF)

    sum_expand = chip_sum(lambda i: dot_tn(hidden_low, grad_expands[i])).reshape(width, depth, middle, piece)
    sum_expand = reduce_even([sum_expand[:, :, i].reshape(width, block) for i in range(middle)], True)
    branch_blocks = jnp.concatenate(
        [lax.dynamic_slice_in_dim(grad_branch, (me ^ k) * own_width, own_width, 1) for k in order], axis=1
    )
    sum_output = chip_sum(
        lambda i: dot_tn(context_low, branch_blocks[:, i * width // 2 : (i + 1) * width // 2])
    )
    sum_output = reduce_even(jnp.split(sum_output, middle, axis=1), False)
    sum_expand = jnp.concatenate([sum_expand, sum_output], axis=1)
    sum_expand = lax.psum_scatter(sum_expand, "fsdp", scatter_dimension=0, tiled=True)

    grads = []
    for s in range(batch):
        even, odd, qkv, mask_q, mask_k, out, lse = kept[s]
        dc = lanes(rows_to_heads(grad_context[s * rows : (s + 1) * rows], own_width))
        got = attend_back(qkv, mask_q, mask_k, dc, out, lse, heads, rows)
        if own_width != LANES:
            got = jnp.concatenate([got[:, i * LANES : i * LANES + own_width] for i in range(3)], axis=1)
        grads.append(got)
    middle_row = count * rows // 2
    grad_heads = sum(
        dot_tn(kept[s][0], grads[s][:middle_row]) + dot_tn(kept[s][1], grads[s][middle_row:]) for s in range(batch)
    ).astype(BF)
    grad_head_bias = jnp.pad(
        jnp.stack(in_terms(sum(column_sums(g) for g in grads), 2)), ((0, 14), (0, 0))
    )
    home_heads = jnp.concatenate(
        [grad_heads.reshape(depth, shard, line), jnp.broadcast_to(grad_head_bias, (depth, 16, line))], axis=1
    )
    home_heads = reduce_shards(home_heads)
    home_heads = jnp.concatenate(
        [home_heads[:shard].astype(BF)]
        + [v[None] for v in in_terms(home_heads[shard] + home_heads[shard + 1], 2)]
        + [jnp.zeros((14, line), BF)],
        axis=0,
    )
    back_rows = [heads_to_rows(g) for g in grads]
    back_even = jnp.concatenate([jnp.concatenate(r[:middle], axis=1) for r in back_rows], axis=0)
    back_odd = jnp.concatenate([jnp.concatenate(r[middle:], axis=1) for r in back_rows], axis=0)
    grad_in = grad_pre + dot_nt(back_even, half_heads) + dot_nt(back_odd, other_heads)

    def spread(value, low_first):
        got = gather_even(value, low_first)
        odd = peer(jnp.stack(got), 1)
        return by_owner([v[None] for v in got] + [odd[i : i + 1] for i in range(middle)], 0)

    wide = lax.all_gather(sum_expand, "ctx", axis=0)
    grad_expand_weight = jnp.transpose(wide[:, :, :block].reshape(count, shard, depth, piece), (1, 2, 0, 3))
    grad_expand_weight = grad_expand_weight.reshape(shard, hidden).astype(F32)
    grad_output_weight = jnp.transpose(wide[:, :, block:], (1, 0, 2)).reshape(shard, width).astype(F32)
    grad_reduce_weight = lax.all_gather(sum_reduce, "ctx", axis=0, tiled=True).astype(F32)
    wide_heads = spread(home_heads, True)
    wide_shards = jnp.transpose(wide_heads[:, :shard].reshape(count, shard, 3, own_width), (2, 1, 0, 3))
    grad_query_weight, grad_key_weight, grad_value_weight = (
        wide_shards[i].reshape(shard, width).astype(F32) for i in range(3)
    )
    wide_biases = jnp.sum(wide_heads[:, shard : shard + 2].astype(F32), axis=1).reshape(count, 3, own_width)
    own_shard = lambda v: lax.dynamic_slice_in_dim(v.reshape(width), my_shard * shard, shard, 0)

    vectors = (
        grad_bias_output,
        grad_gain_first,
        grad_shift_first,
        grad_bias_reduce,
        grad_gain_second,
        grad_shift_second,
    )
    wide_bias = by_owner([g[:, i] for g in grad_bias_expand for i in range(middle)], 1)
    small = jnp.concatenate([v.reshape(depth, shard) for v in vectors] + [wide_bias], axis=1)
    for b in range(count.bit_length() - 1):
        small = small + peer(small, 1 << b)
    small = reduce_shards(small)
    vec = [small[i * shard : (i + 1) * shard] for i in range(len(vectors))]
    vec_expand = small[len(vectors) * shard :]
    return (
        result.reshape(batch, rows, width),
        grad_in.reshape(batch, rows, width),
        grad_query_weight,
        own_shard(wide_biases[:, 0]),
        grad_key_weight,
        grad_value_weight,
        own_shard(wide_biases[:, 2]),
        grad_output_weight,
        vec[0],
        vec[1],
        vec[2],
        grad_expand_weight,
        vec_expand,
        grad_reduce_weight,
        vec[3],
        vec[4],
        vec[5],
    )


def even_pieces(own, other):
    rows = own.shape[0]
    both = jnp.concatenate([own, other], axis=1)
    middle = lax.axis_size("ctx") // 2
    rows = rows // middle
    pieces = [both[i * rows : (i + 1) * rows] for i in range(middle)]
    return [pieces[0]] + [peer(pieces[i], 2 * i) for i in range(1, middle)]


def body(
    tokens,
    segments,
    query_weight,
    query_bias,
    key_weight,
    value_weight,
    value_bias,
    output_weight,
    output_bias,
    first_gain,
    first_shift,
    expand_weight,
    expand_bias,
    reduce_weight,
    reduce_bias,
    second_gain,
    second_shift,
    cotangent,
):
    batch, rows, width = tokens.shape
    count, depth = lax.axis_size("ctx"), lax.axis_size("fsdp")
    me, my_shard = lax.axis_index("ctx"), lax.axis_index("fsdp")
    me_array = me.astype(jnp.int32).reshape(1)
    shard = query_weight.shape[0]
    hidden = expand_weight.shape[1]
    own_width = width // count
    heads = own_width // HEAD
    piece = hidden // depth // count
    block = depth * piece
    middle = count // 2
    order = plane_order()
    evens, odds = order[:middle], order[middle:]
    scale = HEAD**-0.5
    bits = (count * rows - 1).bit_length()
    all_rows = batch * rows

    columns = lambda w: lax.dynamic_slice_in_dim(w, me * own_width, own_width, 1).astype(BF)
    names = (query_bias, value_bias, output_bias, first_gain, first_shift, reduce_bias, second_gain, second_shift)
    packed = jnp.concatenate(names + (expand_bias,))
    size = packed.shape[0]
    terms = jnp.concatenate(in_terms(packed, 3))
    line = 3 * own_width
    lines = -(-terms.shape[0] // (16 * line)) * 16
    terms = jnp.pad(terms, (0, lines * line - terms.shape[0])).reshape(lines, line)
    own_heads = jnp.concatenate([columns(query_weight), columns(key_weight), columns(value_weight)], axis=1)
    shard_parts = gather_doubling(jnp.concatenate([own_heads, terms], axis=0))

    def plane(value, *needed):
        first, second = after((peer(value, 2), peer(value, 4)), *needed)
        part = value.shape[0] // 2
        return first, second, (peer(first[:part], 4), peer(second[part:], 2))

    def chip(blocks):
        return blocks + [jax.tree.map(lambda v: peer(v, 1), b) for b in blocks]

    def direct(value):
        return [value] + [peer(value, k) for k in evens[1:]]

    low_in = []
    for s in range(batch):
        numbers = jnp.concatenate([segments[s] // 64, segments[s] % 64]).astype(BF)
        numbers = jnp.pad(numbers[None], ((0, EXTRA - 1), (0, width - 2 * rows)))
        low_in.append(jnp.concatenate([tokens[s].astype(BF), numbers], axis=0))

    reduce_blocks = [lax.dynamic_slice_in_dim(reduce_weight, (me ^ k) * piece, piece, 0).astype(BF) for k in evens]
    reduce_blocks = jnp.stack(reduce_blocks)

    first_got, shard_parts, low_in, reduce_blocks = join(direct(low_in[0]), shard_parts, low_in, reduce_blocks)
    first_blocks = chip(first_got)
    own_heads = by_owner([shard_parts[j : j + 1] for j in range(depth)], 0, list(range(depth)), "fsdp")
    packed = own_heads[:, shard:].reshape(depth, lines * line)[:, : 3 * size]
    packed = jnp.sum(packed.reshape(depth, 3, -1).astype(F32), axis=1)
    own_heads = own_heads[:, :shard].reshape(width, line)
    (bias_query, bias_value, bias_output, gain_first, shift_first, bias_reduce, gain_second, shift_second) = (
        packed[:, i * shard : (i + 1) * shard].reshape(width) for i in range(len(names))
    )
    wide_bias = packed[:, len(names) * shard :].reshape(depth, count, piece)
    bias_halves = [
        jnp.stack([lax.dynamic_index_in_dim(wide_bias, me ^ k, 1, keepdims=False).reshape(1, block) for k in ks])
        for ks in (evens, odds)
    ]
    own_part = lambda v: lax.dynamic_slice_in_dim(v, me * own_width, own_width, 0)
    head_bias = jnp.concatenate([own_part(bias_query), jnp.zeros((own_width,), F32), own_part(bias_value)])
    head_scale = jnp.concatenate([jnp.full((own_width,), scale * LOG2E, F32), jnp.ones((2 * own_width,), F32)])

    thin = shard // count
    folds = width // block
    strip = lax.dynamic_slice_in_dim(output_weight, me * thin, thin, 0).astype(BF)
    strip = jnp.concatenate([strip[:, i * block : (i + 1) * block] for i in range(folds)], axis=0)
    block_expand = [
        lax.dynamic_slice_in_dim(expand_weight, (z * count + me) * piece, piece, 1).astype(BF) for z in range(depth)
    ]
    block_expand = jnp.concatenate([jnp.concatenate(block_expand, axis=1), strip], axis=0)
    block_expand = lax.all_gather(after(block_expand, first_got[1]), "fsdp", axis=0)

    halfway = count * rows // 2
    heads_across = own_heads.T
    first_qkv, *first_masks = project(first_blocks, rows, own_heads, head_bias, head_scale, bits)
    first_out, first_lse, second_got = join(
        *attend(first_qkv, *first_masks, heads, rows), direct(low_in[1])
    )
    second_blocks = chip(second_got)
    (second_qkv, *second_masks), other_out = join(
        project(second_blocks, rows, own_heads, head_bias, head_scale, bits), peer(first_out[halfway:], 1)
    )

    reduce_own = lax.all_gather(after(reduce_blocks, second_got[1]), "fsdp", axis=0)
    second_out, second_lse, first_pieces, near = join(
        *attend(second_qkv, *second_masks, heads, rows),
        even_pieces(first_out[:halfway], other_out),
        (block_expand, peer(block_expand, 2), peer(block_expand, 4)),
    )
    part = depth // 2
    far = peer(near[1][:part], 4), peer(near[2][part:], 2)
    far, other_out, near_other = join(far, peer(second_out[halfway:], 1), [peer(v, 1) for v in near])
    got_expand = [*((v,) for v in near), far, *((v,) for v in near_other), tuple(peer(v, 1) for v in far)]
    full_output = assemble_output(got_expand, shard, thin, me_array)
    second_pieces = even_pieces(second_out[:halfway], other_out)
    kept = [
        (first_blocks, first_qkv, *first_masks, first_out, first_lse),
        (second_blocks, second_qkv, *second_masks, second_out, second_lse),
    ]

    earlier = None
    for s, pieces in enumerate((first_pieces, second_pieces)):
        earlier = branch(s, me_array, pieces, full_output, tokens, bias_output, gain_first, shift_first, earlier)
    context_low, hidden_in, hidden_low, normed_first, inverse_first = (
        v.reshape(all_rows, v.shape[2]) for v in earlier
    )

    hidden_low, reduce_own = join(hidden_low, reduce_own)
    (
        (act_even, act_odd, de_even, de_odd, sums_even, sums_odd, result, dr, grad_pre, da, sums_second, sums_first),
        other_low,
        other_context,
    ) = join(
        feed(
            hidden_low,
            inverse_first,
            bias_halves,
            bias_reduce,
            gain_second,
            shift_second,
            gain_first,
            hidden_in,
            cotangent.reshape(all_rows, width),
            normed_first,
            [reduce_own, peer(reduce_own, 1)],
            got_expand,
            shard,
        ),
        peer(hidden_low, 1),
        peer(context_low, 1),
    )

    vectors = (sums_first[2], sums_first[0], sums_first[1], sums_second[2], sums_second[0], sums_second[1])
    wide_bias = by_owner(
        [sums[i, 0].reshape(depth, 1, piece) for sums in (sums_even, sums_odd) for i in range(middle)], 1
    ).reshape(depth, hidden // depth)
    small = jnp.concatenate([v.reshape(depth, shard) for v in vectors] + [wide_bias], axis=1)
    share = -(-small.shape[1] // (count * LANES)) * LANES
    small = jnp.pad(small, ((0, 0), (0, share * count - small.shape[1])))
    da, de_even, de_odd, act_even, dr, small, own_grads, other_grads, other_act, other_dr = join(
        da,
        de_even,
        de_odd,
        act_even,
        dr,
        small,
        *context_back(me_array, da, full_output, own_width, middle),
        peer(act_odd, 1),
        peer(dr, 1),
    )

    sum_reduce, de_even, da, small, other_grads, other_de, other_da, other_small = join(
        reduce_gradient(act_even, other_act, dr, other_dr, depth, piece),
        de_even,
        da,
        small,
        peer(other_grads, 1),
        peer(de_odd, 1),
        peer(da, 1),
        peer(small, 1),
    )
    sum_reduce = lax.psum_scatter(sum_reduce, "fsdp", scatter_dimension=0, tiled=False)

    sums, dc = join(
        expand_gradient(
            me_array,
            hidden_low,
            other_low,
            context_low,
            other_context,
            de_even,
            other_de,
            da,
            other_da,
            small + other_small,
            own_width,
        ),
        even_pieces(own_grads, other_grads),
    )
    kept_a, sent_a, kept_b, sent_b = sums

    add = lambda a, b: (a.astype(F32) + b.astype(F32)).astype(BF)
    to_owner = lambda parts, count=middle: [parts[0]] + [peer(parts[i], 2 * i) for i in range(1, count)]

    def back(s, dc, part=None, before=None):
        _, qkv, mask_q, mask_k, out, lse = kept[s]
        return attend_back(qkv, mask_q, mask_k, dc, out, lse, heads, rows, part, before, s)

    first_grads = back(0, dc)
    first_grads, odd, got_a, got_b = join(
        first_grads, input_part(first_grads, heads_across, 1), peer(sent_a, 4), peer(sent_b, 2)
    )
    kept_a, sent_a, kept_b, sent_b = add_steps(kept_a, got_a, kept_b, got_b)
    home, before, got_a, got_b, dc, sum_reduce = join(
        input_part(first_grads, heads_across, 0, peer(odd, 1), middle),
        heads_gradient(kept[0][0], first_grads),
        peer(sent_a, 2),
        peer(sent_b, 4),
        dc,
        sum_reduce,
    )
    sum_expand, dc = join(add_last(kept_a, got_a, kept_b, got_b), dc)
    sum_expand = lax.psum_scatter(sum_expand, "fsdp", scatter_dimension=0, tiled=True)
    upper, got_reduce, last_step, home = join(
        back(1, dc, 0), to_owner(sum_reduce), peer(home[-1], 2 * (middle - 1)), home[:-1]
    )
    sum_reduce = sum(v.astype(F32) for v in got_reduce).astype(BF)
    upper, sum_reduce = join(upper, sum_reduce)
    second_grads, from_first, sum_reduce = join(
        back(1, dc, 1, upper),
        to_owner(home, middle - 1) + [last_step],
        sum_reduce,
    )

    wide_expand = lax.all_gather(after(sum_expand, second_grads), "ctx", axis=0)
    home_heads = heads_gradient(kept[1][0], second_grads, before, depth)[0]
    home_heads, second_grads = join(home_heads, second_grads)
    odd, got_reduce, second_grads = join(
        input_part(second_grads, heads_across, 1), direct(sum_reduce), second_grads
    )
    home = input_part(second_grads, heads_across, 0, peer(odd, 1), middle)
    grad_reduce_weight = unpack_reduce(me_array, chip(after(got_reduce, home[0])))
    home_heads, wide_expand = after((home_heads, wide_expand), home[0])
    home_heads = lax.psum_scatter(after(home_heads, wide_expand), "fsdp", scatter_dimension=0, tiled=False)
    from_second, from_first, home_heads, grad_reduce_weight, unpacked = join(
        to_owner(home),
        from_first,
        home_heads,
        grad_reduce_weight,
        unpack_expand(wide_expand, depth, hidden, width, share),
    )
    grad_expand_weight, grad_output_weight, small_sum = unpacked
    tail = home_heads[shard].astype(F32) + home_heads[shard + 1].astype(F32)
    home_heads = jnp.concatenate(
        [home_heads[:shard]] + [v[None] for v in in_terms(tail, 2)] + [jnp.zeros((14, line), BF)], axis=0
    )
    heads_got, grad_in = join(direct(home_heads), input_sum(grad_pre, from_first, from_second))
    heads_got = chip(heads_got)
    small_sum = small_sum.reshape(-1)
    grad_query_weight, grad_key_weight, grad_value_weight, wide_biases = unpack_heads(
        me_array, heads_got, shard, width
    )
    own_shard = lambda v: lax.dynamic_slice_in_dim(v, my_shard * shard, shard, 0)

    vec = [small_sum[i * shard : (i + 1) * shard] for i in range(len(vectors))]
    vec_expand = small_sum[len(vectors) * shard : len(vectors) * shard + hidden // depth]
    return (
        result.reshape(batch, rows, width),
        grad_in,
        grad_query_weight,
        own_shard(wide_biases[0]),
        grad_key_weight,
        grad_value_weight,
        own_shard(wide_biases[2]),
        grad_output_weight,
        vec[0],
        vec[1],
        vec[2],
        grad_expand_weight,
        vec_expand,
        grad_reduce_weight,
        vec[3],
        vec[4],
        vec[5],
    )


def solution(mesh):
    seq = P("fsdp", "ctx", None)
    mat = P("fsdp", None)
    vec = P("fsdp")
    in_specs = (
        seq,
        P("fsdp", "ctx"),
        mat,
        vec,
        mat,
        mat,
        vec,
        mat,
        vec,
        vec,
        vec,
        mat,
        vec,
        mat,
        vec,
        vec,
        vec,
        seq,
    )
    out_specs = (seq, seq, mat, vec, mat, mat, vec, mat, vec, vec, vec, mat, vec, mat, vec, vec, vec)
    count, depth = mesh.shape["ctx"], mesh.shape["fsdp"]

    def layer(*args):
        width, hidden = args[0].shape[2], args[11].shape[1]
        piece, own_width = hidden // depth // count, width // count
        tiled = count == 8 and depth == 4 and args[0].shape[0] == 2 and piece % LANES == 0 and own_width == LANES
        tiled = tiled and width // depth // count % 16 == 0
        return (body if tiled else plain_body)(*args)

    return jax.shard_map(layer, mesh=mesh, in_specs=in_specs, out_specs=out_specs, check_vma=False)
```

```python
import functools

import jax
import jax.numpy as jnp
from jax import lax
from jax.experimental import pallas as pl
from jax.experimental.pallas import tpu as pltpu
from jax.sharding import PartitionSpec as P

HEAD = 64
LANES = 128
VMEM_LIMIT = 62 << 20
COST_SHARE = 64
EPS = 1e-05
BIG = 1e30
LOG2E = 1.4426950408889634
SQRT_HALF = 0.7071067811865476
DENSITY = 0.3989422804014327
BF = jnp.bfloat16
F32 = jnp.float32


def dot_nn(left, right):
    return jnp.dot(left, right, preferred_element_type=F32)


def dot_tn(left, right):
    return lax.dot_general(left, right, (((0,), (0,)), ((), ())), preferred_element_type=F32)


def dot_nt(left, right):
    return lax.dot_general(left, right, (((1,), (1,)), ((), ())), preferred_element_type=F32)


def exchange(value, axis, k):
    count = lax.axis_size(axis)
    return lax.ppermute(value, axis, [(i, i ^ k) for i in range(count)])


def peer(value, k):
    return exchange(value, "ctx", k)


def after(value, *needed):
    return lax.optimization_barrier((value, needed))[0]


def join(*values):
    return lax.optimization_barrier(values)


def plane_list(count):
    return list(range(0, count, 2)) + list(range(1, count, 2))


def plane_order():
    return plane_list(lax.axis_size("ctx"))


def gather_even(value, low_first):
    count = lax.axis_size("ctx")
    got = {0: value}
    for k in range(2, count, 2):
        bits = [1 << b for b in range(1, count.bit_length()) if k >> b & 1]
        step = bits[-1] if low_first else bits[0]
        got[k] = peer(got[k ^ step], step)
    return [got[k] for k in range(0, count, 2)]


def by_owner(parts, axis, order=None, mesh_axis="ctx"):
    order = order or plane_order()
    stacked = jnp.stack([parts[order.index(k)] for k in range(len(order))])
    me = lax.axis_index(mesh_axis)
    return jnp.concatenate(
        [lax.dynamic_index_in_dim(stacked, me ^ g, 0, keepdims=False) for g in range(len(order))], axis=axis
    )


def rows_to_heads(value, width):
    count = lax.axis_size("ctx")
    me = lax.axis_index("ctx")
    mine, other = [], []
    for k in range(0, count, 2):
        to = me ^ k
        first = lax.dynamic_slice_in_dim(value, to * width, width, 1)
        second = lax.dynamic_slice_in_dim(value, (to ^ 1) * width, width, 1)
        got = jnp.concatenate([first, second], axis=1)
        if k:
            got = peer(got, k)
        mine.append(got[:, :width])
        other.append(got[:, width:])
    return jnp.concatenate(mine + [peer(jnp.concatenate(other, axis=0), 1)], axis=0)


def heads_to_rows(value):
    count = lax.axis_size("ctx")
    rows, width = value.shape[0] // count, value.shape[1]
    half = value.shape[0] // 2
    both = jnp.concatenate([value[:half], peer(value[half:], 1)], axis=1)
    even, odd = [], []
    for i, k in enumerate(range(0, count, 2)):
        got = both[i * rows : (i + 1) * rows]
        if k:
            got = peer(got, k)
        even.append(got[:, :width])
        odd.append(got[:, width:])
    return even + odd


def reduce_even(blocks, low_first):
    count = lax.axis_size("ctx")
    bits = [1 << b for b in range(1, count.bit_length() - 1)]
    if not low_first:
        bits = bits[::-1]
    held = dict(zip(range(0, count, 2), blocks))
    for bit in bits:
        sent = [k for k in held if k & bit]
        got = peer(jnp.stack([held[k] for k in sent]), bit)
        got = {k ^ bit: got[i] for i, k in enumerate(sent)}
        held = {k: (held[k].astype(F32) + got[k].astype(F32)).astype(BF) for k in held if not k & bit}
    return held[0]


def gather_shards(value):
    depth = lax.axis_size("fsdp")
    parts = [value[None]] + [exchange(value, "fsdp", j)[None] for j in range(1, depth)]
    return by_owner(parts, 0, list(range(depth)), "fsdp")


def reduce_shards(value):
    depth = lax.axis_size("fsdp")
    me = lax.axis_index("fsdp")
    total = lax.dynamic_index_in_dim(value, me, 0, keepdims=False).astype(F32)
    for j in range(1, depth):
        sent = lax.dynamic_index_in_dim(value, me ^ j, 0, keepdims=False)
        total = total + exchange(sent, "fsdp", j).astype(F32)
    return total


def gather_doubling(value):
    got = value[None]
    step = 1
    while step < lax.axis_size("fsdp"):
        got = jnp.concatenate([got, exchange(got, "fsdp", step)], axis=0)
        step *= 2
    return got


def in_terms(vector, count):
    terms = []
    for _ in range(count):
        terms.append(vector.astype(BF))
        vector = vector - terms[-1].astype(F32)
    return terms


def whole(shape):
    return pl.BlockSpec(shape, lambda *i: (0,) * len(shape))


def params(limit=VMEM_LIMIT):
    return pltpu.CompilerParams(vmem_limit_bytes=limit)


def cost(flops, size, exps=0):
    return pl.CostEstimate(
        flops=flops // COST_SHARE, bytes_accessed=size // COST_SHARE, transcendentals=exps // COST_SHARE
    )


def mask_columns(seg, bits):
    lane = jnp.arange(LANES) % HEAD
    bit = (seg[:, None] >> jnp.minimum(lane // 2, 30)) & 1
    flip = bit ^ (lane & 1)
    used = lane < 2 * bits
    for_query = jnp.where(used & (flip == 1), -BIG, 0.0).astype(BF)
    for_key = jnp.where(used, 1 - flip, ((lane >= 60) & (lane < 63)).astype(jnp.int32)).astype(BF)
    return for_query, for_key


def lane_index():
    return lax.broadcasted_iota(jnp.int32, (1, LANES), 1)


def merge(main, extra, h):
    lane = lane_index()
    return jnp.where((lane < HEAD) if h == 0 else (lane >= HEAD), main, extra)


def with_terms(extra, number):
    lane = lane_index() % HEAD
    first = number.astype(BF).astype(F32)
    rest = number - first
    second = rest.astype(BF).astype(F32)
    third = rest - second
    terms = jnp.where(lane == 60, first, jnp.where(lane == 61, second, third)).astype(BF)
    return jnp.where((lane >= 60) & (lane < 63), terms, extra)


def forward_kernel(q, k, v, mask_q, mask_k, out, lse, key_side, value_side, *, heads):
    lane = lane_index()

    @pl.when(pl.program_id(0) == 0)
    def _():
        for h in range(heads):
            key_side[h] = merge(k[...], mask_k[...], h)
            value_side[h] = merge(v[...], jnp.ones((1, LANES), BF), h)

    whole, whole_lse = None, None
    for h in range(heads):
        scores = dot_nt(merge(q[...], mask_q[...], h), key_side[h])
        top = jnp.max(scores, axis=1, keepdims=True)
        weights = jnp.exp2(scores - top).astype(BF)
        both = dot_nn(weights, value_side[h])
        total = pltpu.roll(both, HEAD, 1)
        context, log_total = both / total, top + jnp.log2(total)
        if whole is None:
            whole, whole_lse = context, log_total
        else:
            whole = jnp.where(lane < HEAD, whole, context)
            whole_lse = jnp.where(lane < HEAD, whole_lse, log_total)
    out[...] = whole.astype(BF)
    lse[...] = whole_lse


def attend(qkv, mask_q, mask_k, heads, block):
    count = qkv.shape[0]
    part = lambda j: pl.BlockSpec((block, LANES), lambda i: (i, j))
    full = lambda j: pl.BlockSpec((count, LANES), lambda i: (0, j))
    products = 2 * 2 * count * count * LANES * heads
    return pl.pallas_call(
        functools.partial(forward_kernel, heads=heads),
        grid=(count // block,),
        in_specs=[part(0), full(1), full(2), part(0), full(0)],
        out_specs=[part(0), part(0)],
        out_shape=[jax.ShapeDtypeStruct((count, LANES), BF), jax.ShapeDtypeStruct((count, LANES), F32)],
        scratch_shapes=[pltpu.VMEM((heads, count, LANES), BF), pltpu.VMEM((heads, count, LANES), BF)],
        compiler_params=params(),
        cost_estimate=cost(products * 2, 12 * count * LANES, count * count * heads),
        name="attend",
    )(qkv, qkv, qkv, mask_q, mask_k)


def backward_kernel(*refs, heads, first, steps, total, block, pieces):
    q, k, v, mask_q, mask_k, out, lse = refs[:7]
    parts = refs[7 : 7 + pieces]
    refs = refs[7 + pieces :]
    if first:
        grads_before, dk_before, dv_before = refs[:3]
        refs = refs[3:]
    grads = refs[0]
    if steps < total:
        dk_t, dv_t = refs[1:3]
        key_side, value_side, dc_all = refs[3:]
    else:
        key_side, value_side, dc_all, dk_t, dv_t = refs[1:]
    lane = lane_index()
    step = pl.program_id(0)

    @pl.when(step == 0)
    def _():
        ones = ((lane % HEAD >= 60) & (lane % HEAD < 63)).astype(F32).astype(BF)
        for h in range(heads):
            key_side[h] = merge(k[...], mask_k[...], h)
            value_side[h] = merge(v[...], ones, h)
        if first:
            dk_t[...] = dk_before[...]
            dv_t[...] = dv_before[...]
            grads[: first * block, :LANES] = grads_before[...]
        else:
            dk_t[...] = jnp.zeros_like(dk_t)
            dv_t[...] = jnp.zeros_like(dv_t)
        if pieces == 1:
            dc_all[...] = parts[0][...]
        else:
            for i in range(pieces):
                dc_all[i * block : (i + 1) * block, :] = parts[i][:, :LANES]
                dc_all[(pieces + i) * block : (pieces + i + 1) * block, :] = parts[i][:, LANES:]

    dc = dc_all.at[pl.ds(pl.multiple_of((first + step) * block, block), block), :]
    product = dc[...].astype(F32) * out[...].astype(F32)
    low = jnp.sum(jnp.where(lane < HEAD, product, 0.0), axis=1, keepdims=True)
    high = jnp.sum(jnp.where(lane < HEAD, 0.0, product), axis=1, keepdims=True)
    query_extra = with_terms(mask_q[...], -pltpu.roll(lse[...], HEAD, 1))
    grad_extra = with_terms(jnp.zeros((1, LANES), BF), jnp.where(lane < HEAD, -high, -low))
    q_t, dc_t = q[...].T, dc[...].T
    dq = None
    for h in range(heads):
        probs = jnp.exp2(dot_nt(merge(q[...], query_extra, h), key_side[h]))
        centred = dot_nt(merge(dc[...], grad_extra, h), value_side[h])
        ds = (probs * centred).astype(BF)
        part = dot_nn(ds, key_side[h])
        dq = part if dq is None else jnp.where(lane < HEAD, dq, part)
        own = slice(HEAD * h, HEAD * h + HEAD)
        dk_t[own, :] += dot_nn(q_t[own, :], ds)
        dv_t[own, :] += dot_nn(dc_t[own, :], probs.astype(BF))
    at = step * block if steps < total else (first + step) * block
    grads[pl.ds(pl.multiple_of(at, block), block), :LANES] = (dq.astype(BF).astype(F32) * HEAD**-0.5).astype(BF)
    if steps == total:

        @pl.when(step == steps - first - 1)
        def _():
            grads[:, LANES : 2 * LANES] = (dk_t[...] * (1.0 / LOG2E)).T.astype(BF)
            grads[:, 2 * LANES :] = dv_t[...].T.astype(BF)


def attend_back(qkv, mask_q, mask_k, dc, out, lse, heads, block, part=None, before=None, place=0):
    dc = dc if isinstance(dc, list) else [dc]
    count = qkv.shape[0]
    total = count // block
    first = total // 2 if part == 1 else 0
    steps = total // 2 if part == 0 else total
    piece = lambda j: pl.BlockSpec((block, LANES), lambda i: (first + i, j))
    full = lambda j: pl.BlockSpec((count, LANES), lambda i: (0, j))
    products = 5 * 2 * count * count * LANES * heads
    side = (LANES, count)
    shapes = [jax.ShapeDtypeStruct((count, 3 * LANES), BF)]
    scratch = [
        pltpu.VMEM((heads, count, LANES), BF),
        pltpu.VMEM((heads, count, LANES), BF),
        pltpu.VMEM((count, LANES), BF),
    ]
    if part == 0:
        shapes = [jax.ShapeDtypeStruct((count // 2, LANES), BF)] + [jax.ShapeDtypeStruct(side, F32)] * 2
    else:
        scratch += [pltpu.VMEM(side, F32)] * 2
    before = before or []
    got = pl.pallas_call(
        functools.partial(
            backward_kernel, heads=heads, first=first, steps=steps, total=total, block=block, pieces=len(dc)
        ),
        grid=(steps - first,),
        in_specs=[piece(0), full(1), full(2), piece(0), full(0), piece(0), piece(0)]
        + [pl.BlockSpec((block if len(dc) > 1 else count, v.shape[1]), lambda i: (place, 0)) for v in dc]
        + [whole(v.shape) for v in before],
        out_specs=[whole(v.shape) for v in shapes],
        out_shape=shapes,
        scratch_shapes=scratch,
        compiler_params=params(),
        cost_estimate=cost(products, 16 * count * LANES, count * count * heads),
        name="attend_back",
    )(qkv, qkv, qkv, mask_q, mask_k, out, lse, *dc, *before)
    return got if part == 0 else got[0]


def project_kernel(*refs, blocks, rows, bits):
    weight, bias, factor, out, mask_q, mask_k = refs[blocks:]
    lane = lane_index() % HEAD
    used = lane < 2 * bits
    fixed = ((lane >= 60) & (lane < 63)).astype(F32).astype(BF)
    for i, ref in enumerate(refs[:blocks]):
        at = slice(i * rows, (i + 1) * rows)
        got = (dot_nn(ref[:rows, :], weight[...]) + bias[...]) * factor[...]
        out[at, :] = got.astype(BF)
        parts = ref[rows : rows + 16, : 2 * rows].astype(F32)
        number = (parts[:8, :rows] * 64 + parts[:8, rows:]).T[:, :1].astype(jnp.int32)
        flip = ((number >> (lane // 2)) & 1) ^ (lane & 1)
        mask_q[at, :] = jnp.where(used & (flip == 1), -BIG, 0.0).astype(BF)
        mask_k[at, :] = jnp.where(used, (1 - flip).astype(F32).astype(BF), fixed)


def project(blocks, rows, weight, bias, factor, bits):
    width, line = weight.shape
    args = (*blocks, weight, bias[None], factor[None])
    count = rows * len(blocks)
    shapes = [(count, line), (count, LANES), (count, LANES)]
    return pl.pallas_call(
        functools.partial(project_kernel, blocks=len(blocks), rows=rows, bits=bits),
        in_specs=[whole(v.shape) for v in args],
        out_specs=[whole(v) for v in shapes],
        out_shape=[jax.ShapeDtypeStruct(v, BF) for v in shapes],
        grid=(1,),
        compiler_params=params(),
        cost_estimate=cost(2 * count * width * line, 2 * count * (width + line)),
        name="project",
    )(*args)


def flatten_blocks(blocks):
    flat, parts = [], []
    for n, block in enumerate(blocks):
        first = 0
        for part in block:
            flat.append(part)
            parts.append((n, first))
            first += part.shape[0]
    return flat, tuple(parts)


def assemble_kernel(me, *refs, parts, thin, folds):
    out = refs[-1]
    shard = len({n for n, _ in parts}) * thin
    block = refs[0].shape[2]
    order = plane_list(len({n for n, _ in parts}))
    for ref, (n, first) in zip(refs, parts):
        for z in range(ref.shape[0]):
            row = pl.multiple_of((first + z) * shard + (me[0] ^ order[n]) * thin, thin)
            for f in range(folds):
                out[pl.ds(row, thin), f * block : (f + 1) * block] = ref[z, f * thin : (f + 1) * thin, :]


def assemble_output(blocks, shard, thin, me):
    flat, parts = flatten_blocks(blocks)
    _, tall, block = flat[0].shape
    strip = tall - shard
    folds = strip // thin
    width = folds * block
    specs = [pl.BlockSpec((v.shape[0], strip, block), lambda i: (0, shard // strip, 0)) for v in flat]
    return pl.pallas_call(
        functools.partial(assemble_kernel, parts=parts, thin=thin, folds=folds),
        grid=(1,),
        in_specs=[pl.BlockSpec(memory_space=pltpu.SMEM)] + specs,
        out_specs=whole((width, width)),
        out_shape=jax.ShapeDtypeStruct((width, width), BF),
        compiler_params=params(),
        cost_estimate=cost(0, 4 * width * width),
        name="assemble_output",
    )(me, *flat)


def branch_kernel(me, *refs, pieces, aliased):
    weight, tokens, bias, gain, shift = refs[pieces : pieces + 5]
    context, hidden, low, normed, inverse = refs[pieces + 5 + aliased :]
    second = (me[0] & 1) == 1
    pair = refs[0].shape[1]
    for i in range(pieces):
        at = pl.multiple_of(((me[0] ^ (2 * i)) // 2) * pair, pair)
        got = refs[i][...]
        swapped = jnp.concatenate([got[:, pair // 2 :], got[:, : pair // 2]], axis=1)
        context[:, pl.ds(at, pair)] = jnp.where(second, swapped, got)
    total = tokens[...] + dot_nn(context[...], weight[...]) + bias[...]
    mean = jnp.mean(total, axis=1, keepdims=True)
    centred = total - mean
    scale = lax.rsqrt(jnp.mean(centred * centred, axis=1, keepdims=True) + EPS)
    unit = centred * scale
    out = unit * gain[...] + shift[...]
    hidden[...] = out
    low[...] = out.astype(BF)
    normed[...] = unit
    inverse[...] = jnp.broadcast_to(scale, inverse.shape)


def branch(s, me, pieces, weight, tokens, bias, gain, shift, earlier):
    batch, rows, width = tokens.shape
    at = pl.BlockSpec((None, rows, width), lambda i: (s, 0, 0))
    thin = pl.BlockSpec((None, rows, LANES), lambda i: (s, 0, 0))
    vec = whole((1, width))
    earlier = earlier or ()
    first = 1 + len(pieces) + 5
    full = lambda t: jax.ShapeDtypeStruct((batch, rows, width), t)
    return pl.pallas_call(
        functools.partial(branch_kernel, pieces=len(pieces), aliased=len(earlier)),
        grid=(1,),
        in_specs=[pl.BlockSpec(memory_space=pltpu.SMEM)]
        + [whole(v.shape) for v in pieces]
        + [whole(weight.shape), at, vec, vec, vec]
        + [pl.BlockSpec(memory_space=pl.ANY)] * len(earlier),
        out_specs=[at, at, at, at, thin],
        out_shape=[full(BF), full(F32), full(BF), full(F32), jax.ShapeDtypeStruct((batch, rows, LANES), F32)],
        input_output_aliases={first + i: i for i in range(len(earlier))},
        compiler_params=params(),
        cost_estimate=cost(2 * rows * width * width, 2 * width * width + 18 * rows * width),
        name="branch",
    )(me, *pieces, weight, tokens, bias[None], gain[None], shift[None], *earlier)


def norm_back(grad, normed, inverse, gain):
    scaled = grad * gain
    first = jnp.mean(scaled, axis=1, keepdims=True)
    second = jnp.mean(scaled * normed, axis=1, keepdims=True)
    return inverse * (scaled - first - normed * second)


def feed_kernel(*refs, middle, depth, parts):
    low, inverse, bias_even, bias_odd, bias_reduce, gain_second, shift_second, gain_first = refs[:8]
    hidden_at, cot_at, normed_at, second_even, second_odd = refs[8:13]
    blocks = refs[13 : 13 + len(parts)]
    refs = refs[13 + len(parts) :]
    act_even, act_odd, de_even, de_odd, sums_even, sums_odd, result_at, dr_at, du, da, sums_second, sums_first = refs[:12]
    w_first, w_second, slope, hidden, cot, normed, result, dr, total, block_sems, second_sems, sems = refs[12:]
    step = pl.program_id(0)
    rows, width = total.shape
    shard, block = w_first.shape[3], w_first.shape[4]
    chunk = 64

    def first_copies(i):
        made = []
        for j, (ref, (n, first)) in enumerate(zip(blocks, parts)):
            if n % middle == i:
                target = w_first.at[i, n // middle, pl.ds(first, ref.shape[0])]
                made.append(pltpu.make_async_copy(ref.at[:, :shard, :], target, block_sems.at[j]))
        return made

    def second_copies(i):
        return [
            pltpu.make_async_copy(ref.at[:, i], w_second.at[i, parity], second_sems.at[i, parity])
            for parity, ref in enumerate((second_even, second_odd))
        ]

    rest = [
        pltpu.make_async_copy(source, target, sems.at[i])
        for i, (source, target) in enumerate(((hidden_at, hidden), (cot_at, cot), (normed_at, normed)))
    ]
    back = [
        pltpu.make_async_copy(source, target, sems.at[3 + i])
        for i, (source, target) in enumerate(((result, result_at), (dr, dr_at)))
    ]

    @pl.when(step == 0)
    def _():
        for i in range(middle):
            for copy in first_copies(i) + second_copies(i):
                copy.start()
        for copy in rest:
            copy.start()
        sums_second[...] = jnp.zeros_like(sums_second)
        sums_first[...] = jnp.zeros_like(sums_first)

    for i in range(middle):

        @pl.when(step == i)
        def _():
            for copy in first_copies(i) + second_copies(i):
                copy.wait()

    @pl.when(step < middle)
    def _():
        part = None
        for parity, (bias, act) in enumerate(((bias_even, act_even), (bias_odd, act_odd))):
            for at in (slice(0, rows // 2), slice(rows // 2, rows)):
                value = bias[...]
                for z in range(depth):
                    value = value + dot_nn(low[at, z * shard : (z + 1) * shard], w_first[step, parity, z])
                cdf = 0.5 * (1.0 + lax.erf(value * SQRT_HALF))
                act[at, :] = (value * cdf).astype(BF)
                grad = cdf + value * DENSITY * jnp.exp(-0.5 * value * value)
                slope[step, parity, at, :] = grad.astype(BF)
            got = dot_nn(act[...], w_second[step, parity].reshape(block, width))
            part = got if part is None else part + got

        @pl.when(step == 0)
        def _():
            total[...] = part + bias_reduce[...]

        @pl.when(step > 0)
        def _():
            total[...] += part

    @pl.when(step == middle - 1)
    def _():
        rest[0].wait()
        rest[1].wait()

        @pl.loop(0, rows // chunk)
        def _(i):
            at = pl.ds(pl.multiple_of(i * chunk, chunk), chunk)
            value = total[at, :] + hidden[at, :]
            mean = jnp.mean(value, axis=1, keepdims=True)
            centred = value - mean
            scale = lax.rsqrt(jnp.mean(centred * centred, axis=1, keepdims=True) + EPS)
            unit = centred * scale
            result[at, :] = unit * gain_second[...] + shift_second[...]
            grad = cot[at, :]
            grad_sum = norm_back(grad, unit, scale, gain_second[...])
            total[at, :] = grad_sum
            rounded = grad_sum.astype(BF)
            dr[at, :] = rounded
            sums_second[0:1, :] += jnp.sum(grad * unit, axis=0, keepdims=True)
            sums_second[1:2, :] += jnp.sum(grad, axis=0, keepdims=True)
            sums_second[2:3, :] += jnp.sum(rounded.astype(F32), axis=0, keepdims=True)

        for copy in back:
            copy.start()

    @pl.when(step >= middle)
    def _():
        i = step - middle
        for parity, (de, sums) in enumerate(((de_even, sums_even), (de_odd, sums_odd))):
            grad = dot_nt(dr[...], w_second[i, parity].reshape(block, width)) * slope[i, parity].astype(F32)
            rounded = grad.astype(BF)
            de[...] = rounded
            sums[...] = jnp.sum(rounded.astype(F32), axis=0, keepdims=True)
            for z in range(depth):
                total[:, z * shard : (z + 1) * shard] += dot_nt(rounded, w_first[i, parity, z])

    @pl.when(step == 2 * middle - 1)
    def _():
        rest[2].wait()

        @pl.loop(0, rows // chunk)
        def _(i):
            at = pl.ds(pl.multiple_of(i * chunk, chunk), chunk)
            grad, unit = total[at, :], normed[at, :]
            grad_sum = norm_back(grad, unit, inverse[at, 0:1], gain_first[...])
            du[at, :] = grad_sum
            rounded = grad_sum.astype(BF)
            da[at, :] = rounded
            sums_first[0:1, :] += jnp.sum(grad * unit, axis=0, keepdims=True)
            sums_first[1:2, :] += jnp.sum(grad, axis=0, keepdims=True)
            sums_first[2:3, :] += jnp.sum(rounded.astype(F32), axis=0, keepdims=True)

        for copy in back:
            copy.wait()


def feed(low, inverse, bias_halves, bias_reduce, gain_second, shift_second, gain_first, hidden, cot, normed, second, blocks, shard):
    rows, width = low.shape
    depth, middle, piece, _ = second[0].shape
    block = depth * piece
    flat, parts = flatten_blocks(blocks)
    ahead = lambda i: jnp.minimum(i, middle - 1)
    behind = lambda i: jnp.maximum(i - middle, 0)
    bias = pl.BlockSpec((None, 1, block), lambda i: (ahead(i), 0, 0))
    sums = pl.BlockSpec((None, 1, block), lambda i: (behind(i), 0, 0))
    act = pl.BlockSpec((rows, block), lambda i: (0, ahead(i)))
    de = pl.BlockSpec((rows, block), lambda i: (0, behind(i)))
    full, vec, anywhere = whole((rows, width)), whole((1, width)), pl.BlockSpec(memory_space=pl.ANY)
    shape = jax.ShapeDtypeStruct
    return pl.pallas_call(
        functools.partial(feed_kernel, middle=middle, depth=depth, parts=parts),
        grid=(2 * middle,),
        in_specs=[full, whole((rows, LANES)), bias, bias, vec, vec, vec, vec] + [anywhere] * (5 + len(flat)),
        out_specs=[act, act, de, de, sums, sums, anywhere, anywhere, full, full, whole((8, width)), whole((8, width))],
        out_shape=[shape((rows, middle * block), BF)] * 4
        + [shape((middle, 1, block), F32)] * 2
        + [shape((rows, width), F32), shape((rows, width), BF), shape((rows, width), F32), shape((rows, width), BF)]
        + [shape((8, width), F32)] * 2,
        scratch_shapes=[
            pltpu.VMEM((middle, 2, depth, shard, block), BF),
            pltpu.VMEM((middle, 2, depth, piece, width), BF),
            pltpu.VMEM((middle, 2, rows, block), BF),
            pltpu.VMEM((rows, width), F32),
            pltpu.VMEM((rows, width), F32),
            pltpu.VMEM((rows, width), F32),
            pltpu.VMEM((rows, width), F32),
            pltpu.VMEM((rows, width), BF),
            pltpu.VMEM((rows, width), F32),
            pltpu.SemaphoreType.DMA((len(flat),)),
            pltpu.SemaphoreType.DMA((middle, 2)),
            pltpu.SemaphoreType.DMA((5,)),
        ],
        compiler_params=params(),
        cost_estimate=cost(16 * rows * width * middle * block, 8 * width * middle * block + 40 * rows * width),
        name="feed",
    )(
        low,
        inverse,
        *bias_halves,
        bias_reduce[None],
        gain_second[None],
        shift_second[None],
        gain_first[None],
        hidden,
        cot,
        normed,
        *second,
        *flat,
    )


def context_back_kernel(me, da, weight, *refs, middle):
    outs, whole_grad = refs[:-1], refs[-1]
    whole_grad[...] = dot_nt(da[...], weight[...]).astype(BF)
    rows = da.shape[0]
    mine, other = outs
    width = mine.shape[1]
    second = (me[0] & 1) == 1
    for i in range(middle):
        at = pl.multiple_of(((me[0] ^ (2 * i)) // 2) * 2 * width, 2 * width)
        pair = whole_grad[:, pl.ds(at, 2 * width)]
        low, high = pair[:, :width], pair[:, width:]
        mine[i * rows : (i + 1) * rows, :] = jnp.where(second, high, low)
        other[i * rows : (i + 1) * rows, :] = jnp.where(second, low, high)


def context_back(me, da, weight, own_width, middle):
    rows, width = da.shape
    shape = (middle * rows, own_width)
    return pl.pallas_call(
        functools.partial(context_back_kernel, middle=middle),
        grid=(1,),
        in_specs=[pl.BlockSpec(memory_space=pltpu.SMEM), whole(da.shape), whole(weight.shape)],
        out_specs=[whole(shape)] * 2,
        out_shape=[jax.ShapeDtypeStruct(shape, BF)] * 2,
        scratch_shapes=[pltpu.VMEM((rows, width), BF)],
        compiler_params=params(),
        cost_estimate=cost(2 * rows * width * width, 2 * width * width + 4 * rows * width),
        name="context_back",
    )(me, da, weight)


def gradient_kernel(act, other_act, grad, other_grad, out):
    depth, piece, width = out.shape
    total = dot_tn(act[...], grad[...]) + dot_tn(other_act[...], other_grad[...])
    out[...] = total.astype(BF).reshape(depth, piece, width)


def reduce_gradient(act, other_act, grad, other_grad, depth, piece):
    rows, width = grad.shape
    block = depth * piece
    middle = act.shape[1] // block
    column = pl.BlockSpec((rows, block), lambda i: (0, i))
    full = whole((rows, width))
    return pl.pallas_call(
        gradient_kernel,
        grid=(middle,),
        in_specs=[column, column, full, full],
        out_specs=pl.BlockSpec((depth, None, piece, width), lambda i: (0, i, 0, 0)),
        out_shape=jax.ShapeDtypeStruct((depth, middle, piece, width), BF),
        compiler_params=params(),
        cost_estimate=cost(4 * rows * width * middle * block, 2 * width * middle * block + 4 * rows * middle * block),
        name="reduce_gradient",
    )(act, other_act, grad, other_grad)


EXTRA = 16


def expand_gradient_kernel(
    me, low, other_low, context, other_context, de, other_de, da, other_da, small, *outs, middle, own, share
):
    block = de.shape[1] // middle
    depth = small.shape[0]
    shard = low.shape[1] // depth
    tall = shard + EXTRA
    first, second = low[...].T, other_low[...].T
    third, fourth = context[...].T, other_context[...].T
    kept_a, sent_a, kept_b, sent_b = outs
    for i in range(middle):
        at = slice(i * block, (i + 1) * block)
        target = me[0] ^ (2 * i)
        wide = (dot_nn(first, de[:, at]) + dot_nn(second, other_de[:, at])).astype(BF)
        where = pl.ds(pl.multiple_of(target * own, own), own)
        thin = (dot_nn(third, da[:, where]) + dot_nn(fourth, other_da[:, where])).astype(BF)
        for out, n, part in (
            (sent_a if i >= 2 else kept_a, i % 2, range(depth // 2)),
            (sent_b if i % 2 else kept_b, i // 2, range(depth // 2, depth)),
        ):
            for z in part:
                row = (z - part[0]) * tall
                out[n, row : row + shard, :block] = wide[z * shard : (z + 1) * shard]
                out[n, row : row + shard, block:] = thin[z * shard : (z + 1) * shard]
                line = small[z : z + 1, pl.ds(pl.multiple_of(target * share, share), share)].astype(BF)
                line = jnp.concatenate([line, jnp.zeros((1, block + own - share), BF)], axis=1)
                out[n, row + shard : row + tall, :] = jnp.broadcast_to(line, (EXTRA, block + own))


def expand_gradient(me, low, other_low, context, other_context, de, other_de, da, other_da, small, own):
    rows, width = low.shape
    middle = 4
    depth = small.shape[0]
    block = de.shape[1] // middle
    args = (low, other_low, context, other_context, de, other_de, da, other_da, small)
    shape = (2, width // 2 + EXTRA * depth // 2, block + own)
    share = small.shape[1] // (2 * middle)
    return pl.pallas_call(
        functools.partial(expand_gradient_kernel, middle=middle, own=own, share=share),
        grid=(1,),
        in_specs=[pl.BlockSpec(memory_space=pltpu.SMEM)] + [whole(v.shape) for v in args],
        out_specs=[whole(shape)] * 4,
        out_shape=[jax.ShapeDtypeStruct(shape, BF)] * 4,
        compiler_params=params(),
        cost_estimate=cost(4 * rows * width * middle * (block + own), 4 * width * middle * block),
        name="expand_gradient",
    )(me, *args)


def add_kernel(*refs, count):
    for i in range(count):
        mine, got, out = refs[2 * i], refs[2 * i + 1], refs[2 * count + i]
        out[...] = (mine[...].astype(F32) + got[...].astype(F32)).astype(BF)


def add_steps(kept_a, got_a, kept_b, got_b):
    _, rows, width = kept_a.shape
    block = lambda n: pl.BlockSpec((None, rows // 2, width), lambda i: (n, i, 0))
    args = (kept_a, got_a, kept_a, got_a, kept_b, got_b, kept_b, got_b)
    return pl.pallas_call(
        functools.partial(add_kernel, count=4),
        grid=(2,),
        in_specs=[block(n) for n in (0, 0, 1, 1)] * 2,
        out_specs=[pl.BlockSpec((rows // 2, width), lambda i: (i, 0))] * 4,
        out_shape=[jax.ShapeDtypeStruct((rows, width), BF)] * 4,
        compiler_params=params(),
        cost_estimate=cost(0, 12 * rows * width),
        name="add_steps",
    )(*args)


def add_last_kernel(kept_a, got_a, kept_b, got_b, out):
    rows = kept_a.shape[0]
    out[:rows, :] = (kept_a[...].astype(F32) + got_a[...].astype(F32)).astype(BF)
    out[rows:, :] = (kept_b[...].astype(F32) + got_b[...].astype(F32)).astype(BF)


def add_last(kept_a, got_a, kept_b, got_b):
    rows, width = kept_a.shape
    shape = (2 * rows, width)
    return pl.pallas_call(
        add_last_kernel,
        grid=(1,),
        in_specs=[whole((rows, width))] * 4,
        out_specs=whole(shape),
        out_shape=jax.ShapeDtypeStruct(shape, BF),
        compiler_params=params(),
        cost_estimate=cost(0, 12 * rows * width),
        name="add_last",
    )(kept_a, got_a, kept_b, got_b)


def unpack_expand_kernel(blocks, wide, thin, small, *, depth):
    count = blocks.shape[0]
    shard = wide.shape[0]
    block = wide.shape[1] // count
    piece, own = block // depth, thin.shape[1] // count
    for g in range(count):
        for z in range(depth):
            at = (z * count + g) * piece
            wide[:, at : at + piece] = blocks[g, :shard, z * piece : (z + 1) * piece].astype(F32)
        thin[:, g * own : (g + 1) * own] = blocks[g, :shard, block:].astype(F32)
        small[g : g + 1, :] = blocks[g, shard : shard + EXTRA, : small.shape[1]].astype(F32)[0:1]


def unpack_expand(blocks, depth, hidden, width, share):
    shard = blocks.shape[1] - EXTRA
    shapes = [(shard, hidden), (shard, width), (blocks.shape[0], share)]
    return pl.pallas_call(
        functools.partial(unpack_expand_kernel, depth=depth),
        grid=(1,),
        in_specs=[whole(blocks.shape)],
        out_specs=[whole(v) for v in shapes],
        out_shape=[jax.ShapeDtypeStruct(v, F32) for v in shapes],
        compiler_params=params(),
        cost_estimate=cost(0, 6 * shard * (hidden + width)),
        name="unpack_expand",
    )(blocks)


def unpack_reduce_kernel(me, *refs):
    out = refs[-1]
    rows = refs[0].shape[0]
    for n, k in enumerate(plane_list(len(refs) - 1)):
        out[pl.ds(pl.multiple_of((me[0] ^ k) * rows, rows), rows), :] = refs[n][...].astype(F32)


def unpack_reduce(me, blocks):
    rows, width = blocks[0].shape
    shape = (rows * len(blocks), width)
    return pl.pallas_call(
        unpack_reduce_kernel,
        grid=(1,),
        in_specs=[pl.BlockSpec(memory_space=pltpu.SMEM)] + [whole(v.shape) for v in blocks],
        out_specs=whole(shape),
        out_shape=jax.ShapeDtypeStruct(shape, F32),
        compiler_params=params(),
        cost_estimate=cost(0, 6 * shape[0] * width),
        name="unpack_reduce",
    )(me, *blocks)


def input_part_kernel(grads, weight, *refs, with_away):
    got = dot_nn(grads[...], weight[...])
    if with_away:
        got = got + refs[0][...].astype(F32)
        outs = refs[1:]
    else:
        outs = refs
    rows = outs[0].shape[0]
    for i, out in enumerate(outs):
        out[...] = got[i * rows : (i + 1) * rows].astype(BF)


def input_part(grads, weight, half, away=None, pieces=1):
    count, line = grads.shape
    rows, width = count // 2, weight.shape[1]
    more = () if away is None else (away,)
    shape = (rows // pieces, width)
    got = pl.pallas_call(
        functools.partial(input_part_kernel, with_away=away is not None),
        grid=(1,),
        in_specs=[pl.BlockSpec((rows, line), lambda i: (half, 0)), whole(weight.shape)] + [whole(v.shape) for v in more],
        out_specs=[whole(shape)] * pieces,
        out_shape=[jax.ShapeDtypeStruct(shape, BF)] * pieces,
        compiler_params=params(),
        cost_estimate=cost(2 * rows * width * line, 4 * rows * width),
        name="input_part",
    )(grads, weight, *more)
    return got if pieces > 1 else got[0]


def input_kernel(before, *refs):
    out = refs[-1]
    rows = refs[0].shape[0]
    half = len(refs) // 2
    for s in range(2):
        total = before[s * rows : (s + 1) * rows, :]
        for ref in refs[s * half : (s + 1) * half]:
            total = total + ref[...].astype(F32)
        out[s] = total


def input_sum(before, first, second):
    rows, width = first[0].shape
    return pl.pallas_call(
        input_kernel,
        grid=(1,),
        in_specs=[whole(before.shape)] + [whole(v.shape) for v in (*first, *second)],
        out_specs=whole((2, rows, width)),
        out_shape=jax.ShapeDtypeStruct((2, rows, width), F32),
        compiler_params=params(),
        cost_estimate=cost(0, 32 * rows * width),
        name="input_sum",
    )(before, *first, *second)


def unpack_heads_kernel(me, *refs):
    outs, bias = refs[-4:-1], refs[-1]
    count = len(refs) - 4
    shard, width = outs[0].shape
    own = width // count
    bias[...] = jnp.zeros_like(bias)
    for n, k in enumerate(plane_list(count)):
        where = pl.ds(pl.multiple_of((me[0] ^ k) * own, own), own)
        tail = refs[n][shard : shard + 16, :].astype(F32)
        for t in range(3):
            at = slice(t * own, (t + 1) * own)
            outs[t][:, where] = refs[n][:shard, at].astype(F32)
            bias[t : t + 1, where] = tail[0:1, at] + tail[1:2, at]


def unpack_heads(me, blocks, shard, width):
    shapes = [(shard, width)] * 3 + [(8, width)]
    return pl.pallas_call(
        unpack_heads_kernel,
        grid=(1,),
        in_specs=[pl.BlockSpec(memory_space=pltpu.SMEM)] + [whole(v.shape) for v in blocks],
        out_specs=[whole(v) for v in shapes],
        out_shape=[jax.ShapeDtypeStruct(v, F32) for v in shapes],
        compiler_params=params(),
        cost_estimate=cost(0, 18 * shard * width),
        name="unpack_heads",
    )(me, *blocks)


def heads_gradient_kernel(*refs, blocks, last):
    grads = refs[blocks]
    if last:
        me, before, sums_before, kept, sent, tokens, turned = refs[blocks + 1 :]
    else:
        out, sums, tokens = refs[blocks + 1 :]
    rows = grads.shape[0] // blocks
    for i, ref in enumerate(refs[:blocks]):
        tokens[i * rows : (i + 1) * rows, :] = ref[:rows, :]
    total = dot_tn(grads[...], tokens[...])
    column = jnp.sum(grads[...].astype(F32), axis=0, keepdims=True)
    if not last:
        out[...] = total
        sums[...] = jnp.broadcast_to(column, sums.shape)
        return
    turned[...] = (total + before[...]).T.astype(BF)
    column = jnp.broadcast_to(column + sums_before[0:1, :], (EXTRA, column.shape[1]))
    first = column.astype(BF).astype(F32)
    place = lax.broadcasted_iota(jnp.int32, (EXTRA, 1), 0)
    extra = jnp.where(place == 0, first, jnp.where(place == 1, column - first, 0.0)).astype(BF)
    depth = 2 * kept.shape[0]
    shard = turned.shape[0] // depth
    for j in range(depth):
        target = (kept, sent)[j // (depth // 2)].at[j % (depth // 2)]
        at = pl.multiple_of((me[0] ^ j) * shard, shard)
        target[:shard, :] = turned[pl.ds(at, shard), :]
        target[shard:, :] = extra


def heads_gradient(blocks, grads, more=None, depth=1):
    line = grads.shape[1]
    width = blocks[0].shape[1]
    last = more is not None
    args = (*blocks, grads) + (more or ())
    specs = [whole(v.shape) for v in (*blocks, grads)]
    scratch = [pltpu.VMEM((grads.shape[0], width), BF)]
    if last:
        shapes = [jax.ShapeDtypeStruct((depth // 2, width // depth + EXTRA, line), BF)] * 2
        specs += [pl.BlockSpec(memory_space=pltpu.SMEM)] + [whole(v.shape) for v in more[1:]]
        scratch.append(pltpu.VMEM((width, line), BF))
    else:
        shapes = [jax.ShapeDtypeStruct((line, width), F32), jax.ShapeDtypeStruct((8, line), F32)]
    return pl.pallas_call(
        functools.partial(heads_gradient_kernel, blocks=len(blocks), last=last),
        grid=(1,),
        in_specs=specs,
        out_specs=[whole(v.shape) for v in shapes],
        out_shape=shapes,
        scratch_shapes=scratch,
        compiler_params=params(),
        cost_estimate=cost(2 * grads.shape[0] * width * line, 2 * grads.shape[0] * width + 6 * width * line),
        name="heads_gradient",
    )(*args)


def normalize(values, gain, shift):
    mean = jnp.mean(values, axis=-1, keepdims=True)
    centred = values - mean
    inverse = lax.rsqrt(jnp.mean(centred * centred, axis=-1, keepdims=True) + EPS)
    normed = centred * inverse
    return normed * gain + shift, normed, inverse


def normalize_back(grad, normed, inverse, gain):
    scaled = grad * gain
    inner = (
        scaled
        - jnp.mean(scaled, axis=-1, keepdims=True)
        - normed * jnp.mean(scaled * normed, axis=-1, keepdims=True)
    )
    return inner * inverse, jnp.sum(grad * normed, axis=0), jnp.sum(grad, axis=0)


def column_sums(values):
    return jnp.sum(values.astype(F32), axis=0)


def plain_body(
    tokens,
    segments,
    query_weight,
    query_bias,
    key_weight,
    value_weight,
    value_bias,
    output_weight,
    output_bias,
    first_gain,
    first_shift,
    expand_weight,
    expand_bias,
    reduce_weight,
    reduce_bias,
    second_gain,
    second_shift,
    cotangent,
):
    batch, rows, width = tokens.shape
    count, depth = lax.axis_size("ctx"), lax.axis_size("fsdp")
    me, my_shard = lax.axis_index("ctx"), lax.axis_index("fsdp")
    shard = query_weight.shape[0]
    hidden = expand_weight.shape[1]
    own_width = width // count
    heads = own_width // HEAD
    piece = hidden // depth // count
    block = depth * piece
    half = hidden // 2
    order = plane_order()
    evens = order[: count // 2]
    scale = HEAD**-0.5
    bits = (count * rows - 1).bit_length()

    columns = lambda w: lax.dynamic_slice_in_dim(w, me * own_width, own_width, 1).astype(BF)
    names = (query_bias, value_bias, output_bias, first_gain, first_shift, reduce_bias, second_gain, second_shift)
    packed = jnp.concatenate(names + (expand_bias,))
    terms = jnp.concatenate(in_terms(packed, 3))
    line = 3 * own_width
    lines = -(-terms.shape[0] // (16 * line)) * 16
    terms = jnp.pad(terms, (0, lines * line - terms.shape[0])).reshape(lines, line)
    own_heads = jnp.concatenate([columns(query_weight), columns(key_weight), columns(value_weight)], axis=1)
    own_heads = gather_shards(jnp.concatenate([own_heads, terms], axis=0))
    packed = own_heads[:, shard:].reshape(depth, lines * line)[:, : 3 * packed.shape[0]]
    packed = jnp.sum(packed.reshape(depth, 3, -1).astype(F32), axis=1)
    own_heads = own_heads[:, :shard].reshape(width, line)
    (bias_query, bias_value, bias_output, gain_first, shift_first, bias_reduce, gain_second, shift_second) = (
        packed[:, i * shard : (i + 1) * shard].reshape(width) for i in range(len(names))
    )
    wide_bias = packed[:, len(names) * shard :].reshape(depth, count, piece)
    bias_halves = [
        jnp.stack([lax.dynamic_index_in_dim(wide_bias, me ^ k, 1, keepdims=False) for k in ks], axis=1).reshape(half)
        for ks in (evens, order[count // 2 :])
    ]
    own_part = lambda v: lax.dynamic_slice_in_dim(v, me * own_width, own_width, 0)
    head_bias = jnp.concatenate([own_part(bias_query), jnp.zeros((own_width,), F32), own_part(bias_value)])
    head_scale = jnp.concatenate([jnp.full((own_width,), scale * LOG2E, F32), jnp.ones((2 * own_width,), F32)])

    thin = shard // count
    folds = width // block
    strip = lax.dynamic_slice_in_dim(output_weight, me * thin, thin, 0).astype(BF)
    strip = jnp.concatenate([strip[:, i * block : (i + 1) * block] for i in range(folds)], axis=0)
    block_expand = lax.dynamic_slice_in_dim(expand_weight.reshape(shard, depth, count * piece), me * piece, piece, 2)
    block_expand = jnp.concatenate([block_expand.reshape(shard, block).astype(BF), strip], axis=0)
    block_expand = lax.all_gather(block_expand, "fsdp", axis=0)
    block_reduce = lax.dynamic_slice_in_dim(reduce_weight, me * piece, piece, 0).astype(BF)
    block_reduce = lax.all_gather(block_reduce, "fsdp", axis=0)

    groups = jnp.stack([w.reshape(shard, count, own_width) for w in (query_weight, key_weight, value_weight)], axis=2)
    half_heads = jnp.concatenate(
        [lax.dynamic_index_in_dim(groups, me ^ k, 1, keepdims=False).reshape(shard, line).astype(BF) for k in evens],
        axis=1,
    )
    half_heads = lax.all_gather(half_heads, "fsdp", axis=0, tiled=True)
    other_heads = peer(half_heads, 1)

    seg = segments
    for b in range(count.bit_length() - 1):
        seg = jnp.concatenate([seg, peer(seg, 1 << b)], axis=1)
    seg = seg.reshape(batch, count, rows)
    seg = jnp.concatenate([seg[:, k] for k in order], axis=1)

    lanes = lambda v: v if own_width == LANES else jnp.pad(v, ((0, 0), (0, LANES - own_width)))
    kept, context_parts = [], []
    for s in range(batch):
        even = jnp.concatenate(gather_even(tokens[s].astype(BF), s % 2 == 0), axis=0)
        odd = peer(even, 1)
        qkv = jnp.concatenate([dot_nn(even, own_heads), dot_nn(odd, own_heads)], axis=0)
        qkv = ((qkv + head_bias) * head_scale).astype(BF)
        if own_width != LANES:
            qkv = jnp.concatenate([lanes(qkv[:, i * own_width : (i + 1) * own_width]) for i in range(3)], axis=1)
        mask_q, mask_k = mask_columns(seg[s], bits)
        out, lse = attend(qkv, mask_q, mask_k, heads, rows)
        kept.append((even, odd, qkv, mask_q, mask_k, out, lse))
        context_parts.append(by_owner(heads_to_rows(out[:, :own_width]), 1))

    got_expand = gather_even(block_expand, True)
    got_expand += [peer(v, 1) for v in got_expand]
    got_reduce = gather_even(block_reduce, False)
    got_reduce += [peer(v, 1) for v in got_reduce]
    full_output = by_owner(
        [
            jnp.concatenate([v[:, shard + i * thin : shard + (i + 1) * thin] for i in range(folds)], axis=2)
            for v in got_expand
        ],
        1,
    ).reshape(width, width)
    middle = count // 2
    expand_halves = [
        jnp.concatenate([v[:, :shard].reshape(width, depth, piece) for v in vs], axis=2).reshape(width, half)
        for vs in (got_expand[:middle], got_expand[middle:])
    ]
    reduce_halves = [
        jnp.concatenate(vs, axis=1).reshape(half, width) for vs in (got_reduce[:middle], got_reduce[middle:])
    ]

    firsts = []
    for s in range(batch):
        branch = dot_nn(context_parts[s], full_output) + bias_output
        firsts.append(normalize(tokens[s] + branch, gain_first, shift_first))
    hidden_in, normed_first, inverse_first = (jnp.concatenate(v, axis=0) for v in zip(*firsts))
    context_low = jnp.concatenate(context_parts, axis=0)
    hidden_low = hidden_in.astype(BF)
    halves = []
    reduced = bias_reduce
    for weight, back, bias in zip(expand_halves, reduce_halves, bias_halves):
        expand = dot_nn(hidden_low, weight) + bias
        cdf = 0.5 * (1.0 + lax.erf(expand * SQRT_HALF))
        active = (expand * cdf).astype(BF)
        slope = cdf + expand * DENSITY * jnp.exp(-0.5 * expand * expand)
        reduced = reduced + dot_nn(active, back)
        halves.append((weight, back, active, slope.astype(BF)))
    result, normed_second, inverse_second = normalize(hidden_in + reduced, gain_second, shift_second)

    grad_out = cotangent.reshape(batch * rows, width)
    grad_sum_second, grad_gain_second, grad_shift_second = normalize_back(
        grad_out, normed_second, inverse_second, gain_second
    )
    grad_reduced = grad_sum_second.astype(BF)
    grad_bias_reduce = column_sums(grad_reduced)

    def chip_sum(make):
        got = peer(make(1).astype(BF), 1)
        return (make(0) + got.astype(F32)).astype(BF)

    sum_reduce = chip_sum(lambda i: dot_tn(halves[i][2], grad_reduced))
    sum_reduce = lax.psum_scatter(sum_reduce, "fsdp", scatter_dimension=0, tiled=True)
    sum_reduce = reduce_even(jnp.split(sum_reduce, middle, axis=0), False)

    grad_hidden = grad_sum_second
    grad_expands = []
    for weight, back, active, slope in halves:
        grad_expand = (dot_nt(grad_reduced, back) * slope.astype(F32)).astype(BF)
        grad_hidden = grad_hidden + dot_nt(grad_expand, weight)
        grad_expands.append(grad_expand)
    grad_bias_expand = [column_sums(g).reshape(depth, middle, piece) for g in grad_expands]
    grad_pre, grad_gain_first, grad_shift_first = normalize_back(
        grad_hidden, normed_first, inverse_first, gain_first
    )
    grad_branch = grad_pre.astype(BF)
    grad_bias_output = column_sums(grad_branch)
    grad_context = dot_nt(grad_branch, full_output).astype(BF)

    sum_expand = chip_sum(lambda i: dot_tn(hidden_low, grad_expands[i])).reshape(width, depth, middle, piece)
    sum_expand = reduce_even([sum_expand[:, :, i].reshape(width, block) for i in range(middle)], True)
    branch_blocks = jnp.concatenate(
        [lax.dynamic_slice_in_dim(grad_branch, (me ^ k) * own_width, own_width, 1) for k in order], axis=1
    )
    sum_output = chip_sum(
        lambda i: dot_tn(context_low, branch_blocks[:, i * width // 2 : (i + 1) * width // 2])
    )
    sum_output = reduce_even(jnp.split(sum_output, middle, axis=1), False)
    sum_expand = jnp.concatenate([sum_expand, sum_output], axis=1)
    sum_expand = lax.psum_scatter(sum_expand, "fsdp", scatter_dimension=0, tiled=True)

    grads = []
    for s in range(batch):
        even, odd, qkv, mask_q, mask_k, out, lse = kept[s]
        dc = lanes(rows_to_heads(grad_context[s * rows : (s + 1) * rows], own_width))
        got = attend_back(qkv, mask_q, mask_k, dc, out, lse, heads, rows)
        if own_width != LANES:
            got = jnp.concatenate([got[:, i * LANES : i * LANES + own_width] for i in range(3)], axis=1)
        grads.append(got)
    middle_row = count * rows // 2
    grad_heads = sum(
        dot_tn(kept[s][0], grads[s][:middle_row]) + dot_tn(kept[s][1], grads[s][middle_row:]) for s in range(batch)
    ).astype(BF)
    grad_head_bias = jnp.pad(
        jnp.stack(in_terms(sum(column_sums(g) for g in grads), 2)), ((0, 14), (0, 0))
    )
    home_heads = jnp.concatenate(
        [grad_heads.reshape(depth, shard, line), jnp.broadcast_to(grad_head_bias, (depth, 16, line))], axis=1
    )
    home_heads = reduce_shards(home_heads)
    home_heads = jnp.concatenate(
        [home_heads[:shard].astype(BF)]
        + [v[None] for v in in_terms(home_heads[shard] + home_heads[shard + 1], 2)]
        + [jnp.zeros((14, line), BF)],
        axis=0,
    )
    back_rows = [heads_to_rows(g) for g in grads]
    back_even = jnp.concatenate([jnp.concatenate(r[:middle], axis=1) for r in back_rows], axis=0)
    back_odd = jnp.concatenate([jnp.concatenate(r[middle:], axis=1) for r in back_rows], axis=0)
    grad_in = grad_pre + dot_nt(back_even, half_heads) + dot_nt(back_odd, other_heads)

    def spread(value, low_first):
        got = gather_even(value, low_first)
        odd = peer(jnp.stack(got), 1)
        return by_owner([v[None] for v in got] + [odd[i : i + 1] for i in range(middle)], 0)

    wide = lax.all_gather(sum_expand, "ctx", axis=0)
    grad_expand_weight = jnp.transpose(wide[:, :, :block].reshape(count, shard, depth, piece), (1, 2, 0, 3))
    grad_expand_weight = grad_expand_weight.reshape(shard, hidden).astype(F32)
    grad_output_weight = jnp.transpose(wide[:, :, block:], (1, 0, 2)).reshape(shard, width).astype(F32)
    grad_reduce_weight = lax.all_gather(sum_reduce, "ctx", axis=0, tiled=True).astype(F32)
    wide_heads = spread(home_heads, True)
    wide_shards = jnp.transpose(wide_heads[:, :shard].reshape(count, shard, 3, own_width), (2, 1, 0, 3))
    grad_query_weight, grad_key_weight, grad_value_weight = (
        wide_shards[i].reshape(shard, width).astype(F32) for i in range(3)
    )
    wide_biases = jnp.sum(wide_heads[:, shard : shard + 2].astype(F32), axis=1).reshape(count, 3, own_width)
    own_shard = lambda v: lax.dynamic_slice_in_dim(v.reshape(width), my_shard * shard, shard, 0)

    vectors = (
        grad_bias_output,
        grad_gain_first,
        grad_shift_first,
        grad_bias_reduce,
        grad_gain_second,
        grad_shift_second,
    )
    wide_bias = by_owner([g[:, i] for g in grad_bias_expand for i in range(middle)], 1)
    small = jnp.concatenate([v.reshape(depth, shard) for v in vectors] + [wide_bias], axis=1)
    for b in range(count.bit_length() - 1):
        small = small + peer(small, 1 << b)
    small = reduce_shards(small)
    vec = [small[i * shard : (i + 1) * shard] for i in range(len(vectors))]
    vec_expand = small[len(vectors) * shard :]
    return (
        result.reshape(batch, rows, width),
        grad_in.reshape(batch, rows, width),
        grad_query_weight,
        own_shard(wide_biases[:, 0]),
        grad_key_weight,
        grad_value_weight,
        own_shard(wide_biases[:, 2]),
        grad_output_weight,
        vec[0],
        vec[1],
        vec[2],
        grad_expand_weight,
        vec_expand,
        grad_reduce_weight,
        vec[3],
        vec[4],
        vec[5],
    )


def even_pieces(own, other):
    rows = own.shape[0]
    both = jnp.concatenate([own, other], axis=1)
    middle = lax.axis_size("ctx") // 2
    rows = rows // middle
    pieces = [both[i * rows : (i + 1) * rows] for i in range(middle)]
    return [pieces[0]] + [peer(pieces[i], 2 * i) for i in range(1, middle)]


def body(
    tokens,
    segments,
    query_weight,
    query_bias,
    key_weight,
    value_weight,
    value_bias,
    output_weight,
    output_bias,
    first_gain,
    first_shift,
    expand_weight,
    expand_bias,
    reduce_weight,
    reduce_bias,
    second_gain,
    second_shift,
    cotangent,
):
    batch, rows, width = tokens.shape
    count, depth = lax.axis_size("ctx"), lax.axis_size("fsdp")
    me, my_shard = lax.axis_index("ctx"), lax.axis_index("fsdp")
    me_array = me.astype(jnp.int32).reshape(1)
    shard = query_weight.shape[0]
    hidden = expand_weight.shape[1]
    own_width = width // count
    heads = own_width // HEAD
    piece = hidden // depth // count
    block = depth * piece
    middle = count // 2
    order = plane_order()
    evens, odds = order[:middle], order[middle:]
    scale = HEAD**-0.5
    bits = (count * rows - 1).bit_length()
    all_rows = batch * rows

    columns = lambda w: lax.dynamic_slice_in_dim(w, me * own_width, own_width, 1).astype(BF)
    names = (query_bias, value_bias, output_bias, first_gain, first_shift, reduce_bias, second_gain, second_shift)
    packed = jnp.concatenate(names + (expand_bias,))
    size = packed.shape[0]
    terms = jnp.concatenate(in_terms(packed, 3))
    line = 3 * own_width
    lines = -(-terms.shape[0] // (16 * line)) * 16
    terms = jnp.pad(terms, (0, lines * line - terms.shape[0])).reshape(lines, line)
    own_heads = jnp.concatenate([columns(query_weight), columns(key_weight), columns(value_weight)], axis=1)
    shard_parts = gather_doubling(jnp.concatenate([own_heads, terms], axis=0))

    def plane(value, *needed):
        first, second = after((peer(value, 2), peer(value, 4)), *needed)
        part = value.shape[0] // 2
        return first, second, (peer(first[:part], 4), peer(second[part:], 2))

    def chip(blocks):
        return blocks + [jax.tree.map(lambda v: peer(v, 1), b) for b in blocks]

    def direct(value):
        return [value] + [peer(value, k) for k in evens[1:]]

    low_in = []
    for s in range(batch):
        numbers = jnp.concatenate([segments[s] // 64, segments[s] % 64]).astype(BF)
        numbers = jnp.pad(numbers[None], ((0, EXTRA - 1), (0, width - 2 * rows)))
        low_in.append(jnp.concatenate([tokens[s].astype(BF), numbers], axis=0))

    reduce_blocks = [lax.dynamic_slice_in_dim(reduce_weight, (me ^ k) * piece, piece, 0).astype(BF) for k in evens]
    reduce_blocks = jnp.stack(reduce_blocks)

    first_got, shard_parts, low_in, reduce_blocks = join(direct(low_in[0]), shard_parts, low_in, reduce_blocks)
    first_blocks = chip(first_got)
    own_heads = by_owner([shard_parts[j : j + 1] for j in range(depth)], 0, list(range(depth)), "fsdp")
    packed = own_heads[:, shard:].reshape(depth, lines * line)[:, : 3 * size]
    packed = jnp.sum(packed.reshape(depth, 3, -1).astype(F32), axis=1)
    own_heads = own_heads[:, :shard].reshape(width, line)
    (bias_query, bias_value, bias_output, gain_first, shift_first, bias_reduce, gain_second, shift_second) = (
        packed[:, i * shard : (i + 1) * shard].reshape(width) for i in range(len(names))
    )
    wide_bias = packed[:, len(names) * shard :].reshape(depth, count, piece)
    bias_halves = [
        jnp.stack([lax.dynamic_index_in_dim(wide_bias, me ^ k, 1, keepdims=False).reshape(1, block) for k in ks])
        for ks in (evens, odds)
    ]
    own_part = lambda v: lax.dynamic_slice_in_dim(v, me * own_width, own_width, 0)
    head_bias = jnp.concatenate([own_part(bias_query), jnp.zeros((own_width,), F32), own_part(bias_value)])
    head_scale = jnp.concatenate([jnp.full((own_width,), scale * LOG2E, F32), jnp.ones((2 * own_width,), F32)])

    thin = shard // count
    folds = width // block
    strip = lax.dynamic_slice_in_dim(output_weight, me * thin, thin, 0).astype(BF)
    strip = jnp.concatenate([strip[:, i * block : (i + 1) * block] for i in range(folds)], axis=0)
    block_expand = [
        lax.dynamic_slice_in_dim(expand_weight, (z * count + me) * piece, piece, 1).astype(BF) for z in range(depth)
    ]
    block_expand = jnp.concatenate([jnp.concatenate(block_expand, axis=1), strip], axis=0)
    block_expand = lax.all_gather(after(block_expand, first_got[1]), "fsdp", axis=0)

    halfway = count * rows // 2
    heads_across = own_heads.T
    first_qkv, *first_masks = project(first_blocks, rows, own_heads, head_bias, head_scale, bits)
    first_out, first_lse, second_got = join(
        *attend(first_qkv, *first_masks, heads, rows), direct(low_in[1])
    )
    second_blocks = chip(second_got)
    (second_qkv, *second_masks), other_out = join(
        project(second_blocks, rows, own_heads, head_bias, head_scale, bits), peer(first_out[halfway:], 1)
    )

    reduce_own = lax.all_gather(after(reduce_blocks, second_got[1]), "fsdp", axis=0)
    second_out, second_lse, first_pieces, near = join(
        *attend(second_qkv, *second_masks, heads, rows),
        even_pieces(first_out[:halfway], other_out),
        (block_expand, peer(block_expand, 2), peer(block_expand, 4)),
    )
    part = depth // 2
    far = peer(near[1][:part], 4), peer(near[2][part:], 2)
    far, other_out, near_other = join(far, peer(second_out[halfway:], 1), [peer(v, 1) for v in near])
    got_expand = [*((v,) for v in near), far, *((v,) for v in near_other), tuple(peer(v, 1) for v in far)]
    full_output = assemble_output(got_expand, shard, thin, me_array)
    second_pieces = even_pieces(second_out[:halfway], other_out)
    kept = [
        (first_blocks, first_qkv, *first_masks, first_out, first_lse),
        (second_blocks, second_qkv, *second_masks, second_out, second_lse),
    ]

    earlier = None
    for s, pieces in enumerate((first_pieces, second_pieces)):
        earlier = branch(s, me_array, pieces, full_output, tokens, bias_output, gain_first, shift_first, earlier)
    context_low, hidden_in, hidden_low, normed_first, inverse_first = (
        v.reshape(all_rows, v.shape[2]) for v in earlier
    )

    hidden_low, reduce_own = join(hidden_low, reduce_own)
    (
        (act_even, act_odd, de_even, de_odd, sums_even, sums_odd, result, dr, grad_pre, da, sums_second, sums_first),
        other_low,
        other_context,
    ) = join(
        feed(
            hidden_low,
            inverse_first,
            bias_halves,
            bias_reduce,
            gain_second,
            shift_second,
            gain_first,
            hidden_in,
            cotangent.reshape(all_rows, width),
            normed_first,
            [reduce_own, peer(reduce_own, 1)],
            got_expand,
            shard,
        ),
        peer(hidden_low, 1),
        peer(context_low, 1),
    )

    vectors = (sums_first[2], sums_first[0], sums_first[1], sums_second[2], sums_second[0], sums_second[1])
    wide_bias = by_owner(
        [sums[i, 0].reshape(depth, 1, piece) for sums in (sums_even, sums_odd) for i in range(middle)], 1
    ).reshape(depth, hidden // depth)
    small = jnp.concatenate([v.reshape(depth, shard) for v in vectors] + [wide_bias], axis=1)
    share = -(-small.shape[1] // (count * LANES)) * LANES
    small = jnp.pad(small, ((0, 0), (0, share * count - small.shape[1])))
    da, de_even, de_odd, act_even, dr, small, own_grads, other_grads, other_act, other_dr = join(
        da,
        de_even,
        de_odd,
        act_even,
        dr,
        small,
        *context_back(me_array, da, full_output, own_width, middle),
        peer(act_odd, 1),
        peer(dr, 1),
    )

    sum_reduce, de_even, da, small, other_grads, other_de, other_da, other_small = join(
        reduce_gradient(act_even, other_act, dr, other_dr, depth, piece),
        de_even,
        da,
        small,
        peer(other_grads, 1),
        peer(de_odd, 1),
        peer(da, 1),
        peer(small, 1),
    )
    sum_reduce = lax.psum_scatter(sum_reduce, "fsdp", scatter_dimension=0, tiled=False)

    sums, dc = join(
        expand_gradient(
            me_array,
            hidden_low,
            other_low,
            context_low,
            other_context,
            de_even,
            other_de,
            da,
            other_da,
            small + other_small,
            own_width,
        ),
        even_pieces(own_grads, other_grads),
    )
    kept_a, sent_a, kept_b, sent_b = sums

    add = lambda a, b: (a.astype(F32) + b.astype(F32)).astype(BF)
    to_owner = lambda parts, count=middle: [parts[0]] + [peer(parts[i], 2 * i) for i in range(1, count)]

    def back(s, dc, part=None, before=None):
        _, qkv, mask_q, mask_k, out, lse = kept[s]
        return attend_back(qkv, mask_q, mask_k, dc, out, lse, heads, rows, part, before, s)

    first_grads = back(0, dc)
    first_grads, odd, got_a, got_b = join(
        first_grads, input_part(first_grads, heads_across, 1), peer(sent_a, 4), peer(sent_b, 2)
    )
    kept_a, sent_a, kept_b, sent_b = add_steps(kept_a, got_a, kept_b, got_b)
    before = heads_gradient(kept[0][0], first_grads)
    home, before, dc = join(input_part(first_grads, heads_across, 0, peer(odd, 1), middle), before, dc)
    upper, got_a, got_b, last_step, home = join(
        back(1, dc, 0), peer(sent_a, 2), peer(sent_b, 4), peer(home[-1], 2 * (middle - 1)), home[:-1]
    )
    upper, sum_expand, sum_reduce = join(upper, add_last(kept_a, got_a, kept_b, got_b), sum_reduce)
    sum_expand = lax.psum_scatter(sum_expand, "fsdp", scatter_dimension=0, tiled=True)
    second_grads, from_first, got_reduce = join(
        back(1, dc, 1, upper), to_owner(home, middle - 1) + [last_step], to_owner(sum_reduce)
    )
    sum_reduce = sum(v.astype(F32) for v in got_reduce).astype(BF)

    (shard_got, shard_sent), second_grads, sum_reduce = join(
        heads_gradient(kept[1][0], second_grads, (my_shard.astype(jnp.int32).reshape(1), *before), depth),
        second_grads,
        sum_reduce,
    )
    wide_expand = lax.all_gather(after(sum_expand, shard_got), "ctx", axis=0)
    odd = input_part(second_grads, heads_across, 1)
    away, got, got_reduce, second_grads = join(
        peer(odd, 1), exchange(shard_sent, "fsdp", depth // 2), direct(sum_reduce), second_grads
    )
    shard_got = add(shard_got, got)
    step = depth // 4
    home, got_reduce = join(input_part(second_grads, heads_across, 0, away, middle), chip(got_reduce))
    home_heads = add(shard_got[:step], exchange(shard_got[step:], "fsdp", step))[0]
    tail = home_heads[shard].astype(F32) + home_heads[shard + 1].astype(F32)
    home_heads = jnp.concatenate(
        [home_heads[:shard]] + [v[None] for v in in_terms(tail, 2)] + [jnp.zeros((14, line), BF)], axis=0
    )
    from_second, from_first, heads_got, grad_reduce_weight, unpacked = join(
        to_owner(home),
        from_first,
        [home_heads, peer(home_heads, 2), peer(home_heads, 4)],
        unpack_reduce(me_array, got_reduce),
        unpack_expand(wide_expand, depth, hidden, width, share),
    )
    grad_expand_weight, grad_output_weight, small_sum = unpacked
    last_head, near_heads, grad_in = join(
        peer(heads_got[0], 2 * (middle - 1)),
        [peer(v, 1) for v in heads_got],
        input_sum(grad_pre, from_first, from_second),
    )
    heads_got = [*heads_got, last_head, *near_heads, peer(last_head, 1)]
    small_sum = small_sum.reshape(-1)
    grad_query_weight, grad_key_weight, grad_value_weight, wide_biases = unpack_heads(
        me_array, heads_got, shard, width
    )
    own_shard = lambda v: lax.dynamic_slice_in_dim(v, my_shard * shard, shard, 0)

    vec = [small_sum[i * shard : (i + 1) * shard] for i in range(len(vectors))]
    vec_expand = small_sum[len(vectors) * shard : len(vectors) * shard + hidden // depth]
    return (
        result.reshape(batch, rows, width),
        grad_in,
        grad_query_weight,
        own_shard(wide_biases[0]),
        grad_key_weight,
        grad_value_weight,
        own_shard(wide_biases[2]),
        grad_output_weight,
        vec[0],
        vec[1],
        vec[2],
        grad_expand_weight,
        vec_expand,
        grad_reduce_weight,
        vec[3],
        vec[4],
        vec[5],
    )


def solution(mesh):
    seq = P("fsdp", "ctx", None)
    mat = P("fsdp", None)
    vec = P("fsdp")
    in_specs = (
        seq,
        P("fsdp", "ctx"),
        mat,
        vec,
        mat,
        mat,
        vec,
        mat,
        vec,
        vec,
        vec,
        mat,
        vec,
        mat,
        vec,
        vec,
        vec,
        seq,
    )
    out_specs = (seq, seq, mat, vec, mat, mat, vec, mat, vec, vec, vec, mat, vec, mat, vec, vec, vec)
    count, depth = mesh.shape["ctx"], mesh.shape["fsdp"]

    def layer(*args):
        width, hidden = args[0].shape[2], args[11].shape[1]
        piece, own_width = hidden // depth // count, width // count
        tiled = count == 8 and depth == 4 and args[0].shape[0] == 2 and piece % LANES == 0 and own_width == LANES
        tiled = tiled and width // depth // count % 16 == 0
        return (body if tiled else plain_body)(*args)

    return jax.shard_map(layer, mesh=mesh, in_specs=in_specs, out_specs=out_specs, check_vma=False)
```

```python
import functools

import jax
import jax.numpy as jnp
from jax import lax
from jax.experimental import pallas as pl
from jax.experimental.pallas import tpu as pltpu
from jax.sharding import PartitionSpec as P

HEAD = 64
LANES = 128
VMEM_LIMIT = 62 << 20
COST_SHARE = 64
EPS = 1e-05
BIG = 1e30
LOG2E = 1.4426950408889634
SQRT_HALF = 0.7071067811865476
DENSITY = 0.3989422804014327
BF = jnp.bfloat16
F32 = jnp.float32


def dot_nn(left, right):
    return jnp.dot(left, right, preferred_element_type=F32)


def dot_tn(left, right):
    return lax.dot_general(left, right, (((0,), (0,)), ((), ())), preferred_element_type=F32)


def dot_nt(left, right):
    return lax.dot_general(left, right, (((1,), (1,)), ((), ())), preferred_element_type=F32)


def exchange(value, axis, k):
    count = lax.axis_size(axis)
    return lax.ppermute(value, axis, [(i, i ^ k) for i in range(count)])


def peer(value, k):
    return exchange(value, "ctx", k)


def after(value, *needed):
    return lax.optimization_barrier((value, needed))[0]


def join(*values):
    return lax.optimization_barrier(values)


def plane_list(count):
    return list(range(0, count, 2)) + list(range(1, count, 2))


def plane_order():
    return plane_list(lax.axis_size("ctx"))


def gather_even(value, low_first):
    count = lax.axis_size("ctx")
    got = {0: value}
    for k in range(2, count, 2):
        bits = [1 << b for b in range(1, count.bit_length()) if k >> b & 1]
        step = bits[-1] if low_first else bits[0]
        got[k] = peer(got[k ^ step], step)
    return [got[k] for k in range(0, count, 2)]


def by_owner(parts, axis, order=None, mesh_axis="ctx"):
    order = order or plane_order()
    stacked = jnp.stack([parts[order.index(k)] for k in range(len(order))])
    me = lax.axis_index(mesh_axis)
    return jnp.concatenate(
        [lax.dynamic_index_in_dim(stacked, me ^ g, 0, keepdims=False) for g in range(len(order))], axis=axis
    )


def rows_to_heads(value, width):
    count = lax.axis_size("ctx")
    me = lax.axis_index("ctx")
    mine, other = [], []
    for k in range(0, count, 2):
        to = me ^ k
        first = lax.dynamic_slice_in_dim(value, to * width, width, 1)
        second = lax.dynamic_slice_in_dim(value, (to ^ 1) * width, width, 1)
        got = jnp.concatenate([first, second], axis=1)
        if k:
            got = peer(got, k)
        mine.append(got[:, :width])
        other.append(got[:, width:])
    return jnp.concatenate(mine + [peer(jnp.concatenate(other, axis=0), 1)], axis=0)


def heads_to_rows(value):
    count = lax.axis_size("ctx")
    rows, width = value.shape[0] // count, value.shape[1]
    half = value.shape[0] // 2
    both = jnp.concatenate([value[:half], peer(value[half:], 1)], axis=1)
    even, odd = [], []
    for i, k in enumerate(range(0, count, 2)):
        got = both[i * rows : (i + 1) * rows]
        if k:
            got = peer(got, k)
        even.append(got[:, :width])
        odd.append(got[:, width:])
    return even + odd


def reduce_even(blocks, low_first):
    count = lax.axis_size("ctx")
    bits = [1 << b for b in range(1, count.bit_length() - 1)]
    if not low_first:
        bits = bits[::-1]
    held = dict(zip(range(0, count, 2), blocks))
    for bit in bits:
        sent = [k for k in held if k & bit]
        got = peer(jnp.stack([held[k] for k in sent]), bit)
        got = {k ^ bit: got[i] for i, k in enumerate(sent)}
        held = {k: (held[k].astype(F32) + got[k].astype(F32)).astype(BF) for k in held if not k & bit}
    return held[0]


def gather_shards(value):
    depth = lax.axis_size("fsdp")
    parts = [value[None]] + [exchange(value, "fsdp", j)[None] for j in range(1, depth)]
    return by_owner(parts, 0, list(range(depth)), "fsdp")


def reduce_shards(value):
    depth = lax.axis_size("fsdp")
    me = lax.axis_index("fsdp")
    total = lax.dynamic_index_in_dim(value, me, 0, keepdims=False).astype(F32)
    for j in range(1, depth):
        sent = lax.dynamic_index_in_dim(value, me ^ j, 0, keepdims=False)
        total = total + exchange(sent, "fsdp", j).astype(F32)
    return total


def gather_doubling(value):
    got = value[None]
    step = 1
    while step < lax.axis_size("fsdp"):
        got = jnp.concatenate([got, exchange(got, "fsdp", step)], axis=0)
        step *= 2
    return got


def in_terms(vector, count):
    terms = []
    for _ in range(count):
        terms.append(vector.astype(BF))
        vector = vector - terms[-1].astype(F32)
    return terms


def whole(shape):
    return pl.BlockSpec(shape, lambda *i: (0,) * len(shape))


def params(limit=VMEM_LIMIT):
    return pltpu.CompilerParams(vmem_limit_bytes=limit)


def cost(flops, size, exps=0):
    return pl.CostEstimate(
        flops=flops // COST_SHARE, bytes_accessed=size // COST_SHARE, transcendentals=exps // COST_SHARE
    )


def mask_columns(seg, bits):
    lane = jnp.arange(LANES) % HEAD
    bit = (seg[:, None] >> jnp.minimum(lane // 2, 30)) & 1
    flip = bit ^ (lane & 1)
    used = lane < 2 * bits
    for_query = jnp.where(used & (flip == 1), -BIG, 0.0).astype(BF)
    for_key = jnp.where(used, 1 - flip, ((lane >= 60) & (lane < 63)).astype(jnp.int32)).astype(BF)
    return for_query, for_key


def lane_index():
    return lax.broadcasted_iota(jnp.int32, (1, LANES), 1)


def merge(main, extra, h):
    lane = lane_index()
    return jnp.where((lane < HEAD) if h == 0 else (lane >= HEAD), main, extra)


def with_terms(extra, number):
    lane = lane_index() % HEAD
    first = number.astype(BF).astype(F32)
    rest = number - first
    second = rest.astype(BF).astype(F32)
    third = rest - second
    terms = jnp.where(lane == 60, first, jnp.where(lane == 61, second, third)).astype(BF)
    return jnp.where((lane >= 60) & (lane < 63), terms, extra)


def forward_kernel(q, k, v, mask_q, mask_k, out, lse, key_side, value_side, *, heads):
    lane = lane_index()

    @pl.when(pl.program_id(0) == 0)
    def _():
        for h in range(heads):
            key_side[h] = merge(k[...], mask_k[...], h)
            value_side[h] = merge(v[...], jnp.ones((1, LANES), BF), h)

    whole, whole_lse = None, None
    for h in range(heads):
        scores = dot_nt(merge(q[...], mask_q[...], h), key_side[h])
        top = jnp.max(scores, axis=1, keepdims=True)
        weights = jnp.exp2(scores - top).astype(BF)
        both = dot_nn(weights, value_side[h])
        total = pltpu.roll(both, HEAD, 1)
        context, log_total = both / total, top + jnp.log2(total)
        if whole is None:
            whole, whole_lse = context, log_total
        else:
            whole = jnp.where(lane < HEAD, whole, context)
            whole_lse = jnp.where(lane < HEAD, whole_lse, log_total)
    out[...] = whole.astype(BF)
    lse[...] = whole_lse


def attend(qkv, mask_q, mask_k, heads, block):
    count = qkv.shape[0]
    part = lambda j: pl.BlockSpec((block, LANES), lambda i: (i, j))
    full = lambda j: pl.BlockSpec((count, LANES), lambda i: (0, j))
    products = 2 * 2 * count * count * LANES * heads
    return pl.pallas_call(
        functools.partial(forward_kernel, heads=heads),
        grid=(count // block,),
        in_specs=[part(0), full(1), full(2), part(0), full(0)],
        out_specs=[part(0), part(0)],
        out_shape=[jax.ShapeDtypeStruct((count, LANES), BF), jax.ShapeDtypeStruct((count, LANES), F32)],
        scratch_shapes=[pltpu.VMEM((heads, count, LANES), BF), pltpu.VMEM((heads, count, LANES), BF)],
        compiler_params=params(),
        cost_estimate=cost(products * 2, 12 * count * LANES, count * count * heads),
        name="attend",
    )(qkv, qkv, qkv, mask_q, mask_k)


def backward_kernel(*refs, heads, first, steps, total, block, pieces):
    q, k, v, mask_q, mask_k, out, lse = refs[:7]
    parts = refs[7 : 7 + pieces]
    refs = refs[7 + pieces :]
    if first:
        grads_before, dk_before, dv_before = refs[:3]
        refs = refs[3:]
    grads = refs[0]
    if steps < total:
        dk_t, dv_t = refs[1:3]
        key_side, value_side, dc_all = refs[3:]
    else:
        key_side, value_side, dc_all, dk_t, dv_t = refs[1:]
    lane = lane_index()
    step = pl.program_id(0)

    @pl.when(step == 0)
    def _():
        ones = ((lane % HEAD >= 60) & (lane % HEAD < 63)).astype(F32).astype(BF)
        for h in range(heads):
            key_side[h] = merge(k[...], mask_k[...], h)
            value_side[h] = merge(v[...], ones, h)
        if first:
            dk_t[...] = dk_before[...]
            dv_t[...] = dv_before[...]
            grads[: first * block, :LANES] = grads_before[...]
        else:
            dk_t[...] = jnp.zeros_like(dk_t)
            dv_t[...] = jnp.zeros_like(dv_t)
        if pieces == 1:
            dc_all[...] = parts[0][...]
        else:
            for i in range(pieces):
                dc_all[i * block : (i + 1) * block, :] = parts[i][:, :LANES]
                dc_all[(pieces + i) * block : (pieces + i + 1) * block, :] = parts[i][:, LANES:]

    dc = dc_all.at[pl.ds(pl.multiple_of((first + step) * block, block), block), :]
    product = dc[...].astype(F32) * out[...].astype(F32)
    low = jnp.sum(jnp.where(lane < HEAD, product, 0.0), axis=1, keepdims=True)
    high = jnp.sum(jnp.where(lane < HEAD, 0.0, product), axis=1, keepdims=True)
    query_extra = with_terms(mask_q[...], -pltpu.roll(lse[...], HEAD, 1))
    grad_extra = with_terms(jnp.zeros((1, LANES), BF), jnp.where(lane < HEAD, -high, -low))
    q_t, dc_t = q[...].T, dc[...].T
    dq = None
    for h in range(heads):
        probs = jnp.exp2(dot_nt(merge(q[...], query_extra, h), key_side[h]))
        centred = dot_nt(merge(dc[...], grad_extra, h), value_side[h])
        ds = (probs * centred).astype(BF)
        part = dot_nn(ds, key_side[h])
        dq = part if dq is None else jnp.where(lane < HEAD, dq, part)
        own = slice(HEAD * h, HEAD * h + HEAD)
        dk_t[own, :] += dot_nn(q_t[own, :], ds)
        dv_t[own, :] += dot_nn(dc_t[own, :], probs.astype(BF))
    at = step * block if steps < total else (first + step) * block
    grads[pl.ds(pl.multiple_of(at, block), block), :LANES] = (dq.astype(BF).astype(F32) * HEAD**-0.5).astype(BF)
    if steps == total:

        @pl.when(step == steps - first - 1)
        def _():
            grads[:, LANES : 2 * LANES] = (dk_t[...] * (1.0 / LOG2E)).T.astype(BF)
            grads[:, 2 * LANES :] = dv_t[...].T.astype(BF)


def attend_back(qkv, mask_q, mask_k, dc, out, lse, heads, block, part=None, before=None, place=0):
    dc = dc if isinstance(dc, list) else [dc]
    count = qkv.shape[0]
    total = count // block
    first = total // 2 if part == 1 else 0
    steps = total // 2 if part == 0 else total
    piece = lambda j: pl.BlockSpec((block, LANES), lambda i: (first + i, j))
    full = lambda j: pl.BlockSpec((count, LANES), lambda i: (0, j))
    products = 5 * 2 * count * count * LANES * heads
    side = (LANES, count)
    shapes = [jax.ShapeDtypeStruct((count, 3 * LANES), BF)]
    scratch = [
        pltpu.VMEM((heads, count, LANES), BF),
        pltpu.VMEM((heads, count, LANES), BF),
        pltpu.VMEM((count, LANES), BF),
    ]
    if part == 0:
        shapes = [jax.ShapeDtypeStruct((count // 2, LANES), BF)] + [jax.ShapeDtypeStruct(side, F32)] * 2
    else:
        scratch += [pltpu.VMEM(side, F32)] * 2
    before = before or []
    got = pl.pallas_call(
        functools.partial(
            backward_kernel, heads=heads, first=first, steps=steps, total=total, block=block, pieces=len(dc)
        ),
        grid=(steps - first,),
        in_specs=[piece(0), full(1), full(2), piece(0), full(0), piece(0), piece(0)]
        + [pl.BlockSpec((block if len(dc) > 1 else count, v.shape[1]), lambda i: (place, 0)) for v in dc]
        + [whole(v.shape) for v in before],
        out_specs=[whole(v.shape) for v in shapes],
        out_shape=shapes,
        scratch_shapes=scratch,
        compiler_params=params(),
        cost_estimate=cost(products, 16 * count * LANES, count * count * heads),
        name="attend_back",
    )(qkv, qkv, qkv, mask_q, mask_k, out, lse, *dc, *before)
    return got if part == 0 else got[0]


def project_kernel(*refs, blocks, rows, bits):
    weight, bias, factor, out, mask_q, mask_k = refs[blocks:]
    lane = lane_index() % HEAD
    used = lane < 2 * bits
    fixed = ((lane >= 60) & (lane < 63)).astype(F32).astype(BF)
    for i, ref in enumerate(refs[:blocks]):
        at = slice(i * rows, (i + 1) * rows)
        got = (dot_nn(ref[:rows, :], weight[...]) + bias[...]) * factor[...]
        out[at, :] = got.astype(BF)
        parts = ref[rows : rows + 16, : 2 * rows].astype(F32)
        number = (parts[:8, :rows] * 64 + parts[:8, rows:]).T[:, :1].astype(jnp.int32)
        flip = ((number >> (lane // 2)) & 1) ^ (lane & 1)
        mask_q[at, :] = jnp.where(used & (flip == 1), -BIG, 0.0).astype(BF)
        mask_k[at, :] = jnp.where(used, (1 - flip).astype(F32).astype(BF), fixed)


def project(blocks, rows, weight, bias, factor, bits):
    width, line = weight.shape
    args = (*blocks, weight, bias[None], factor[None])
    count = rows * len(blocks)
    shapes = [(count, line), (count, LANES), (count, LANES)]
    return pl.pallas_call(
        functools.partial(project_kernel, blocks=len(blocks), rows=rows, bits=bits),
        in_specs=[whole(v.shape) for v in args],
        out_specs=[whole(v) for v in shapes],
        out_shape=[jax.ShapeDtypeStruct(v, BF) for v in shapes],
        grid=(1,),
        compiler_params=params(),
        cost_estimate=cost(2 * count * width * line, 2 * count * (width + line)),
        name="project",
    )(*args)


def flatten_blocks(blocks):
    flat, parts = [], []
    for n, block in enumerate(blocks):
        first = 0
        for part in block:
            flat.append(part)
            parts.append((n, first))
            first += part.shape[0]
    return flat, tuple(parts)


def assemble_kernel(me, *refs, parts, thin, folds):
    out = refs[-1]
    shard = len({n for n, _ in parts}) * thin
    block = refs[0].shape[2]
    order = plane_list(len({n for n, _ in parts}))
    for ref, (n, first) in zip(refs, parts):
        for z in range(ref.shape[0]):
            row = pl.multiple_of((first + z) * shard + (me[0] ^ order[n]) * thin, thin)
            for f in range(folds):
                out[pl.ds(row, thin), f * block : (f + 1) * block] = ref[z, f * thin : (f + 1) * thin, :]


def assemble_output(blocks, shard, thin, me):
    flat, parts = flatten_blocks(blocks)
    _, tall, block = flat[0].shape
    strip = tall - shard
    folds = strip // thin
    width = folds * block
    specs = [pl.BlockSpec((v.shape[0], strip, block), lambda i: (0, shard // strip, 0)) for v in flat]
    return pl.pallas_call(
        functools.partial(assemble_kernel, parts=parts, thin=thin, folds=folds),
        grid=(1,),
        in_specs=[pl.BlockSpec(memory_space=pltpu.SMEM)] + specs,
        out_specs=whole((width, width)),
        out_shape=jax.ShapeDtypeStruct((width, width), BF),
        compiler_params=params(),
        cost_estimate=cost(0, 4 * width * width),
        name="assemble_output",
    )(me, *flat)


def branch_kernel(me, *refs, pieces, aliased):
    weight, tokens, bias, gain, shift = refs[pieces : pieces + 5]
    context, hidden, low, normed, inverse = refs[pieces + 5 + aliased :]
    second = (me[0] & 1) == 1
    pair = refs[0].shape[1]
    for i in range(pieces):
        at = pl.multiple_of(((me[0] ^ (2 * i)) // 2) * pair, pair)
        got = refs[i][...]
        swapped = jnp.concatenate([got[:, pair // 2 :], got[:, : pair // 2]], axis=1)
        context[:, pl.ds(at, pair)] = jnp.where(second, swapped, got)
    total = tokens[...] + dot_nn(context[...], weight[...]) + bias[...]
    mean = jnp.mean(total, axis=1, keepdims=True)
    centred = total - mean
    scale = lax.rsqrt(jnp.mean(centred * centred, axis=1, keepdims=True) + EPS)
    unit = centred * scale
    out = unit * gain[...] + shift[...]
    hidden[...] = out
    low[...] = out.astype(BF)
    normed[...] = unit
    inverse[...] = jnp.broadcast_to(scale, inverse.shape)


def branch(s, me, pieces, weight, tokens, bias, gain, shift, earlier):
    batch, rows, width = tokens.shape
    at = pl.BlockSpec((None, rows, width), lambda i: (s, 0, 0))
    thin = pl.BlockSpec((None, rows, LANES), lambda i: (s, 0, 0))
    vec = whole((1, width))
    earlier = earlier or ()
    first = 1 + len(pieces) + 5
    full = lambda t: jax.ShapeDtypeStruct((batch, rows, width), t)
    return pl.pallas_call(
        functools.partial(branch_kernel, pieces=len(pieces), aliased=len(earlier)),
        grid=(1,),
        in_specs=[pl.BlockSpec(memory_space=pltpu.SMEM)]
        + [whole(v.shape) for v in pieces]
        + [whole(weight.shape), at, vec, vec, vec]
        + [pl.BlockSpec(memory_space=pl.ANY)] * len(earlier),
        out_specs=[at, at, at, at, thin],
        out_shape=[full(BF), full(F32), full(BF), full(F32), jax.ShapeDtypeStruct((batch, rows, LANES), F32)],
        input_output_aliases={first + i: i for i in range(len(earlier))},
        compiler_params=params(),
        cost_estimate=cost(2 * rows * width * width, 2 * width * width + 18 * rows * width),
        name="branch",
    )(me, *pieces, weight, tokens, bias[None], gain[None], shift[None], *earlier)


def norm_back(grad, normed, inverse, gain):
    scaled = grad * gain
    first = jnp.mean(scaled, axis=1, keepdims=True)
    second = jnp.mean(scaled * normed, axis=1, keepdims=True)
    return inverse * (scaled - first - normed * second)


def feed_kernel(*refs, middle, depth, parts):
    low, inverse, bias_even, bias_odd, bias_reduce, gain_second, shift_second, gain_first = refs[:8]
    hidden_at, cot_at, normed_at, second_even, second_odd = refs[8:13]
    blocks = refs[13 : 13 + len(parts)]
    refs = refs[13 + len(parts) :]
    act_even, act_odd, de_even, de_odd, sums_even, sums_odd, result_at, dr_at, du, da, sums_second, sums_first = refs[:12]
    w_first, w_second, slope, hidden, cot, normed, result, dr, total, block_sems, second_sems, sems = refs[12:]
    step = pl.program_id(0)
    rows, width = total.shape
    shard, block = w_first.shape[3], w_first.shape[4]
    chunk = 64

    def first_copies(i):
        made = []
        for j, (ref, (n, first)) in enumerate(zip(blocks, parts)):
            if n % middle == i:
                target = w_first.at[i, n // middle, pl.ds(first, ref.shape[0])]
                made.append(pltpu.make_async_copy(ref.at[:, :shard, :], target, block_sems.at[j]))
        return made

    def second_copies(i):
        return [
            pltpu.make_async_copy(ref.at[:, i], w_second.at[i, parity], second_sems.at[i, parity])
            for parity, ref in enumerate((second_even, second_odd))
        ]

    rest = [
        pltpu.make_async_copy(source, target, sems.at[i])
        for i, (source, target) in enumerate(((hidden_at, hidden), (cot_at, cot), (normed_at, normed)))
    ]
    back = [
        pltpu.make_async_copy(source, target, sems.at[3 + i])
        for i, (source, target) in enumerate(((result, result_at), (dr, dr_at)))
    ]

    @pl.when(step == 0)
    def _():
        for i in range(middle):
            for copy in first_copies(i) + second_copies(i):
                copy.start()
        for copy in rest:
            copy.start()
        sums_second[...] = jnp.zeros_like(sums_second)
        sums_first[...] = jnp.zeros_like(sums_first)

    for i in range(middle):

        @pl.when(step == i)
        def _():
            for copy in first_copies(i) + second_copies(i):
                copy.wait()

    @pl.when(step < middle)
    def _():
        part = None
        for parity, (bias, act) in enumerate(((bias_even, act_even), (bias_odd, act_odd))):
            for at in (slice(0, rows // 2), slice(rows // 2, rows)):
                value = bias[...]
                for z in range(depth):
                    value = value + dot_nn(low[at, z * shard : (z + 1) * shard], w_first[step, parity, z])
                cdf = 0.5 * (1.0 + lax.erf(value * SQRT_HALF))
                act[at, :] = (value * cdf).astype(BF)
                grad = cdf + value * DENSITY * jnp.exp(-0.5 * value * value)
                slope[step, parity, at, :] = grad.astype(BF)
            got = dot_nn(act[...], w_second[step, parity].reshape(block, width))
            part = got if part is None else part + got

        @pl.when(step == 0)
        def _():
            total[...] = part + bias_reduce[...]

        @pl.when(step > 0)
        def _():
            total[...] += part

    @pl.when(step == middle - 1)
    def _():
        rest[0].wait()
        rest[1].wait()

        @pl.loop(0, rows // chunk)
        def _(i):
            at = pl.ds(pl.multiple_of(i * chunk, chunk), chunk)
            value = total[at, :] + hidden[at, :]
            mean = jnp.mean(value, axis=1, keepdims=True)
            centred = value - mean
            scale = lax.rsqrt(jnp.mean(centred * centred, axis=1, keepdims=True) + EPS)
            unit = centred * scale
            result[at, :] = unit * gain_second[...] + shift_second[...]
            grad = cot[at, :]
            grad_sum = norm_back(grad, unit, scale, gain_second[...])
            total[at, :] = grad_sum
            rounded = grad_sum.astype(BF)
            dr[at, :] = rounded
            sums_second[0:1, :] += jnp.sum(grad * unit, axis=0, keepdims=True)
            sums_second[1:2, :] += jnp.sum(grad, axis=0, keepdims=True)
            sums_second[2:3, :] += jnp.sum(rounded.astype(F32), axis=0, keepdims=True)

        for copy in back:
            copy.start()

    @pl.when(step >= middle)
    def _():
        i = step - middle
        for parity, (de, sums) in enumerate(((de_even, sums_even), (de_odd, sums_odd))):
            grad = dot_nt(dr[...], w_second[i, parity].reshape(block, width)) * slope[i, parity].astype(F32)
            rounded = grad.astype(BF)
            de[...] = rounded
            sums[...] = jnp.sum(rounded.astype(F32), axis=0, keepdims=True)
            for z in range(depth):
                total[:, z * shard : (z + 1) * shard] += dot_nt(rounded, w_first[i, parity, z])

    @pl.when(step == 2 * middle - 1)
    def _():
        rest[2].wait()

        @pl.loop(0, rows // chunk)
        def _(i):
            at = pl.ds(pl.multiple_of(i * chunk, chunk), chunk)
            grad, unit = total[at, :], normed[at, :]
            grad_sum = norm_back(grad, unit, inverse[at, 0:1], gain_first[...])
            du[at, :] = grad_sum
            rounded = grad_sum.astype(BF)
            da[at, :] = rounded
            sums_first[0:1, :] += jnp.sum(grad * unit, axis=0, keepdims=True)
            sums_first[1:2, :] += jnp.sum(grad, axis=0, keepdims=True)
            sums_first[2:3, :] += jnp.sum(rounded.astype(F32), axis=0, keepdims=True)

        for copy in back:
            copy.wait()


def feed(low, inverse, bias_halves, bias_reduce, gain_second, shift_second, gain_first, hidden, cot, normed, second, blocks, shard):
    rows, width = low.shape
    depth, middle, piece, _ = second[0].shape
    block = depth * piece
    flat, parts = flatten_blocks(blocks)
    ahead = lambda i: jnp.minimum(i, middle - 1)
    behind = lambda i: jnp.maximum(i - middle, 0)
    bias = pl.BlockSpec((None, 1, block), lambda i: (ahead(i), 0, 0))
    sums = pl.BlockSpec((None, 1, block), lambda i: (behind(i), 0, 0))
    act = pl.BlockSpec((rows, block), lambda i: (0, ahead(i)))
    de = pl.BlockSpec((rows, block), lambda i: (0, behind(i)))
    full, vec, anywhere = whole((rows, width)), whole((1, width)), pl.BlockSpec(memory_space=pl.ANY)
    shape = jax.ShapeDtypeStruct
    return pl.pallas_call(
        functools.partial(feed_kernel, middle=middle, depth=depth, parts=parts),
        grid=(2 * middle,),
        in_specs=[full, whole((rows, LANES)), bias, bias, vec, vec, vec, vec] + [anywhere] * (5 + len(flat)),
        out_specs=[act, act, de, de, sums, sums, anywhere, anywhere, full, full, whole((8, width)), whole((8, width))],
        out_shape=[shape((rows, middle * block), BF)] * 4
        + [shape((middle, 1, block), F32)] * 2
        + [shape((rows, width), F32), shape((rows, width), BF), shape((rows, width), F32), shape((rows, width), BF)]
        + [shape((8, width), F32)] * 2,
        scratch_shapes=[
            pltpu.VMEM((middle, 2, depth, shard, block), BF),
            pltpu.VMEM((middle, 2, depth, piece, width), BF),
            pltpu.VMEM((middle, 2, rows, block), BF),
            pltpu.VMEM((rows, width), F32),
            pltpu.VMEM((rows, width), F32),
            pltpu.VMEM((rows, width), F32),
            pltpu.VMEM((rows, width), F32),
            pltpu.VMEM((rows, width), BF),
            pltpu.VMEM((rows, width), F32),
            pltpu.SemaphoreType.DMA((len(flat),)),
            pltpu.SemaphoreType.DMA((middle, 2)),
            pltpu.SemaphoreType.DMA((5,)),
        ],
        compiler_params=params(),
        cost_estimate=cost(16 * rows * width * middle * block, 8 * width * middle * block + 40 * rows * width),
        name="feed",
    )(
        low,
        inverse,
        *bias_halves,
        bias_reduce[None],
        gain_second[None],
        shift_second[None],
        gain_first[None],
        hidden,
        cot,
        normed,
        *second,
        *flat,
    )


def context_back_kernel(me, da, weight, *refs, middle):
    outs, whole_grad = refs[:-1], refs[-1]
    whole_grad[...] = dot_nt(da[...], weight[...]).astype(BF)
    rows = da.shape[0]
    mine, other = outs
    width = mine.shape[1]
    second = (me[0] & 1) == 1
    for i in range(middle):
        at = pl.multiple_of(((me[0] ^ (2 * i)) // 2) * 2 * width, 2 * width)
        pair = whole_grad[:, pl.ds(at, 2 * width)]
        low, high = pair[:, :width], pair[:, width:]
        mine[i * rows : (i + 1) * rows, :] = jnp.where(second, high, low)
        other[i * rows : (i + 1) * rows, :] = jnp.where(second, low, high)


def context_back(me, da, weight, own_width, middle):
    rows, width = da.shape
    shape = (middle * rows, own_width)
    return pl.pallas_call(
        functools.partial(context_back_kernel, middle=middle),
        grid=(1,),
        in_specs=[pl.BlockSpec(memory_space=pltpu.SMEM), whole(da.shape), whole(weight.shape)],
        out_specs=[whole(shape)] * 2,
        out_shape=[jax.ShapeDtypeStruct(shape, BF)] * 2,
        scratch_shapes=[pltpu.VMEM((rows, width), BF)],
        compiler_params=params(),
        cost_estimate=cost(2 * rows * width * width, 2 * width * width + 4 * rows * width),
        name="context_back",
    )(me, da, weight)


def gradient_kernel(act, other_act, grad, other_grad, out):
    depth, piece, width = out.shape
    total = dot_tn(act[...], grad[...]) + dot_tn(other_act[...], other_grad[...])
    out[...] = total.astype(BF).reshape(depth, piece, width)


def reduce_gradient(act, other_act, grad, other_grad, depth, piece):
    rows, width = grad.shape
    block = depth * piece
    middle = act.shape[1] // block
    column = pl.BlockSpec((rows, block), lambda i: (0, i))
    full = whole((rows, width))
    return pl.pallas_call(
        gradient_kernel,
        grid=(middle,),
        in_specs=[column, column, full, full],
        out_specs=pl.BlockSpec((depth, None, piece, width), lambda i: (0, i, 0, 0)),
        out_shape=jax.ShapeDtypeStruct((depth, middle, piece, width), BF),
        compiler_params=params(),
        cost_estimate=cost(4 * rows * width * middle * block, 2 * width * middle * block + 4 * rows * middle * block),
        name="reduce_gradient",
    )(act, other_act, grad, other_grad)


EXTRA = 16


def expand_gradient_kernel(
    me, low, other_low, context, other_context, de, other_de, da, other_da, small, *outs, middle, own, share
):
    block = de.shape[1] // middle
    depth = small.shape[0]
    shard = low.shape[1] // depth
    tall = shard + EXTRA
    first, second = low[...].T, other_low[...].T
    third, fourth = context[...].T, other_context[...].T
    kept_a, sent_a, kept_b, sent_b = outs
    for i in range(middle):
        at = slice(i * block, (i + 1) * block)
        target = me[0] ^ (2 * i)
        wide = (dot_nn(first, de[:, at]) + dot_nn(second, other_de[:, at])).astype(BF)
        where = pl.ds(pl.multiple_of(target * own, own), own)
        thin = (dot_nn(third, da[:, where]) + dot_nn(fourth, other_da[:, where])).astype(BF)
        for out, n, part in (
            (sent_a if i >= 2 else kept_a, i % 2, range(depth // 2)),
            (sent_b if i % 2 else kept_b, i // 2, range(depth // 2, depth)),
        ):
            for z in part:
                row = (z - part[0]) * tall
                out[n, row : row + shard, :block] = wide[z * shard : (z + 1) * shard]
                out[n, row : row + shard, block:] = thin[z * shard : (z + 1) * shard]
                line = small[z : z + 1, pl.ds(pl.multiple_of(target * share, share), share)].astype(BF)
                line = jnp.concatenate([line, jnp.zeros((1, block + own - share), BF)], axis=1)
                out[n, row + shard : row + tall, :] = jnp.broadcast_to(line, (EXTRA, block + own))


def expand_gradient(me, low, other_low, context, other_context, de, other_de, da, other_da, small, own):
    rows, width = low.shape
    middle = 4
    depth = small.shape[0]
    block = de.shape[1] // middle
    args = (low, other_low, context, other_context, de, other_de, da, other_da, small)
    shape = (2, width // 2 + EXTRA * depth // 2, block + own)
    share = small.shape[1] // (2 * middle)
    return pl.pallas_call(
        functools.partial(expand_gradient_kernel, middle=middle, own=own, share=share),
        grid=(1,),
        in_specs=[pl.BlockSpec(memory_space=pltpu.SMEM)] + [whole(v.shape) for v in args],
        out_specs=[whole(shape)] * 4,
        out_shape=[jax.ShapeDtypeStruct(shape, BF)] * 4,
        compiler_params=params(),
        cost_estimate=cost(4 * rows * width * middle * (block + own), 4 * width * middle * block),
        name="expand_gradient",
    )(me, *args)


def add_kernel(*refs, count):
    for i in range(count):
        mine, got, out = refs[2 * i], refs[2 * i + 1], refs[2 * count + i]
        out[...] = (mine[...].astype(F32) + got[...].astype(F32)).astype(BF)


def add_steps(kept_a, got_a, kept_b, got_b):
    _, rows, width = kept_a.shape
    block = lambda n: pl.BlockSpec((None, rows // 2, width), lambda i: (n, i, 0))
    args = (kept_a, got_a, kept_a, got_a, kept_b, got_b, kept_b, got_b)
    return pl.pallas_call(
        functools.partial(add_kernel, count=4),
        grid=(2,),
        in_specs=[block(n) for n in (0, 0, 1, 1)] * 2,
        out_specs=[pl.BlockSpec((rows // 2, width), lambda i: (i, 0))] * 4,
        out_shape=[jax.ShapeDtypeStruct((rows, width), BF)] * 4,
        compiler_params=params(),
        cost_estimate=cost(0, 12 * rows * width),
        name="add_steps",
    )(*args)


def add_last_kernel(kept_a, got_a, kept_b, got_b, out):
    rows = kept_a.shape[0]
    out[:rows, :] = (kept_a[...].astype(F32) + got_a[...].astype(F32)).astype(BF)
    out[rows:, :] = (kept_b[...].astype(F32) + got_b[...].astype(F32)).astype(BF)


def add_last(kept_a, got_a, kept_b, got_b):
    rows, width = kept_a.shape
    shape = (2 * rows, width)
    return pl.pallas_call(
        add_last_kernel,
        grid=(1,),
        in_specs=[whole((rows, width))] * 4,
        out_specs=whole(shape),
        out_shape=jax.ShapeDtypeStruct(shape, BF),
        compiler_params=params(),
        cost_estimate=cost(0, 12 * rows * width),
        name="add_last",
    )(kept_a, got_a, kept_b, got_b)


def unpack_expand_kernel(blocks, wide, thin, small, *, depth):
    count = blocks.shape[0]
    shard = wide.shape[0]
    block = wide.shape[1] // count
    piece, own = block // depth, thin.shape[1] // count
    for g in range(count):
        for z in range(depth):
            at = (z * count + g) * piece
            wide[:, at : at + piece] = blocks[g, :shard, z * piece : (z + 1) * piece].astype(F32)
        thin[:, g * own : (g + 1) * own] = blocks[g, :shard, block:].astype(F32)
        small[g : g + 1, :] = blocks[g, shard : shard + EXTRA, : small.shape[1]].astype(F32)[0:1]


def unpack_expand(blocks, depth, hidden, width, share):
    shard = blocks.shape[1] - EXTRA
    shapes = [(shard, hidden), (shard, width), (blocks.shape[0], share)]
    return pl.pallas_call(
        functools.partial(unpack_expand_kernel, depth=depth),
        grid=(1,),
        in_specs=[whole(blocks.shape)],
        out_specs=[whole(v) for v in shapes],
        out_shape=[jax.ShapeDtypeStruct(v, F32) for v in shapes],
        compiler_params=params(),
        cost_estimate=cost(0, 6 * shard * (hidden + width)),
        name="unpack_expand",
    )(blocks)


def unpack_reduce_kernel(me, *refs):
    out = refs[-1]
    rows = refs[0].shape[0]
    for n, k in enumerate(plane_list(len(refs) - 1)):
        out[pl.ds(pl.multiple_of((me[0] ^ k) * rows, rows), rows), :] = refs[n][...].astype(F32)


def unpack_reduce(me, blocks):
    rows, width = blocks[0].shape
    shape = (rows * len(blocks), width)
    return pl.pallas_call(
        unpack_reduce_kernel,
        grid=(1,),
        in_specs=[pl.BlockSpec(memory_space=pltpu.SMEM)] + [whole(v.shape) for v in blocks],
        out_specs=whole(shape),
        out_shape=jax.ShapeDtypeStruct(shape, F32),
        compiler_params=params(),
        cost_estimate=cost(0, 6 * shape[0] * width),
        name="unpack_reduce",
    )(me, *blocks)


def input_part_kernel(grads, weight, *refs, with_away):
    got = dot_nn(grads[...], weight[...])
    if with_away:
        got = got + refs[0][...].astype(F32)
        outs = refs[1:]
    else:
        outs = refs
    rows = outs[0].shape[0]
    for i, out in enumerate(outs):
        out[...] = got[i * rows : (i + 1) * rows].astype(BF)


def input_part(grads, weight, half, away=None, pieces=1):
    count, line = grads.shape
    rows, width = count // 2, weight.shape[1]
    more = () if away is None else (away,)
    shape = (rows // pieces, width)
    got = pl.pallas_call(
        functools.partial(input_part_kernel, with_away=away is not None),
        grid=(1,),
        in_specs=[pl.BlockSpec((rows, line), lambda i: (half, 0)), whole(weight.shape)] + [whole(v.shape) for v in more],
        out_specs=[whole(shape)] * pieces,
        out_shape=[jax.ShapeDtypeStruct(shape, BF)] * pieces,
        compiler_params=params(),
        cost_estimate=cost(2 * rows * width * line, 4 * rows * width),
        name="input_part",
    )(grads, weight, *more)
    return got if pieces > 1 else got[0]


def input_kernel(before, *refs):
    out = refs[-1]
    rows = refs[0].shape[0]
    half = len(refs) // 2
    for s in range(2):
        total = before[s * rows : (s + 1) * rows, :]
        for ref in refs[s * half : (s + 1) * half]:
            total = total + ref[...].astype(F32)
        out[s] = total


def input_sum(before, first, second):
    rows, width = first[0].shape
    return pl.pallas_call(
        input_kernel,
        grid=(1,),
        in_specs=[whole(before.shape)] + [whole(v.shape) for v in (*first, *second)],
        out_specs=whole((2, rows, width)),
        out_shape=jax.ShapeDtypeStruct((2, rows, width), F32),
        compiler_params=params(),
        cost_estimate=cost(0, 32 * rows * width),
        name="input_sum",
    )(before, *first, *second)


def unpack_heads_kernel(me, *refs):
    outs, own_bias, bias = refs[-5:-2], refs[-2], refs[-1]
    count = len(refs) - 5
    shard, width = outs[0].shape
    own = width // count
    bias[...] = jnp.zeros_like(bias)
    for n, k in enumerate(plane_list(count)):
        where = pl.ds(pl.multiple_of((me[0] ^ k) * own, own), own)
        tail = refs[n][shard : shard + 16, :].astype(F32)
        for t in range(3):
            at = slice(t * own, (t + 1) * own)
            outs[t][:, where] = refs[n][:shard, at].astype(F32)
            bias[t : t + 1, where] = tail[0:1, at] + tail[1:2, at]
    own_bias[...] = bias[:, pl.ds(pl.multiple_of(me[1] * shard, shard), shard)]


def unpack_heads(me, blocks, shard, width):
    shapes = [(shard, width)] * 3 + [(8, shard)]
    return pl.pallas_call(
        unpack_heads_kernel,
        grid=(1,),
        in_specs=[pl.BlockSpec(memory_space=pltpu.SMEM)] + [whole(v.shape) for v in blocks],
        out_specs=[whole(v) for v in shapes],
        out_shape=[jax.ShapeDtypeStruct(v, F32) for v in shapes],
        scratch_shapes=[pltpu.VMEM((8, width), F32)],
        compiler_params=params(),
        cost_estimate=cost(0, 18 * shard * width),
        name="unpack_heads",
    )(me, *blocks)


def heads_gradient_kernel(*refs, blocks, last):
    grads = refs[blocks]
    if last:
        me, before, sums_before, kept, sent, tokens, turned = refs[blocks + 1 :]
    else:
        out, sums, tokens = refs[blocks + 1 :]
    rows = grads.shape[0] // blocks
    for i, ref in enumerate(refs[:blocks]):
        tokens[i * rows : (i + 1) * rows, :] = ref[:rows, :]
    total = dot_tn(grads[...], tokens[...])
    column = jnp.sum(grads[...].astype(F32), axis=0, keepdims=True)
    if not last:
        out[...] = total
        sums[...] = jnp.broadcast_to(column, sums.shape)
        return
    turned[...] = (total + before[...]).T.astype(BF)
    column = jnp.broadcast_to(column + sums_before[0:1, :], (EXTRA, column.shape[1]))
    first = column.astype(BF).astype(F32)
    place = lax.broadcasted_iota(jnp.int32, (EXTRA, 1), 0)
    extra = jnp.where(place == 0, first, jnp.where(place == 1, column - first, 0.0)).astype(BF)
    depth = 2 * kept.shape[0]
    shard = turned.shape[0] // depth
    for j in range(depth):
        target = (kept, sent)[j // (depth // 2)].at[j % (depth // 2)]
        at = pl.multiple_of((me[0] ^ j) * shard, shard)
        target[:shard, :] = turned[pl.ds(at, shard), :]
        target[shard:, :] = extra


def heads_gradient(blocks, grads, more=None, depth=1):
    line = grads.shape[1]
    width = blocks[0].shape[1]
    last = more is not None
    args = (*blocks, grads) + (more or ())
    specs = [whole(v.shape) for v in (*blocks, grads)]
    scratch = [pltpu.VMEM((grads.shape[0], width), BF)]
    if last:
        shapes = [jax.ShapeDtypeStruct((depth // 2, width // depth + EXTRA, line), BF)] * 2
        specs += [pl.BlockSpec(memory_space=pltpu.SMEM)] + [whole(v.shape) for v in more[1:]]
        scratch.append(pltpu.VMEM((width, line), BF))
    else:
        shapes = [jax.ShapeDtypeStruct((line, width), F32), jax.ShapeDtypeStruct((8, line), F32)]
    return pl.pallas_call(
        functools.partial(heads_gradient_kernel, blocks=len(blocks), last=last),
        grid=(1,),
        in_specs=specs,
        out_specs=[whole(v.shape) for v in shapes],
        out_shape=shapes,
        scratch_shapes=scratch,
        compiler_params=params(),
        cost_estimate=cost(2 * grads.shape[0] * width * line, 2 * grads.shape[0] * width + 6 * width * line),
        name="heads_gradient",
    )(*args)


def normalize(values, gain, shift):
    mean = jnp.mean(values, axis=-1, keepdims=True)
    centred = values - mean
    inverse = lax.rsqrt(jnp.mean(centred * centred, axis=-1, keepdims=True) + EPS)
    normed = centred * inverse
    return normed * gain + shift, normed, inverse


def normalize_back(grad, normed, inverse, gain):
    scaled = grad * gain
    inner = (
        scaled
        - jnp.mean(scaled, axis=-1, keepdims=True)
        - normed * jnp.mean(scaled * normed, axis=-1, keepdims=True)
    )
    return inner * inverse, jnp.sum(grad * normed, axis=0), jnp.sum(grad, axis=0)


def column_sums(values):
    return jnp.sum(values.astype(F32), axis=0)


def plain_body(
    tokens,
    segments,
    query_weight,
    query_bias,
    key_weight,
    value_weight,
    value_bias,
    output_weight,
    output_bias,
    first_gain,
    first_shift,
    expand_weight,
    expand_bias,
    reduce_weight,
    reduce_bias,
    second_gain,
    second_shift,
    cotangent,
):
    batch, rows, width = tokens.shape
    count, depth = lax.axis_size("ctx"), lax.axis_size("fsdp")
    me, my_shard = lax.axis_index("ctx"), lax.axis_index("fsdp")
    shard = query_weight.shape[0]
    hidden = expand_weight.shape[1]
    own_width = width // count
    heads = own_width // HEAD
    piece = hidden // depth // count
    block = depth * piece
    half = hidden // 2
    order = plane_order()
    evens = order[: count // 2]
    scale = HEAD**-0.5
    bits = (count * rows - 1).bit_length()

    columns = lambda w: lax.dynamic_slice_in_dim(w, me * own_width, own_width, 1).astype(BF)
    names = (query_bias, value_bias, output_bias, first_gain, first_shift, reduce_bias, second_gain, second_shift)
    packed = jnp.concatenate(names + (expand_bias,))
    terms = jnp.concatenate(in_terms(packed, 3))
    line = 3 * own_width
    lines = -(-terms.shape[0] // (16 * line)) * 16
    terms = jnp.pad(terms, (0, lines * line - terms.shape[0])).reshape(lines, line)
    own_heads = jnp.concatenate([columns(query_weight), columns(key_weight), columns(value_weight)], axis=1)
    own_heads = gather_shards(jnp.concatenate([own_heads, terms], axis=0))
    packed = own_heads[:, shard:].reshape(depth, lines * line)[:, : 3 * packed.shape[0]]
    packed = jnp.sum(packed.reshape(depth, 3, -1).astype(F32), axis=1)
    own_heads = own_heads[:, :shard].reshape(width, line)
    (bias_query, bias_value, bias_output, gain_first, shift_first, bias_reduce, gain_second, shift_second) = (
        packed[:, i * shard : (i + 1) * shard].reshape(width) for i in range(len(names))
    )
    wide_bias = packed[:, len(names) * shard :].reshape(depth, count, piece)
    bias_halves = [
        jnp.stack([lax.dynamic_index_in_dim(wide_bias, me ^ k, 1, keepdims=False) for k in ks], axis=1).reshape(half)
        for ks in (evens, order[count // 2 :])
    ]
    own_part = lambda v: lax.dynamic_slice_in_dim(v, me * own_width, own_width, 0)
    head_bias = jnp.concatenate([own_part(bias_query), jnp.zeros((own_width,), F32), own_part(bias_value)])
    head_scale = jnp.concatenate([jnp.full((own_width,), scale * LOG2E, F32), jnp.ones((2 * own_width,), F32)])

    thin = shard // count
    folds = width // block
    strip = lax.dynamic_slice_in_dim(output_weight, me * thin, thin, 0).astype(BF)
    strip = jnp.concatenate([strip[:, i * block : (i + 1) * block] for i in range(folds)], axis=0)
    block_expand = lax.dynamic_slice_in_dim(expand_weight.reshape(shard, depth, count * piece), me * piece, piece, 2)
    block_expand = jnp.concatenate([block_expand.reshape(shard, block).astype(BF), strip], axis=0)
    block_expand = lax.all_gather(block_expand, "fsdp", axis=0)
    block_reduce = lax.dynamic_slice_in_dim(reduce_weight, me * piece, piece, 0).astype(BF)
    block_reduce = lax.all_gather(block_reduce, "fsdp", axis=0)

    groups = jnp.stack([w.reshape(shard, count, own_width) for w in (query_weight, key_weight, value_weight)], axis=2)
    half_heads = jnp.concatenate(
        [lax.dynamic_index_in_dim(groups, me ^ k, 1, keepdims=False).reshape(shard, line).astype(BF) for k in evens],
        axis=1,
    )
    half_heads = lax.all_gather(half_heads, "fsdp", axis=0, tiled=True)
    other_heads = peer(half_heads, 1)

    seg = segments
    for b in range(count.bit_length() - 1):
        seg = jnp.concatenate([seg, peer(seg, 1 << b)], axis=1)
    seg = seg.reshape(batch, count, rows)
    seg = jnp.concatenate([seg[:, k] for k in order], axis=1)

    lanes = lambda v: v if own_width == LANES else jnp.pad(v, ((0, 0), (0, LANES - own_width)))
    kept, context_parts = [], []
    for s in range(batch):
        even = jnp.concatenate(gather_even(tokens[s].astype(BF), s % 2 == 0), axis=0)
        odd = peer(even, 1)
        qkv = jnp.concatenate([dot_nn(even, own_heads), dot_nn(odd, own_heads)], axis=0)
        qkv = ((qkv + head_bias) * head_scale).astype(BF)
        if own_width != LANES:
            qkv = jnp.concatenate([lanes(qkv[:, i * own_width : (i + 1) * own_width]) for i in range(3)], axis=1)
        mask_q, mask_k = mask_columns(seg[s], bits)
        out, lse = attend(qkv, mask_q, mask_k, heads, rows)
        kept.append((even, odd, qkv, mask_q, mask_k, out, lse))
        context_parts.append(by_owner(heads_to_rows(out[:, :own_width]), 1))

    got_expand = gather_even(block_expand, True)
    got_expand += [peer(v, 1) for v in got_expand]
    got_reduce = gather_even(block_reduce, False)
    got_reduce += [peer(v, 1) for v in got_reduce]
    full_output = by_owner(
        [
            jnp.concatenate([v[:, shard + i * thin : shard + (i + 1) * thin] for i in range(folds)], axis=2)
            for v in got_expand
        ],
        1,
    ).reshape(width, width)
    middle = count // 2
    expand_halves = [
        jnp.concatenate([v[:, :shard].reshape(width, depth, piece) for v in vs], axis=2).reshape(width, half)
        for vs in (got_expand[:middle], got_expand[middle:])
    ]
    reduce_halves = [
        jnp.concatenate(vs, axis=1).reshape(half, width) for vs in (got_reduce[:middle], got_reduce[middle:])
    ]

    firsts = []
    for s in range(batch):
        branch = dot_nn(context_parts[s], full_output) + bias_output
        firsts.append(normalize(tokens[s] + branch, gain_first, shift_first))
    hidden_in, normed_first, inverse_first = (jnp.concatenate(v, axis=0) for v in zip(*firsts))
    context_low = jnp.concatenate(context_parts, axis=0)
    hidden_low = hidden_in.astype(BF)
    halves = []
    reduced = bias_reduce
    for weight, back, bias in zip(expand_halves, reduce_halves, bias_halves):
        expand = dot_nn(hidden_low, weight) + bias
        cdf = 0.5 * (1.0 + lax.erf(expand * SQRT_HALF))
        active = (expand * cdf).astype(BF)
        slope = cdf + expand * DENSITY * jnp.exp(-0.5 * expand * expand)
        reduced = reduced + dot_nn(active, back)
        halves.append((weight, back, active, slope.astype(BF)))
    result, normed_second, inverse_second = normalize(hidden_in + reduced, gain_second, shift_second)

    grad_out = cotangent.reshape(batch * rows, width)
    grad_sum_second, grad_gain_second, grad_shift_second = normalize_back(
        grad_out, normed_second, inverse_second, gain_second
    )
    grad_reduced = grad_sum_second.astype(BF)
    grad_bias_reduce = column_sums(grad_reduced)

    def chip_sum(make):
        got = peer(make(1).astype(BF), 1)
        return (make(0) + got.astype(F32)).astype(BF)

    sum_reduce = chip_sum(lambda i: dot_tn(halves[i][2], grad_reduced))
    sum_reduce = lax.psum_scatter(sum_reduce, "fsdp", scatter_dimension=0, tiled=True)
    sum_reduce = reduce_even(jnp.split(sum_reduce, middle, axis=0), False)

    grad_hidden = grad_sum_second
    grad_expands = []
    for weight, back, active, slope in halves:
        grad_expand = (dot_nt(grad_reduced, back) * slope.astype(F32)).astype(BF)
        grad_hidden = grad_hidden + dot_nt(grad_expand, weight)
        grad_expands.append(grad_expand)
    grad_bias_expand = [column_sums(g).reshape(depth, middle, piece) for g in grad_expands]
    grad_pre, grad_gain_first, grad_shift_first = normalize_back(
        grad_hidden, normed_first, inverse_first, gain_first
    )
    grad_branch = grad_pre.astype(BF)
    grad_bias_output = column_sums(grad_branch)
    grad_context = dot_nt(grad_branch, full_output).astype(BF)

    sum_expand = chip_sum(lambda i: dot_tn(hidden_low, grad_expands[i])).reshape(width, depth, middle, piece)
    sum_expand = reduce_even([sum_expand[:, :, i].reshape(width, block) for i in range(middle)], True)
    branch_blocks = jnp.concatenate(
        [lax.dynamic_slice_in_dim(grad_branch, (me ^ k) * own_width, own_width, 1) for k in order], axis=1
    )
    sum_output = chip_sum(
        lambda i: dot_tn(context_low, branch_blocks[:, i * width // 2 : (i + 1) * width // 2])
    )
    sum_output = reduce_even(jnp.split(sum_output, middle, axis=1), False)
    sum_expand = jnp.concatenate([sum_expand, sum_output], axis=1)
    sum_expand = lax.psum_scatter(sum_expand, "fsdp", scatter_dimension=0, tiled=True)

    grads = []
    for s in range(batch):
        even, odd, qkv, mask_q, mask_k, out, lse = kept[s]
        dc = lanes(rows_to_heads(grad_context[s * rows : (s + 1) * rows], own_width))
        got = attend_back(qkv, mask_q, mask_k, dc, out, lse, heads, rows)
        if own_width != LANES:
            got = jnp.concatenate([got[:, i * LANES : i * LANES + own_width] for i in range(3)], axis=1)
        grads.append(got)
    middle_row = count * rows // 2
    grad_heads = sum(
        dot_tn(kept[s][0], grads[s][:middle_row]) + dot_tn(kept[s][1], grads[s][middle_row:]) for s in range(batch)
    ).astype(BF)
    grad_head_bias = jnp.pad(
        jnp.stack(in_terms(sum(column_sums(g) for g in grads), 2)), ((0, 14), (0, 0))
    )
    home_heads = jnp.concatenate(
        [grad_heads.reshape(depth, shard, line), jnp.broadcast_to(grad_head_bias, (depth, 16, line))], axis=1
    )
    home_heads = reduce_shards(home_heads)
    home_heads = jnp.concatenate(
        [home_heads[:shard].astype(BF)]
        + [v[None] for v in in_terms(home_heads[shard] + home_heads[shard + 1], 2)]
        + [jnp.zeros((14, line), BF)],
        axis=0,
    )
    back_rows = [heads_to_rows(g) for g in grads]
    back_even = jnp.concatenate([jnp.concatenate(r[:middle], axis=1) for r in back_rows], axis=0)
    back_odd = jnp.concatenate([jnp.concatenate(r[middle:], axis=1) for r in back_rows], axis=0)
    grad_in = grad_pre + dot_nt(back_even, half_heads) + dot_nt(back_odd, other_heads)

    def spread(value, low_first):
        got = gather_even(value, low_first)
        odd = peer(jnp.stack(got), 1)
        return by_owner([v[None] for v in got] + [odd[i : i + 1] for i in range(middle)], 0)

    wide = lax.all_gather(sum_expand, "ctx", axis=0)
    grad_expand_weight = jnp.transpose(wide[:, :, :block].reshape(count, shard, depth, piece), (1, 2, 0, 3))
    grad_expand_weight = grad_expand_weight.reshape(shard, hidden).astype(F32)
    grad_output_weight = jnp.transpose(wide[:, :, block:], (1, 0, 2)).reshape(shard, width).astype(F32)
    grad_reduce_weight = lax.all_gather(sum_reduce, "ctx", axis=0, tiled=True).astype(F32)
    wide_heads = spread(home_heads, True)
    wide_shards = jnp.transpose(wide_heads[:, :shard].reshape(count, shard, 3, own_width), (2, 1, 0, 3))
    grad_query_weight, grad_key_weight, grad_value_weight = (
        wide_shards[i].reshape(shard, width).astype(F32) for i in range(3)
    )
    wide_biases = jnp.sum(wide_heads[:, shard : shard + 2].astype(F32), axis=1).reshape(count, 3, own_width)
    own_shard = lambda v: lax.dynamic_slice_in_dim(v.reshape(width), my_shard * shard, shard, 0)

    vectors = (
        grad_bias_output,
        grad_gain_first,
        grad_shift_first,
        grad_bias_reduce,
        grad_gain_second,
        grad_shift_second,
    )
    wide_bias = by_owner([g[:, i] for g in grad_bias_expand for i in range(middle)], 1)
    small = jnp.concatenate([v.reshape(depth, shard) for v in vectors] + [wide_bias], axis=1)
    for b in range(count.bit_length() - 1):
        small = small + peer(small, 1 << b)
    small = reduce_shards(small)
    vec = [small[i * shard : (i + 1) * shard] for i in range(len(vectors))]
    vec_expand = small[len(vectors) * shard :]
    return (
        result.reshape(batch, rows, width),
        grad_in.reshape(batch, rows, width),
        grad_query_weight,
        own_shard(wide_biases[:, 0]),
        grad_key_weight,
        grad_value_weight,
        own_shard(wide_biases[:, 2]),
        grad_output_weight,
        vec[0],
        vec[1],
        vec[2],
        grad_expand_weight,
        vec_expand,
        grad_reduce_weight,
        vec[3],
        vec[4],
        vec[5],
    )


def even_pieces(own, other):
    rows = own.shape[0]
    both = jnp.concatenate([own, other], axis=1)
    middle = lax.axis_size("ctx") // 2
    rows = rows // middle
    pieces = [both[i * rows : (i + 1) * rows] for i in range(middle)]
    return [pieces[0]] + [peer(pieces[i], 2 * i) for i in range(1, middle)]


def body(
    tokens,
    segments,
    query_weight,
    query_bias,
    key_weight,
    value_weight,
    value_bias,
    output_weight,
    output_bias,
    first_gain,
    first_shift,
    expand_weight,
    expand_bias,
    reduce_weight,
    reduce_bias,
    second_gain,
    second_shift,
    cotangent,
):
    batch, rows, width = tokens.shape
    count, depth = lax.axis_size("ctx"), lax.axis_size("fsdp")
    me, my_shard = lax.axis_index("ctx"), lax.axis_index("fsdp")
    me_array = me.astype(jnp.int32).reshape(1)
    shard = query_weight.shape[0]
    hidden = expand_weight.shape[1]
    own_width = width // count
    heads = own_width // HEAD
    piece = hidden // depth // count
    block = depth * piece
    middle = count // 2
    order = plane_order()
    evens, odds = order[:middle], order[middle:]
    scale = HEAD**-0.5
    bits = (count * rows - 1).bit_length()
    all_rows = batch * rows

    columns = lambda w: lax.dynamic_slice_in_dim(w, me * own_width, own_width, 1).astype(BF)
    names = (query_bias, value_bias, output_bias, first_gain, first_shift, reduce_bias, second_gain, second_shift)
    packed = jnp.concatenate(names + (expand_bias,))
    size = packed.shape[0]
    terms = jnp.concatenate(in_terms(packed, 3))
    line = 3 * own_width
    lines = -(-terms.shape[0] // (16 * line)) * 16
    terms = jnp.pad(terms, (0, lines * line - terms.shape[0])).reshape(lines, line)
    own_heads = jnp.concatenate([columns(query_weight), columns(key_weight), columns(value_weight)], axis=1)
    shard_parts = gather_doubling(jnp.concatenate([own_heads, terms], axis=0))

    def plane(value, *needed):
        first, second = after((peer(value, 2), peer(value, 4)), *needed)
        part = value.shape[0] // 2
        return first, second, (peer(first[:part], 4), peer(second[part:], 2))

    def chip(blocks):
        return blocks + [jax.tree.map(lambda v: peer(v, 1), b) for b in blocks]

    def direct(value):
        return [value] + [peer(value, k) for k in evens[1:]]

    low_in = []
    for s in range(batch):
        numbers = jnp.concatenate([segments[s] // 64, segments[s] % 64]).astype(BF)
        numbers = jnp.pad(numbers[None], ((0, EXTRA - 1), (0, width - 2 * rows)))
        low_in.append(jnp.concatenate([tokens[s].astype(BF), numbers], axis=0))

    reduce_blocks = [lax.dynamic_slice_in_dim(reduce_weight, (me ^ k) * piece, piece, 0).astype(BF) for k in evens]
    reduce_blocks = jnp.stack(reduce_blocks)

    first_got, shard_parts, low_in, reduce_blocks = join(direct(low_in[0]), shard_parts, low_in, reduce_blocks)
    first_blocks = chip(first_got)
    own_heads = by_owner([shard_parts[j : j + 1] for j in range(depth)], 0, list(range(depth)), "fsdp")
    packed = own_heads[:, shard:].reshape(depth, lines * line)[:, : 3 * size]
    packed = jnp.sum(packed.reshape(depth, 3, -1).astype(F32), axis=1)
    own_heads = own_heads[:, :shard].reshape(width, line)
    (bias_query, bias_value, bias_output, gain_first, shift_first, bias_reduce, gain_second, shift_second) = (
        packed[:, i * shard : (i + 1) * shard].reshape(width) for i in range(len(names))
    )
    wide_bias = packed[:, len(names) * shard :].reshape(depth, count, piece)
    bias_halves = [
        jnp.stack([lax.dynamic_index_in_dim(wide_bias, me ^ k, 1, keepdims=False).reshape(1, block) for k in ks])
        for ks in (evens, odds)
    ]
    own_part = lambda v: lax.dynamic_slice_in_dim(v, me * own_width, own_width, 0)
    head_bias = jnp.concatenate([own_part(bias_query), jnp.zeros((own_width,), F32), own_part(bias_value)])
    head_scale = jnp.concatenate([jnp.full((own_width,), scale * LOG2E, F32), jnp.ones((2 * own_width,), F32)])

    thin = shard // count
    folds = width // block
    strip = lax.dynamic_slice_in_dim(output_weight, me * thin, thin, 0).astype(BF)
    strip = jnp.concatenate([strip[:, i * block : (i + 1) * block] for i in range(folds)], axis=0)
    block_expand = [
        lax.dynamic_slice_in_dim(expand_weight, (z * count + me) * piece, piece, 1).astype(BF) for z in range(depth)
    ]
    block_expand = jnp.concatenate([jnp.concatenate(block_expand, axis=1), strip], axis=0)
    block_expand = lax.all_gather(after(block_expand, first_got[1]), "fsdp", axis=0)

    halfway = count * rows // 2
    heads_across = own_heads.T
    first_qkv, *first_masks = project(first_blocks, rows, own_heads, head_bias, head_scale, bits)
    first_out, first_lse, second_got = join(
        *attend(first_qkv, *first_masks, heads, rows), direct(low_in[1])
    )
    second_blocks = chip(second_got)
    (second_qkv, *second_masks), other_out = join(
        project(second_blocks, rows, own_heads, head_bias, head_scale, bits), peer(first_out[halfway:], 1)
    )

    reduce_own = lax.all_gather(after(reduce_blocks, second_got[1]), "fsdp", axis=0)
    second_out, second_lse, first_pieces, near = join(
        *attend(second_qkv, *second_masks, heads, rows),
        even_pieces(first_out[:halfway], other_out),
        (block_expand, peer(block_expand, 2), peer(block_expand, 4)),
    )
    part = depth // 2
    far = peer(near[1][:part], 4), peer(near[2][part:], 2)
    far, other_out, near_other = join(far, peer(second_out[halfway:], 1), [peer(v, 1) for v in near])
    got_expand = [*((v,) for v in near), far, *((v,) for v in near_other), tuple(peer(v, 1) for v in far)]
    full_output = assemble_output(got_expand, shard, thin, me_array)
    second_pieces = even_pieces(second_out[:halfway], other_out)
    kept = [
        (first_blocks, first_qkv, *first_masks, first_out, first_lse),
        (second_blocks, second_qkv, *second_masks, second_out, second_lse),
    ]

    earlier = None
    for s, pieces in enumerate((first_pieces, second_pieces)):
        earlier = branch(s, me_array, pieces, full_output, tokens, bias_output, gain_first, shift_first, earlier)
    context_low, hidden_in, hidden_low, normed_first, inverse_first = (
        v.reshape(all_rows, v.shape[2]) for v in earlier
    )

    hidden_low, reduce_own = join(hidden_low, reduce_own)
    (
        (act_even, act_odd, de_even, de_odd, sums_even, sums_odd, result, dr, grad_pre, da, sums_second, sums_first),
        other_low,
        other_context,
    ) = join(
        feed(
            hidden_low,
            inverse_first,
            bias_halves,
            bias_reduce,
            gain_second,
            shift_second,
            gain_first,
            hidden_in,
            cotangent.reshape(all_rows, width),
            normed_first,
            [reduce_own, peer(reduce_own, 1)],
            got_expand,
            shard,
        ),
        peer(hidden_low, 1),
        peer(context_low, 1),
    )

    vectors = (sums_first[2], sums_first[0], sums_first[1], sums_second[2], sums_second[0], sums_second[1])
    wide_bias = by_owner(
        [sums[i, 0].reshape(depth, 1, piece) for sums in (sums_even, sums_odd) for i in range(middle)], 1
    ).reshape(depth, hidden // depth)
    small = jnp.concatenate([v.reshape(depth, shard) for v in vectors] + [wide_bias], axis=1)
    share = -(-small.shape[1] // (count * LANES)) * LANES
    small = jnp.pad(small, ((0, 0), (0, share * count - small.shape[1])))
    da, de_even, de_odd, act_even, dr, small, own_grads, other_grads, other_act, other_dr = join(
        da,
        de_even,
        de_odd,
        act_even,
        dr,
        small,
        *context_back(me_array, da, full_output, own_width, middle),
        peer(act_odd, 1),
        peer(dr, 1),
    )

    sum_reduce, de_even, da, small, other_grads, other_de, other_da, other_small = join(
        reduce_gradient(act_even, other_act, dr, other_dr, depth, piece),
        de_even,
        da,
        small,
        peer(other_grads, 1),
        peer(de_odd, 1),
        peer(da, 1),
        peer(small, 1),
    )
    sum_reduce = lax.psum_scatter(sum_reduce, "fsdp", scatter_dimension=0, tiled=False)

    sums, dc = join(
        expand_gradient(
            me_array,
            hidden_low,
            other_low,
            context_low,
            other_context,
            de_even,
            other_de,
            da,
            other_da,
            small + other_small,
            own_width,
        ),
        even_pieces(own_grads, other_grads),
    )
    kept_a, sent_a, kept_b, sent_b = sums

    add = lambda a, b: (a.astype(F32) + b.astype(F32)).astype(BF)
    to_owner = lambda parts, count=middle: [parts[0]] + [peer(parts[i], 2 * i) for i in range(1, count)]

    def back(s, dc, part=None, before=None):
        _, qkv, mask_q, mask_k, out, lse = kept[s]
        return attend_back(qkv, mask_q, mask_k, dc, out, lse, heads, rows, part, before, s)

    first_grads = back(0, dc)
    first_grads, odd, got_a, got_b = join(
        first_grads, input_part(first_grads, heads_across, 1), peer(sent_a, 4), peer(sent_b, 2)
    )
    kept_a, sent_a, kept_b, sent_b = add_steps(kept_a, got_a, kept_b, got_b)
    before = heads_gradient(kept[0][0], first_grads)
    home, before, dc = join(input_part(first_grads, heads_across, 0, peer(odd, 1), middle), before, dc)
    upper, got_a, got_b, last_step, home = join(
        back(1, dc, 0), peer(sent_a, 2), peer(sent_b, 4), peer(home[-1], 2 * (middle - 1)), home[:-1]
    )
    upper, sum_expand, sum_reduce = join(upper, add_last(kept_a, got_a, kept_b, got_b), sum_reduce)
    sum_expand = lax.psum_scatter(sum_expand, "fsdp", scatter_dimension=0, tiled=True)
    second_grads, from_first, got_reduce = join(
        back(1, dc, 1, upper), to_owner(home, middle - 1) + [last_step], to_owner(sum_reduce)
    )
    sum_reduce = sum(v.astype(F32) for v in got_reduce).astype(BF)

    (shard_got, shard_sent), second_grads, sum_reduce = join(
        heads_gradient(kept[1][0], second_grads, (my_shard.astype(jnp.int32).reshape(1), *before), depth),
        second_grads,
        sum_reduce,
    )
    wide_expand = lax.all_gather(after(sum_expand, shard_got), "ctx", axis=0)
    odd = input_part(second_grads, heads_across, 1)
    away, got, got_reduce, second_grads = join(
        peer(odd, 1), exchange(shard_sent, "fsdp", depth // 2), direct(sum_reduce), second_grads
    )
    shard_got = add(shard_got, got)
    step = depth // 4
    home, got_reduce = join(input_part(second_grads, heads_across, 0, away, middle), chip(got_reduce))
    home_heads = add(shard_got[:step], exchange(shard_got[step:], "fsdp", step))[0]
    tail = home_heads[shard].astype(F32) + home_heads[shard + 1].astype(F32)
    home_heads = jnp.concatenate(
        [home_heads[:shard]] + [v[None] for v in in_terms(tail, 2)] + [jnp.zeros((14, line), BF)], axis=0
    )
    from_second, from_first, heads_got, grad_reduce_weight, unpacked = join(
        to_owner(home),
        from_first,
        [home_heads, peer(home_heads, 2), peer(home_heads, 4)],
        unpack_reduce(me_array, got_reduce),
        unpack_expand(wide_expand, depth, hidden, width, share),
    )
    grad_expand_weight, grad_output_weight, small_sum = unpacked
    last_head, near_heads, grad_in = join(
        peer(heads_got[0], 2 * (middle - 1)),
        [peer(v, 1) for v in heads_got],
        input_sum(grad_pre, from_first, from_second),
    )
    heads_got = [*heads_got, last_head, *near_heads, peer(last_head, 1)]
    small_sum = small_sum.reshape(-1)
    grad_query_weight, grad_key_weight, grad_value_weight, wide_biases = unpack_heads(
        jnp.stack([me, my_shard]).astype(jnp.int32), heads_got, shard, width
    )

    vec = [small_sum[i * shard : (i + 1) * shard] for i in range(len(vectors))]
    vec_expand = small_sum[len(vectors) * shard : len(vectors) * shard + hidden // depth]
    return (
        result.reshape(batch, rows, width),
        grad_in,
        grad_query_weight,
        wide_biases[0],
        grad_key_weight,
        grad_value_weight,
        wide_biases[2],
        grad_output_weight,
        vec[0],
        vec[1],
        vec[2],
        grad_expand_weight,
        vec_expand,
        grad_reduce_weight,
        vec[3],
        vec[4],
        vec[5],
    )


def solution(mesh):
    seq = P("fsdp", "ctx", None)
    mat = P("fsdp", None)
    vec = P("fsdp")
    in_specs = (
        seq,
        P("fsdp", "ctx"),
        mat,
        vec,
        mat,
        mat,
        vec,
        mat,
        vec,
        vec,
        vec,
        mat,
        vec,
        mat,
        vec,
        vec,
        vec,
        seq,
    )
    out_specs = (seq, seq, mat, vec, mat, mat, vec, mat, vec, vec, vec, mat, vec, mat, vec, vec, vec)
    count, depth = mesh.shape["ctx"], mesh.shape["fsdp"]

    def layer(*args):
        width, hidden = args[0].shape[2], args[11].shape[1]
        piece, own_width = hidden // depth // count, width // count
        tiled = count == 8 and depth == 4 and args[0].shape[0] == 2 and piece % LANES == 0 and own_width == LANES
        tiled = tiled and width // depth // count % 16 == 0
        return (body if tiled else plain_body)(*args)

    return jax.shard_map(layer, mesh=mesh, in_specs=in_specs, out_specs=out_specs, check_vma=False)
```
